32 devices in a mesh: dp: 8 (over z, x), seq: 4 (over y, core).
Axes of the slice: x: 2, y: 2, z: 4, core: 2. Of those that a mesh axis runs over, the one named last changes fastest.
Arguments:
- tokens: bfloat16 [8192, 1024], P(('dp', 'seq')), may hold values from -6 to 6
- cotangent: bfloat16 [8192, 1024], P(('dp', 'seq')), may hold values from -6 to 6
- lengths: int32 [8, 4], P('dp'), may hold values from 1 to 769, 1024 in all within a row
- mix_in: float32 [1024, 3072], P(('dp', 'seq')), may hold values from -0.1875 to 0.1875
- mix_in_rows: float32 [1024], P(('dp', 'seq')), may hold values from 4096 to 393216
- mix_in_cols: float32 [3072], replicated, may hold values from 8192 to 32768
- mix_out: float32 [1024, 1024], P(('dp', 'seq')), may hold values from -0.1875 to 0.1875
- mix_out_rows: float32 [1024], P(('dp', 'seq')), may hold values from 4096 to 393216
- mix_out_cols: float32 [1024], replicated, may hold values from 8192 to 32768
- attn_in: float32 [1024, 2048], P(('dp', 'seq')), may hold values from -0.1875 to 0.1875
- attn_in_rows: float32 [1024], P(('dp', 'seq')), may hold values from 2048 to 196608
- attn_in_cols: float32 [2048], replicated, may hold values from 4096 to 16384
- attn_out: float32 [1024, 1024], P(('dp', 'seq')), may hold values from -1 to 1
- attn_out_rows: float32 [1024], P(('dp', 'seq')), may hold values from 64 to 6144
- attn_out_cols: float32 [1024], replicated, may hold values from 128 to 512
- ffn_in: float32 [2, 2, 1024, 4608], P(None, None, ('dp', 'seq')), may hold values from -0.1875 to 0.1875
- ffn_in_rows: float32 [2, 2, 1024], P(None, None, ('dp', 'seq')), may hold values from 512 to 49152
- ffn_in_cols: float32 [2, 2, 4608], replicated, may hold values from 1024 to 4096
- ffn_out: float32 [2, 4608, 1024], P(None, ('dp', 'seq')), may hold values from -0.09375 to 0.09375
- ffn_out_rows: float32 [2, 4608], P(None, ('dp', 'seq')), may hold values from 1365 to 131072
- ffn_out_cols: float32 [2, 1024], replicated, may hold values from 2730 to 10922
- vectors: float32 [7, 1024], P(None, ('dp', 'seq')), may hold values from -1.8 to 2.5
- vectors_moment: float32 [7, 1024], P(None, ('dp', 'seq')), may hold values from 8192 to 32768
- head_gain: float32 [2, 64], replicated, may hold values from 0.6 to 1.6
- head_moment: float32 [2, 64], replicated, may hold values from 65536 to 262144
Outputs:
- result: bfloat16 [8192, 1024], P(('dp', 'seq'))
- token_grad: float32 [8192, 1024], P(('dp', 'seq'))
- mix_in_grad: float32 [1024, 3072], P(('dp', 'seq'))
- mix_in_rows_new: float32 [1024], P(('dp', 'seq'))
- mix_in_cols_new: float32 [3072], replicated
- mix_in_new: float32 [1024, 3072], P(('dp', 'seq'))
- mix_out_grad: float32 [1024, 1024], P(('dp', 'seq'))
- mix_out_rows_new: float32 [1024], P(('dp', 'seq'))
- mix_out_cols_new: float32 [1024], replicated
- mix_out_new: float32 [1024, 1024], P(('dp', 'seq'))
- attn_in_grad: float32 [1024, 2048], P(('dp', 'seq'))
- attn_in_rows_new: float32 [1024], P(('dp', 'seq'))
- attn_in_cols_new: float32 [2048], replicated
- attn_in_new: float32 [1024, 2048], P(('dp', 'seq'))
- attn_out_grad: float32 [1024, 1024], P(('dp', 'seq'))
- attn_out_rows_new: float32 [1024], P(('dp', 'seq'))
- attn_out_cols_new: float32 [1024], replicated
- attn_out_new: float32 [1024, 1024], P(('dp', 'seq'))
- ffn_in_grad: float32 [2, 2, 1024, 4608], P(None, None, ('dp', 'seq'))
- ffn_in_rows_new: float32 [2, 2, 1024], P(None, None, ('dp', 'seq'))
- ffn_in_cols_new: float32 [2, 2, 4608], replicated
- ffn_in_new: float32 [2, 2, 1024, 4608], P(None, None, ('dp', 'seq'))
- ffn_out_grad: float32 [2, 4608, 1024], P(None, ('dp', 'seq'))
- ffn_out_rows_new: float32 [2, 4608], P(None, ('dp', 'seq'))
- ffn_out_cols_new: float32 [2, 1024], replicated
- ffn_out_new: float32 [2, 4608, 1024], P(None, ('dp', 'seq'))
- vectors_grad: float32 [7, 1024], P(None, ('dp', 'seq'))
- vectors_moment_new: float32 [7, 1024], P(None, ('dp', 'seq'))
- vectors_new: float32 [7, 1024], P(None, ('dp', 'seq'))
- head_grad: float32 [2, 64], replicated
- head_moment_new: float32 [2, 64], replicated
- head_new: float32 [2, 64], replicated
The draws below stay inside these ranges and needn't reach their ends.
Inputs may be any that keep to these rules, and one draw needn't show every extreme that they name: Each row lists, in order, the lengths of the documents packed in that group's 1024 tokens; they sum to 1024, and one of them is 769.
All inputs are finite; a program needn't handle non-finite values.
Results may differ from the reference program's by a relative error of at most 0.025.
The reference program's roundings to bfloat16 on the way count: a program that leaves them out, or rounds other values in their place, can miss the bound.
Values may be sent and summed in bfloat16 or wider, within the bound.
A program may use at most 512 MiB of HBM per device.

```python
import math
import jax
import jax.numpy as jnp
import numpy as np
from jax import lax

D = 1024
FF = 4608
HQ = 16
KVH = 8
HEAD = 64
DOCS = 4
GROUP_TOK = 1024
LONG = 769
TOKENS = 8192
N_DP = 8


def draw_vectors(key, part):
    key = jax.random.fold_in(key, 11)
    gain_key, tap_key = jax.random.split(key)
    ramp = jnp.arange(D, dtype=jnp.float32) / (D - 1)
    bottom, spread = (0.6, 1.2)
    gains = (bottom + spread * ramp)[None, :] * jax.random.uniform(gain_key, (4, D), jnp.float32, 0.8, 1.25)
    taps = 0.6 * jnp.clip(jax.random.normal(tap_key, (3, D), jnp.float32), -3.0, 3.0)
    return jnp.concatenate([gains, taps], axis=0)


def falling_states(key, shape, lower, upper, top, bottom):
    length = shape[-1]
    ramp = jnp.arange(length, dtype=jnp.float32) / (length - 1)
    base = jnp.exp(jax.random.uniform(key, shape, jnp.float32, math.log(lower), math.log(upper)))
    return base * jnp.exp(math.log(top) * (1.0 - ramp) + math.log(bottom) * ramp)


def draw_mix_in_rows(key, part):
    key = jax.random.fold_in(key, 21)
    top, bottom = (6.0, 0.6)
    return falling_states(key, (D,), TOKENS * 1.0, TOKENS * 4.0, top, bottom)


def draw_mix_out_rows(key, part):
    key = jax.random.fold_in(key, 22)
    top, bottom = (6.0, 0.6)
    return falling_states(key, (D,), TOKENS * 1.0, TOKENS * 4.0, top, bottom)


def draw_attn_in_rows(key, part):
    key = jax.random.fold_in(key, 23)
    top, bottom = (6.0, 0.6)
    return falling_states(key, (D,), TOKENS * 0.5, TOKENS * 2.0, top, bottom)


def draw_attn_out_rows(key, part):
    key = jax.random.fold_in(key, 24)
    top, bottom = (6.0, 0.6)
    return falling_states(key, (D,), 16.0 * TOKENS / GROUP_TOK, 64.0 * TOKENS / GROUP_TOK, top, bottom)


def draw_ffn_in_rows(key, part):
    key = jax.random.fold_in(key, 25)
    top, bottom = (6.0, 0.6)
    return falling_states(key, (2, 2, D), TOKENS / 8.0, TOKENS / 2.0, top, bottom)


def draw_ffn_out_rows(key, part):
    key = jax.random.fold_in(key, 26)
    top, bottom = (6.0, 0.6)
    return falling_states(key, (2, FF), TOKENS / 3.0, TOKENS * 4.0 / 3.0, top, bottom)


def steps_of(key, dims, shards, least, largest):
    factor_of, own = 1.0, jax.random.fold_in(key, 6)
    for position, parts in shards:
        draws = jnp.exp(jax.random.uniform(jax.random.fold_in(own, position), (parts,), jnp.float32, least / len(shards), largest / len(shards)))
        factor_of = factor_of * jnp.repeat(draws, dims[position] // parts).reshape([-1 if axis == position else 1 for axis in range(len(dims))])
    return factor_of


def split_up(count, total, bound, lean):
    weights = [(1 << 20) // math.isqrt(grade ** lean) + 1 for grade in range(2, count + 1)]
    spare, counts = total - bound - (count - 1), [1] * (count - 1)
    while spare > 0:
        movable = [i for i in range(count - 1) if counts[i] < bound]
        pool, budget = sum([weights[i] for i in movable]), spare
        for i in movable:
            extra = min(bound - counts[i], max(1, budget * weights[i] // pool), spare)
            counts[i] = counts[i] + extra
            spare = spare - extra
    return np.array([bound] + counts)


def ragged_sizes(key, amount, total, limit, slope):
    if amount == 2:
        one = jax.random.randint(key, (), max(1, total - limit), min(limit, total - 1) + 1)
        return jnp.stack([one, total - one])
    tallies = jnp.asarray(split_up(amount, total, limit, slope), jnp.int32)
    couples = (amount - 1) // 2
    source_of, sink = tallies[1:1 + 2 * couples:2], tallies[2:2 + 2 * couples:2]
    margin = jnp.minimum(source_of - 1, limit - sink)
    moved = jax.random.randint(jax.random.fold_in(key, 1), (couples,), 0, 1 << 20) % (margin + 1)
    tallies = tallies.at[1:1 + 2 * couples:2].set(source_of - moved).at[2:2 + 2 * couples:2].set(sink + moved)
    return tallies[jax.random.permutation(jax.random.fold_in(key, 2), amount)]


def centred(own_key, extent, scale, most, cuts=(), held_as=jnp.bfloat16):
    drawn = jax.random.normal(own_key, extent, jnp.float32) * scale
    if len(cuts) > 0:
        drawn = steps_of(own_key, extent, cuts, -0.22, 0.18) * drawn
    return jnp.clip(drawn, min=-most, max=most).astype(held_as)


def setup_inputs(seed: int = 0) -> dict:
    streams_of = jax.random.split(jax.random.key(seed), 26)
    return {
        "tokens": centred(streams_of[0], (TOKENS, D), 1.0, 6.0, ((0, 32),)),
        "cotangent": centred(streams_of[1], (TOKENS, D), 1.0, 6.0, ((0, 32),)),
        "lengths": jax.vmap(lambda own: ragged_sizes(own, DOCS, GROUP_TOK, LONG, 2))(jax.random.split(streams_of[2], N_DP)).reshape((N_DP, DOCS)).astype(jnp.int32),
        "mix_in": centred(streams_of[3], (D, 3 * D), D ** -0.5, 0.1875, ((0, 32),), jnp.float32),
        "mix_in_rows": draw_mix_in_rows(jax.random.fold_in(streams_of[25], 71), 0),
        "mix_in_cols": jnp.clip(jnp.exp(jax.random.uniform(streams_of[5], (3 * D,), jnp.float32, math.log(8192.0), math.log(32768.0))), 8192.0, 32768.0),
        "mix_out": centred(streams_of[6], (D, D), D ** -0.5, 0.1875, ((0, 32),), jnp.float32),
        "mix_out_rows": draw_mix_out_rows(jax.random.fold_in(streams_of[25], 71), 0),
        "mix_out_cols": jnp.clip(jnp.exp(jax.random.uniform(streams_of[8], (D,), jnp.float32, math.log(8192.0), math.log(32768.0))), 8192.0, 32768.0),
        "attn_in": centred(streams_of[9], (D, 2 * D), D ** -0.5, 0.1875, ((0, 32),), jnp.float32),
        "attn_in_rows": draw_attn_in_rows(jax.random.fold_in(streams_of[25], 71), 0),
        "attn_in_cols": jnp.clip(jnp.exp(jax.random.uniform(streams_of[11], (2 * D,), jnp.float32, math.log(4096.0), math.log(16384.0))), 4096.0, 16384.0),
        "attn_out": centred(streams_of[12], (D, D), (max(1, 32 * D // GROUP_TOK)) ** -0.5, 1.0, ((0, 32),), jnp.float32),
        "attn_out_rows": draw_attn_out_rows(jax.random.fold_in(streams_of[25], 71), 0),
        "attn_out_cols": jnp.clip(jnp.exp(jax.random.uniform(streams_of[14], (D,), jnp.float32, math.log(128.0), math.log(512.0))), 128.0, 512.0),
        "ffn_in": centred(streams_of[15], (2, 2, D, FF), D ** -0.5, 0.1875, ((2, 32),), jnp.float32),
        "ffn_in_rows": draw_ffn_in_rows(jax.random.fold_in(streams_of[25], 71), 0),
        "ffn_in_cols": jnp.clip(jnp.exp(jax.random.uniform(streams_of[17], (2, 2, FF), jnp.float32, math.log(1024.0), math.log(4096.0))), 1024.0, 4096.0),
        "ffn_out": centred(streams_of[18], (2, FF, D), FF ** -0.5, 0.09375, ((1, 32),), jnp.float32),
        "ffn_out_rows": draw_ffn_out_rows(jax.random.fold_in(streams_of[25], 71), 0),
        "ffn_out_cols": jnp.clip(jnp.exp(jax.random.uniform(streams_of[20], (2, D), jnp.float32, math.log(2730.0), math.log(10922.0))), 2730.0, 10922.0),
        "vectors": draw_vectors(jax.random.fold_in(streams_of[25], 71), 0),
        "vectors_moment": jnp.clip(jnp.exp(math.log(32768.0) - 1.3862944 * jax.random.uniform(streams_of[22], (7, D), jnp.float32) ** steps_of(streams_of[22], (7, D), ((1, 32),), -0.2, 0.2)), 8192.0, 32768.0),
        "head_gain": jnp.clip(jax.random.uniform(streams_of[23], (2, HEAD), jnp.float32, 0.6, 1.6), 0.6, 1.6),
        "head_moment": jnp.clip(jnp.exp(jax.random.uniform(streams_of[24], (2, HEAD), jnp.float32, math.log(65536.0), math.log(262144.0))), 65536.0, 262144.0),
    }


@jax.custom_vjp
def low(v):
    return lax.optimization_barrier(v.astype(jnp.bfloat16)).astype(jnp.float32)

@jax.custom_vjp
def low_back(v):
    return v

def low_keep(v):
    return (low(v), None)

def low_pass(kept, grad):
    return (grad,)

def back_keep(v):
    return (v, None)

def back_low(kept, grad):
    return (low(grad),)
low.defvjp(low_keep, low_pass)
low_back.defvjp(back_keep, back_low)
PRECISE = lax.Precision.HIGHEST
EPSILON = 1e-05
SQUARE_FLOOR = 1e-30
DECAY_RATE = 0.5
CLIP_LEVEL = 0.25
STEP_SCALE = 1.0
RATE_FLOOR = 0.001
MASKED_SCORE = -1e+30

def matmul(operand, weight):
    return jnp.dot(operand, weight, preferred_element_type=jnp.float32, precision=PRECISE)

def normalize(values, gain):
    return values * lax.rsqrt(lax.optimization_barrier(jnp.mean(values * values, axis=-1, keepdims=True)) + EPSILON) * gain

def doc_layout(lens, places):
    bounds = jnp.cumsum(lens).astype(jnp.int32)
    passed = bounds[None, :] <= places[:, None]
    docs = lax.optimization_barrier(jnp.sum(passed.astype(jnp.int32), axis=1)).astype(jnp.int32)
    starts = lax.optimization_barrier(jnp.sum(jnp.where(passed, lens[None, :], 0), axis=1)).astype(jnp.int32)
    return (docs, places - starts)

def rotate(values, places):
    half = values.shape[-1] // 2
    freqs = jnp.exp(jnp.arange(half, dtype=jnp.float32) * (-2.0 * math.log(1000000.0) / values.shape[-1]))
    angles = places.astype(jnp.float32)[:, None] * freqs[None, :]
    cosine = jnp.cos(angles)[:, None, :]
    sine = jnp.sin(angles)[:, None, :]
    front = values[..., :half]
    behind = values[..., half:]
    return jnp.concatenate([front * cosine - behind * sine, behind * cosine + front * sine], axis=-1)

def feed_forward(resid, gain, w_in, w_down):
    normed = low(normalize(resid, gain))
    gate = low_back(matmul(normed, w_in[0]))
    upper = low_back(matmul(normed, w_in[1]))
    hidden = low(jax.nn.silu(gate) * upper)
    return resid + low_back(matmul(hidden, w_down))

def attention(q_rot, k_rot, v_low, docs):
    keys_wide = jnp.repeat(k_rot, HQ // KVH, axis=1)
    values_wide = jnp.repeat(v_low, HQ // KVH, axis=1)
    block = min(512, GROUP_TOK)
    places = jnp.arange(GROUP_TOK, dtype=jnp.int32)
    factor = HEAD ** (-0.5)

    def one_block(index):
        begin = index * block
        query_block = lax.dynamic_slice_in_dim(q_rot, begin, block, 0)
        rows = lax.dynamic_slice_in_dim(places, begin, block, 0)
        row_docs = lax.dynamic_slice_in_dim(docs, begin, block, 0)
        allowed = (places[None, :] <= rows[:, None]) & (docs[None, :] == row_docs[:, None])
        scores = low_back(jnp.einsum('qhd,khd->hqk', query_block, keys_wide, precision=PRECISE) * factor)
        scores = jnp.where(allowed[None], scores, MASKED_SCORE)
        peak = lax.optimization_barrier(jnp.max(scores, axis=-1, keepdims=True))
        expo = jnp.exp(scores - peak)
        probs = expo / lax.optimization_barrier(jnp.sum(expo, axis=-1, keepdims=True))
        return jnp.einsum('hqk,khd->qhd', low(probs), values_wide, precision=PRECISE)
    blocks = lax.map(jax.checkpoint(one_block), jnp.arange(GROUP_TOK // block, dtype=jnp.int32))
    return blocks.reshape(GROUP_TOK, HQ, HEAD)

def group_forward(inputs, lens, lowered):
    mix_in, mix_out, attn_in, attn_out, ffn_in, ffn_out, vectors, head_gain = lowered
    docs, positions = doc_layout(lens, jnp.arange(GROUP_TOK, dtype=jnp.int32))
    normed = low(normalize(inputs, vectors[0]))
    projected = low_back(matmul(normed, mix_in))
    part_b = projected[:, :D]
    part_c = projected[:, D:2 * D]
    part_v = projected[:, 2 * D:]
    mixed = low_back(low(part_b * part_v))
    once = (positions >= 1).astype(jnp.float32)[:, None]
    twice = (positions >= 2).astype(jnp.float32)[:, None]
    shift_one = jnp.concatenate([jnp.zeros((1, D), jnp.float32), mixed[:-1]], axis=0)
    shift_two = jnp.concatenate([jnp.zeros((2, D), jnp.float32), mixed[:-2]], axis=0)
    conv = vectors[6] * mixed + vectors[5] * shift_one * once + vectors[4] * shift_two * twice
    gated = low(part_c * conv)
    first = inputs + low_back(matmul(gated, mix_out))
    second = feed_forward(first, vectors[1], ffn_in[0], ffn_out[0])
    normed_three = low(normalize(second, vectors[2]))
    projected_three = low_back(matmul(normed_three, attn_in))
    kv_width = KVH * HEAD
    queries = projected_three[:, :D].reshape(GROUP_TOK, HQ, HEAD)
    keys = projected_three[:, D:D + kv_width].reshape(GROUP_TOK, KVH, HEAD)
    values = projected_three[:, D + kv_width:].reshape(GROUP_TOK, KVH, HEAD)
    q_rot = low_back(low(rotate(normalize(queries, head_gain[0]), positions)))
    k_rot = low_back(low(rotate(normalize(keys, head_gain[1]), positions)))
    v_low = low_back(low(values))
    attended = low_back(low(attention(q_rot, k_rot, v_low, docs))).reshape(GROUP_TOK, D)
    third = second + low_back(matmul(attended, attn_out))
    return feed_forward(third, vectors[3], ffn_in[1], ffn_out[1])

def factored(grad, weight, rows, cols):
    squares = grad * grad + SQUARE_FLOOR
    rows_new = DECAY_RATE * rows + (1.0 - DECAY_RATE) * lax.optimization_barrier(jnp.mean(squares, axis=-1))
    cols_new = DECAY_RATE * cols + (1.0 - DECAY_RATE) * lax.optimization_barrier(jnp.mean(squares, axis=-2))
    second = rows_new[..., :, None] * cols_new[..., None, :] / lax.optimization_barrier(jnp.mean(rows_new, axis=-1))[..., None, None]
    update = grad / jnp.sqrt(second)
    divisor = jnp.maximum(1.0, jnp.sqrt(lax.optimization_barrier(jnp.mean(update * update, axis=(-2, -1)))) / CLIP_LEVEL)
    rate = STEP_SCALE * jnp.maximum(RATE_FLOOR, jnp.sqrt(lax.optimization_barrier(jnp.mean(weight * weight, axis=(-2, -1)))))
    return (grad, rows_new, cols_new, weight - (rate / divisor)[..., None, None] * update)

def plain_update(grad, param, moment):
    moment_new = DECAY_RATE * moment + (1.0 - DECAY_RATE) * (grad * grad + SQUARE_FLOOR)
    update = grad * lax.rsqrt(moment_new)
    divisor = jnp.maximum(1.0, jnp.sqrt(lax.optimization_barrier(jnp.mean(update * update, axis=-1, keepdims=True))) / CLIP_LEVEL)
    rate = STEP_SCALE * jnp.maximum(RATE_FLOOR, jnp.sqrt(lax.optimization_barrier(jnp.mean(param * param, axis=-1, keepdims=True))))
    return (grad, moment_new, param - rate / divisor * update)

def reference(tokens, cotangent, lengths, mix_in, mix_in_rows, mix_in_cols, mix_out, mix_out_rows, mix_out_cols, attn_in, attn_in_rows, attn_in_cols, attn_out, attn_out_rows, attn_out_cols, ffn_in, ffn_in_rows, ffn_in_cols, ffn_out, ffn_out_rows, ffn_out_cols, vectors, vectors_moment, head_gain, head_moment):
    params = (mix_in, mix_out, attn_in, attn_out, ffn_in, ffn_out, vectors, head_gain)

    def forward(inputs, weights):
        lowered = jax.tree.map(low, weights)
        grouped = inputs.reshape(N_DP, GROUP_TOK, D)

        def run(both):
            return group_forward(both[0], both[1], lowered)
        outputs = lax.map(jax.checkpoint(run), (grouped, lengths))
        return outputs.reshape(TOKENS, D)
    result, pullback = jax.vjp(forward, tokens.astype(jnp.float32), params)
    token_grad, grads = pullback(cotangent.astype(jnp.float32))
    first_in = factored(grads[0], mix_in, mix_in_rows, mix_in_cols)
    first_out = factored(grads[1], mix_out, mix_out_rows, mix_out_cols)
    second_in = factored(grads[2], attn_in, attn_in_rows, attn_in_cols)
    second_out = factored(grads[3], attn_out, attn_out_rows, attn_out_cols)
    forward_in = factored(grads[4], ffn_in, ffn_in_rows, ffn_in_cols)
    forward_out = factored(grads[5], ffn_out, ffn_out_rows, ffn_out_cols)
    vector_step = plain_update(grads[6], vectors, vectors_moment)
    head_step = plain_update(grads[7], head_gain, head_moment)
    return (result.astype(jnp.bfloat16), token_grad, first_in[0], first_in[1], first_in[2], first_in[3], first_out[0], first_out[1], first_out[2], first_out[3], second_in[0], second_in[1], second_in[2], second_in[3], second_out[0], second_out[1], second_out[2], second_out[3], forward_in[0], forward_in[1], forward_in[2], forward_in[3], forward_out[0], forward_out[1], forward_out[2], forward_out[3], vector_step[0], vector_step[1], vector_step[2], head_step[0], head_step[1], head_step[2])
```

```python
import math

import jax
import jax.numpy as jnp
from jax import lax
from jax.sharding import PartitionSpec as P

HQ = 16
KVH = 8
HEAD = 64

EPSILON = 1e-05
SQUARE_FLOOR = 1e-30
DECAY_RATE = 0.5
CLIP_LEVEL = 0.25
STEP_SCALE = 1.0
RATE_FLOOR = 0.001
MASKED_SCORE = -1e30


def matmul(operand, weight):
    return jnp.dot(operand, weight, preferred_element_type=jnp.float32)


def contract_first(operand, other):
    return lax.dot_general(
        operand, other, (((0,), (0,)), ((), ())), preferred_element_type=jnp.float32
    )


def contract_last(operand, other):
    return lax.dot_general(
        operand,
        other,
        (((operand.ndim - 1,), (other.ndim - 1,)), ((), ())),
        preferred_element_type=jnp.float32,
    )


def to_low(values):
    return values.astype(jnp.bfloat16)


def normalize(values, gain):
    scale = lax.rsqrt(jnp.mean(values * values, axis=-1, keepdims=True) + EPSILON)
    return (values * scale * gain, scale)


def normalize_back(grad_out, values, scale, gain):
    unit = values * scale
    grad_gain = jnp.sum(grad_out * unit, axis=tuple(range(values.ndim - 1)))
    weighted = grad_out * gain
    grad_values = scale * (weighted - unit * jnp.mean(weighted * unit, axis=-1, keepdims=True))
    return (grad_values, grad_gain)


def doc_layout(lens, places):
    bounds = jnp.cumsum(lens)
    passed = bounds[None, :] <= places[:, None]
    docs = jnp.sum(passed.astype(jnp.int32), axis=1)
    starts = jnp.sum(jnp.where(passed, lens[None, :], 0), axis=1)
    return (docs, places - starts)


def angles_for(places, width):
    half = width // 2
    freqs = jnp.exp(jnp.arange(half, dtype=jnp.float32) * (-2.0 * math.log(1000000.0) / width))
    angles = places.astype(jnp.float32)[:, None] * freqs[None, :]
    return (jnp.cos(angles)[:, None, :], jnp.sin(angles)[:, None, :], half)


def rotate(values, angles):
    cosine, sine, half = angles
    front = values[..., :half]
    behind = values[..., half:]
    return jnp.concatenate(
        [front * cosine - behind * sine, behind * cosine + front * sine], axis=-1
    )


def rotate_back(grads, angles):
    cosine, sine, half = angles
    front = grads[..., :half]
    behind = grads[..., half:]
    return jnp.concatenate(
        [front * cosine + behind * sine, behind * cosine - front * sine], axis=-1
    )


def swap(value, axis, mask):
    count = lax.axis_size(axis)
    return lax.ppermute(value, axis, [(place, place ^ mask) for place in range(count)])


def bits_of(axis):
    return lax.axis_size(axis).bit_length() - 1


def relative_masks(axis):
    masks = [0]
    for bit in reversed(range(bits_of(axis))):
        masks = masks + [mask ^ (1 << bit) for mask in masks]
    return masks


def gather_tokens(value):
    held = value[None]
    for bit in reversed(range(bits_of("seq"))):
        held = jnp.concatenate([held, swap(held, "seq", 1 << bit)], axis=0)
    return held.reshape((-1,) + value.shape[1:])


def scatter_tokens(partial):
    count = lax.axis_size("seq")
    held = partial.reshape(count, partial.shape[0] // count, partial.shape[1])
    for bit in range(bits_of("seq")):
        half = held.shape[0] // 2
        sent = held[half:]
        if bit > 0:
            sent = to_low(sent)
        held = held[:half] + swap(sent, "seq", 1 << bit).astype(jnp.float32)
    return held[0]


def trade(chunks, axis):
    here = lax.axis_index(axis)
    out = chunks
    for mask in relative_masks(axis):
        place = here ^ mask
        chunk = lax.dynamic_index_in_dim(chunks, place, 0, keepdims=True)
        if mask:
            chunk = swap(chunk, axis, mask)
        out = lax.dynamic_update_slice_in_dim(out, chunk, place, 0)
    return out


def gather_rows(shard):
    here = lax.axis_index("dp")
    count = lax.axis_size("dp")
    held = shard[None]
    masks = relative_masks("dp")
    bits = list(reversed(range(bits_of("dp"))))
    for bit in bits[:-1]:
        held = jnp.concatenate([held, swap(held, "dp", 1 << bit)], axis=0)
    other = swap(held, "dp", 1 << bits[-1])
    out = jnp.zeros((count,) + shard.shape, shard.dtype)
    half = count // 2
    for place, mask in enumerate(masks):
        source = held if place < half else other
        out = lax.dynamic_update_slice_in_dim(
            out, source[place % half][None], here ^ mask, 0
        )
    return out.reshape((-1,) + shard.shape[1:])


def my_bit(axis, bit):
    return (lax.axis_index(axis) >> bit) & 1


def reduce_rows(mine, other):
    held = mine + swap(other, "dp", 1)
    for bit in range(1, bits_of("dp")):
        pairs = held.reshape((held.shape[0] // 2, 2) + held.shape[1:])
        own = my_bit("dp", bit)
        kept = lax.dynamic_index_in_dim(pairs, own, 1, keepdims=False)
        sent = lax.dynamic_index_in_dim(pairs, 1 - own, 1, keepdims=False)
        held = kept + swap(sent, "dp", 1 << bit)
    return held[0]


def reduce_natural(grad):
    count = lax.axis_size("dp")
    pairs = grad.reshape(count // 2, 2, grad.shape[0] // count, grad.shape[1])
    own = my_bit("dp", 0)
    return reduce_rows(
        lax.dynamic_index_in_dim(pairs, own, 1, keepdims=False),
        lax.dynamic_index_in_dim(pairs, 1 - own, 1, keepdims=False),
    )


def reduce_columns(operand, grad):
    count = lax.axis_size("dp")
    depth = operand.shape[1] // count
    blocks = [operand[:, place * depth : (place + 1) * depth] for place in range(count)]
    even = jnp.concatenate(blocks[0::2], axis=1)
    odd = jnp.concatenate(blocks[1::2], axis=1)
    own = my_bit("dp", 0) == 1
    mine = jnp.where(own, odd, even)
    other = jnp.where(own, even, odd)
    shape = (count // 2, depth, grad.shape[1])
    return reduce_rows(
        contract_first(mine, grad).reshape(shape), contract_first(other, grad).reshape(shape)
    )


def moved_to_rank(shard):
    seq, dp = lax.axis_size("seq"), lax.axis_size("dp")
    pairs = [
        (block, (block % dp) * seq + block // dp) for block in range(seq * dp)
    ]
    return lax.ppermute(shard, ("dp", "seq"), pairs)


def moved_to_owner(shard):
    seq, dp = lax.axis_size("seq"), lax.axis_size("dp")
    pairs = [
        ((block % dp) * seq + block // dp, block) for block in range(seq * dp)
    ]
    return lax.ppermute(shard, ("dp", "seq"), pairs)


def total(values):
    sizes = [value.size for value in values]
    flat = jnp.concatenate([value.reshape(-1) for value in values])
    padded = -flat.shape[0] % 1024
    flat = jnp.pad(flat, (0, padded)).reshape(-1, 128)
    for axis in ("seq", "dp"):
        for bit in range(bits_of(axis)):
            flat = flat + swap(flat, axis, 1 << bit)
    flat = flat.reshape(-1)
    out, begin = [], 0
    for value, size in zip(values, sizes):
        out.append(flat[begin : begin + size].reshape(value.shape))
        begin += size
    return out


def split_columns(weight, widths):
    count = lax.axis_size("seq")
    low = to_low(weight)
    parts, begin = [], 0
    for width in widths:
        each = width // count
        part = low[..., begin : begin + width].reshape(low.shape[:-1] + (count, each))
        parts.append(part)
        begin += width
    joined = parts[0] if len(parts) == 1 else jnp.concatenate(parts, axis=-1)
    return jnp.moveaxis(joined, -2, 0)


def join_columns(chunks, widths):
    count = lax.axis_size("seq")
    parts, begin = [], 0
    for width in widths:
        each = width // count
        part = jnp.moveaxis(chunks[..., begin : begin + each], 0, -2)
        parts.append(part.reshape(part.shape[:-2] + (width,)))
        begin += each
    return parts[0] if len(parts) == 1 else jnp.concatenate(parts, axis=-1)


def gather_in(weight, widths):
    chunks = trade(split_columns(weight, widths), "seq")
    return gather_rows(chunks.reshape(-1, chunks.shape[-1]))


def gather_out(weight):
    return gather_rows(moved_to_rank(to_low(weight)))


def owner_in(block, widths):
    count = lax.axis_size("seq")
    chunks = trade(block.reshape(count, block.shape[0] // count, block.shape[1]), "seq")
    return join_columns(chunks, widths)


def feed_forward(resid, gain, w_in, w_down):
    normed, scale = normalize(resid, gain)
    normed_all = gather_tokens(to_low(normed))
    both = matmul(normed_all, w_in)
    half = both.shape[1] // 2
    gate, upper = both[:, :half], both[:, half:]
    hidden_low = to_low(jax.nn.silu(gate) * upper)
    return (
        resid + scatter_tokens(matmul(hidden_low, w_down)),
        (normed_all, scale, gate, upper, hidden_low),
    )


def feed_back(grad_resid, grad_all, resid, kept, gain, w_in, w_down):
    normed_all, scale, gate, upper, hidden_low = kept
    grad_hidden = contract_last(grad_all, w_down)
    sigma = jax.nn.sigmoid(gate)
    grad_gate = to_low(grad_hidden * upper * (sigma * (1.0 + gate * (1.0 - sigma))))
    grad_upper = to_low(grad_hidden * (gate * sigma))
    grad_both = jnp.concatenate([grad_gate, grad_upper], axis=1)
    grad_normed = scatter_tokens(contract_last(grad_both, w_in))
    grad_in = reduce_columns(normed_all, grad_both)
    grad_down = reduce_natural(contract_first(hidden_low, grad_all))
    grad_branch, grad_gain = normalize_back(grad_normed, resid, scale, gain)
    return (grad_resid + grad_branch, grad_in, grad_down, grad_gain)


def attend(q_rot, k_rot, values, allowed):
    factor = HEAD ** (-0.5)
    scores = (
        jnp.einsum("qjhd,kjd->jhqk", q_rot, k_rot, preferred_element_type=jnp.float32) * factor
    )
    scores = jnp.where(allowed[None, None], scores, MASKED_SCORE)
    peak = jnp.max(scores, axis=-1, keepdims=True)
    expo = jnp.exp(scores - peak)
    count = jnp.sum(expo, axis=-1, keepdims=True)
    output = jnp.einsum(
        "jhqk,kjd->qjhd", to_low(expo / count), values, preferred_element_type=jnp.float32
    )
    return (to_low(output), peak + jnp.log(count))


def attend_back(q_rot, k_rot, values, lse, grad, allowed):
    factor = HEAD ** (-0.5)
    scores = (
        jnp.einsum("qjhd,kjd->jhqk", q_rot, k_rot, preferred_element_type=jnp.float32) * factor
    )
    scores = jnp.where(allowed[None, None], scores, MASKED_SCORE)
    probs = jnp.exp(scores - lse)
    grad_probs = jnp.einsum("qjhd,kjd->jhqk", grad, values, preferred_element_type=jnp.float32)
    row_dot = jnp.sum(probs * grad_probs, axis=-1, keepdims=True)
    grad_scores = to_low(probs * (grad_probs - row_dot))
    grad_q = (
        jnp.einsum("jhqk,kjd->qjhd", grad_scores, k_rot, preferred_element_type=jnp.float32)
        * factor
    )
    grad_k = (
        jnp.einsum("jhqk,qjhd->kjd", grad_scores, q_rot, preferred_element_type=jnp.float32)
        * factor
    )
    grad_v = jnp.einsum(
        "jhqk,qjhd->kjd", to_low(probs), grad, preferred_element_type=jnp.float32
    )
    return (to_low(grad_q), to_low(grad_k), to_low(grad_v))


def body(
    tokens,
    cotangent,
    lengths,
    mix_in,
    mix_in_rows,
    mix_in_cols,
    mix_out,
    mix_out_rows,
    mix_out_cols,
    attn_in,
    attn_in_rows,
    attn_in_cols,
    attn_out,
    attn_out_rows,
    attn_out_cols,
    ffn_in,
    ffn_in_rows,
    ffn_in_cols,
    ffn_out,
    ffn_out_rows,
    ffn_out_cols,
    vectors,
    vectors_moment,
    head_gain,
    head_moment,
):
    rows_here, width = tokens.shape
    seq_count = lax.axis_size("seq")
    devices = lax.axis_size("dp") * seq_count
    here = lax.axis_index("seq")
    masks = relative_masks("seq")
    ranks = jnp.asarray([masks.index(place) for place in range(seq_count)], jnp.int32)
    blocks = here ^ jnp.asarray(masks, jnp.int32)
    places = (
        blocks[:, None] * rows_here + jnp.arange(rows_here, dtype=jnp.int32)[None, :]
    ).reshape(-1)
    docs, positions = doc_layout(lengths[0], places)
    allowed = (places[None, :] <= places[:, None]) & (docs[None, :] == docs[:, None])
    once = (positions >= 1).astype(jnp.float32).reshape(seq_count, rows_here, 1)
    twice = (positions >= 2).astype(jnp.float32).reshape(seq_count, rows_here, 1)
    channels = width // seq_count
    heads = HQ // seq_count
    kv_heads = KVH // seq_count
    kv_width = KVH * HEAD
    hidden = ffn_in.shape[-1]

    gains = lax.all_gather(to_low(vectors), ("dp", "seq"), axis=1, tiled=True).astype(jnp.float32)
    head_gains = to_low(head_gain).astype(jnp.float32)
    taps = lax.dynamic_slice_in_dim(gains[4:7], here * channels, channels, 1)
    tokens_all = gather_tokens(tokens)
    mix_widths = (width, width, width)
    attn_widths = (width, kv_width, kv_width)

    def pair_in(layer):
        chunks = split_columns(ffn_in[layer], (hidden,))
        chunks = trade(jnp.concatenate([chunks[:, 0], chunks[:, 1]], axis=-1), "seq")
        return gather_rows(chunks.reshape(-1, chunks.shape[-1]))

    w_mix_in = gather_in(mix_in, mix_widths)
    w_mix_out = gather_out(mix_out)
    w_in_one = pair_in(0)
    w_down_one = gather_out(ffn_out[0])
    w_attn_in = gather_in(attn_in, attn_widths)
    w_attn_out = gather_out(attn_out)
    w_in_two = pair_in(1)
    w_down_two = gather_out(ffn_out[1])

    inputs = tokens.astype(jnp.float32)
    scale_one = normalize(inputs, gains[0])[1]
    low_one = to_low(normalize(tokens_all.astype(jnp.float32), gains[0])[0])
    projected = matmul(low_one, w_mix_in)
    part_b = projected[:, :channels]
    part_c = projected[:, channels : 2 * channels]
    part_v = projected[:, 2 * channels :]
    mixed = to_low(part_b * part_v).reshape(seq_count, rows_here, channels)
    before = jnp.take(ranks, ((blocks - 1) % seq_count) ^ here)
    rims = jnp.take(mixed[:, rows_here - 2 :], before, axis=0)
    extended = jnp.concatenate([rims, mixed], axis=1).astype(jnp.float32)
    conv = (
        taps[2] * extended[:, 2:]
        + taps[1] * extended[:, 1:-1] * once
        + taps[0] * extended[:, :-2] * twice
    ).reshape(-1, channels)
    gated = to_low(part_c * conv)
    first = inputs + scatter_tokens(matmul(gated, w_mix_out))
    second, kept_one = feed_forward(first, gains[1], w_in_one, w_down_one)

    normed_three, scale_three = normalize(second, gains[2])
    low_three = gather_tokens(to_low(normed_three))
    projected_three = matmul(low_three, w_attn_in)
    total_rows = rows_here * seq_count
    q_width, k_width = heads * HEAD, kv_heads * HEAD
    queries = projected_three[:, :q_width].reshape(total_rows, heads, HEAD)
    keys = projected_three[:, q_width : q_width + k_width].reshape(total_rows, kv_heads, HEAD)
    values = projected_three[:, q_width + k_width :].reshape(total_rows, kv_heads, HEAD)
    angles = angles_for(positions, HEAD)
    q_normed, q_scale = normalize(queries, head_gains[0])
    k_normed, k_scale = normalize(keys, head_gains[1])
    q_rot = to_low(rotate(q_normed, angles)).reshape(total_rows, kv_heads, heads // kv_heads, HEAD)
    k_rot = to_low(rotate(k_normed, angles))
    v_low = to_low(values)
    attended, lse = attend(q_rot, k_rot, v_low, allowed)
    attended = attended.reshape(total_rows, q_width)
    third = second + scatter_tokens(matmul(attended, w_attn_out))
    fourth, kept_two = feed_forward(third, gains[3], w_in_two, w_down_two)

    cotangent_all = gather_tokens(cotangent)
    grad_third, grad_in_two, grad_down_two, grad_gain_three = feed_back(
        cotangent.astype(jnp.float32), cotangent_all, third, kept_two, gains[3], w_in_two, w_down_two
    )
    branch_all = gather_tokens(to_low(grad_third))
    grad_attended = to_low(contract_last(branch_all, w_attn_out)).reshape(q_rot.shape)
    grad_attn_out = reduce_natural(contract_first(attended, branch_all))
    grad_q, grad_k, grad_v = attend_back(q_rot, k_rot, v_low, lse, grad_attended, allowed)
    grad_q = rotate_back(grad_q.reshape(queries.shape).astype(jnp.float32), angles)
    grad_k = rotate_back(grad_k.astype(jnp.float32), angles)
    grad_queries, grad_head_q = normalize_back(grad_q, queries, q_scale, head_gains[0])
    grad_keys, grad_head_k = normalize_back(grad_k, keys, k_scale, head_gains[1])
    grad_projected = jnp.concatenate(
        [
            to_low(grad_queries).reshape(total_rows, q_width),
            to_low(grad_keys).reshape(total_rows, k_width),
            grad_v.reshape(total_rows, k_width),
        ],
        axis=1,
    )
    grad_normed_three = scatter_tokens(contract_last(grad_projected, w_attn_in))
    grad_attn_in = reduce_columns(low_three, grad_projected)
    grad_branch_three, grad_gain_two = normalize_back(
        grad_normed_three, second, scale_three, gains[2]
    )
    grad_second = grad_third + grad_branch_three
    grad_first, grad_in_one, grad_down_one, grad_gain_one = feed_back(
        grad_second,
        gather_tokens(to_low(grad_second)),
        first,
        kept_one,
        gains[1],
        w_in_one,
        w_down_one,
    )
    branch_one = gather_tokens(to_low(grad_first))
    grad_gated = contract_last(branch_one, w_mix_out)
    grad_part_c = grad_gated * conv
    grad_conv = (grad_gated * part_c).reshape(seq_count, rows_here, channels)
    tap_grads = jnp.stack(
        [
            jnp.sum(grad_conv * extended[:, :-2] * twice, axis=(0, 1)),
            jnp.sum(grad_conv * extended[:, 1:-1] * once, axis=(0, 1)),
            jnp.sum(grad_conv * extended[:, 2:], axis=(0, 1)),
        ]
    )
    back_one = taps[1] * grad_conv * once
    back_two = taps[0] * grad_conv * twice
    after = jnp.take(ranks, ((blocks + 1) % seq_count) ^ here)
    follows = (blocks < seq_count - 1).astype(jnp.float32)[:, None, None]
    next_one = jnp.take(back_one[:, :1], after, axis=0) * follows
    next_two = jnp.take(back_two[:, :2], after, axis=0) * follows
    grad_mixed = (
        taps[2] * grad_conv
        + jnp.concatenate([back_one[:, 1:], next_one], axis=1)
        + jnp.concatenate([back_two[:, 2:], next_two], axis=1)
    )
    mixed_grad_low = to_low(grad_mixed).reshape(-1, channels)
    grad_projected_one = to_low(
        jnp.concatenate([mixed_grad_low * part_v, grad_part_c, mixed_grad_low * part_b], axis=1)
    )
    grad_mix_in = reduce_columns(low_one, grad_projected_one)
    grad_mix_out = reduce_natural(contract_first(gated, branch_one))
    grad_branch_zero, grad_gain_zero = normalize_back(
        scatter_tokens(contract_last(grad_projected_one, w_mix_in)), inputs, scale_one, gains[0]
    )
    token_grad = grad_first + grad_branch_zero

    gain_grads = jnp.stack([grad_gain_zero, grad_gain_one, grad_gain_two, grad_gain_three])
    tap_full = lax.dynamic_update_slice_in_dim(
        jnp.zeros((3, width), jnp.float32), tap_grads, here * channels, 1
    )
    matrices = (mix_in, mix_out, attn_in, attn_out, ffn_in, ffn_out)
    early = total(
        [jnp.concatenate([gain_grads, tap_full], axis=0), jnp.stack([grad_head_q, grad_head_k])]
        + [jnp.sum(matrix * matrix, axis=(-2, -1)) for matrix in matrices]
        + [jnp.sum(vectors * vectors, axis=-1)]
    )
    weight_norms = early[2:8]
    vector_norm = early[8]
    index = lax.axis_index("dp") * seq_count + here
    vector_grad = lax.dynamic_slice_in_dim(early[0], index * vectors.shape[1], vectors.shape[1], 1)
    head_grad = early[1]

    def owner_pair(block):
        full = owner_in(block, (hidden, hidden))
        return jnp.stack([full[:, :hidden], full[:, hidden:]])

    reduced = (
        owner_in(grad_mix_in, mix_widths),
        moved_to_owner(grad_mix_out),
        owner_in(grad_attn_in, attn_widths),
        moved_to_owner(grad_attn_out),
        jnp.stack([owner_pair(grad_in_one), owner_pair(grad_in_two)]),
        jnp.stack([moved_to_owner(grad_down_one), moved_to_owner(grad_down_two)]),
    )
    row_states = (mix_in_rows, mix_out_rows, attn_in_rows, attn_out_rows, ffn_in_rows, ffn_out_rows)
    col_states = (mix_in_cols, mix_out_cols, attn_in_cols, attn_out_cols, ffn_in_cols, ffn_out_cols)
    new_rows, column_sums, row_sums = [], [], []
    for index in range(6):
        grad = reduced[index]
        squares = grad * grad + SQUARE_FLOOR
        rows_new = DECAY_RATE * row_states[index] + (1.0 - DECAY_RATE) * jnp.mean(squares, axis=-1)
        new_rows.append(rows_new)
        column_sums.append(jnp.sum(squares, axis=-2))
        row_sums.append(jnp.sum(rows_new, axis=-1))
    vector_moment_new = DECAY_RATE * vectors_moment + (1.0 - DECAY_RATE) * (
        vector_grad * vector_grad + SQUARE_FLOOR
    )
    vector_update = vector_grad * lax.rsqrt(vector_moment_new)
    summed = total(
        column_sums + row_sums + [jnp.sum(vector_update * vector_update, axis=-1)]
    )
    finished = []
    for index in range(6):
        rows_new = new_rows[index]
        total_count = rows_new.shape[-1] * devices
        cols_new = (
            DECAY_RATE * col_states[index] + (1.0 - DECAY_RATE) * summed[index] / total_count
        )
        mean_rows = summed[6 + index] / total_count
        update = reduced[index] / jnp.sqrt(
            rows_new[..., :, None] * cols_new[..., None, :] / mean_rows[..., None, None]
        )
        update_squares = jnp.sum(update * update, axis=(-2, -1))
        finished.append((cols_new, update, update_squares, total_count * cols_new.shape[-1]))
    update_totals = total([finished[index][2] for index in range(6)])
    new_weights = []
    for index in range(6):
        count = finished[index][3]
        divisor = jnp.maximum(1.0, jnp.sqrt(update_totals[index] / count) / CLIP_LEVEL)
        rate = STEP_SCALE * jnp.maximum(RATE_FLOOR, jnp.sqrt(weight_norms[index] / count))
        new_weights.append(matrices[index] - (rate / divisor)[..., None, None] * finished[index][1])
    full_width = vectors.shape[-1] * devices
    vector_divisor = jnp.maximum(1.0, jnp.sqrt(summed[12] / full_width) / CLIP_LEVEL)
    vector_rate = STEP_SCALE * jnp.maximum(RATE_FLOOR, jnp.sqrt(vector_norm / full_width))
    vectors_new = vectors - (vector_rate / vector_divisor)[:, None] * vector_update
    head_moment_new = DECAY_RATE * head_moment + (1.0 - DECAY_RATE) * (
        head_grad * head_grad + SQUARE_FLOOR
    )
    head_update = head_grad * lax.rsqrt(head_moment_new)
    head_divisor = jnp.maximum(
        1.0, jnp.sqrt(jnp.mean(head_update * head_update, axis=-1, keepdims=True)) / CLIP_LEVEL
    )
    head_rate = STEP_SCALE * jnp.maximum(
        RATE_FLOOR, jnp.sqrt(jnp.mean(head_gain * head_gain, axis=-1, keepdims=True))
    )
    head_new = head_gain - head_rate / head_divisor * head_update
    outputs = [to_low(fourth), token_grad]
    for index in range(6):
        outputs += [reduced[index], new_rows[index], finished[index][0], new_weights[index]]
    return tuple(
        outputs
        + [vector_grad, vector_moment_new, vectors_new, head_grad, head_moment_new, head_new]
    )


def solution(mesh):
    return jax.shard_map(
        body,
        mesh=mesh,
        in_specs=(
            P(("dp", "seq"), None),
            P(("dp", "seq"), None),
            P("dp", None),
            P(("dp", "seq"), None),
            P(("dp", "seq")),
            P(),
            P(("dp", "seq"), None),
            P(("dp", "seq")),
            P(),
            P(("dp", "seq"), None),
            P(("dp", "seq")),
            P(),
            P(("dp", "seq"), None),
            P(("dp", "seq")),
            P(),
            P(None, None, ("dp", "seq"), None),
            P(None, None, ("dp", "seq")),
            P(),
            P(None, ("dp", "seq"), None),
            P(None, ("dp", "seq")),
            P(),
            P(None, ("dp", "seq")),
            P(None, ("dp", "seq")),
            P(),
            P(),
        ),
        out_specs=(
            P(("dp", "seq"), None),
            P(("dp", "seq"), None),
            P(("dp", "seq"), None),
            P(("dp", "seq")),
            P(),
            P(("dp", "seq"), None),
            P(("dp", "seq"), None),
            P(("dp", "seq")),
            P(),
            P(("dp", "seq"), None),
            P(("dp", "seq"), None),
            P(("dp", "seq")),
            P(),
            P(("dp", "seq"), None),
            P(("dp", "seq"), None),
            P(("dp", "seq")),
            P(),
            P(("dp", "seq"), None),
            P(None, None, ("dp", "seq"), None),
            P(None, None, ("dp", "seq")),
            P(),
            P(None, None, ("dp", "seq"), None),
            P(None, ("dp", "seq"), None),
            P(None, ("dp", "seq")),
            P(),
            P(None, ("dp", "seq"), None),
            P(None, ("dp", "seq")),
            P(None, ("dp", "seq")),
            P(None, ("dp", "seq")),
            P(),
            P(),
            P(),
        ),
        check_vma=False,
    )
```

```python
import math

import jax
import jax.numpy as jnp
from jax import lax
from jax.experimental import pallas as pl
from jax.experimental.pallas import tpu as pltpu
from jax.sharding import PartitionSpec as P

HQ = 16
KVH = 8
HEAD = 64

EPSILON = 1e-05
SQUARE_FLOOR = 1e-30
DECAY_RATE = 0.5
CLIP_LEVEL = 0.25
STEP_SCALE = 1.0
RATE_FLOOR = 0.001
MASKED_SCORE = -1e30


def matmul(operand, weight):
    return jnp.dot(operand, weight, preferred_element_type=jnp.float32)


def contract_first(operand, other):
    return lax.dot_general(
        operand, other, (((0,), (0,)), ((), ())), preferred_element_type=jnp.float32
    )


def contract_last(operand, other):
    return lax.dot_general(
        operand,
        other,
        (((operand.ndim - 1,), (other.ndim - 1,)), ((), ())),
        preferred_element_type=jnp.float32,
    )


def to_low(values):
    return values.astype(jnp.bfloat16)


def normalize(values, gain):
    scale = lax.rsqrt(jnp.mean(values * values, axis=-1, keepdims=True) + EPSILON)
    return (values * scale * gain, scale)


def normalize_back(grad_out, values, scale, gain):
    unit = values * scale
    grad_gain = jnp.sum(grad_out * unit, axis=tuple(range(values.ndim - 1)))
    weighted = grad_out * gain
    grad_values = scale * (weighted - unit * jnp.mean(weighted * unit, axis=-1, keepdims=True))
    return (grad_values, grad_gain)


def doc_layout(lens, places):
    bounds = jnp.cumsum(lens)
    passed = bounds[None, :] <= places[:, None]
    docs = jnp.sum(passed.astype(jnp.int32), axis=1)
    starts = jnp.sum(jnp.where(passed, lens[None, :], 0), axis=1)
    return (docs, places - starts)


def angles_for(places, width):
    half = width // 2
    freqs = jnp.exp(jnp.arange(half, dtype=jnp.float32) * (-2.0 * math.log(1000000.0) / width))
    angles = places.astype(jnp.float32)[:, None] * freqs[None, :]
    return (jnp.cos(angles)[:, None, :], jnp.sin(angles)[:, None, :], half)


def rotate(values, angles):
    cosine, sine, half = angles
    front = values[..., :half]
    behind = values[..., half:]
    return jnp.concatenate(
        [front * cosine - behind * sine, behind * cosine + front * sine], axis=-1
    )


def rotate_back(grads, angles):
    cosine, sine, half = angles
    front = grads[..., :half]
    behind = grads[..., half:]
    return jnp.concatenate(
        [front * cosine + behind * sine, behind * cosine - front * sine], axis=-1
    )


def bits_of(axis):
    return lax.axis_size(axis).bit_length() - 1


def flipped(value, mask):
    for bit in range(mask.bit_length()):
        if (mask >> bit) & 1:
            value = value + (1 - 2 * ((value // (1 << bit)) % 2)) * (1 << bit)
    return value


def spread(bits):
    masks = [0]
    for bit in bits:
        masks = masks + [mask | (1 << bit) for mask in masks]
    return masks


class Split:
    def __init__(self, with_z):
        dp_bits = bits_of("dp")
        x_bits = dp_bits // 2
        self.shared = [x_bits] if with_z else []
        self.x_bits = list(range(x_bits))
        self.z_bits = [bit for bit in range(x_bits, dp_bits) if bit not in self.shared]
        self.free = self.x_bits + self.z_bits
        self.seq_bits = bits_of("seq")
        self.ranks = 1 << (self.seq_bits + len(self.shared))
        self.copies = 1 << len(self.free)
        self.links = [
            (dp_mask, seq_mask)
            for dp_mask in spread(self.shared)
            for seq_mask in spread(range(1, self.seq_bits))
        ]
        self.peers = [
            (dp_mask, seq_mask)
            for dp_mask in spread(self.shared)
            for seq_mask in range(1 << self.seq_bits)
        ]

    def pick(self, value, bits):
        out = 0
        for place, bit in enumerate(bits):
            out = out + ((value // (1 << bit)) % 2) * (1 << place)
        return out

    def rank(self, dp, seq):
        return self.pick(dp, self.shared) * (1 << self.seq_bits) + seq

    def copy(self, dp):
        return self.pick(dp, self.free)

    def groups(self):
        count = lax.axis_size("dp")
        table = {}
        for dp in range(count):
            table.setdefault(self.pick(dp, self.shared), []).append((self.pick(dp, self.free), dp))
        return [[dp for _, dp in sorted(table[key])] for key in sorted(table)]

    def owner_order(self):
        return sorted(
            range(lax.axis_size("dp")),
            key=lambda dp: (self.pick(dp, self.free), self.pick(dp, self.shared)),
        )


MESH = pl.DeviceIdType.MESH


class Job:
    scratch = ()
    copies = 0
    locals = 0
    out_in_vmem = False

    def bind(self, operands, outs, scratch, send, recv, local):
        self.ins, self.outs, self.held = operands, outs, scratch
        self.send, self.recv, self.local = send, recv, local
        self.dp, self.seq = lax.axis_index("dp"), lax.axis_index("seq")

    def away(self, number, source, target, mask):
        return pltpu.make_async_remote_copy(
            src_ref=source,
            dst_ref=target,
            send_sem=self.send.at[number],
            recv_sem=self.recv.at[number],
            device_id=(flipped(self.dp, mask[0]), flipped(self.seq, mask[1])),
            device_id_type=MESH,
        )

    def near(self, number, source, target):
        return pltpu.make_async_copy(source, target, self.local.at[number])

    def start(self):
        pass

    def middle(self):
        return iter(())

    def finish(self):
        pass


class GatherTokens(Job):
    def __init__(self, split, value):
        self.split = split
        self.operands = (value,)
        self.chips = len(split.links)
        self.results = (jax.ShapeDtypeStruct((2, self.chips) + value.shape, value.dtype),)
        self.masks = [mask for mask in split.links[1:]] + [(0, 1)]
        self.copies = 2 * self.chips - 1
        self.locals = 1

    def start(self):
        own, out = self.ins[0], self.outs[0]
        self.mine = self.near(0, own, out.at[0, 0])
        self.mine.start()
        self.far = [
            self.away(chip - 1, own, out.at[0, chip], self.split.links[chip])
            for chip in range(1, self.chips)
        ]
        for copy in self.far:
            copy.start()
        self.beside = [self.away(self.chips - 1, own, out.at[1, 0], (0, 1))]
        self.beside[0].start()

    def middle(self):
        out = self.outs[0]
        for chip in range(1, self.chips):
            self.far[chip - 1].wait_recv()
            copy = self.away(self.chips - 1 + chip, out.at[0, chip], out.at[1, chip], (0, 1))
            copy.start()
            self.beside.append(copy)
            yield True

    def finish(self):
        self.mine.wait()
        for copy in self.far:
            copy.wait_send()
        for copy in self.beside:
            copy.wait()


STRIP = 32


class ScatterTokens(Job):
    out_in_vmem = True

    def __init__(self, split, partial):
        self.split = split
        rows, width = partial.shape[-2:]
        self.chips = len(split.links)
        self.operands = (partial.reshape(2, self.chips, rows, width),)
        self.results = (jax.ShapeDtypeStruct((rows, width), jnp.float32),)
        self.masks = [mask for mask in split.links[1:]] + [(0, 1)]
        self.copies = 2 * self.chips - 1
        self.locals = self.chips
        self.scratch = (
            pltpu.VMEM((self.chips, rows, width), jnp.float32),
            pltpu.VMEM((self.chips, rows, width), jnp.float32),
            pltpu.VMEM((max(1, self.chips - 1), rows, width), jnp.bfloat16),
            pltpu.VMEM((max(1, self.chips - 1), rows, width), jnp.bfloat16),
        )
        self.rows = rows

    def start(self):
        partial = self.ins[0]
        theirs, mine, _, _ = self.held
        self.beside, self.loads = [None] * self.chips, [None] * self.chips
        for chip in list(range(1, self.chips)) + [0]:
            self.beside[chip] = self.away(
                self.chips - 1 + chip, partial.at[1, chip], theirs.at[chip], (0, 1)
            )
            self.beside[chip].start()
            self.loads[chip] = self.near(chip, partial.at[0, chip], mine.at[chip])
            self.loads[chip].start()

    def middle(self):
        theirs, mine, sent, landed = self.held
        self.far = []
        for chip in range(1, self.chips):
            self.beside[chip].wait_recv()
            self.loads[chip].wait()

            @pl.loop(0, self.rows // STRIP)
            def _(strip, chip=chip):
                place = pl.ds(pl.multiple_of(strip * STRIP, STRIP), STRIP)
                sent[chip - 1, place] = to_low(theirs[chip, place] + mine[chip, place])

            copy = self.away(
                chip - 1, sent.at[chip - 1], landed.at[chip - 1], self.split.links[chip]
            )
            copy.start()
            self.far.append(copy)
            yield True

    def finish(self):
        theirs, mine, sent, landed = self.held
        out = self.outs[0]
        self.beside[0].wait_recv()
        self.loads[0].wait()
        for copy in self.far:
            copy.wait_recv()

        @pl.loop(0, self.rows // STRIP)
        def _(strip):
            place = pl.ds(pl.multiple_of(strip * STRIP, STRIP), STRIP)
            total = theirs[0, place] + mine[0, place]
            for chip in range(1, self.chips):
                total = total + landed[chip - 1, place].astype(jnp.float32)
            out[place] = total

        for copy in self.far:
            copy.wait_send()
        for copy in self.beside:
            copy.wait_send()


class Trade(Job):
    def __init__(self, split, value):
        self.split = split
        self.operands = (value,)
        self.results = (jax.ShapeDtypeStruct(value.shape, value.dtype),)
        self.masks = split.peers[1:]
        self.copies = len(self.masks)
        self.locals = 1

    def start(self):
        given, out = self.ins[0], self.outs[0]
        rank = self.split.rank(self.dp, self.seq)
        self.mine = self.near(0, given.at[rank], out.at[rank])
        self.mine.start()
        self.far = []
        for number, mask in enumerate(self.masks):
            other = self.split.rank(flipped(self.dp, mask[0]), flipped(self.seq, mask[1]))
            copy = self.away(number, given.at[other], out.at[rank], mask)
            copy.start()
            self.far.append(copy)

    def finish(self):
        self.mine.wait()
        for copy in self.far:
            copy.wait()


def pieces_of(rows, most, tile):
    for count in range(most, 1, -1):
        if rows % (count * tile) == 0:
            return count
    return 1


class GatherWeights(Job):
    def __init__(self, split, value, most=1):
        self.split = split
        self.operands = (value,)
        self.results = (jax.ShapeDtypeStruct((split.copies,) + value.shape, value.dtype),)
        self.z_masks = spread(split.z_bits)
        self.x_masks = spread(split.x_bits)
        self.masks = [(mask, 0) for mask in self.z_masks[1:] + self.x_masks[1:]]
        self.count = pieces_of(value.shape[0], most, 16)
        self.depth = value.shape[0] // self.count
        self.copies = (len(self.z_masks) * len(self.x_masks) - 1) * self.count
        self.locals = 1

    def part(self, ref, piece):
        return ref if self.count == 1 else ref.at[pl.ds(piece * self.depth, self.depth)]

    def slot(self, mask, piece):
        return self.part(self.outs[0].at[self.split.copy(flipped(self.dp, mask))], piece)

    def start(self):
        own = self.ins[0]
        self.mine = self.near(0, own, self.outs[0].at[self.split.copy(self.dp)])
        self.mine.start()
        self.number = 0
        self.along_z, self.rest = [], []
        for piece in range(min(2, self.count)):
            self.send_z(piece)

    def send_z(self, piece):
        source = self.part(self.ins[0], piece)
        sent = []
        for mask in self.z_masks[1:]:
            copy = self.away(self.number, source, self.slot(0, piece), (mask, 0))
            copy.start()
            arrival = self.away(self.number, source, self.slot(mask, piece), (mask, 0))
            sent.append((mask, copy, arrival))
            self.number += 1
        self.along_z.append(sent)

    def pass_on(self, from_mask, source, piece):
        for mask in self.x_masks[1:]:
            copy = self.away(self.number, source, self.slot(from_mask, piece), (mask, 0))
            copy.start()
            arrival = self.away(
                self.number, source, self.slot(from_mask ^ mask, piece), (mask, 0)
            )
            self.rest.append((copy, arrival))
            self.number += 1

    def middle(self):
        for piece in range(self.count):
            self.pass_on(0, self.part(self.ins[0], piece), piece)
            for mask, _, arrival in self.along_z[piece]:
                arrival.wait_recv()
                self.pass_on(mask, self.slot(mask, piece), piece)
            if piece + 2 < self.count:
                self.send_z(piece + 2)
            yield True

    def finish(self):
        self.mine.wait()
        for sent in self.along_z:
            for _, copy, _ in sent:
                copy.wait_send()
        for copy, arrival in self.rest:
            arrival.wait_recv()
            copy.wait_send()


class ReduceWeights(Job):
    out_in_vmem = True

    def __init__(self, split, grad, most=1):
        self.split = split
        self.operands = (grad,)
        shape = grad.shape[1:]
        self.results = (jax.ShapeDtypeStruct(shape, jnp.float32),)
        self.z_masks = spread(split.z_bits)
        self.x_masks = spread(split.x_bits)
        self.masks = [(mask, 0) for mask in self.z_masks[1:] + self.x_masks[1:]]
        self.count = pieces_of(shape[0], most, 8)
        self.depth = shape[0] // self.count
        far_z, far_x = len(self.z_masks) - 1, len(self.x_masks) - 1
        self.units = [
            (piece, place) for piece in range(self.count) for place in range(1, far_z + 1)
        ] + [(piece, 0) for piece in range(self.count)]
        self.copies = self.count * (far_z + (far_z + 1) * far_x)
        self.locals = len(self.units)
        self.scratch = (
            pltpu.VMEM((far_x, far_z + 1) + shape, jnp.float32),
            pltpu.VMEM((far_z + 1,) + shape, jnp.float32),
            pltpu.VMEM((far_z,) + shape, jnp.float32),
        )

    def rows(self, piece):
        return pl.ds(piece * self.depth, self.depth)

    def start(self):
        self.number = 0
        self.sent, self.loads, self.far = {}, {}, {}
        for index in range(min(2, len(self.units))):
            self.send_x(index)

    def send_x(self, index):
        piece, place = self.units[index]
        mask = self.z_masks[place]
        grad = self.ins[0]
        by_x, mine, _ = self.held
        copies = []
        for number, x_mask in enumerate(self.x_masks[1:]):
            target = self.split.copy(flipped(self.dp, mask ^ x_mask))
            copy = self.away(
                self.number,
                grad.at[target, self.rows(piece)],
                by_x.at[number, place, self.rows(piece)],
                (x_mask, 0),
            )
            copy.start()
            copies.append(copy)
            self.number += 1
        self.sent[index] = copies
        target = self.split.copy(flipped(self.dp, mask))
        load = self.near(
            index, grad.at[target, self.rows(piece)], mine.at[place, self.rows(piece)]
        )
        load.start()
        self.loads[index] = load

    def strips(self, piece, update):
        step = 8
        for size in (64, 32, 16):
            if self.depth % size == 0:
                step = size
                break

        @pl.loop(0, self.depth // step)
        def _(strip):
            update(pl.ds(pl.multiple_of(piece * self.depth + strip * step, 8), step))

    def middle(self):
        by_x, mine, by_z = self.held
        out = self.outs[0]
        for index, (piece, place) in enumerate(self.units):
            self.loads[index].wait()
            for copy in self.sent[index]:
                copy.wait_recv()
            if index + 2 < len(self.units):
                self.send_x(index + 2)

            def update(rows, place=place):
                value = mine[place, rows]
                for number in range(len(self.x_masks) - 1):
                    value = value + by_x[number, place, rows]
                mine[place, rows] = value

            self.strips(piece, update)
            if place:
                copy = self.away(
                    self.number,
                    mine.at[place, self.rows(piece)],
                    by_z.at[place - 1, self.rows(piece)],
                    (self.z_masks[place], 0),
                )
                copy.start()
                self.far[(piece, place)] = copy
                self.number += 1
            yield True

    def finish(self):
        _, mine, by_z = self.held
        out = self.outs[0]
        for piece in range(self.count):
            for place in range(1, len(self.z_masks)):
                self.far[(piece, place)].wait_recv()

            def update(rows):
                value = mine[0, rows]
                for place in range(1, len(self.z_masks)):
                    value = value + by_z[place - 1, rows]
                out[rows] = value

            self.strips(piece, update)
        for copy in self.far.values():
            copy.wait_send()
        for copies in self.sent.values():
            for copy in copies:
                copy.wait_send()


class Everyone(Job):
    def __init__(self, value):
        self.operands = (value,)
        seq, dp = lax.axis_size("seq"), lax.axis_size("dp")
        self.results = (jax.ShapeDtypeStruct((dp, seq) + value.shape, value.dtype),)
        self.seq_masks, self.dp_masks = range(1, seq), range(1, dp)
        self.masks = [(0, mask) for mask in self.seq_masks] + [(mask, 0) for mask in self.dp_masks]
        self.copies = len(self.masks)
        self.locals = 1

    def start(self):
        out = self.outs[0]
        self.mine = self.near(0, self.ins[0], out.at[self.dp, self.seq])
        self.mine.start()
        self.first, self.second = [], []
        for mask in self.seq_masks:
            copy = self.away(mask - 1, self.ins[0], out.at[self.dp, self.seq], (0, mask))
            copy.start()
            arrival = self.away(
                mask - 1, self.ins[0], out.at[self.dp, flipped(self.seq, mask)], (0, mask)
            )
            self.first.append((copy, arrival))

    def middle(self):
        out = self.outs[0]
        self.mine.wait()
        for _, arrival in self.first:
            arrival.wait_recv()
        base = len(self.first) - 1
        for mask in self.dp_masks:
            copy = self.away(base + mask, out.at[self.dp], out.at[self.dp], (mask, 0))
            copy.start()
            arrival = self.away(
                base + mask, out.at[self.dp], out.at[flipped(self.dp, mask)], (mask, 0)
            )
            self.second.append((copy, arrival))
        yield True

    def finish(self):
        for copy, _ in self.first:
            copy.wait_send()
        for copy, arrival in self.second:
            arrival.wait_recv()
            copy.wait_send()


class SumAll(Job):
    out_in_vmem = True

    def __init__(self, value):
        self.operands = (value,)
        self.results = (jax.ShapeDtypeStruct(value.shape, value.dtype),)
        seq, dp = value.shape[:2]
        self.seq_masks, self.dp_masks = range(1, seq), range(1, dp)
        self.masks = [(0, mask) for mask in self.seq_masks] + [(mask, 0) for mask in self.dp_masks]
        self.copies = 2 * len(self.masks)
        self.locals = 1
        self.scratch = (
            pltpu.VMEM(value.shape, jnp.float32),
            pltpu.VMEM((seq - 1,) + value.shape[1:], jnp.float32),
            pltpu.VMEM((dp - 1,) + value.shape[2:], jnp.float32),
        )

    def start(self):
        self.load = self.near(0, self.ins[0], self.held[0])
        self.load.start()
        self.load.wait()
        given, by_seq, _ = self.held
        self.first = []
        for mask in self.seq_masks:
            copy = self.away(
                mask - 1, given.at[flipped(self.seq, mask)], by_seq.at[mask - 1], (0, mask)
            )
            copy.start()
            self.first.append(copy)

    def middle(self):
        given, by_seq, by_dp = self.held
        out = self.outs[0]
        for copy in self.first:
            copy.wait_recv()
        part = given[self.seq]
        for mask in self.seq_masks:
            part = part + by_seq[mask - 1]
        given[self.seq] = part
        yield True
        base = len(self.first)
        second = []
        for mask in self.dp_masks:
            copy = self.away(
                base + mask - 1,
                given.at[self.seq, flipped(self.dp, mask)],
                by_dp.at[mask - 1],
                (mask, 0),
            )
            copy.start()
            second.append(copy)
        for copy in second:
            copy.wait_recv()
        value = given[self.seq, self.dp]
        for mask in self.dp_masks:
            value = value + by_dp[mask - 1]
        out[self.seq, self.dp] = value
        yield True
        base += len(second)
        third = []
        for mask in self.dp_masks:
            block = out.at[self.seq, self.dp]
            copy = self.away(base + mask - 1, block, block, (mask, 0))
            copy.start()
            arrival = self.away(
                base + mask - 1, block, out.at[self.seq, flipped(self.dp, mask)], (mask, 0)
            )
            third.append((copy, arrival))
        for _, arrival in third:
            arrival.wait_recv()
        yield True
        base += len(third)
        fourth = []
        for mask in self.seq_masks:
            block = out.at[self.seq]
            copy = self.away(base + mask - 1, block, block, (0, mask))
            copy.start()
            arrival = self.away(
                base + mask - 1, block, out.at[flipped(self.seq, mask)], (0, mask)
            )
            fourth.append((copy, arrival))
        for _, arrival in fourth:
            arrival.wait_recv()
        self.all = self.first + second + [c for c, _ in third] + [c for c, _ in fourth]

    def finish(self):
        for copy in self.all:
            copy.wait_send()


class Courier:
    def __init__(self):
        self.calls = 0

    def __call__(self, *jobs):
        number = self.calls
        self.calls += 1
        masks = []
        for job in jobs:
            for mask in job.masks:
                if mask not in masks:
                    masks.append(mask)
        operands = [value for job in jobs for value in job.operands]
        results = [value for job in jobs for value in job.results]
        in_vmem = [job.out_in_vmem for job in jobs for _ in job.results]
        scratch = []
        for job in jobs:
            scratch += list(job.scratch)
            scratch += [
                pltpu.SemaphoreType.DMA((max(1, job.copies),)),
                pltpu.SemaphoreType.DMA((max(1, job.copies),)),
                pltpu.SemaphoreType.DMA((max(1, job.locals),)),
            ]

        def kernel(*refs):
            ins = list(refs[: len(operands)])
            outs = list(refs[len(operands) : len(operands) + len(results)])
            held = list(refs[len(operands) + len(results) :])
            dp, seq = lax.axis_index("dp"), lax.axis_index("seq")
            barrier = pltpu.get_barrier_semaphore()
            for mask in masks:
                pl.semaphore_signal(
                    barrier,
                    inc=1,
                    device_id=(flipped(dp, mask[0]), flipped(seq, mask[1])),
                    device_id_type=MESH,
                )
            pl.semaphore_wait(barrier, len(masks))
            for job in jobs:
                count_in, count_out = len(job.operands), len(job.results)
                own = len(job.scratch)
                job.bind(
                    ins[:count_in], outs[:count_out], held[:own], *held[own : own + 3]
                )
                ins, outs, held = ins[count_in:], outs[count_out:], held[own + 3 :]
            for job in jobs:
                job.start()
            turns = [job.middle() for job in jobs]
            while turns:
                turns = [turn for turn in turns if next(turn, None) is not None]
            for job in jobs:
                job.finish()

        sent = sum(value.size * value.dtype.itemsize for value in operands)
        outs = pl.pallas_call(
            kernel,
            out_shape=results,
            in_specs=[pl.BlockSpec(memory_space=pl.ANY)] * len(operands),
            out_specs=[
                pl.BlockSpec(memory_space=pltpu.VMEM if vmem else pl.ANY) for vmem in in_vmem
            ],
            scratch_shapes=scratch,
            compiler_params=pltpu.CompilerParams(
                collective_id=number, has_side_effects=True, vmem_limit_bytes=48 << 20
            ),
            cost_estimate=pl.CostEstimate(flops=0, bytes_accessed=8 * sent, transcendentals=0),
            name="courier_%d" % number,
        )(*operands)
        return outs


def packed(values, blocks):
    flat = jnp.concatenate([value.reshape(-1).astype(jnp.float32) for value in values])
    each = -(-flat.shape[0] // (blocks * 1024)) * 1024
    return jnp.pad(flat, (0, blocks * each - flat.shape[0])).reshape(blocks, each // 128, 128)


def unpacked(flat, values):
    flat = flat.reshape(-1)
    out, begin = [], 0
    for value in values:
        out.append(flat[begin : begin + value.size].reshape(value.shape))
        begin += value.size
    return out


def large_sum(values):
    seq, dp = lax.axis_size("seq"), lax.axis_size("dp")
    blocks = packed(values, seq * dp)
    return SumAll(blocks.reshape((seq, dp) + blocks.shape[1:]))


def small_sum(values):
    return Everyone(packed(values, 1)[0])


def by_rank(weight, split):
    dp_count, seq_count = lax.axis_size("dp"), lax.axis_size("seq")
    lead = weight.shape[:-1]
    each = weight.shape[-1] // (dp_count * seq_count)
    value = weight.reshape(lead + (dp_count, seq_count, each))
    parts = []
    for shared in range(split.ranks // seq_count):
        picked = [dp for dp in split.owner_order() if split.pick(dp, split.shared) == shared]
        part = jnp.stack([value[..., dp, :, :] for dp in picked], axis=-3)
        parts.append(jnp.moveaxis(part, -2, 0))
    joined = jnp.concatenate(parts, axis=0) if len(parts) > 1 else parts[0]
    return joined.reshape((split.ranks,) + lead + (split.copies * each,))


def from_ranks(chunks, split):
    dp_count, seq_count = lax.axis_size("dp"), lax.axis_size("seq")
    lead = chunks.shape[1:-1]
    each = chunks.shape[-1] // split.copies
    value = chunks.reshape(
        (split.ranks // seq_count, seq_count) + lead + (split.copies, each)
    )
    parts = []
    for dp in range(dp_count):
        part = value[split.pick(dp, split.shared)][..., split.pick(dp, split.free), :]
        parts.append(jnp.moveaxis(part, 0, -2))
    return jnp.stack(parts, axis=-3).reshape(lead + (dp_count * seq_count * each,))


def owner_columns(value, split):
    count = lax.axis_size("dp")
    each = value.shape[-1] // count
    order = split.owner_order()
    if order == list(range(count)):
        return value
    return jnp.concatenate([value[..., dp * each : (dp + 1) * each] for dp in order], axis=-1)


def natural_columns(value, split):
    count = lax.axis_size("dp")
    each = value.shape[-1] // count
    order = split.owner_order()
    if order == list(range(count)):
        return value
    return jnp.concatenate(
        [value[..., order.index(dp) * each : (order.index(dp) + 1) * each] for dp in range(count)],
        axis=-1,
    )


def moved_to_rank(shard):
    seq, dp = lax.axis_size("seq"), lax.axis_size("dp")
    pairs = [(block, (block % dp) * seq + block // dp) for block in range(seq * dp)]
    return lax.ppermute(shard, ("dp", "seq"), pairs)


def moved_to_owner(shard):
    seq, dp = lax.axis_size("seq"), lax.axis_size("dp")
    pairs = [((block % dp) * seq + block // dp, block) for block in range(seq * dp)]
    return lax.ppermute(shard, ("dp", "seq"), pairs)


def rows_of(value, like):
    return value.reshape((-1,) + like.shape)


def flat(value):
    return value.reshape(-1, value.shape[-1])


def feed_forward(courier, split, resid, gain, w_in, w_down, beside_gather=(), beside_scatter=()):
    normed, scale = normalize(resid, gain)
    normed_all, *first = courier(
        GatherTokens(split, owner_columns(to_low(normed), split)), *beside_gather
    )
    normed_all = flat(normed_all)
    both = matmul(normed_all, w_in)
    half = both.shape[1] // 2
    gate, upper = both[:, :half], both[:, half:]
    hidden_low = to_low(jax.nn.silu(gate) * upper)
    added, *second = courier(
        ScatterTokens(split, rows_of(matmul(hidden_low, w_down), resid)), *beside_scatter
    )
    return (resid + added, (normed_all, scale, gate, upper, hidden_low), first, second)


def feed_back(courier, split, grad_resid, grad_all, resid, kept, gain, w_in, w_down, beside):
    normed_all, scale, gate, upper, hidden_low = kept
    grad_down = by_copy(contract_first(hidden_low, grad_all), split)
    grad_hidden = contract_last(grad_all, w_down)
    sigma = jax.nn.sigmoid(gate)
    grad_gate = to_low(grad_hidden * upper * (sigma * (1.0 + gate * (1.0 - sigma))))
    grad_upper = to_low(grad_hidden * (gate * sigma))
    grad_both = jnp.concatenate([grad_gate, grad_upper], axis=1)
    grad_normed, *rest = courier(
        ScatterTokens(split, rows_of(contract_last(grad_both, w_in), resid)), *beside(grad_down)
    )
    grad_in = by_copy(contract_first(normed_all, grad_both), split)
    grad_normed = natural_columns(grad_normed, split)
    grad_branch, grad_gain = normalize_back(grad_normed, resid, scale, gain)
    return (grad_resid + grad_branch, grad_in, grad_gain, rest)


def by_copy(grad, split):
    return grad.reshape(split.copies, -1, grad.shape[-1])


def attend(q_rot, k_rot, values, allowed):
    factor = HEAD ** (-0.5)
    scores = (
        jnp.einsum("qjhd,kjd->jhqk", q_rot, k_rot, preferred_element_type=jnp.float32) * factor
    )
    scores = jnp.where(allowed[None, None], scores, MASKED_SCORE)
    peak = jnp.max(scores, axis=-1, keepdims=True)
    expo = jnp.exp(scores - peak)
    count = jnp.sum(expo, axis=-1, keepdims=True)
    output = jnp.einsum(
        "jhqk,kjd->qjhd", to_low(expo / count), values, preferred_element_type=jnp.float32
    )
    return (to_low(output), peak + jnp.log(count))


def attend_back(q_rot, k_rot, values, lse, grad, allowed):
    factor = HEAD ** (-0.5)
    scores = (
        jnp.einsum("qjhd,kjd->jhqk", q_rot, k_rot, preferred_element_type=jnp.float32) * factor
    )
    scores = jnp.where(allowed[None, None], scores, MASKED_SCORE)
    probs = jnp.exp(scores - lse)
    grad_probs = jnp.einsum("qjhd,kjd->jhqk", grad, values, preferred_element_type=jnp.float32)
    row_dot = jnp.sum(probs * grad_probs, axis=-1, keepdims=True)
    grad_scores = to_low(probs * (grad_probs - row_dot))
    grad_q = (
        jnp.einsum("jhqk,kjd->qjhd", grad_scores, k_rot, preferred_element_type=jnp.float32)
        * factor
    )
    grad_k = (
        jnp.einsum("jhqk,qjhd->kjd", grad_scores, q_rot, preferred_element_type=jnp.float32)
        * factor
    )
    grad_v = jnp.einsum(
        "jhqk,qjhd->kjd", to_low(probs), grad, preferred_element_type=jnp.float32
    )
    return (to_low(grad_q), to_low(grad_k), to_low(grad_v))


def body(
    tokens,
    cotangent,
    lengths,
    mix_in,
    mix_in_rows,
    mix_in_cols,
    mix_out,
    mix_out_rows,
    mix_out_cols,
    attn_in,
    attn_in_rows,
    attn_in_cols,
    attn_out,
    attn_out_rows,
    attn_out_cols,
    ffn_in,
    ffn_in_rows,
    ffn_in_cols,
    ffn_out,
    ffn_out_rows,
    ffn_out_cols,
    vectors,
    vectors_moment,
    head_gain,
    head_moment,
):
    rows_here, width = tokens.shape
    seq_count = lax.axis_size("seq")
    devices = lax.axis_size("dp") * seq_count
    here = lax.axis_index("seq")
    courier = Courier()
    near, wide = Split(False), Split(True)
    masks = [mask ^ core for core in (0, 1) for _, mask in near.links]
    ranks = jnp.asarray([masks.index(place) for place in range(seq_count)], jnp.int32)
    blocks = here ^ jnp.asarray(masks, jnp.int32)
    places = (
        blocks[:, None] * rows_here + jnp.arange(rows_here, dtype=jnp.int32)[None, :]
    ).reshape(-1)
    docs, positions = doc_layout(lengths[0], places)
    allowed = (places[None, :] <= places[:, None]) & (docs[None, :] == docs[:, None])
    once = (positions >= 1).astype(jnp.float32).reshape(seq_count, rows_here, 1)
    twice = (positions >= 2).astype(jnp.float32).reshape(seq_count, rows_here, 1)
    channels = width // seq_count
    heads = HQ // seq_count
    kv_heads = KVH // seq_count
    kv_width = KVH * HEAD
    hidden = ffn_in.shape[-1]

    head_gains = to_low(head_gain).astype(jnp.float32)
    def chunk_of(weight, widths):
        low = to_low(weight)
        parts, begin = [], 0
        for each in widths:
            part = low[:, begin : begin + each].reshape(low.shape[0], seq_count, -1)
            parts.append(jnp.moveaxis(part, 1, 0))
            begin += each
        return jnp.concatenate(parts, axis=-1)

    def joined(chunks, widths):
        parts, begin = [], 0
        for each in widths:
            part = chunks[..., begin : begin + each // seq_count]
            parts.append(jnp.moveaxis(part, 0, 1).reshape(chunks.shape[1], each))
            begin += each // seq_count
        return jnp.concatenate(parts, axis=-1)

    attn_widths = (width, kv_width, kv_width)
    mix_chunk = by_rank(to_low(mix_in).reshape(-1, 3, width), near).reshape(
        seq_count, mix_in.shape[0], 3 * channels
    )
    ffn_chunks = [
        jnp.concatenate([by_rank(to_low(ffn_in[layer, part]), wide) for part in (0, 1)], axis=-1)
        for layer in (0, 1)
    ]
    attn_out_chunk = moved_to_rank(to_low(attn_out))
    vector_block = jnp.pad(to_low(vectors).reshape(-1), (0, 2048 - vectors.size))
    mix_traded, one_traded, tokens_all, gathered = courier(
        Trade(near, mix_chunk),
        Trade(wide, ffn_chunks[0]),
        GatherTokens(near, tokens),
        Everyone(vector_block.reshape(16, 128)),
    )
    gains = gathered.reshape(devices, -1)[:, : vectors.size].reshape(devices, 7, -1)
    gains = jnp.moveaxis(gains, 0, 1).reshape(7, width).astype(jnp.float32)
    tokens_all = tokens_all.reshape(-1, width)
    w_mix_in, w_mix_out, w_down_one, attn_traded, two_traded, cotangent_all = (
        flat(value)
        for value in courier(
            GatherWeights(near, flat(mix_traded), 2),
            GatherWeights(near, to_low(mix_out)),
            GatherWeights(wide, to_low(ffn_out[0]), 3),
            Trade(near, chunk_of(attn_in, attn_widths)),
            Trade(wide, ffn_chunks[1]),
            GatherTokens(wide, cotangent),
        )
    )
    taps = lax.dynamic_index_in_dim(
        gains[4:7].reshape(3, -1, seq_count, width // devices), here, 2, keepdims=False
    ).reshape(3, channels)

    inputs = tokens.astype(jnp.float32)
    scale_one = normalize(inputs, gains[0])[1]
    low_one = to_low(normalize(tokens_all.astype(jnp.float32), gains[0])[0])
    projected = matmul(low_one, w_mix_in)
    part_b = projected[:, :channels]
    part_c = projected[:, channels : 2 * channels]
    part_v = projected[:, 2 * channels :]
    mixed = to_low(part_b * part_v).reshape(seq_count, rows_here, channels)
    before = jnp.take(ranks, ((blocks - 1) % seq_count) ^ here)
    rims = jnp.take(mixed[:, rows_here - 2 :], before, axis=0)
    extended = jnp.concatenate([rims, mixed], axis=1).astype(jnp.float32)
    conv = (
        taps[2] * extended[:, 2:]
        + taps[1] * extended[:, 1:-1] * once
        + taps[0] * extended[:, :-2] * twice
    ).reshape(-1, channels)
    gated = to_low(part_c * conv)
    added, w_in_one = courier(
        ScatterTokens(near, rows_of(matmul(gated, w_mix_out), inputs)),
        GatherWeights(wide, flat(one_traded), 4),
    )
    first = inputs + added
    second, kept_one, (w_attn_in, w_attn_out), (w_in_two,) = feed_forward(
        courier,
        wide,
        first,
        gains[1],
        flat(w_in_one),
        w_down_one,
        (GatherWeights(near, attn_traded, 2), GatherWeights(near, attn_out_chunk)),
        (GatherWeights(wide, two_traded, 4),),
    )
    w_attn_in, w_attn_out, w_in_two = flat(w_attn_in), flat(w_attn_out), flat(w_in_two)

    normed_three, scale_three = normalize(second, gains[2])
    low_three, w_down_two = (
        flat(value)
        for value in courier(
            GatherTokens(near, to_low(normed_three)), GatherWeights(wide, to_low(ffn_out[1]), 3)
        )
    )
    projected_three = matmul(low_three, w_attn_in)
    total_rows = rows_here * seq_count
    q_width, k_width = heads * HEAD, kv_heads * HEAD
    queries = projected_three[:, :q_width].reshape(total_rows, heads, HEAD)
    keys = projected_three[:, q_width : q_width + k_width].reshape(total_rows, kv_heads, HEAD)
    values = projected_three[:, q_width + k_width :].reshape(total_rows, kv_heads, HEAD)
    angles = angles_for(positions, HEAD)
    q_normed, q_scale = normalize(queries, head_gains[0])
    k_normed, k_scale = normalize(keys, head_gains[1])
    q_rot = to_low(rotate(q_normed, angles)).reshape(total_rows, kv_heads, heads // kv_heads, HEAD)
    k_rot = to_low(rotate(k_normed, angles))
    v_low = to_low(values)
    attended, lse = attend(q_rot, k_rot, v_low, allowed)
    attended = attended.reshape(total_rows, q_width)
    (added,) = courier(ScatterTokens(near, rows_of(matmul(attended, w_attn_out), second)))
    third = second + added
    fourth, kept_two, _, _ = feed_forward(
        courier, wide, third, gains[3], w_in_two, w_down_two
    )

    grad_third, grad_in_two, grad_gain_three, (reduced_down_two,) = feed_back(
        courier,
        wide,
        cotangent.astype(jnp.float32),
        cotangent_all,
        third,
        kept_two,
        gains[3],
        w_in_two,
        w_down_two,
        lambda grad_down: (ReduceWeights(wide, grad_down, 2),),
    )
    branch_all, reduced_in_two = courier(
        GatherTokens(near, to_low(grad_third)), ReduceWeights(wide, grad_in_two, 2)
    )
    branch_all = flat(branch_all)
    grad_attended = to_low(contract_last(branch_all, w_attn_out)).reshape(q_rot.shape)
    grad_attn_out = by_copy(contract_first(attended, branch_all), near)
    grad_q, grad_k, grad_v = attend_back(q_rot, k_rot, v_low, lse, grad_attended, allowed)
    grad_q = rotate_back(grad_q.reshape(queries.shape).astype(jnp.float32), angles)
    grad_k = rotate_back(grad_k.astype(jnp.float32), angles)
    grad_queries, grad_head_q = normalize_back(grad_q, queries, q_scale, head_gains[0])
    grad_keys, grad_head_k = normalize_back(grad_k, keys, k_scale, head_gains[1])
    grad_projected = jnp.concatenate(
        [
            to_low(grad_queries).reshape(total_rows, q_width),
            to_low(grad_keys).reshape(total_rows, k_width),
            grad_v.reshape(total_rows, k_width),
        ],
        axis=1,
    )
    grad_normed_three, reduced_attn_out = courier(
        ScatterTokens(near, rows_of(contract_last(grad_projected, w_attn_in), second)),
        ReduceWeights(near, grad_attn_out),
    )
    grad_attn_in = by_copy(contract_first(low_three, grad_projected), near)
    grad_branch_three, grad_gain_two = normalize_back(
        grad_normed_three, second, scale_three, gains[2]
    )
    grad_second = grad_third + grad_branch_three
    second_all, reduced_attn_in = courier(
        GatherTokens(wide, to_low(grad_second)), ReduceWeights(near, grad_attn_in)
    )
    grad_first, grad_in_one, grad_gain_one, (reduced_down_one,) = feed_back(
        courier,
        wide,
        grad_second,
        flat(second_all),
        first,
        kept_one,
        gains[1],
        w_in_one.reshape(-1, w_in_one.shape[-1]),
        w_down_one,
        lambda grad_down: (ReduceWeights(wide, grad_down, 2),),
    )
    branch_one, reduced_in_one = courier(
        GatherTokens(near, to_low(grad_first)), ReduceWeights(wide, grad_in_one, 2)
    )
    branch_one = flat(branch_one)
    grad_gated = contract_last(branch_one, w_mix_out)
    grad_part_c = grad_gated * conv
    grad_conv = (grad_gated * part_c).reshape(seq_count, rows_here, channels)
    tap_grads = jnp.stack(
        [
            jnp.sum(grad_conv * extended[:, :-2] * twice, axis=(0, 1)),
            jnp.sum(grad_conv * extended[:, 1:-1] * once, axis=(0, 1)),
            jnp.sum(grad_conv * extended[:, 2:], axis=(0, 1)),
        ]
    )
    back_one = taps[1] * grad_conv * once
    back_two = taps[0] * grad_conv * twice
    after = jnp.take(ranks, ((blocks + 1) % seq_count) ^ here)
    follows = (blocks < seq_count - 1).astype(jnp.float32)[:, None, None]
    next_one = jnp.take(back_one[:, :1], after, axis=0) * follows
    next_two = jnp.take(back_two[:, :2], after, axis=0) * follows
    grad_mixed = (
        taps[2] * grad_conv
        + jnp.concatenate([back_one[:, 1:], next_one], axis=1)
        + jnp.concatenate([back_two[:, 2:], next_two], axis=1)
    )
    mixed_grad_low = to_low(grad_mixed).reshape(-1, channels)
    grad_projected_one = to_low(
        jnp.concatenate([mixed_grad_low * part_v, grad_part_c, mixed_grad_low * part_b], axis=1)
    )
    grad_mix_in = by_copy(contract_first(low_one, grad_projected_one), near)
    grad_mix_out = by_copy(contract_first(gated, branch_one), near)
    def to_trade(block, split):
        return block.reshape(split.ranks, -1, block.shape[-1])

    grad_normed_one, reduced_mix_in, reduced_mix_out, attn_back, one_back, two_back = courier(
        ScatterTokens(near, rows_of(contract_last(grad_projected_one, w_mix_in), inputs)),
        ReduceWeights(near, grad_mix_in),
        ReduceWeights(near, grad_mix_out),
        Trade(near, to_trade(reduced_attn_in, near)),
        Trade(wide, to_trade(reduced_in_one, wide)),
        Trade(wide, to_trade(reduced_in_two, wide)),
    )
    grad_branch_zero, grad_gain_zero = normalize_back(
        grad_normed_one, inputs, scale_one, gains[0]
    )
    token_grad = grad_first + grad_branch_zero

    gain_grads = jnp.stack([grad_gain_zero, grad_gain_one, grad_gain_two, grad_gain_three])
    tap_full = lax.dynamic_update_slice_in_dim(
        jnp.zeros((3, lax.axis_size("dp"), seq_count, width // devices), jnp.float32),
        tap_grads.reshape(3, lax.axis_size("dp"), 1, width // devices),
        here,
        2,
    ).reshape(3, width)
    matrices = (mix_in, mix_out, attn_in, attn_out, ffn_in, ffn_out)
    early_parts = (
        [jnp.concatenate([gain_grads, tap_full], axis=0), jnp.stack([grad_head_q, grad_head_k])]
        + [jnp.sum(matrix * matrix, axis=(-2, -1)) for matrix in matrices]
        + [jnp.sum(vectors * vectors, axis=-1)]
    )
    mix_back, early = courier(
        Trade(near, to_trade(reduced_mix_in, near)), large_sum(early_parts)
    )
    early = unpacked(early, early_parts)
    weight_norms = early[2:8]
    vector_norm = early[8]
    index = lax.axis_index("dp") * seq_count + here
    vector_grad = lax.dynamic_slice_in_dim(early[0], index * vectors.shape[1], vectors.shape[1], 1)
    head_grad = early[1]

    def owner_pair(chunks):
        half = chunks.shape[-1] // 2
        return jnp.stack(
            [from_ranks(chunks[..., :half], wide), from_ranks(chunks[..., half:], wide)]
        )

    reduced = (
        from_ranks(mix_back.reshape(seq_count, -1, 3, channels), near).reshape(mix_in.shape),
        reduced_mix_out,
        joined(attn_back, attn_widths),
        moved_to_owner(reduced_attn_out),
        jnp.stack([owner_pair(one_back), owner_pair(two_back)]),
        jnp.stack([reduced_down_one, reduced_down_two]),
    )
    row_states = (mix_in_rows, mix_out_rows, attn_in_rows, attn_out_rows, ffn_in_rows, ffn_out_rows)
    col_states = (mix_in_cols, mix_out_cols, attn_in_cols, attn_out_cols, ffn_in_cols, ffn_out_cols)
    new_rows, column_sums, row_sums = [], [], []
    for index in range(6):
        grad = reduced[index]
        squares = grad * grad + SQUARE_FLOOR
        rows_new = DECAY_RATE * row_states[index] + (1.0 - DECAY_RATE) * jnp.mean(squares, axis=-1)
        new_rows.append(rows_new)
        column_sums.append(jnp.sum(squares, axis=-2))
        row_sums.append(jnp.sum(rows_new, axis=-1))
    vector_moment_new = DECAY_RATE * vectors_moment + (1.0 - DECAY_RATE) * (
        vector_grad * vector_grad + SQUARE_FLOOR
    )
    vector_update = vector_grad * lax.rsqrt(vector_moment_new)
    late_parts = column_sums + row_sums + [jnp.sum(vector_update * vector_update, axis=-1)]
    (late,) = courier(large_sum(late_parts))
    summed = unpacked(late, late_parts)
    finished = []
    for index in range(6):
        rows_new = new_rows[index]
        total_count = rows_new.shape[-1] * devices
        cols_new = (
            DECAY_RATE * col_states[index] + (1.0 - DECAY_RATE) * summed[index] / total_count
        )
        mean_rows = summed[6 + index] / total_count
        update = reduced[index] / jnp.sqrt(
            rows_new[..., :, None] * cols_new[..., None, :] / mean_rows[..., None, None]
        )
        update_squares = jnp.sum(update * update, axis=(-2, -1))
        finished.append((cols_new, update, update_squares, total_count * cols_new.shape[-1]))
    last_parts = [finished[index][2] for index in range(6)]
    (last,) = courier(small_sum(last_parts))
    update_totals = unpacked(jnp.sum(last, axis=(0, 1)), last_parts)
    new_weights = []
    for index in range(6):
        count = finished[index][3]
        divisor = jnp.maximum(1.0, jnp.sqrt(update_totals[index] / count) / CLIP_LEVEL)
        rate = STEP_SCALE * jnp.maximum(RATE_FLOOR, jnp.sqrt(weight_norms[index] / count))
        new_weights.append(matrices[index] - (rate / divisor)[..., None, None] * finished[index][1])
    full_width = vectors.shape[-1] * devices
    vector_divisor = jnp.maximum(1.0, jnp.sqrt(summed[12] / full_width) / CLIP_LEVEL)
    vector_rate = STEP_SCALE * jnp.maximum(RATE_FLOOR, jnp.sqrt(vector_norm / full_width))
    vectors_new = vectors - (vector_rate / vector_divisor)[:, None] * vector_update
    head_moment_new = DECAY_RATE * head_moment + (1.0 - DECAY_RATE) * (
        head_grad * head_grad + SQUARE_FLOOR
    )
    head_update = head_grad * lax.rsqrt(head_moment_new)
    head_divisor = jnp.maximum(
        1.0, jnp.sqrt(jnp.mean(head_update * head_update, axis=-1, keepdims=True)) / CLIP_LEVEL
    )
    head_rate = STEP_SCALE * jnp.maximum(
        RATE_FLOOR, jnp.sqrt(jnp.mean(head_gain * head_gain, axis=-1, keepdims=True))
    )
    head_new = head_gain - head_rate / head_divisor * head_update
    outputs = [to_low(fourth), token_grad]
    for index in range(6):
        outputs += [reduced[index], new_rows[index], finished[index][0], new_weights[index]]
    return tuple(
        outputs
        + [vector_grad, vector_moment_new, vectors_new, head_grad, head_moment_new, head_new]
    )


def solution(mesh):
    return jax.shard_map(
        body,
        mesh=mesh,
        in_specs=(
            P(("dp", "seq"), None),
            P(("dp", "seq"), None),
            P("dp", None),
            P(("dp", "seq"), None),
            P(("dp", "seq")),
            P(),
            P(("dp", "seq"), None),
            P(("dp", "seq")),
            P(),
            P(("dp", "seq"), None),
            P(("dp", "seq")),
            P(),
            P(("dp", "seq"), None),
            P(("dp", "seq")),
            P(),
            P(None, None, ("dp", "seq"), None),
            P(None, None, ("dp", "seq")),
            P(),
            P(None, ("dp", "seq"), None),
            P(None, ("dp", "seq")),
            P(),
            P(None, ("dp", "seq")),
            P(None, ("dp", "seq")),
            P(),
            P(),
        ),
        out_specs=(
            P(("dp", "seq"), None),
            P(("dp", "seq"), None),
            P(("dp", "seq"), None),
            P(("dp", "seq")),
            P(),
            P(("dp", "seq"), None),
            P(("dp", "seq"), None),
            P(("dp", "seq")),
            P(),
            P(("dp", "seq"), None),
            P(("dp", "seq"), None),
            P(("dp", "seq")),
            P(),
            P(("dp", "seq"), None),
            P(("dp", "seq"), None),
            P(("dp", "seq")),
            P(),
            P(("dp", "seq"), None),
            P(None, None, ("dp", "seq"), None),
            P(None, None, ("dp", "seq")),
            P(),
            P(None, None, ("dp", "seq"), None),
            P(None, ("dp", "seq"), None),
            P(None, ("dp", "seq")),
            P(),
            P(None, ("dp", "seq"), None),
            P(None, ("dp", "seq")),
            P(None, ("dp", "seq")),
            P(None, ("dp", "seq")),
            P(),
            P(),
            P(),
        ),
        check_vma=False,
    )
```

```python
import math

import jax
import jax.numpy as jnp
from jax import lax
from jax.experimental import pallas as pl
from jax.experimental.pallas import tpu as pltpu
from jax.sharding import PartitionSpec as P

HQ = 16
KVH = 8
HEAD = 64

EPSILON = 1e-05
SQUARE_FLOOR = 1e-30
DECAY_RATE = 0.5
CLIP_LEVEL = 0.25
STEP_SCALE = 1.0
RATE_FLOOR = 0.001
MASKED_SCORE = -1e30


def matmul(operand, weight):
    return jnp.dot(operand, weight, preferred_element_type=jnp.float32)


def contract_first(operand, other):
    return lax.dot_general(
        operand, other, (((0,), (0,)), ((), ())), preferred_element_type=jnp.float32
    )


def contract_last(operand, other):
    return lax.dot_general(
        operand,
        other,
        (((operand.ndim - 1,), (other.ndim - 1,)), ((), ())),
        preferred_element_type=jnp.float32,
    )


def to_low(values):
    return values.astype(jnp.bfloat16)


def normalize(values, gain):
    scale = lax.rsqrt(jnp.mean(values * values, axis=-1, keepdims=True) + EPSILON)
    return (values * scale * gain, scale)


def normalize_back(grad_out, values, scale, gain):
    unit = values * scale
    grad_gain = jnp.sum(grad_out * unit, axis=tuple(range(values.ndim - 1)))
    weighted = grad_out * gain
    grad_values = scale * (weighted - unit * jnp.mean(weighted * unit, axis=-1, keepdims=True))
    return (grad_values, grad_gain)


def doc_layout(lens, places):
    bounds = jnp.cumsum(lens)
    passed = bounds[None, :] <= places[:, None]
    docs = jnp.sum(passed.astype(jnp.int32), axis=1)
    starts = jnp.sum(jnp.where(passed, lens[None, :], 0), axis=1)
    return (docs, places - starts)


def angles_for(places, width):
    half = width // 2
    freqs = jnp.exp(jnp.arange(half, dtype=jnp.float32) * (-2.0 * math.log(1000000.0) / width))
    angles = places.astype(jnp.float32)[:, None] * freqs[None, :]
    return (jnp.cos(angles), jnp.sin(angles))


def bits_of(axis):
    return lax.axis_size(axis).bit_length() - 1


def flipped(value, mask):
    for bit in range(mask.bit_length()):
        if (mask >> bit) & 1:
            value = value + (1 - 2 * ((value // (1 << bit)) % 2)) * (1 << bit)
    return value


def spread(bits):
    masks = [0]
    for bit in bits:
        masks = masks + [mask | (1 << bit) for mask in masks]
    return masks


class Split:
    def __init__(self, with_z):
        dp_bits = bits_of("dp")
        x_bits = dp_bits // 2
        self.shared = [x_bits] if with_z else []
        self.x_bits = list(range(x_bits))
        self.z_bits = [bit for bit in range(x_bits, dp_bits) if bit not in self.shared]
        self.free = self.x_bits + self.z_bits
        self.seq_bits = bits_of("seq")
        self.ranks = 1 << (self.seq_bits + len(self.shared))
        self.copies = 1 << len(self.free)
        self.links = [
            (dp_mask, seq_mask)
            for dp_mask in spread(self.shared)
            for seq_mask in spread(range(1, self.seq_bits))
        ]
        self.peers = [
            (dp_mask, seq_mask)
            for dp_mask in spread(self.shared)
            for seq_mask in range(1 << self.seq_bits)
        ]

    def pick(self, value, bits):
        out = 0
        for place, bit in enumerate(bits):
            out = out + ((value // (1 << bit)) % 2) * (1 << place)
        return out

    def rank(self, dp, seq):
        return self.pick(dp, self.shared) * (1 << self.seq_bits) + seq

    def copy(self, dp):
        return self.pick(dp, self.free)

    def groups(self):
        count = lax.axis_size("dp")
        table = {}
        for dp in range(count):
            table.setdefault(self.pick(dp, self.shared), []).append((self.pick(dp, self.free), dp))
        return [[dp for _, dp in sorted(table[key])] for key in sorted(table)]

    def owner_order(self):
        return sorted(
            range(lax.axis_size("dp")),
            key=lambda dp: (self.pick(dp, self.free), self.pick(dp, self.shared)),
        )


MESH = pl.DeviceIdType.MESH


class Job:
    scratch = ()
    copies = 0
    locals = 0
    out_in_vmem = False
    in_vmem = ()
    given_in_vmem = ()

    def bind(self, operands, outs, scratch, send, recv, local):
        self.ins, self.outs, self.held = operands, outs, scratch
        self.send, self.recv, self.local = send, recv, local
        self.dp, self.seq = lax.axis_index("dp"), lax.axis_index("seq")

    def away(self, number, source, target, mask):
        return pltpu.make_async_remote_copy(
            src_ref=source,
            dst_ref=target,
            send_sem=self.send.at[number],
            recv_sem=self.recv.at[number],
            device_id=(flipped(self.dp, mask[0]), flipped(self.seq, mask[1])),
            device_id_type=MESH,
        )

    def near(self, number, source, target):
        return pltpu.make_async_copy(source, target, self.local.at[number])

    def start(self):
        pass

    def middle(self):
        return iter(())

    def finish(self):
        pass


class GatherTokens(Job):
    def __init__(self, split, value):
        self.split = split
        self.operands = (value,)
        self.chips = len(split.links)
        self.results = (jax.ShapeDtypeStruct((2, self.chips) + value.shape, value.dtype),)
        self.masks = [mask for mask in split.links[1:]] + [(0, 1)]
        self.copies = 2 * self.chips - 1
        self.locals = 1

    def start(self):
        own, out = self.ins[0], self.outs[0]
        self.mine = self.near(0, own, out.at[0, 0])
        self.mine.start()
        self.far = [
            self.away(chip - 1, own, out.at[0, chip], self.split.links[chip])
            for chip in range(1, self.chips)
        ]
        for copy in self.far:
            copy.start()
        self.beside = [self.away(self.chips - 1, own, out.at[1, 0], (0, 1))]
        self.beside[0].start()

    def middle(self):
        out = self.outs[0]
        for chip in range(1, self.chips):
            self.far[chip - 1].wait_recv()
            copy = self.away(self.chips - 1 + chip, out.at[0, chip], out.at[1, chip], (0, 1))
            copy.start()
            self.beside.append(copy)
            yield True

    def finish(self):
        self.mine.wait()
        for copy in self.far:
            copy.wait_send()
        for copy in self.beside:
            copy.wait()


STRIP = 32


class ScatterTokens(Job):
    out_in_vmem = True

    def __init__(self, split, partial):
        self.split = split
        rows, width = partial.shape[-2:]
        self.chips = len(split.links)
        self.operands = (partial.reshape(2, self.chips, rows, width),)
        self.results = (jax.ShapeDtypeStruct((rows, width), jnp.float32),)
        self.masks = [mask for mask in split.links[1:]] + [(0, 1)]
        self.copies = 2 * self.chips - 1
        self.locals = self.chips
        self.scratch = (
            pltpu.VMEM((self.chips, rows, width), jnp.float32),
            pltpu.VMEM((self.chips, rows, width), jnp.float32),
            pltpu.VMEM((max(1, self.chips - 1), rows, width), jnp.bfloat16),
            pltpu.VMEM((max(1, self.chips - 1), rows, width), jnp.bfloat16),
        )
        self.rows = rows

    def start(self):
        partial = self.ins[0]
        theirs, mine, _, _ = self.held
        self.beside, self.loads = [None] * self.chips, [None] * self.chips
        for chip in list(range(1, self.chips)) + [0]:
            self.beside[chip] = self.away(
                self.chips - 1 + chip, partial.at[1, chip], theirs.at[chip], (0, 1)
            )
            self.beside[chip].start()
            self.loads[chip] = self.near(chip, partial.at[0, chip], mine.at[chip])
            self.loads[chip].start()

    def middle(self):
        theirs, mine, sent, landed = self.held
        self.far = []
        for chip in range(1, self.chips):
            self.beside[chip].wait_recv()
            self.loads[chip].wait()

            @pl.loop(0, self.rows // STRIP)
            def _(strip, chip=chip):
                place = pl.ds(pl.multiple_of(strip * STRIP, STRIP), STRIP)
                sent[chip - 1, place] = to_low(theirs[chip, place] + mine[chip, place])

            copy = self.away(
                chip - 1, sent.at[chip - 1], landed.at[chip - 1], self.split.links[chip]
            )
            copy.start()
            self.far.append(copy)
            yield True

    def finish(self):
        theirs, mine, sent, landed = self.held
        out = self.outs[0]
        self.beside[0].wait_recv()
        self.loads[0].wait()
        for copy in self.far:
            copy.wait_recv()

        @pl.loop(0, self.rows // STRIP)
        def _(strip):
            place = pl.ds(pl.multiple_of(strip * STRIP, STRIP), STRIP)
            total = theirs[0, place] + mine[0, place]
            for chip in range(1, self.chips):
                total = total + landed[chip - 1, place].astype(jnp.float32)
            out[place] = total

        for copy in self.far:
            copy.wait_send()
        for copy in self.beside:
            copy.wait_send()


class Trade(Job):
    def __init__(self, split, value):
        self.split = split
        self.operands = (value,)
        self.results = (jax.ShapeDtypeStruct(value.shape, value.dtype),)
        self.masks = split.peers[1:]
        self.copies = len(self.masks)
        self.locals = 1

    def start(self):
        given, out = self.ins[0], self.outs[0]
        rank = self.split.rank(self.dp, self.seq)
        self.mine = self.near(0, given.at[rank], out.at[rank])
        self.mine.start()
        self.far = []
        for number, mask in enumerate(self.masks):
            other = self.split.rank(flipped(self.dp, mask[0]), flipped(self.seq, mask[1]))
            copy = self.away(number, given.at[other], out.at[rank], mask)
            copy.start()
            self.far.append(copy)

    def finish(self):
        self.mine.wait()
        for copy in self.far:
            copy.wait()


def pieces_of(rows, most, tile):
    for count in range(most, 1, -1):
        if rows % (count * tile) == 0:
            return count
    return 1


class GatherWeights(Job):
    def __init__(self, split, value, most=1):
        self.split = split
        self.operands = (value,)
        self.results = (jax.ShapeDtypeStruct((split.copies,) + value.shape, value.dtype),)
        self.z_masks = spread(split.z_bits)
        self.x_masks = spread(split.x_bits)
        self.masks = [(mask, 0) for mask in self.z_masks[1:] + self.x_masks[1:]]
        self.count = pieces_of(value.shape[0], most, 16)
        self.depth = value.shape[0] // self.count
        self.copies = (len(self.z_masks) * len(self.x_masks) - 1) * self.count
        self.locals = 1

    def part(self, ref, piece):
        return ref if self.count == 1 else ref.at[pl.ds(piece * self.depth, self.depth)]

    def slot(self, mask, piece):
        return self.part(self.outs[0].at[self.split.copy(flipped(self.dp, mask))], piece)

    def start(self):
        own = self.ins[0]
        self.mine = self.near(0, own, self.outs[0].at[self.split.copy(self.dp)])
        self.mine.start()
        self.number = 0
        self.along_z, self.rest = [], []
        for piece in range(min(2, self.count)):
            self.send_z(piece)

    def send_z(self, piece):
        source = self.part(self.ins[0], piece)
        sent = []
        for mask in self.z_masks[1:]:
            copy = self.away(self.number, source, self.slot(0, piece), (mask, 0))
            copy.start()
            arrival = self.away(self.number, source, self.slot(mask, piece), (mask, 0))
            sent.append((mask, copy, arrival))
            self.number += 1
        self.along_z.append(sent)

    def pass_on(self, from_mask, source, piece):
        for mask in self.x_masks[1:]:
            copy = self.away(self.number, source, self.slot(from_mask, piece), (mask, 0))
            copy.start()
            arrival = self.away(
                self.number, source, self.slot(from_mask ^ mask, piece), (mask, 0)
            )
            self.rest.append((copy, arrival))
            self.number += 1

    def middle(self):
        for piece in range(self.count):
            self.pass_on(0, self.part(self.ins[0], piece), piece)
            for mask, _, arrival in self.along_z[piece]:
                arrival.wait_recv()
                self.pass_on(mask, self.slot(mask, piece), piece)
            if piece + 2 < self.count:
                self.send_z(piece + 2)
            yield True

    def finish(self):
        self.mine.wait()
        for sent in self.along_z:
            for _, copy, _ in sent:
                copy.wait_send()
        for copy, arrival in self.rest:
            arrival.wait_recv()
            copy.wait_send()


class ReduceWeights(Job):
    out_in_vmem = True

    def __init__(self, split, grad, most=1):
        self.split = split
        self.operands = (grad,)
        shape = grad.shape[1:]
        self.results = (jax.ShapeDtypeStruct(shape, jnp.float32),)
        self.z_masks = spread(split.z_bits)
        self.x_masks = spread(split.x_bits)
        self.masks = [(mask, 0) for mask in self.z_masks[1:] + self.x_masks[1:]]
        self.count = pieces_of(shape[0], most, 8)
        self.depth = shape[0] // self.count
        far_z, far_x = len(self.z_masks) - 1, len(self.x_masks) - 1
        self.units = [
            (piece, place) for piece in range(self.count) for place in range(1, far_z + 1)
        ] + [(piece, 0) for piece in range(self.count)]
        self.copies = self.count * (far_z + (far_z + 1) * far_x)
        self.locals = len(self.units)
        self.scratch = (
            pltpu.VMEM((far_x, far_z + 1) + shape, jnp.float32),
            pltpu.VMEM((far_z + 1,) + shape, jnp.float32),
            pltpu.VMEM((far_z,) + shape, jnp.float32),
        )

    def rows(self, piece):
        return pl.ds(piece * self.depth, self.depth)

    def start(self):
        self.number = 0
        self.sent, self.loads, self.far = {}, {}, {}
        for index in range(min(2, len(self.units))):
            self.send_x(index)

    def send_x(self, index):
        piece, place = self.units[index]
        mask = self.z_masks[place]
        grad = self.ins[0]
        by_x, mine, _ = self.held
        copies = []
        for number, x_mask in enumerate(self.x_masks[1:]):
            target = self.split.copy(flipped(self.dp, mask ^ x_mask))
            copy = self.away(
                self.number,
                grad.at[target, self.rows(piece)],
                by_x.at[number, place, self.rows(piece)],
                (x_mask, 0),
            )
            copy.start()
            copies.append(copy)
            self.number += 1
        self.sent[index] = copies
        target = self.split.copy(flipped(self.dp, mask))
        load = self.near(
            index, grad.at[target, self.rows(piece)], mine.at[place, self.rows(piece)]
        )
        load.start()
        self.loads[index] = load

    def strips(self, piece, update):
        step = 8
        for size in (64, 32, 16):
            if self.depth % size == 0:
                step = size
                break

        @pl.loop(0, self.depth // step)
        def _(strip):
            update(pl.ds(pl.multiple_of(piece * self.depth + strip * step, 8), step))

    def middle(self):
        by_x, mine, by_z = self.held
        out = self.outs[0]
        for index, (piece, place) in enumerate(self.units):
            self.loads[index].wait()
            for copy in self.sent[index]:
                copy.wait_recv()
            if index + 2 < len(self.units):
                self.send_x(index + 2)

            def update(rows, place=place):
                value = mine[place, rows]
                for number in range(len(self.x_masks) - 1):
                    value = value + by_x[number, place, rows]
                mine[place, rows] = value

            self.strips(piece, update)
            if place:
                copy = self.away(
                    self.number,
                    mine.at[place, self.rows(piece)],
                    by_z.at[place - 1, self.rows(piece)],
                    (self.z_masks[place], 0),
                )
                copy.start()
                self.far[(piece, place)] = copy
                self.number += 1
            yield True

    def finish(self):
        _, mine, by_z = self.held
        out = self.outs[0]
        for piece in range(self.count):
            for place in range(1, len(self.z_masks)):
                self.far[(piece, place)].wait_recv()

            def update(rows):
                value = mine[0, rows]
                for place in range(1, len(self.z_masks)):
                    value = value + by_z[place - 1, rows]
                out[rows] = value

            self.strips(piece, update)
        for copy in self.far.values():
            copy.wait_send()
        for copies in self.sent.values():
            for copy in copies:
                copy.wait_send()


class Return:
    def __init__(self, job, first, scratch, out):
        self.job, self.first, self.out = job, first, out
        self.theirs, self.mine, self.stage, self.sent, self.landed = scratch
        self.beside, self.far = {}, {}

    @staticmethod
    def scratch(chips, rows, width):
        return (
            pltpu.VMEM((chips, rows, width), jnp.float32),
            pltpu.VMEM((2, rows, width), jnp.float32),
            pltpu.VMEM((2, rows, width), jnp.float32),
            pltpu.VMEM((2, rows, width), jnp.bfloat16),
            pltpu.VMEM((max(1, chips - 1), rows, width), jnp.bfloat16),
        )

    def put(self, core, chip, value):
        chips = self.job.chips
        if core == 0:
            self.mine[min(chip, 1)] = value
            return
        order = list(self.beside)
        if len(order) >= 2:
            self.beside[order[-2]].wait_send()
        spot = len(order) % 2
        self.stage[spot] = value
        copy = self.job.away(
            self.first + chips - 1 + chip, self.stage.at[spot], self.theirs.at[chip], (0, 1)
        )
        copy.start()
        self.beside[chip] = copy

    def strips(self, update):
        @pl.loop(0, self.job.rows // STRIP)
        def _(strip):
            update(pl.ds(pl.multiple_of(strip * STRIP, STRIP), STRIP))

    def pass_on(self, chip):
        if chip == 0:
            return
        self.beside[chip].wait_recv()
        order = list(self.far)
        if len(order) >= 2:
            self.far[order[-2]].wait_send()
        spot = len(order) % 2

        def update(rows):
            self.sent[spot, rows] = to_low(self.theirs[chip, rows] + self.mine[1, rows])

        self.strips(update)
        copy = self.job.away(
            self.first + chip - 1,
            self.sent.at[spot],
            self.landed.at[chip - 1],
            self.job.split.links[chip],
        )
        copy.start()
        self.far[chip] = copy

    def finish(self):
        chips = self.job.chips
        self.beside[0].wait_recv()
        for chip in range(1, chips):
            self.far[chip].wait_recv()

        def update(rows):
            value = self.theirs[0, rows] + self.mine[0, rows]
            for chip in range(1, chips):
                value = value + self.landed[chip - 1, rows].astype(jnp.float32)
            self.out[rows] = value

        self.strips(update)
        for chip in list(self.beside)[-2:]:
            self.beside[chip].wait_send()
        for chip in list(self.far)[-2:]:
            self.far[chip].wait_send()


class Arrive:
    def __init__(self, job, source, slots, local):
        self.job, self.source, self.slots = job, source, slots
        self.mine = job.near(local, source, slots.at[0, 0])
        self.mine.start()
        self.far = [
            job.away(chip - 1, source, slots.at[0, chip], job.split.links[chip])
            for chip in range(1, job.chips)
        ]
        self.beside = [job.away(job.chips - 1, source, slots.at[1, 0], (0, 1))]
        for copy in self.beside + self.far:
            copy.start()

    def ready(self, core, chip):
        job = self.job
        if core:
            self.beside[chip].wait_recv()
        elif chip == 0:
            self.mine.wait()
        else:
            self.far[chip - 1].wait_recv()
            copy = job.away(
                job.chips - 1 + chip, self.slots.at[0, chip], self.slots.at[1, chip], (0, 1)
            )
            copy.start()
            self.beside.append(copy)

    def finish(self):
        for copy in self.far + self.beside:
            copy.wait_send()


class Layer(Job):
    def __init__(self, split, own, others, results, scratch=()):
        self.split = split
        self.chips = len(split.links)
        self.rows, self.width = own.shape
        self.total = 2 * self.chips * self.rows
        self.operands = (own,) + tuple(others)
        self.given_in_vmem = (False,) + (True,) * len(others)
        slots = (2, self.chips, self.rows, self.width)
        self.results = (jax.ShapeDtypeStruct((self.rows, self.width), jnp.float32),) + tuple(results)
        self.in_vmem = (True,) * len(self.results)
        self.scratch = (
            (pltpu.VMEM(slots, jnp.bfloat16),)
            + Return.scratch(self.chips, self.rows, self.width)
            + tuple(scratch)
        )
        self.masks = [mask for mask in split.links[1:]] + [(0, 1)]
        self.copies = 2 * (2 * self.chips - 1)
        self.locals = 2
        self.places = [(core, chip) for chip in range(self.chips) for core in (0, 1)]

    def start(self):
        self.slots = self.held[0]
        self.back = Return(self, 2 * self.chips - 1, self.held[1:6], self.outs[0])
        self.more = self.held[6:]
        self.arrive = Arrive(self, self.ins[0], self.slots, 0)

    def at(self, core, chip):
        place = flipped(self.seq, 2 * chip + core)
        return pl.ds(pl.multiple_of(place * self.rows, self.rows), self.rows)

    def middle(self):
        self.open()
        for core, chip in self.places:
            self.arrive.ready(core, chip)
            self.take(core, chip)
            yield True
        yield from self.work()
        for chip in list(range(1, self.chips)) + [0]:
            for core in (1, 0):
                self.back.put(core, chip, self.give(core, chip))
            yield True
            self.back.pass_on(chip)
        yield from self.after()

    def open(self):
        pass

    def work(self):
        return iter(())

    def after(self):
        return iter(())

    def finish(self):
        self.back.finish()
        self.arrive.finish()


def turned(value, steps):
    return pltpu.roll(value, steps % value.shape[0], 0)


class MixForward(Layer):
    def __init__(self, split, own, w_in, w_out, taps, once, twice):
        rows = 2 * len(split.links) * own.shape[0]
        channels = w_out.shape[0]
        super().__init__(
            split,
            own,
            (w_in, w_out, taps, once, twice),
            (
                jax.ShapeDtypeStruct((2, len(split.links)) + own.shape, jnp.bfloat16),
                jax.ShapeDtypeStruct((rows, 3 * channels), jnp.float32),
                jax.ShapeDtypeStruct((rows, channels), jnp.float32),
                jax.ShapeDtypeStruct((rows, channels), jnp.bfloat16),
            ),
        )
        self.channels = channels

    def open(self):
        _, self.w_in, self.w_out, self.taps, self.once, self.twice = self.ins
        _, self.kept, self.projected, self.conv, self.gated = self.outs

    def take(self, core, chip):
        value = self.slots[core, chip]
        self.kept[core, chip] = value
        self.projected[self.at(core, chip)] = matmul(value, self.w_in[...])

    def work(self):
        each = self.channels
        mixed = to_low(self.projected[:, :each] * self.projected[:, 2 * each :]).astype(jnp.float32)
        conv = (
            self.taps[2:3] * mixed
            + self.taps[1:2] * turned(mixed, 1) * self.once[...]
            + self.taps[0:1] * turned(mixed, 2) * self.twice[...]
        )
        self.conv[...] = conv
        self.gated[...] = to_low(self.projected[:, each : 2 * each] * conv)
        yield True

    def give(self, core, chip):
        return matmul(self.gated[self.at(core, chip)], self.w_out[...])


class MixBack(Layer):
    def __init__(self, split, own, w_in, w_out, taps, once, twice, kept, projected, conv, gated):
        rows = 2 * len(split.links) * own.shape[0]
        channels = w_out.shape[0]
        super().__init__(
            split,
            own,
            (w_in, w_out, taps, once, twice, kept, projected, conv, gated),
            (
                jax.ShapeDtypeStruct(w_in.shape, jnp.float32),
                jax.ShapeDtypeStruct(w_out.shape, jnp.float32),
                jax.ShapeDtypeStruct(taps.shape, jnp.float32),
            ),
            (
                pltpu.VMEM((rows, channels), jnp.float32),
                pltpu.VMEM((rows, 3 * channels), jnp.bfloat16),
            ),
        )
        self.channels = channels

    def open(self):
        _, self.w_in, self.w_out, self.taps, self.once, self.twice = self.ins[:6]
        self.kept, self.projected, self.conv, self.gated = self.ins[6:]
        _, self.grad_in, self.grad_out, self.grad_taps = self.outs
        self.grad_gated, self.grad_projected = self.more

    def take(self, core, chip):
        grad = self.slots[core, chip]
        self.grad_gated[self.at(core, chip)] = contract_last(grad, self.w_out[...])
        term = contract_first(self.gated[self.at(core, chip)], grad)
        if (core, chip) == (0, 0):
            self.grad_out[...] = term
        else:
            self.grad_out[...] += term

    def work(self):
        each = self.channels
        part_b = self.projected[:, :each]
        part_c = self.projected[:, each : 2 * each]
        part_v = self.projected[:, 2 * each :]
        once, twice = self.once[...], self.twice[...]
        mixed = to_low(part_b * part_v).astype(jnp.float32)
        grad_gated = self.grad_gated[...]
        grad_conv = grad_gated * part_c
        back_one, back_two = grad_conv * once, grad_conv * twice
        self.grad_taps[...] = jnp.zeros(self.grad_taps.shape, jnp.float32)
        self.grad_taps[0:1] = jnp.sum(back_two * turned(mixed, 2), axis=0, keepdims=True)
        self.grad_taps[1:2] = jnp.sum(back_one * turned(mixed, 1), axis=0, keepdims=True)
        self.grad_taps[2:3] = jnp.sum(grad_conv * mixed, axis=0, keepdims=True)
        grad_mixed = (
            self.taps[2:3] * grad_conv
            + turned(self.taps[1:2] * back_one, -1)
            + turned(self.taps[0:1] * back_two, -2)
        )
        grad_mixed = to_low(grad_mixed).astype(jnp.float32)
        self.grad_projected[:, :each] = to_low(grad_mixed * part_v)
        self.grad_projected[:, each : 2 * each] = to_low(grad_gated * self.conv[...])
        self.grad_projected[:, 2 * each :] = to_low(grad_mixed * part_b)
        yield True

    def give(self, core, chip):
        return contract_last(self.grad_projected[self.at(core, chip)], self.w_in[...])

    def after(self):
        for core, chip in self.places:
            term = contract_first(
                self.kept[core, chip], self.grad_projected[self.at(core, chip)]
            )
            if (core, chip) == (0, 0):
                self.grad_in[...] = term
            else:
                self.grad_in[...] += term
            yield True


LANES = 128


def head_means(value):
    row = lax.broadcasted_iota(jnp.int32, (LANES, LANES), 0) // HEAD
    column = lax.broadcasted_iota(jnp.int32, (LANES, LANES), 1) // HEAD
    same = jnp.where(row == column, 1.0 / HEAD, 0.0)
    return jnp.dot(
        value, same, preferred_element_type=jnp.float32, precision=lax.Precision.HIGHEST
    )


def half_turned(value):
    lane = lax.broadcasted_iota(jnp.int32, value.shape, 1) % HEAD
    ahead = pltpu.roll(value, LANES - HEAD // 2, 1)
    behind = pltpu.roll(value, HEAD // 2, 1)
    return jnp.where(lane < HEAD // 2, ahead, behind)


class Heads:
    def __init__(self, heads, kv_heads):
        self.heads, self.kv_heads = heads, kv_heads
        self.shared = heads // kv_heads
        self.turned = (heads + kv_heads) * HEAD
        self.width = (heads + 2 * kv_heads) * HEAD

    def tiles(self):
        for begin in range(0, self.width, LANES):
            yield slice(begin, begin + LANES), min(LANES, max(0, self.turned - begin))

    def q(self, head):
        return slice(head * HEAD, (head + 1) * HEAD)

    def k(self, head):
        begin = self.heads + head // self.shared
        return slice(begin * HEAD, (begin + 1) * HEAD)

    def v(self, head):
        begin = self.heads + self.kv_heads + head // self.shared
        return slice(begin * HEAD, (begin + 1) * HEAD)

    @staticmethod
    def some(lanes, value, other):
        if lanes == LANES:
            return value
        lane = lax.broadcasted_iota(jnp.int32, value.shape, 1)
        return jnp.where(lane < lanes, value, other)


class AttendForward(Layer):
    def __init__(self, split, heads, own, w_in, w_out, cosine, sine, gain, begins):
        rows = 2 * len(split.links) * own.shape[0]
        self.heads = heads
        super().__init__(
            split,
            own,
            (w_in, w_out, cosine, sine, gain, begins),
            (
                jax.ShapeDtypeStruct((2, len(split.links)) + own.shape, jnp.bfloat16),
                jax.ShapeDtypeStruct((rows, heads.width), jnp.float32),
                jax.ShapeDtypeStruct((rows, heads.width), jnp.bfloat16),
                jax.ShapeDtypeStruct((rows, heads.heads * HEAD), jnp.bfloat16),
                jax.ShapeDtypeStruct((rows, heads.heads), jnp.float32),
            ),
        )

    def open(self):
        _, self.w_in, self.w_out, self.cosine, self.sine, self.gain, self.begins = self.ins
        _, self.kept, self.projected, self.turned, self.out, self.lse = self.outs

    def take(self, core, chip):
        value = self.slots[core, chip]
        self.kept[core, chip] = value
        rows = self.at(core, chip)
        projected = matmul(value, self.w_in[...])
        self.projected[rows] = projected
        for lanes, count in self.heads.tiles():
            raw = projected[:, lanes]
            if count:
                unit = raw * lax.rsqrt(head_means(raw * raw) + EPSILON)
                normed = unit * self.gain[:, lanes]
                spun = normed * self.cosine[rows] + half_turned(normed) * self.sine[rows]
                raw = self.heads.some(count, spun, raw)
            self.turned[rows, lanes] = to_low(raw)

    def work(self):
        for place in range(2 * self.chips):
            rows = slice(place * self.rows, (place + 1) * self.rows)
            bias, seen = hidden_scores(self.begins[rows], place, self.rows)
            for head in range(self.heads.heads):
                scores = (
                    contract_last(
                        self.turned[rows, self.heads.q(head)], self.turned[:seen, self.heads.k(head)]
                    )
                    * HEAD ** (-0.5)
                    + bias
                )
                peak = jnp.max(scores, axis=-1, keepdims=True)
                expo = jnp.exp(scores - peak)
                count = jnp.sum(expo, axis=-1, keepdims=True)
                probs = to_low(expo * (1.0 / count))
                self.out[rows, self.heads.q(head)] = to_low(
                    matmul(probs, self.turned[:seen, self.heads.v(head)])
                )
                self.lse[rows, head : head + 1] = peak + jnp.log(count)
            yield True

    def give(self, core, chip):
        return matmul(self.out[self.at(core, chip)], self.w_out[...])


def hidden_scores(begins, place, rows):
    seen = (place + 1) * rows
    row = place * rows + lax.broadcasted_iota(jnp.int32, (rows, seen), 0)
    column = lax.broadcasted_iota(jnp.int32, (rows, seen), 1)
    allowed = (column >= begins) & (column <= row)
    return jnp.where(allowed, 0.0, MASKED_SCORE), seen


class AttendBack(Layer):
    def __init__(
        self, split, heads, own, w_in, w_out, cosine, sine, gain, begins, kept, projected, turned, out, lse
    ):
        rows = 2 * len(split.links) * own.shape[0]
        self.heads = heads
        super().__init__(
            split,
            own,
            (w_in, w_out, cosine, sine, gain, begins, kept, projected, turned, out, lse),
            (
                jax.ShapeDtypeStruct(w_in.shape, jnp.float32),
                jax.ShapeDtypeStruct(w_out.shape, jnp.float32),
                jax.ShapeDtypeStruct((8, heads.width), jnp.float32),
            ),
            (
                pltpu.VMEM((rows, heads.heads * HEAD), jnp.bfloat16),
                pltpu.VMEM((rows, heads.width), jnp.float32),
                pltpu.VMEM((rows, heads.width), jnp.bfloat16),
            ),
        )

    def open(self):
        _, self.w_in, self.w_out, self.cosine, self.sine, self.gain, self.begins = self.ins[:7]
        self.kept, self.projected, self.turned, self.out, self.lse = self.ins[7:]
        _, self.grad_in, self.grad_out, self.grad_gain = self.outs
        self.grad_heads, self.grad_turned, self.grad_projected = self.more

    def take(self, core, chip):
        grad = self.slots[core, chip]
        rows = self.at(core, chip)
        self.grad_heads[rows] = to_low(contract_last(grad, self.w_out[...]))
        term = contract_first(self.out[rows], grad)
        if (core, chip) == (0, 0):
            self.grad_out[...] = term
        else:
            self.grad_out[...] += term

    def work(self):
        factor = HEAD ** (-0.5)
        self.grad_turned[...] = jnp.zeros(self.grad_turned.shape, jnp.float32)
        self.grad_gain[...] = jnp.zeros(self.grad_gain.shape, jnp.float32)
        for place in range(2 * self.chips):
            rows = slice(place * self.rows, (place + 1) * self.rows)
            bias, seen = hidden_scores(self.begins[rows], place, self.rows)
            for head in range(self.heads.heads):
                own, key, value = self.heads.q(head), self.heads.k(head), self.heads.v(head)
                query, grad = self.turned[rows, own], self.grad_heads[rows, own]
                scores = contract_last(query, self.turned[:seen, key]) * factor + bias
                probs = jnp.exp(scores - self.lse[rows, head : head + 1])
                grad_probs = contract_last(grad, self.turned[:seen, value])
                row_dot = jnp.sum(probs * grad_probs, axis=-1, keepdims=True)
                grad_scores = to_low(probs * (grad_probs - row_dot))
                self.grad_turned[rows, own] = matmul(grad_scores, self.turned[:seen, key]) * factor
                self.grad_turned[:seen, key] += contract_first(grad_scores, query) * factor
                self.grad_turned[:seen, value] += contract_first(to_low(probs), grad)
            yield True
        for place in range(2 * self.chips):
            rows = slice(place * self.rows, (place + 1) * self.rows)
            for lanes, count in self.heads.tiles():
                low = to_low(self.grad_turned[rows, lanes])
                if count:
                    grad = low.astype(jnp.float32)
                    normed = grad * self.cosine[rows] + half_turned(grad * self.sine[rows])
                    raw = self.projected[rows, lanes]
                    scale = lax.rsqrt(head_means(raw * raw) + EPSILON)
                    unit = raw * scale
                    gain_term = self.heads.some(count, normed * unit, jnp.zeros_like(unit))
                    self.grad_gain[0:1, lanes] += jnp.sum(gain_term, axis=0, keepdims=True)
                    weighted = normed * self.gain[:, lanes]
                    back = scale * (weighted - unit * head_means(weighted * unit))
                    low = to_low(self.heads.some(count, back, grad))
                self.grad_projected[rows, lanes] = low
            yield True

    def give(self, core, chip):
        return contract_last(self.grad_projected[self.at(core, chip)], self.w_in[...])

    def after(self):
        for core, chip in self.places:
            term = contract_first(
                self.kept[core, chip], self.grad_projected[self.at(core, chip)]
            )
            if (core, chip) == (0, 0):
                self.grad_in[...] = term
            else:
                self.grad_in[...] += term
            yield True


class FeedForward(Job):
    def __init__(self, split, normed, grad, w_in, w_down, forward):
        self.split, self.forward, self.back = split, forward, grad is not None
        self.chips = len(split.links)
        width = w_in.shape[0]
        gathered = normed if normed.ndim == 2 else grad
        given = (grad if normed.ndim == 2 else normed) if self.back else None
        self.gather_normed = normed.ndim == 2
        self.rows = gathered.shape[0]
        self.half = w_in.shape[1] // 2
        self.operands = (gathered, w_in, w_down) + (() if given is None else (given,))
        row_sum = jax.ShapeDtypeStruct((self.rows, width), jnp.float32)
        self.results, self.in_vmem = (), ()
        if forward:
            self.results += (row_sum,)
            self.in_vmem += (True,)
        if self.back:
            self.results += (
                row_sum,
                jax.ShapeDtypeStruct(w_in.shape, jnp.float32),
                jax.ShapeDtypeStruct(w_down.shape, jnp.float32),
            )
            self.in_vmem += (True, True, True)
        else:
            self.results += (
                jax.ShapeDtypeStruct((2, self.chips, self.rows, width), jnp.bfloat16),
            )
            self.in_vmem += (False,)
        self.masks = [mask for mask in split.links[1:]] + [(0, 1)]
        self.channels = int(forward) + int(self.back)
        self.copies = (2 * self.chips - 1) * (1 + self.channels)
        self.locals = 3 + 2 * self.chips
        all_rows = pltpu.VMEM((2, self.chips, self.rows, width), jnp.bfloat16)
        self.scratch = (
            (all_rows,)
            + ((all_rows,) if given is not None else ())
            + (pltpu.VMEM(w_in.shape, jnp.bfloat16), pltpu.VMEM(w_down.shape, jnp.bfloat16))
        )
        for _ in range(self.channels):
            self.scratch += Return.scratch(self.chips, self.rows, width)

    def start(self):
        held = list(self.held)
        self.slots = held.pop(0)
        self.given = held.pop(0) if self.back else None
        self.w_in, self.w_down = held.pop(0), held.pop(0)
        outs = list(self.outs)
        first = 2 * self.chips - 1
        self.forth = self.backward = None
        if self.forward:
            self.forth = Return(self, first, held[:5], outs.pop(0))
            held, first = held[5:], first + 2 * self.chips - 1
        if self.back:
            self.backward = Return(self, first, held[:5], outs.pop(0))
            self.grad_in, self.grad_down = outs
        else:
            self.kept = outs.pop(0)
        self.mine = self.near(0, self.ins[0], self.slots.at[0, 0])
        self.mine.start()
        self.far = [
            self.away(chip - 1, self.ins[0], self.slots.at[0, chip], self.split.links[chip])
            for chip in range(1, self.chips)
        ]
        self.beside = [self.away(self.chips - 1, self.ins[0], self.slots.at[1, 0], (0, 1))]
        for copy in self.beside + self.far:
            copy.start()
        self.loads = [
            self.near(1, self.ins[1], self.w_in),
            self.near(2, self.ins[2], self.w_down),
        ]
        if self.back:
            self.rest = [
                self.near(3 + 2 * chip + core, self.ins[3].at[core, chip], self.given.at[core, chip])
                for chip in range(self.chips)
                for core in (0, 1)
            ]
            self.loads.append(self.rest[0])
        for copy in self.loads:
            copy.start()
        if self.back:
            for copy in self.rest[1:]:
                copy.start()

    def middle(self):
        chips = self.chips
        self.mine.wait()
        self.loads[0].wait()
        self.loads[1].wait()
        self.stores = []
        for chip in range(chips):
            for core in (0, 1):
                if core == 0 and chip:
                    self.far[chip - 1].wait_recv()
                    copy = self.away(
                        chips - 1 + chip, self.slots.at[0, chip], self.slots.at[1, chip], (0, 1)
                    )
                    copy.start()
                    self.beside.append(copy)
                if core == 1:
                    self.beside[chip].wait_recv()
                if self.back:
                    self.rest[2 * chip + core].wait()
                else:
                    store = self.near(
                        3 + 2 * chip + core, self.slots.at[core, chip], self.kept.at[core, chip]
                    )
                    store.start()
                    self.stores.append(store)
                self.compute(core, chip)
                yield True
            for channel in (self.forth, self.backward):
                if channel is not None:
                    channel.pass_on(chip)
            yield True

    def compute(self, core, chip):
        arrived = self.slots[core, chip]
        normed = arrived if self.gather_normed else self.given[core, chip]
        both = matmul(normed, self.w_in[...])
        gate, upper = both[:, : self.half], both[:, self.half :]
        sigma = jax.nn.sigmoid(gate)
        active = gate * sigma
        hidden = to_low(active * upper)
        if self.forth is not None:
            self.forth.put(core, chip, matmul(hidden, self.w_down[...]))
        if self.back:
            grad = self.given[core, chip] if self.gather_normed else arrived
            grad_hidden = contract_last(grad, self.w_down[...])
            grad_gate = to_low(grad_hidden * upper * (sigma * (1.0 + gate * (1.0 - sigma))))
            grad_upper = to_low(grad_hidden * active)
            grad_both = jnp.concatenate([grad_gate, grad_upper], axis=1)
            self.backward.put(core, chip, contract_last(grad_both, self.w_in[...]))
            if core == 0 and chip == 0:
                self.grad_in[...] = contract_first(normed, grad_both)
                self.grad_down[...] = contract_first(hidden, grad)
            else:
                self.grad_in[...] += contract_first(normed, grad_both)
                self.grad_down[...] += contract_first(hidden, grad)

    def finish(self):
        for channel in (self.backward, self.forth):
            if channel is not None:
                channel.finish()
        for copy in self.far:
            copy.wait_send()
        for copy in self.beside:
            copy.wait_send()
        for store in self.stores:
            store.wait()


class Everyone(Job):
    def __init__(self, value):
        self.operands = (value,)
        seq, dp = lax.axis_size("seq"), lax.axis_size("dp")
        self.results = (jax.ShapeDtypeStruct((dp, seq) + value.shape, value.dtype),)
        self.seq_masks, self.dp_masks = range(1, seq), range(1, dp)
        self.masks = [(0, mask) for mask in self.seq_masks] + [(mask, 0) for mask in self.dp_masks]
        self.copies = len(self.masks)
        self.locals = 1

    def start(self):
        out = self.outs[0]
        self.mine = self.near(0, self.ins[0], out.at[self.dp, self.seq])
        self.mine.start()
        self.first, self.second = [], []
        for mask in self.seq_masks:
            copy = self.away(mask - 1, self.ins[0], out.at[self.dp, self.seq], (0, mask))
            copy.start()
            arrival = self.away(
                mask - 1, self.ins[0], out.at[self.dp, flipped(self.seq, mask)], (0, mask)
            )
            self.first.append((copy, arrival))

    def middle(self):
        out = self.outs[0]
        self.mine.wait()
        for _, arrival in self.first:
            arrival.wait_recv()
        base = len(self.first) - 1
        for mask in self.dp_masks:
            copy = self.away(base + mask, out.at[self.dp], out.at[self.dp], (mask, 0))
            copy.start()
            arrival = self.away(
                base + mask, out.at[self.dp], out.at[flipped(self.dp, mask)], (mask, 0)
            )
            self.second.append((copy, arrival))
        yield True

    def finish(self):
        for copy, _ in self.first:
            copy.wait_send()
        for copy, arrival in self.second:
            arrival.wait_recv()
            copy.wait_send()


class SumAll(Job):
    out_in_vmem = True

    def __init__(self, value):
        self.operands = (value,)
        self.results = (jax.ShapeDtypeStruct(value.shape, value.dtype),)
        seq, dp = value.shape[:2]
        self.seq_masks, self.dp_masks = range(1, seq), range(1, dp)
        self.masks = [(0, mask) for mask in self.seq_masks] + [(mask, 0) for mask in self.dp_masks]
        self.copies = 2 * len(self.masks)
        self.locals = 1
        self.scratch = (
            pltpu.VMEM(value.shape, jnp.float32),
            pltpu.VMEM((seq - 1,) + value.shape[1:], jnp.float32),
            pltpu.VMEM((dp - 1,) + value.shape[2:], jnp.float32),
        )

    def start(self):
        self.load = self.near(0, self.ins[0], self.held[0])
        self.load.start()
        self.load.wait()
        given, by_seq, _ = self.held
        self.first = []
        for mask in self.seq_masks:
            copy = self.away(
                mask - 1, given.at[flipped(self.seq, mask)], by_seq.at[mask - 1], (0, mask)
            )
            copy.start()
            self.first.append(copy)

    def middle(self):
        given, by_seq, by_dp = self.held
        out = self.outs[0]
        for copy in self.first:
            copy.wait_recv()
        part = given[self.seq]
        for mask in self.seq_masks:
            part = part + by_seq[mask - 1]
        given[self.seq] = part
        yield True
        base = len(self.first)
        second = []
        for mask in self.dp_masks:
            copy = self.away(
                base + mask - 1,
                given.at[self.seq, flipped(self.dp, mask)],
                by_dp.at[mask - 1],
                (mask, 0),
            )
            copy.start()
            second.append(copy)
        for copy in second:
            copy.wait_recv()
        value = given[self.seq, self.dp]
        for mask in self.dp_masks:
            value = value + by_dp[mask - 1]
        out[self.seq, self.dp] = value
        yield True
        base += len(second)
        third = []
        for mask in self.dp_masks:
            block = out.at[self.seq, self.dp]
            copy = self.away(base + mask - 1, block, block, (mask, 0))
            copy.start()
            arrival = self.away(
                base + mask - 1, block, out.at[self.seq, flipped(self.dp, mask)], (mask, 0)
            )
            third.append((copy, arrival))
        for _, arrival in third:
            arrival.wait_recv()
        yield True
        base += len(third)
        fourth = []
        for mask in self.seq_masks:
            block = out.at[self.seq]
            copy = self.away(base + mask - 1, block, block, (0, mask))
            copy.start()
            arrival = self.away(
                base + mask - 1, block, out.at[flipped(self.seq, mask)], (0, mask)
            )
            fourth.append((copy, arrival))
        for _, arrival in fourth:
            arrival.wait_recv()
        self.all = self.first + second + [c for c, _ in third] + [c for c, _ in fourth]

    def finish(self):
        for copy in self.all:
            copy.wait_send()


class Courier:
    def __init__(self):
        self.calls = 0

    def __call__(self, *jobs):
        number = self.calls
        self.calls += 1
        masks = []
        for job in jobs:
            for mask in job.masks:
                if mask not in masks:
                    masks.append(mask)
        operands = [value for job in jobs for value in job.operands]
        results = [value for job in jobs for value in job.results]
        in_vmem, given = [], []
        for job in jobs:
            given += list(job.given_in_vmem or [False] * len(job.operands))
            in_vmem += list(job.in_vmem or [job.out_in_vmem] * len(job.results))
        scratch = []
        for job in jobs:
            scratch += list(job.scratch)
            scratch += [
                pltpu.SemaphoreType.DMA((max(1, job.copies),)),
                pltpu.SemaphoreType.DMA((max(1, job.copies),)),
                pltpu.SemaphoreType.DMA((max(1, job.locals),)),
            ]

        def kernel(*refs):
            ins = list(refs[: len(operands)])
            outs = list(refs[len(operands) : len(operands) + len(results)])
            held = list(refs[len(operands) + len(results) :])
            dp, seq = lax.axis_index("dp"), lax.axis_index("seq")
            barrier = pltpu.get_barrier_semaphore()
            for mask in masks:
                pl.semaphore_signal(
                    barrier,
                    inc=1,
                    device_id=(flipped(dp, mask[0]), flipped(seq, mask[1])),
                    device_id_type=MESH,
                )
            pl.semaphore_wait(barrier, len(masks))
            for job in jobs:
                count_in, count_out = len(job.operands), len(job.results)
                own = len(job.scratch)
                job.bind(
                    ins[:count_in], outs[:count_out], held[:own], *held[own : own + 3]
                )
                ins, outs, held = ins[count_in:], outs[count_out:], held[own + 3 :]
            for job in jobs:
                job.start()
            turns = [job.middle() for job in jobs]
            while turns:
                turns = [turn for turn in turns if next(turn, None) is not None]
            for job in jobs:
                job.finish()

        sent = sum(value.size * value.dtype.itemsize for value in operands)
        outs = pl.pallas_call(
            kernel,
            out_shape=results,
            in_specs=[
                pl.BlockSpec(memory_space=pltpu.VMEM if vmem else pl.ANY) for vmem in given
            ],
            out_specs=[
                pl.BlockSpec(memory_space=pltpu.VMEM if vmem else pl.ANY) for vmem in in_vmem
            ],
            scratch_shapes=scratch,
            compiler_params=pltpu.CompilerParams(
                collective_id=number, has_side_effects=True, vmem_limit_bytes=60 << 20
            ),
            cost_estimate=pl.CostEstimate(flops=0, bytes_accessed=8 * sent, transcendentals=0),
            name="courier_%d" % number,
        )(*operands)
        return outs


def packed(values, blocks):
    flat = jnp.concatenate([value.reshape(-1).astype(jnp.float32) for value in values])
    each = -(-flat.shape[0] // (blocks * 1024)) * 1024
    return jnp.pad(flat, (0, blocks * each - flat.shape[0])).reshape(blocks, each // 128, 128)


def unpacked(flat, values):
    flat = flat.reshape(-1)
    out, begin = [], 0
    for value in values:
        out.append(flat[begin : begin + value.size].reshape(value.shape))
        begin += value.size
    return out


def large_sum(values):
    seq, dp = lax.axis_size("seq"), lax.axis_size("dp")
    blocks = packed(values, seq * dp)
    return SumAll(blocks.reshape((seq, dp) + blocks.shape[1:]))


def small_sum(values):
    return Everyone(packed(values, 1)[0])


def local_call(kernel, name, results, operands, flops=0):
    moved = sum(value.size * value.dtype.itemsize for value in list(operands) + list(results))
    return pl.pallas_call(
        kernel,
        out_shape=results,
        in_specs=[pl.BlockSpec(memory_space=pltpu.VMEM)] * len(operands),
        out_specs=[pl.BlockSpec(memory_space=pltpu.VMEM)] * len(results),
        compiler_params=pltpu.CompilerParams(vmem_limit_bytes=56 << 20),
        cost_estimate=pl.CostEstimate(flops=flops, bytes_accessed=moved, transcendentals=0),
        name=name,
    )(*operands)


def pieces_by_rank(split, columns):
    dp_count, seq_count = lax.axis_size("dp"), lax.axis_size("seq")
    each = columns // (dp_count * seq_count)
    out = []
    for dp in range(dp_count):
        for seq in range(seq_count):
            out.append(
                (split.rank(dp, seq), split.copy(dp) * each, (dp * seq_count + seq) * each)
            )
    return each, out


def lowered_chunks(near, wide, attn_widths, mix_in, mix_out, attn_in, attn_out, ffn_in, ffn_out, vectors):
    seq_count = lax.axis_size("seq")
    rows, width = mix_out.shape
    hidden = ffn_in.shape[-1]
    channels, mine = width // seq_count, hidden // wide.ranks

    def kernel(mix_in, mix_out, attn_in, attn_out, ffn_in, ffn_out, vectors, *outs):
        mix_chunk, attn_chunk, one, two, low_mix_out, low_attn_out, down_one, down_two, block = outs
        each, pieces = pieces_by_rank(near, width)
        for part in range(3):
            for rank, inner, outer in pieces:
                mix_chunk[rank, :, pl.ds(part * channels + inner, each)] = to_low(
                    mix_in[:, pl.ds(part * width + outer, each)]
                )
        begin, target = 0, 0
        for columns in attn_widths:
            each = columns // seq_count
            for rank in range(seq_count):
                attn_chunk[rank, :, pl.ds(target, each)] = to_low(
                    attn_in[:, pl.ds(begin + rank * each, each)]
                )
            begin, target = begin + columns, target + each
        each, pieces = pieces_by_rank(wide, hidden)
        for layer, chunk in enumerate((one, two)):
            for part in range(2):
                for rank, inner, outer in pieces:
                    chunk[rank, :, pl.ds(part * mine + inner, each)] = to_low(
                        ffn_in[layer, part, :, pl.ds(outer, each)]
                    )
        low_mix_out[...] = to_low(mix_out[...])
        low_attn_out[...] = to_low(attn_out[...])
        down_one[...] = to_low(ffn_out[0])
        down_two[...] = to_low(ffn_out[1])
        block[...] = jnp.zeros(block.shape, jnp.bfloat16)
        block[pl.ds(0, vectors.shape[0]), pl.ds(0, vectors.shape[1])] = to_low(vectors[...])

    def low(*shape):
        return jax.ShapeDtypeStruct(shape, jnp.bfloat16)

    results = (
        low(seq_count, rows, 3 * channels),
        low(seq_count, rows, sum(attn_widths) // seq_count),
        low(wide.ranks, rows, 2 * mine),
        low(wide.ranks, rows, 2 * mine),
        low(*mix_out.shape),
        low(*attn_out.shape),
        low(*ffn_out.shape[1:]),
        low(*ffn_out.shape[1:]),
        low(16, 128),
    )
    return local_call(
        kernel,
        "lower",
        results,
        (mix_in, mix_out, attn_in, attn_out, ffn_in, ffn_out, vectors),
    )


LINE = 512


class Step:
    def __init__(self, weights):
        self.weights = weights
        self.matrices = []
        begin, line = 0, 0
        for number, weight in enumerate(weights):
            lead = weight.shape[:-2]
            rows, columns = weight.shape[-2:]
            indices = [()]
            for size in lead:
                indices = [index + (place,) for index in indices for place in range(size)]
            for index in indices:
                self.matrices.append((number, index, rows, columns, begin, line))
                begin += rows
                line += columns // LINE
        self.rows, self.scalars = begin, line
        devices = lax.axis_size("dp") * lax.axis_size("seq")
        self.devices = devices
        self.lines = -(-(line + 1) // devices)
        self.sums = (lax.axis_size("seq"), lax.axis_size("dp"), self.lines, 1, LINE)

    def line(self, ref, number):
        per = self.lines
        dp = lax.axis_size("dp")
        return ref.at[number // (per * dp), (number // per) % dp, number % per]

    def natural(self):
        return [jax.ShapeDtypeStruct(weight.shape, jnp.float32) for weight in self.weights]

    def columns(self):
        return [
            jax.ShapeDtypeStruct(weight.shape[:-2] + (1, weight.shape[-1]), jnp.float32)
            for weight in self.weights
        ]

    def first(self, near, wide, attn_widths, traded, row_states, extra):
        seq_count = lax.axis_size("seq")

        def kernel(mix, attn, one, two, mix_out, attn_out, down_one, down_two, *refs):
            weights, (states, extra), refs = refs[:6], refs[6:8], refs[8:]
            grads, (rows_new, sums) = refs[:6], refs[6:]
            width = mix_out.shape[-1]
            channels = mix.shape[-1] // 3
            each, pieces = pieces_by_rank(near, width)
            for part in range(3):
                for rank, inner, outer in pieces:
                    grads[0][:, pl.ds(part * width + outer, each)] = mix[
                        rank, :, pl.ds(part * channels + inner, each)
                    ]
            grads[1][...] = mix_out[...]
            begin, source = 0, 0
            for columns in attn_widths:
                each = columns // seq_count
                for rank in range(seq_count):
                    grads[2][:, pl.ds(begin + rank * each, each)] = attn[
                        rank, :, pl.ds(source, each)
                    ]
                begin, source = begin + columns, source + each
            grads[3][...] = attn_out[...]
            hidden = grads[4].shape[-1]
            mine = one.shape[-1] // 2
            each, pieces = pieces_by_rank(wide, hidden)
            for layer, chunk in enumerate((one, two)):
                for part in range(2):
                    for rank, inner, outer in pieces:
                        grads[4][layer, part, :, pl.ds(outer, each)] = chunk[
                            rank, :, pl.ds(part * mine + inner, each)
                        ]
            grads[5][0] = down_one[...]
            grads[5][1] = down_two[...]
            lanes = lax.broadcasted_iota(jnp.int32, (1, LINE), 1)
            scalars = extra[...]
            for place in range(self.scalars + 1, self.lines * self.devices):
                self.line(sums, place)[...] = jnp.zeros((1, LINE), jnp.float32)
            for number, (which, index, rows, columns, begin, line) in enumerate(self.matrices):
                by_row = jnp.zeros((rows, 1), jnp.float32)
                norm = jnp.zeros((1, 1), jnp.float32)
                for strip in range(columns // LINE):
                    place = pl.ds(strip * LINE, LINE)
                    grad = grads[which][index + (slice(None), place)]
                    squares = grad * grad + SQUARE_FLOOR
                    by_row = by_row + jnp.sum(squares, axis=1, keepdims=True)
                    self.line(sums, line + strip)[...] = jnp.sum(squares, axis=0, keepdims=True)
                    weight = weights[which][index + (slice(None), place)]
                    norm = norm + jnp.sum(
                        jnp.sum(weight * weight, axis=1, keepdims=True), axis=0, keepdims=True
                    )
                fresh = DECAY_RATE * states[pl.ds(begin, rows)] + (1.0 - DECAY_RATE) * (
                    by_row / columns
                )
                rows_new[pl.ds(begin, rows)] = fresh
                scalars = jnp.where(
                    lanes == number, jnp.sum(fresh, axis=0, keepdims=True), scalars
                )
                scalars = jnp.where(lanes == 16 + number, norm, scalars)
            self.line(sums, self.scalars)[...] = scalars

        results = self.natural() + [
            jax.ShapeDtypeStruct((self.rows, 1), jnp.float32),
            jax.ShapeDtypeStruct(self.sums, jnp.float32),
        ]
        return local_call(
            kernel, "step_first", results, tuple(traded) + tuple(self.weights) + (row_states, extra)
        )

    def scaled(self, grads, rows_new, scalars, cols_new, entry, strip):
        number, which, index, rows, columns, begin = entry
        place = pl.ds(strip * LINE, LINE)
        mean_rows = scalars[:, number : number + 1] / (rows * self.devices)
        grad = grads[which][index + (slice(None), place)]
        by_column = lax.rsqrt(cols_new) * jnp.sqrt(mean_rows)
        return grad * lax.rsqrt(rows_new[pl.ds(begin, rows)]) * by_column

    def second(self, grads, rows_new, sums, col_states):
        def kernel(*refs):
            grads, (rows_new, sums), refs = refs[:6], refs[6:8], refs[8:]
            states, cols_out, squares_out = refs[:6], refs[6:12], refs[12]
            scalars = self.line(sums, self.scalars)[...]
            lanes = lax.broadcasted_iota(jnp.int32, squares_out.shape, 1)
            out = jnp.zeros(squares_out.shape, jnp.float32)
            for number, (which, index, rows, columns, begin, line) in enumerate(self.matrices):
                norm = jnp.zeros((1, 1), jnp.float32)
                for strip in range(columns // LINE):
                    place = pl.ds(strip * LINE, LINE)
                    spot = index + (slice(None), place)
                    cols_new = DECAY_RATE * states[which][spot] + (1.0 - DECAY_RATE) * (
                        self.line(sums, line + strip)[...] / (rows * self.devices)
                    )
                    cols_out[which][spot] = cols_new
                    update = self.scaled(
                        grads, rows_new, scalars, cols_new,
                        (number, which, index, rows, columns, begin), strip,
                    )
                    norm = norm + jnp.sum(
                        jnp.sum(update * update, axis=1, keepdims=True), axis=0, keepdims=True
                    )
                out = jnp.where(lanes == number, norm, out)
            squares_out[...] = out

        results = self.columns() + [jax.ShapeDtypeStruct((8, 128), jnp.float32)]
        return local_call(
            kernel, "step_second", results, tuple(grads) + (rows_new, sums) + tuple(col_states)
        )

    def third(self, grads, rows_new, sums, cols_new, squares):
        def kernel(*refs):
            grads, (rows_new, sums, squares), refs = refs[:6], refs[6:9], refs[9:]
            cols_new, weights, outs = refs[:6], refs[6:12], refs[12:]
            scalars = self.line(sums, self.scalars)[...]
            totals = jnp.sum(squares[...], axis=(0, 1))[0:1]
            for number, (which, index, rows, columns, begin, line) in enumerate(self.matrices):
                count = rows * self.devices * columns
                divisor = jnp.maximum(
                    1.0, jnp.sqrt(totals[:, number : number + 1] / count) / CLIP_LEVEL
                )
                rate = STEP_SCALE * jnp.maximum(
                    RATE_FLOOR, jnp.sqrt(scalars[:, 16 + number : 17 + number] / count)
                )
                for strip in range(columns // LINE):
                    spot = index + (slice(None), pl.ds(strip * LINE, LINE))
                    update = self.scaled(
                        grads, rows_new, scalars, cols_new[which][spot],
                        (number, which, index, rows, columns, begin), strip,
                    )
                    outs[which][spot] = weights[which][spot] - (rate / divisor) * update

        return local_call(
            kernel,
            "step_third",
            self.natural(),
            tuple(grads) + (rows_new, sums, squares) + tuple(cols_new) + tuple(self.weights),
        )


def owner_columns(value, split):
    count = lax.axis_size("dp")
    each = value.shape[-1] // count
    order = split.owner_order()
    if order == list(range(count)):
        return value
    return jnp.concatenate([value[..., dp * each : (dp + 1) * each] for dp in order], axis=-1)


def natural_columns(value, split):
    count = lax.axis_size("dp")
    each = value.shape[-1] // count
    order = split.owner_order()
    if order == list(range(count)):
        return value
    return jnp.concatenate(
        [value[..., order.index(dp) * each : (order.index(dp) + 1) * each] for dp in range(count)],
        axis=-1,
    )


def moved_to_rank(shard):
    seq, dp = lax.axis_size("seq"), lax.axis_size("dp")
    pairs = [(block, (block % dp) * seq + block // dp) for block in range(seq * dp)]
    return lax.ppermute(shard, ("dp", "seq"), pairs)


def moved_to_owner(shard):
    seq, dp = lax.axis_size("seq"), lax.axis_size("dp")
    pairs = [((block % dp) * seq + block // dp, block) for block in range(seq * dp)]
    return lax.ppermute(shard, ("dp", "seq"), pairs)


def rows_of(value, like):
    return value.reshape((-1,) + like.shape)


def flat(value):
    return value.reshape(-1, value.shape[-1])


def to_trade(block, split):
    return block.reshape(split.ranks, -1, block.shape[-1])


def by_copy(grad, split):
    return grad.reshape(split.copies, -1, grad.shape[-1])


def body(
    tokens,
    cotangent,
    lengths,
    mix_in,
    mix_in_rows,
    mix_in_cols,
    mix_out,
    mix_out_rows,
    mix_out_cols,
    attn_in,
    attn_in_rows,
    attn_in_cols,
    attn_out,
    attn_out_rows,
    attn_out_cols,
    ffn_in,
    ffn_in_rows,
    ffn_in_cols,
    ffn_out,
    ffn_out_rows,
    ffn_out_cols,
    vectors,
    vectors_moment,
    head_gain,
    head_moment,
):
    rows_here, width = tokens.shape
    seq_count = lax.axis_size("seq")
    devices = lax.axis_size("dp") * seq_count
    here = lax.axis_index("seq")
    courier = Courier()
    near, wide = Split(False), Split(True)
    total_rows = rows_here * seq_count
    positions = doc_layout(lengths[0], jnp.arange(total_rows, dtype=jnp.int32))[1]
    begins = (jnp.arange(total_rows, dtype=jnp.int32) - positions)[:, None]
    once = (positions >= 1).astype(jnp.float32)[:, None]
    twice = (positions >= 2).astype(jnp.float32)[:, None]
    cosine, sine = angles_for(positions, HEAD)
    cosine = jnp.concatenate([cosine, cosine] * (LANES // HEAD), axis=1)
    sine = jnp.concatenate([-sine, sine] * (LANES // HEAD), axis=1)
    channels = width // seq_count
    heads = HQ // seq_count
    kv_heads = KVH // seq_count
    kv_width = KVH * HEAD

    form = Heads(heads, kv_heads)
    head_gains = to_low(head_gain).astype(jnp.float32)
    gain_row = jnp.concatenate(
        [head_gains[0]] * heads + [head_gains[1]] * kv_heads + [jnp.ones(kv_heads * HEAD)]
    )[None]
    attn_widths = (width, kv_width, kv_width)
    (
        mix_chunk,
        attn_chunk,
        one_chunk,
        two_chunk,
        low_mix_out,
        attn_out_chunk,
        low_down_one,
        low_down_two,
        vector_block,
    ) = lowered_chunks(
        near, wide, attn_widths, mix_in, mix_out, attn_in, attn_out, ffn_in, ffn_out, vectors
    )
    attn_out_chunk = moved_to_rank(attn_out_chunk)
    mix_traded, gathered, one_traded = courier(
        Trade(near, mix_chunk), Everyone(vector_block), Trade(wide, one_chunk)
    )
    gains = gathered.reshape(devices, 16, 128)[:, : vectors.shape[0], : vectors.shape[1]]
    gains = jnp.moveaxis(gains, 0, 1).reshape(-1, width).astype(jnp.float32)
    inputs = tokens.astype(jnp.float32)
    low_one, scale_one = normalize(inputs, gains[0])
    w_mix_in, w_mix_out, w_down_one, attn_traded, two_traded = (
        flat(value)
        for value in courier(
            GatherWeights(near, flat(mix_traded), 4),
            GatherWeights(near, low_mix_out),
            GatherWeights(wide, low_down_one, 3),
            Trade(near, attn_chunk),
            Trade(wide, two_chunk),
        )
    )
    taps = lax.dynamic_index_in_dim(
        gains[4:7].reshape(3, -1, seq_count, width // devices), here, 2, keepdims=False
    ).reshape(3, channels)

    taps = jnp.pad(taps, ((0, 5), (0, 0)))
    added, *mix_kept, w_in_one, w_attn_in, w_attn_out = courier(
        MixForward(near, to_low(low_one), w_mix_in, w_mix_out, taps, once, twice),
        GatherWeights(wide, flat(one_traded), 4),
        GatherWeights(near, attn_traded, 2),
        GatherWeights(near, attn_out_chunk),
    )
    w_attn_in, w_attn_out = flat(w_attn_in), flat(w_attn_out)
    first = inputs + added
    w_in_one = flat(w_in_one)
    normed_one, scale_two = normalize(first, gains[1])
    added, rows_one = courier(
        FeedForward(wide, owner_columns(to_low(normed_one), wide), None, w_in_one, w_down_one, True)
    )
    second = first + added

    normed_three, scale_three = normalize(second, gains[2])
    added, *attn_kept, w_in_two, w_down_two, cotangent_all = courier(
        AttendForward(
            near, form, to_low(normed_three), w_attn_in, w_attn_out, cosine, sine, gain_row, begins
        ),
        GatherWeights(wide, two_traded, 4),
        GatherWeights(wide, low_down_two, 3),
        GatherTokens(wide, cotangent),
    )
    third = second + added
    w_in_two, w_down_two = flat(w_in_two), flat(w_down_two)
    normed_four, scale_four = normalize(third, gains[3])
    added, grad_normed, grad_in_two, grad_down_two = courier(
        FeedForward(
            wide, owner_columns(to_low(normed_four), wide), cotangent_all, w_in_two, w_down_two, True
        )
    )
    fourth = third + added
    grad_branch, grad_gain_three = normalize_back(
        natural_columns(grad_normed, wide), third, scale_four, gains[3]
    )
    grad_third = cotangent.astype(jnp.float32) + grad_branch
    (
        grad_normed_three,
        grad_attn_in,
        grad_attn_out,
        grad_heads,
        reduced_down_two,
        reduced_in_two,
    ) = courier(
        AttendBack(
            near,
            form,
            to_low(grad_third),
            w_attn_in,
            w_attn_out,
            cosine,
            sine,
            gain_row,
            begins,
            *attn_kept,
        ),
        ReduceWeights(wide, by_copy(grad_down_two, wide), 3),
        ReduceWeights(wide, by_copy(grad_in_two, wide), 4),
    )
    grad_heads = grad_heads[0].reshape(-1, HEAD)
    grad_head_q = jnp.sum(grad_heads[:heads], axis=0)
    grad_head_k = jnp.sum(grad_heads[heads : heads + kv_heads], axis=0)
    grad_branch_three, grad_gain_two = normalize_back(
        grad_normed_three, second, scale_three, gains[2]
    )
    grad_second = grad_third + grad_branch_three
    grad_normed, grad_in_one, grad_down_one, reduced_attn_in, reduced_attn_out = courier(
        FeedForward(wide, rows_one, to_low(grad_second), w_in_one, w_down_one, False),
        ReduceWeights(near, by_copy(grad_attn_in, near), 2),
        ReduceWeights(near, by_copy(grad_attn_out, near)),
    )
    grad_branch, grad_gain_one = normalize_back(
        natural_columns(grad_normed, wide), first, scale_two, gains[1]
    )
    grad_first = grad_second + grad_branch
    (
        grad_normed_one,
        grad_mix_in,
        grad_mix_out,
        tap_grads,
        reduced_down_one,
        reduced_in_one,
        two_back,
    ) = courier(
        MixBack(
            near, to_low(grad_first), w_mix_in, w_mix_out, taps, once, twice, *mix_kept
        ),
        ReduceWeights(wide, by_copy(grad_down_one, wide), 3),
        ReduceWeights(wide, by_copy(grad_in_one, wide), 4),
        Trade(wide, to_trade(reduced_in_two, wide)),
    )
    tap_grads = tap_grads[:3]
    reduced_mix_in, reduced_mix_out, attn_back, one_back = courier(
        ReduceWeights(near, by_copy(grad_mix_in, near), 4),
        ReduceWeights(near, by_copy(grad_mix_out, near)),
        Trade(near, to_trade(reduced_attn_in, near)),
        Trade(wide, to_trade(reduced_in_one, wide)),
    )
    grad_branch_zero, grad_gain_zero = normalize_back(
        grad_normed_one, inputs, scale_one, gains[0]
    )
    token_grad = grad_first + grad_branch_zero

    gain_grads = jnp.stack([grad_gain_zero, grad_gain_one, grad_gain_two, grad_gain_three])
    tap_full = lax.dynamic_update_slice_in_dim(
        jnp.zeros((3, lax.axis_size("dp"), seq_count, width // devices), jnp.float32),
        tap_grads.reshape(3, lax.axis_size("dp"), 1, width // devices),
        here,
        2,
    ).reshape(3, width)
    early_parts = [
        jnp.concatenate([gain_grads, tap_full], axis=0),
        jnp.stack([grad_head_q, grad_head_k]),
        jnp.sum(vectors * vectors, axis=-1),
    ]
    mix_back, early = courier(
        Trade(near, to_trade(reduced_mix_in, near)), large_sum(early_parts)
    )
    early = unpacked(early, early_parts)
    vector_norm = early[2]
    index = lax.axis_index("dp") * seq_count + here
    vector_grad = lax.dynamic_slice_in_dim(early[0], index * vectors.shape[1], vectors.shape[1], 1)
    head_grad = early[1]
    vector_moment_new = DECAY_RATE * vectors_moment + (1.0 - DECAY_RATE) * (
        vector_grad * vector_grad + SQUARE_FLOOR
    )
    vector_update = vector_grad * lax.rsqrt(vector_moment_new)
    vector_squares = jnp.sum(vector_update * vector_update, axis=-1)
    extra = jnp.pad(vector_squares[None], ((0, 0), (32, LINE - 32 - vector_squares.shape[0])))

    step = Step((mix_in, mix_out, attn_in, attn_out, ffn_in, ffn_out))
    row_states = (mix_in_rows, mix_out_rows, attn_in_rows, attn_out_rows, ffn_in_rows, ffn_out_rows)
    col_states = (mix_in_cols, mix_out_cols, attn_in_cols, attn_out_cols, ffn_in_cols, ffn_out_cols)
    *grads, rows_new, sums = step.first(
        near,
        wide,
        attn_widths,
        (
            mix_back,
            attn_back,
            one_back,
            two_back,
            reduced_mix_out,
            moved_to_owner(reduced_attn_out),
            reduced_down_one,
            reduced_down_two,
        ),
        jnp.concatenate([state.reshape(-1) for state in row_states])[:, None],
        extra,
    )
    (sums,) = courier(SumAll(sums))
    *cols_new, squares = step.second(
        grads, rows_new, sums, [state[..., None, :] for state in col_states]
    )
    (squares,) = courier(Everyone(squares))
    new_weights = step.third(grads, rows_new, sums, cols_new, squares)
    new_rows, begin = [], 0
    for state in row_states:
        new_rows.append(rows_new[begin : begin + state.size, 0].reshape(state.shape))
        begin += state.size
    vector_sums = sums.reshape(-1, LINE)[step.scalars, 32 : 32 + vector_squares.shape[0]]
    full_width = vectors.shape[-1] * devices
    vector_divisor = jnp.maximum(1.0, jnp.sqrt(vector_sums / full_width) / CLIP_LEVEL)
    vector_rate = STEP_SCALE * jnp.maximum(RATE_FLOOR, jnp.sqrt(vector_norm / full_width))
    vectors_new = vectors - (vector_rate / vector_divisor)[:, None] * vector_update
    head_moment_new = DECAY_RATE * head_moment + (1.0 - DECAY_RATE) * (
        head_grad * head_grad + SQUARE_FLOOR
    )
    head_update = head_grad * lax.rsqrt(head_moment_new)
    head_divisor = jnp.maximum(
        1.0, jnp.sqrt(jnp.mean(head_update * head_update, axis=-1, keepdims=True)) / CLIP_LEVEL
    )
    head_rate = STEP_SCALE * jnp.maximum(
        RATE_FLOOR, jnp.sqrt(jnp.mean(head_gain * head_gain, axis=-1, keepdims=True))
    )
    head_new = head_gain - head_rate / head_divisor * head_update
    outputs = [to_low(fourth), token_grad]
    for index in range(6):
        outputs += [grads[index], new_rows[index], cols_new[index][..., 0, :], new_weights[index]]
    return tuple(
        outputs
        + [vector_grad, vector_moment_new, vectors_new, head_grad, head_moment_new, head_new]
    )


def solution(mesh):
    return jax.shard_map(
        body,
        mesh=mesh,
        in_specs=(
            P(("dp", "seq"), None),
            P(("dp", "seq"), None),
            P("dp", None),
            P(("dp", "seq"), None),
            P(("dp", "seq")),
            P(),
            P(("dp", "seq"), None),
            P(("dp", "seq")),
            P(),
            P(("dp", "seq"), None),
            P(("dp", "seq")),
            P(),
            P(("dp", "seq"), None),
            P(("dp", "seq")),
            P(),
            P(None, None, ("dp", "seq"), None),
            P(None, None, ("dp", "seq")),
            P(),
            P(None, ("dp", "seq"), None),
            P(None, ("dp", "seq")),
            P(),
            P(None, ("dp", "seq")),
            P(None, ("dp", "seq")),
            P(),
            P(),
        ),
        out_specs=(
            P(("dp", "seq"), None),
            P(("dp", "seq"), None),
            P(("dp", "seq"), None),
            P(("dp", "seq")),
            P(),
            P(("dp", "seq"), None),
            P(("dp", "seq"), None),
            P(("dp", "seq")),
            P(),
            P(("dp", "seq"), None),
            P(("dp", "seq"), None),
            P(("dp", "seq")),
            P(),
            P(("dp", "seq"), None),
            P(("dp", "seq"), None),
            P(("dp", "seq")),
            P(),
            P(("dp", "seq"), None),
            P(None, None, ("dp", "seq"), None),
            P(None, None, ("dp", "seq")),
            P(),
            P(None, None, ("dp", "seq"), None),
            P(None, ("dp", "seq"), None),
            P(None, ("dp", "seq")),
            P(),
            P(None, ("dp", "seq"), None),
            P(None, ("dp", "seq")),
            P(None, ("dp", "seq")),
            P(None, ("dp", "seq")),
            P(),
            P(),
            P(),
        ),
        check_vma=False,
    )
```

```python
import math

import jax
import jax.numpy as jnp
from jax import lax
from jax.experimental import pallas as pl
from jax.experimental.pallas import tpu as pltpu
from jax.sharding import PartitionSpec as P

HQ = 16
KVH = 8
HEAD = 64

EPSILON = 1e-05
SQUARE_FLOOR = 1e-30
DECAY_RATE = 0.5
CLIP_LEVEL = 0.25
STEP_SCALE = 1.0
RATE_FLOOR = 0.001
MASKED_SCORE = -1e30


def matmul(operand, weight):
    return jnp.dot(operand, weight, preferred_element_type=jnp.float32)


def contract_first(operand, other):
    return lax.dot_general(
        operand, other, (((0,), (0,)), ((), ())), preferred_element_type=jnp.float32
    )


def contract_last(operand, other):
    return lax.dot_general(
        operand,
        other,
        (((operand.ndim - 1,), (other.ndim - 1,)), ((), ())),
        preferred_element_type=jnp.float32,
    )


def to_low(values):
    return values.astype(jnp.bfloat16)


def normalize(values, gain):
    scale = lax.rsqrt(jnp.mean(values * values, axis=-1, keepdims=True) + EPSILON)
    return (values * scale * gain, scale)


def normalize_back(grad_out, values, scale, gain):
    unit = values * scale
    grad_gain = jnp.sum(grad_out * unit, axis=tuple(range(values.ndim - 1)))
    weighted = grad_out * gain
    grad_values = scale * (weighted - unit * jnp.mean(weighted * unit, axis=-1, keepdims=True))
    return (grad_values, grad_gain)


def doc_layout(lens, places):
    bounds = jnp.cumsum(lens)
    passed = bounds[None, :] <= places[:, None]
    docs = jnp.sum(passed.astype(jnp.int32), axis=1)
    starts = jnp.sum(jnp.where(passed, lens[None, :], 0), axis=1)
    return (docs, places - starts)


def angles_for(places, width):
    half = width // 2
    freqs = jnp.exp(jnp.arange(half, dtype=jnp.float32) * (-2.0 * math.log(1000000.0) / width))
    angles = places.astype(jnp.float32)[:, None] * freqs[None, :]
    return (jnp.cos(angles), jnp.sin(angles))


def bits_of(axis):
    return lax.axis_size(axis).bit_length() - 1


def flipped(value, mask):
    for bit in range(mask.bit_length()):
        if (mask >> bit) & 1:
            value = value + (1 - 2 * ((value // (1 << bit)) % 2)) * (1 << bit)
    return value


def spread(bits):
    masks = [0]
    for bit in bits:
        masks = masks + [mask | (1 << bit) for mask in masks]
    return masks


class Split:
    def __init__(self, with_z):
        dp_bits = bits_of("dp")
        x_bits = dp_bits // 2
        self.shared = [x_bits] if with_z else []
        self.x_bits = list(range(x_bits))
        self.z_bits = [bit for bit in range(x_bits, dp_bits) if bit not in self.shared]
        self.free = self.x_bits + self.z_bits
        self.seq_bits = bits_of("seq")
        self.ranks = 1 << (self.seq_bits + len(self.shared))
        self.copies = 1 << len(self.free)
        self.links = [
            (dp_mask, seq_mask)
            for dp_mask in spread(self.shared)
            for seq_mask in spread(range(1, self.seq_bits))
        ]
        self.peers = [
            (dp_mask, seq_mask)
            for dp_mask in spread(self.shared)
            for seq_mask in range(1 << self.seq_bits)
        ]

    def pick(self, value, bits):
        out = 0
        for place, bit in enumerate(bits):
            out = out + ((value // (1 << bit)) % 2) * (1 << place)
        return out

    def rank(self, dp, seq):
        return self.pick(dp, self.shared) * (1 << self.seq_bits) + seq

    def copy(self, dp):
        return self.pick(dp, self.free)

    def row_of(self, dp, piece, pieces, depth):
        per = pieces // (1 << len(self.shared))
        place = piece // per
        for number, bit in enumerate(self.shared):
            own = (dp // (1 << bit)) % 2
            dp = dp + ((place >> number) % 2 - own) * (1 << bit)
        return dp * (per * depth) + (piece % per) * depth

    def owner_order(self):
        return sorted(
            range(lax.axis_size("dp")),
            key=lambda dp: (self.pick(dp, self.free), self.pick(dp, self.shared)),
        )


MESH = pl.DeviceIdType.MESH


class Job:
    scratch = ()
    copies = 0
    locals = 0
    out_in_vmem = False
    in_vmem = ()
    given_in_vmem = ()
    bulk = False
    works = False
    begin = 0.0

    def later(self, begin):
        self.begin = begin
        return self

    def span(self):
        return 10.0

    def steps(self):
        return 0

    def bind(self, operands, outs, scratch, send, recv, local):
        self.ins, self.outs, self.held = operands, outs, scratch
        self.send, self.recv, self.local = send, recv, local
        self.dp, self.seq = lax.axis_index("dp"), lax.axis_index("seq")

    def away(self, number, source, target, mask):
        return pltpu.make_async_remote_copy(
            src_ref=source,
            dst_ref=target,
            send_sem=self.send.at[number],
            recv_sem=self.recv.at[number],
            device_id=(flipped(self.dp, mask[0]), flipped(self.seq, mask[1])),
            device_id_type=MESH,
        )

    def near(self, number, source, target):
        return pltpu.make_async_copy(source, target, self.local.at[number])

    def start(self):
        pass

    def middle(self):
        return iter(())

    def finish(self):
        pass


class Spread:
    def __init__(self, job, source, slots, local):
        self.job, self.source, self.slots = job, source, slots
        links = job.split.links
        self.half = job.rows // 2
        self.mine = job.near(local, source, slots.at[0, 0])
        self.mine.start()
        self.direct, self.hops, self.beside, self.sent = {}, {}, {}, []
        self.done = set()
        number = 0
        for chip in range(1, job.chips):
            if links[chip][0] and links[chip][1]:
                self.hops[chip] = (number, number + 1)
                number += 2
                continue
            copy = job.away(number, source, slots.at[0, chip], links[chip])
            copy.start()
            self.direct[chip] = copy
            self.sent.append(copy)
            number += 1
        self.first = number
        self.send_beside(0, source)

    @staticmethod
    def copies(split):
        both = sum(1 for dp_mask, seq_mask in split.links if dp_mask and seq_mask)
        return 2 * len(split.links) - 1 + both

    def part(self, chip, number):
        return self.slots.at[0, chip, pl.ds(number * self.half, self.half)]

    def send_beside(self, chip, source):
        copy = self.job.away(self.first + chip, source, self.slots.at[1, chip], (0, 1))
        copy.start()
        self.beside[chip] = copy

    def pass_on(self, chip):
        links = self.job.split.links
        for far, numbers in self.hops.items():
            dp_mask, seq_mask = links[far]
            for which, (via, onward) in enumerate(
                (((0, seq_mask), (dp_mask, 0)), ((dp_mask, 0), (0, seq_mask)))
            ):
                if via == links[chip]:
                    copy = self.job.away(
                        numbers[which], self.part(chip, which), self.part(far, which), onward
                    )
                    copy.start()
                    self.sent.append(copy)

    def ready(self, core, chip):
        links = self.job.split.links
        if core:
            self.beside[chip].wait_recv()
            return
        if chip in self.done:
            return
        self.done.add(chip)
        if chip == 0:
            self.mine.wait()
            return
        if chip in self.direct:
            self.direct[chip].wait_recv()
            self.pass_on(chip)
        else:
            for which, number in enumerate(self.hops[chip]):
                onward = ((links[chip][0], 0), (0, links[chip][1]))[which]
                part = self.part(chip, which)
                self.job.away(number, part, part, onward).wait_recv()
        self.send_beside(chip, self.slots.at[0, chip])

    def finish(self):
        for copy in self.sent + list(self.beside.values()):
            copy.wait_send()


class GatherTokens(Job):
    def __init__(self, split, value):
        self.split = split
        self.operands = (value,)
        self.chips = len(split.links)
        self.results = (jax.ShapeDtypeStruct((2, self.chips) + value.shape, value.dtype),)
        self.masks = [mask for mask in split.links[1:]] + [(0, 1)]
        self.rows = value.shape[0]
        self.copies = Spread.copies(split)
        self.locals = 1

    def span(self):
        return 13.0 if self.chips == 2 else 26.0

    def steps(self):
        return self.chips

    def start(self):
        self.arrive = Spread(self, self.ins[0], self.outs[0], 0)

    def middle(self):
        for chip in range(self.chips):
            self.arrive.ready(0, chip)
            yield True

    def finish(self):
        for chip in range(self.chips):
            self.arrive.ready(1, chip)
        self.arrive.finish()


STRIP = 32
AHEAD = 2
STRETCH = 1.0


class ScatterTokens(Job):
    out_in_vmem = True

    def span(self):
        return 3.0 * self.chips

    def steps(self):
        return self.chips - 1

    def __init__(self, split, partial):
        self.split = split
        rows, width = partial.shape[-2:]
        self.chips = len(split.links)
        self.operands = (partial.reshape(2, self.chips, rows, width),)
        self.results = (jax.ShapeDtypeStruct((rows, width), jnp.float32),)
        self.masks = [mask for mask in split.links[1:]] + [(0, 1)]
        self.copies = 2 * self.chips - 1
        self.locals = self.chips
        self.scratch = (
            pltpu.VMEM((self.chips, rows, width), jnp.float32),
            pltpu.VMEM((2, rows, width), jnp.float32),
            pltpu.VMEM((2, rows, width), jnp.bfloat16),
            pltpu.VMEM((max(1, self.chips - 1), rows, width), jnp.bfloat16),
        )
        self.rows = rows

    def start(self):
        partial = self.ins[0]
        theirs = self.held[0]
        self.order = list(range(1, self.chips)) + [0]
        self.beside, self.loads = {}, {}
        for chip in self.order:
            self.beside[chip] = self.away(
                self.chips - 1 + chip, partial.at[1, chip], theirs.at[chip], (0, 1)
            )
            self.beside[chip].start()
        self.load(0)
        self.load(1)

    def load(self, index):
        if index < self.chips:
            chip = self.order[index]
            self.loads[chip] = self.near(
                chip, self.ins[0].at[0, chip], self.held[1].at[index % 2]
            )
            self.loads[chip].start()

    def strips(self, update):
        @pl.loop(0, self.rows // STRIP)
        def _(strip):
            update(pl.ds(pl.multiple_of(strip * STRIP, STRIP), STRIP))

    def middle(self):
        theirs, mine, sent, landed = self.held
        self.far = []
        for index, chip in enumerate(self.order[:-1]):
            self.beside[chip].wait_recv()
            self.loads[chip].wait()
            if index >= 2:
                self.far[index - 2].wait_send()

            def update(rows, index=index, chip=chip):
                sent[index % 2, rows] = to_low(theirs[chip, rows] + mine[index % 2, rows])

            self.strips(update)
            self.load(index + 2)
            copy = self.away(
                chip - 1, sent.at[index % 2], landed.at[chip - 1], self.split.links[chip]
            )
            copy.start()
            self.far.append(copy)
            yield True

    def finish(self):
        theirs, mine, _, landed = self.held
        out = self.outs[0]
        self.beside[0].wait_recv()
        self.loads[0].wait()
        for copy in self.far:
            copy.wait_recv()
        last = (self.chips - 1) % 2

        def update(rows):
            value = theirs[0, rows] + mine[last, rows]
            for chip in range(1, self.chips):
                value = value + landed[chip - 1, rows].astype(jnp.float32)
            out[rows] = value

        self.strips(update)
        for copy in self.far[-2:]:
            copy.wait_send()
        for copy in self.beside.values():
            copy.wait_send()


class Trade(Job):
    def __init__(self, split, value):
        self.split = split
        self.operands = (value,)
        self.results = (jax.ShapeDtypeStruct(value.shape, value.dtype),)
        self.masks = split.peers[1:]
        self.copies = len(self.masks)
        self.locals = 1

    def start(self):
        given, out = self.ins[0], self.outs[0]
        rank = self.split.rank(self.dp, self.seq)
        self.mine = self.near(0, given.at[rank], out.at[rank])
        self.mine.start()
        self.far = []
        for number, mask in enumerate(self.masks):
            other = self.split.rank(flipped(self.dp, mask[0]), flipped(self.seq, mask[1]))
            copy = self.away(number, given.at[other], out.at[rank], mask)
            copy.start()
            self.far.append(copy)

    def finish(self):
        self.mine.wait()
        for copy in self.far:
            copy.wait()


def pieces_of(rows, most, tile):
    for count in range(most, 1, -1):
        if rows % (count * tile) == 0:
            return count
    return 1


class TradeOf(Trade):
    def __init__(self, split, job):
        rows, columns = job.results[0].shape
        self.split, self.job = split, job
        self.depth = rows // split.ranks
        self.operands = ()
        self.results = (
            jax.ShapeDtypeStruct((split.ranks, self.depth, columns), jnp.float32),
        )
        self.masks = split.peers[1:]
        self.copies = len(self.masks)
        self.locals = 1

    def given(self, rank):
        row = pl.multiple_of(rank * self.depth, self.depth)
        return self.job.outs[0].at[pl.ds(row, self.depth)]

    def start(self):
        out = self.outs[0]
        rank = self.split.rank(self.dp, self.seq)
        self.mine = self.near(0, self.given(rank), out.at[rank])
        self.mine.start()
        self.far = []
        for number, mask in enumerate(self.masks):
            other = self.split.rank(flipped(self.dp, mask[0]), flipped(self.seq, mask[1]))
            copy = self.away(number, self.given(other), out.at[rank], mask)
            copy.start()
            self.far.append(copy)


class GatherWeights(Job):
    bulk = True

    def span(self):
        return self.operands[0].size * len(self.z_masks) * len(self.x_masks) * 2.4e-5

    def steps(self):
        return self.count

    def __init__(self, split, value, most=1, across=False):
        self.split = split
        self.operands = (value,)
        self.across = across and bool(split.shared)
        rows, columns = value.shape
        shape = (split.copies * rows, columns) if self.across else (split.copies, rows, columns)
        self.results = (jax.ShapeDtypeStruct(shape, value.dtype),)
        self.z_masks = spread(split.z_bits)
        self.x_masks = spread(split.x_bits)
        self.masks = [(mask, 0) for mask in self.z_masks[1:] + self.x_masks[1:]]
        self.count = pieces_of(rows, most, 16)
        self.depth = rows // self.count
        self.copies = (len(self.z_masks) * len(self.x_masks) - 1) * self.count
        self.locals = self.count

    def part(self, ref, piece):
        return ref if self.count == 1 else ref.at[pl.ds(piece * self.depth, self.depth)]

    def slot(self, mask, piece):
        dp = flipped(self.dp, mask)
        if not self.across:
            return self.part(self.outs[0].at[self.split.copy(dp)], piece)
        row = self.split.row_of(dp, piece, self.count, self.depth)
        return self.outs[0].at[pl.ds(pl.multiple_of(row, self.depth), self.depth)]

    def start(self):
        own = self.ins[0]
        self.mine = [
            self.near(piece, self.part(own, piece), self.slot(0, piece))
            for piece in range(self.count)
        ]
        for copy in self.mine:
            copy.start()
        self.number = 0
        self.sent, self.arrivals, self.rest = [], {}, []
        for piece in range(min(AHEAD, self.count)):
            self.send_z(piece)

    def source(self, mask, piece):
        return self.slot(mask, piece) if mask else self.part(self.ins[0], piece)

    def send_z(self, piece):
        for bit in self.split.z_bits:
            self.hop(0, piece, 1 << bit)

    def hop(self, mask, piece, onward):
        source = self.source(mask, piece)
        copy = self.away(self.number, source, self.slot(mask, piece), (onward, 0))
        copy.start()
        self.sent.append(copy)
        self.arrivals[mask | onward, piece] = self.away(
            self.number, source, self.slot(mask | onward, piece), (onward, 0)
        )
        self.number += 1

    def pass_on(self, from_mask, piece):
        source = self.source(from_mask, piece)
        for mask in self.x_masks[1:]:
            copy = self.away(self.number, source, self.slot(from_mask, piece), (mask, 0))
            copy.start()
            self.sent.append(copy)
            self.rest.append(
                self.away(self.number, source, self.slot(from_mask ^ mask, piece), (mask, 0))
            )
            self.number += 1

    def take(self, masks, piece):
        for mask in masks:
            self.arrivals[mask, piece].wait_recv()
            for bit in self.split.z_bits:
                if (1 << bit) < (mask & -mask):
                    self.hop(mask, piece, 1 << bit)
            self.pass_on(mask, piece)

    def middle(self):
        single = [mask for mask in self.z_masks[1:] if mask & (mask - 1) == 0]
        longer = [mask for mask in self.z_masks[1:] if mask & (mask - 1)]
        for piece in range(self.count):
            self.pass_on(0, piece)
            self.take(single, piece)
            if piece:
                self.take(longer, piece - 1)
            if piece + AHEAD < self.count:
                self.send_z(piece + AHEAD)
            yield True
        self.take(longer, self.count - 1)

    def finish(self):
        for copy in self.mine:
            copy.wait()
        for arrival in self.rest:
            arrival.wait_recv()
        for copy in self.sent:
            copy.wait_send()


class ReduceWeights(Job):
    out_in_vmem = True
    bulk = True

    def span(self):
        return self.size * 4.5e-5

    def steps(self):
        return len(self.units) + self.count

    def __init__(self, split, grad, most=1, across=False, of=None):
        self.split = split
        self.across = across and bool(split.shared)
        shape = (grad.shape[0] // split.copies, grad.shape[1])
        self.of = of
        if of is not None:
            self.operands = ()
        elif self.across:
            self.operands = (grad,)
        else:
            self.operands = (grad.reshape((split.copies,) + shape),)
        self.size = grad.shape[0] * grad.shape[1]
        self.results = (jax.ShapeDtypeStruct(shape, jnp.float32),)
        self.z_masks = spread(split.z_bits)
        self.x_masks = spread(split.x_bits)
        self.masks = [(mask, 0) for mask in self.z_masks[1:] + self.x_masks[1:]]
        self.count = pieces_of(shape[0], most, 8)
        self.depth = shape[0] // self.count
        far_z, far_x = len(self.z_masks) - 1, len(self.x_masks) - 1
        order = sorted(
            range(far_z + 1), key=lambda place: self.low_bit(place) or 1 << 30
        )
        stages = {}
        for place in order:
            stages.setdefault(self.low_bit(place), []).append(place)
        self.units = [
            (piece, place)
            for places in stages.values()
            for piece in range(self.count)
            for place in places
        ]
        self.copies = self.count * (far_z + (far_z + 1) * far_x)
        self.locals = len(self.units)
        self.scratch = (
            pltpu.VMEM((far_x, far_z + 1) + shape, jnp.float32),
            pltpu.VMEM((far_z + 1,) + shape, jnp.float32),
            pltpu.VMEM((far_z,) + shape, jnp.float32),
        )

    def low_bit(self, place):
        return self.z_masks[place] & -self.z_masks[place]

    def children(self, place):
        mask, low = self.z_masks[place], self.low_bit(place) or 1 << 30
        return [
            self.z_masks.index(mask | 1 << bit) for bit in self.split.z_bits if 1 << bit < low
        ]

    def rows(self, piece):
        return pl.ds(piece * self.depth, self.depth)

    def part(self, mask, piece):
        dp = flipped(self.dp, mask)
        if self.of is not None:
            job, number = self.of
            row = (self.split.copy(dp) * self.count + piece) * self.depth
            return job.outs[number].at[pl.ds(pl.multiple_of(row, self.depth), self.depth)]
        if not self.across:
            return self.ins[0].at[self.split.copy(dp), self.rows(piece)]
        row = self.split.row_of(dp, piece, self.count, self.depth)
        return self.ins[0].at[pl.ds(pl.multiple_of(row, self.depth), self.depth)]

    def start(self):
        self.number = 0
        self.sent, self.loads, self.far = {}, {}, {}
        for index in range(min(AHEAD, len(self.units))):
            self.send_x(index)

    def send_x(self, index):
        piece, place = self.units[index]
        mask = self.z_masks[place]
        by_x, mine, _ = self.held
        copies = []
        for number, x_mask in enumerate(self.x_masks[1:]):
            copy = self.away(
                self.number,
                self.part(mask ^ x_mask, piece),
                by_x.at[number, place, self.rows(piece)],
                (x_mask, 0),
            )
            copy.start()
            copies.append(copy)
            self.number += 1
        self.sent[index] = copies
        load = self.near(index, self.part(mask, piece), mine.at[place, self.rows(piece)])
        load.start()
        self.loads[index] = load

    def strips(self, piece, update):
        step = 8
        for size in (64, 32, 16):
            if self.depth % size == 0:
                step = size
                break

        @pl.loop(0, self.depth // step)
        def _(strip):
            update(pl.ds(pl.multiple_of(piece * self.depth + strip * step, 8), step))

    def middle(self):
        by_x, mine, by_z = self.held
        for index, (piece, place) in enumerate(self.units):
            self.loads[index].wait()
            for copy in self.sent[index]:
                copy.wait_recv()
            if index + AHEAD < len(self.units):
                self.send_x(index + AHEAD)

            if not place:
                yield True
                continue
            self.add(piece, place)
            copy = self.away(
                self.number,
                mine.at[place, self.rows(piece)],
                by_z.at[place - 1, self.rows(piece)],
                (self.low_bit(place), 0),
            )
            copy.start()
            self.far[(piece, place)] = copy
            self.number += 1
            yield True
        for piece in range(self.count):
            self.add(piece, 0)
            yield True

    def add(self, piece, place):
        by_x, mine, by_z = self.held
        children = self.children(place)
        for child in children:
            self.far[(piece, child)].wait_recv()
        target = mine.at[place] if place else self.outs[0]

        def update(rows):
            value = mine[place, rows]
            for number in range(len(self.x_masks) - 1):
                value = value + by_x[number, place, rows]
            for child in children:
                value = value + by_z[child - 1, rows]
            target[rows] = value

        self.strips(piece, update)

    def finish(self):
        for copy in self.far.values():
            copy.wait_send()
        for copies in self.sent.values():
            for copy in copies:
                copy.wait_send()


class Return:
    def __init__(self, job, first, scratch, out):
        self.job, self.first, self.out = job, first, out
        self.theirs, self.mine, self.stage, self.sent, self.landed = scratch
        self.beside, self.far = {}, {}

    @staticmethod
    def scratch(chips, rows, width):
        return (
            pltpu.VMEM((chips, rows, width), jnp.float32),
            pltpu.VMEM((2, rows, width), jnp.float32),
            pltpu.VMEM((2, rows, width), jnp.float32),
            pltpu.VMEM((2, rows, width), jnp.bfloat16),
            pltpu.VMEM((max(1, chips - 1), rows, width), jnp.bfloat16),
        )

    def put(self, core, chip, value):
        chips = self.job.chips
        if core == 0:
            self.mine[min(chip, 1)] = value
            return
        order = list(self.beside)
        if len(order) >= 2:
            self.beside[order[-2]].wait_send()
        spot = len(order) % 2
        self.stage[spot] = value
        copy = self.job.away(
            self.first + chips - 1 + chip, self.stage.at[spot], self.theirs.at[chip], (0, 1)
        )
        copy.start()
        self.beside[chip] = copy

    def strips(self, update):
        @pl.loop(0, self.job.rows // STRIP)
        def _(strip):
            update(pl.ds(pl.multiple_of(strip * STRIP, STRIP), STRIP))

    def pass_on(self, chip):
        if chip == 0:
            return
        self.beside[chip].wait_recv()
        order = list(self.far)
        if len(order) >= 2:
            self.far[order[-2]].wait_send()
        spot = len(order) % 2

        def update(rows):
            self.sent[spot, rows] = to_low(self.theirs[chip, rows] + self.mine[1, rows])

        self.strips(update)
        copy = self.job.away(
            self.first + chip - 1,
            self.sent.at[spot],
            self.landed.at[chip - 1],
            self.job.split.links[chip],
        )
        copy.start()
        self.far[chip] = copy

    def finish(self):
        chips = self.job.chips
        self.beside[0].wait_recv()
        for chip in range(1, chips):
            self.far[chip].wait_recv()

        def update(rows):
            value = self.theirs[0, rows] + self.mine[0, rows]
            for chip in range(1, chips):
                value = value + self.landed[chip - 1, rows].astype(jnp.float32)
            self.out[rows] = value

        self.strips(update)
        for chip in list(self.beside)[-2:]:
            self.beside[chip].wait_send()
        for chip in list(self.far)[-2:]:
            self.far[chip].wait_send()


class Layer(Job):
    works = True
    work_steps = 0
    after_steps = 0
    length = 35.0

    def span(self):
        return self.length

    def steps(self):
        return 3 * self.chips + 2 * self.chips * (self.work_steps + self.after_steps) + 2

    def __init__(self, split, own, others, results, scratch=()):
        self.split = split
        self.chips = len(split.links)
        self.rows, self.width = own.shape
        self.total = 2 * self.chips * self.rows
        self.operands = (own,) + tuple(others)
        self.given_in_vmem = (False,) + (True,) * len(others)
        slots = (2, self.chips, self.rows, self.width)
        self.results = (jax.ShapeDtypeStruct((self.rows, self.width), jnp.float32),) + tuple(results)
        self.in_vmem = (True,) * len(self.results)
        self.scratch = (
            (pltpu.VMEM(slots, jnp.bfloat16),)
            + Return.scratch(self.chips, self.rows, self.width)
            + tuple(scratch)
        )
        self.masks = [mask for mask in split.links[1:]] + [(0, 1)]
        self.copies = Spread.copies(split) + 2 * self.chips - 1
        self.locals = 2
        self.places = [(core, chip) for chip in range(self.chips) for core in (0, 1)]

    def start(self):
        self.slots = self.held[0]
        self.back = Return(self, Spread.copies(self.split), self.held[1:6], self.outs[0])
        self.more = self.held[6:]
        self.arrive = Spread(self, self.ins[0], self.slots, 0)

    def at(self, core, chip):
        place = flipped(self.seq, 2 * chip + core)
        return pl.ds(pl.multiple_of(place * self.rows, self.rows), self.rows)

    def middle(self):
        self.open()
        for core, chip in self.places:
            self.arrive.ready(core, chip)
            self.take(core, chip)
            yield True
        yield from self.work()
        for chip in list(range(1, self.chips)) + [0]:
            for core in (1, 0):
                self.back.put(core, chip, self.give(core, chip))
            yield True
            self.back.pass_on(chip)
        yield from self.after()

    def open(self):
        pass

    def work(self):
        return iter(())

    def after(self):
        return iter(())

    def finish(self):
        self.back.finish()
        self.arrive.finish()


def turned(value, steps):
    return pltpu.roll(value, steps % value.shape[0], 0)


class MixForward(Layer):
    def __init__(self, split, own, w_in, w_out, taps, once, twice):
        rows = 2 * len(split.links) * own.shape[0]
        channels = w_out.shape[0]
        super().__init__(
            split,
            own,
            (w_in, w_out, taps, once, twice),
            (
                jax.ShapeDtypeStruct((2, len(split.links)) + own.shape, jnp.bfloat16),
                jax.ShapeDtypeStruct((rows, 3 * channels), jnp.float32),
                jax.ShapeDtypeStruct((rows, channels), jnp.float32),
                jax.ShapeDtypeStruct((rows, channels), jnp.bfloat16),
            ),
        )
        self.channels = channels

    def open(self):
        _, self.w_in, self.w_out, self.taps, self.once, self.twice = self.ins
        _, self.kept, self.projected, self.conv, self.gated = self.outs

    def take(self, core, chip):
        value = self.slots[core, chip]
        self.kept[core, chip] = value
        self.projected[self.at(core, chip)] = matmul(value, self.w_in[...])

    def work(self):
        each = self.channels
        mixed = to_low(self.projected[:, :each] * self.projected[:, 2 * each :]).astype(jnp.float32)
        conv = (
            self.taps[2:3] * mixed
            + self.taps[1:2] * turned(mixed, 1) * self.once[...]
            + self.taps[0:1] * turned(mixed, 2) * self.twice[...]
        )
        self.conv[...] = conv
        self.gated[...] = to_low(self.projected[:, each : 2 * each] * conv)
        yield True

    def give(self, core, chip):
        return matmul(self.gated[self.at(core, chip)], self.w_out[...])


class MixBack(Layer):
    after_steps = 1

    def __init__(self, split, own, w_in, w_out, taps, once, twice, kept, projected, conv, gated):
        rows = 2 * len(split.links) * own.shape[0]
        channels = w_out.shape[0]
        super().__init__(
            split,
            own,
            (w_in, w_out, taps, once, twice, kept, projected, conv, gated),
            (
                jax.ShapeDtypeStruct(w_in.shape, jnp.float32),
                jax.ShapeDtypeStruct(w_out.shape, jnp.float32),
                jax.ShapeDtypeStruct(taps.shape, jnp.float32),
            ),
            (
                pltpu.VMEM((rows, channels), jnp.float32),
                pltpu.VMEM((rows, 3 * channels), jnp.bfloat16),
            ),
        )
        self.channels = channels

    def open(self):
        _, self.w_in, self.w_out, self.taps, self.once, self.twice = self.ins[:6]
        self.kept, self.projected, self.conv, self.gated = self.ins[6:]
        _, self.grad_in, self.grad_out, self.grad_taps = self.outs
        self.grad_gated, self.grad_projected = self.more

    def take(self, core, chip):
        grad = self.slots[core, chip]
        self.grad_gated[self.at(core, chip)] = contract_last(grad, self.w_out[...])
        term = contract_first(self.gated[self.at(core, chip)], grad)
        if (core, chip) == (0, 0):
            self.grad_out[...] = term
        else:
            self.grad_out[...] += term

    def work(self):
        each = self.channels
        part_b = self.projected[:, :each]
        part_c = self.projected[:, each : 2 * each]
        part_v = self.projected[:, 2 * each :]
        once, twice = self.once[...], self.twice[...]
        mixed = to_low(part_b * part_v).astype(jnp.float32)
        grad_gated = self.grad_gated[...]
        grad_conv = grad_gated * part_c
        back_one, back_two = grad_conv * once, grad_conv * twice
        self.grad_taps[...] = jnp.zeros(self.grad_taps.shape, jnp.float32)
        self.grad_taps[0:1] = jnp.sum(back_two * turned(mixed, 2), axis=0, keepdims=True)
        self.grad_taps[1:2] = jnp.sum(back_one * turned(mixed, 1), axis=0, keepdims=True)
        self.grad_taps[2:3] = jnp.sum(grad_conv * mixed, axis=0, keepdims=True)
        grad_mixed = (
            self.taps[2:3] * grad_conv
            + turned(self.taps[1:2] * back_one, -1)
            + turned(self.taps[0:1] * back_two, -2)
        )
        grad_mixed = to_low(grad_mixed).astype(jnp.float32)
        self.grad_projected[:, :each] = to_low(grad_mixed * part_v)
        self.grad_projected[:, each : 2 * each] = to_low(grad_gated * self.conv[...])
        self.grad_projected[:, 2 * each :] = to_low(grad_mixed * part_b)
        yield True

    def give(self, core, chip):
        return contract_last(self.grad_projected[self.at(core, chip)], self.w_in[...])

    def after(self):
        for core, chip in self.places:
            term = contract_first(
                self.kept[core, chip], self.grad_projected[self.at(core, chip)]
            )
            if (core, chip) == (0, 0):
                self.grad_in[...] = term
            else:
                self.grad_in[...] += term
            yield True


LANES = 128


def head_means(value):
    row = lax.broadcasted_iota(jnp.int32, (LANES, LANES), 0) // HEAD
    column = lax.broadcasted_iota(jnp.int32, (LANES, LANES), 1) // HEAD
    same = jnp.where(row == column, 1.0 / HEAD, 0.0)
    return jnp.dot(
        value, same, preferred_element_type=jnp.float32, precision=lax.Precision.HIGHEST
    )


def half_turned(value):
    lane = lax.broadcasted_iota(jnp.int32, value.shape, 1) % HEAD
    ahead = pltpu.roll(value, LANES - HEAD // 2, 1)
    behind = pltpu.roll(value, HEAD // 2, 1)
    return jnp.where(lane < HEAD // 2, ahead, behind)


class Heads:
    def __init__(self, heads, kv_heads):
        self.heads, self.kv_heads = heads, kv_heads
        self.shared = heads // kv_heads
        self.turned = (heads + kv_heads) * HEAD
        self.width = (heads + 2 * kv_heads) * HEAD

    def tiles(self):
        for begin in range(0, self.width, LANES):
            yield slice(begin, begin + LANES), min(LANES, max(0, self.turned - begin))

    def q(self, head):
        return slice(head * HEAD, (head + 1) * HEAD)

    def k(self, head):
        begin = self.heads + head // self.shared
        return slice(begin * HEAD, (begin + 1) * HEAD)

    def v(self, head):
        begin = self.heads + self.kv_heads + head // self.shared
        return slice(begin * HEAD, (begin + 1) * HEAD)

    @staticmethod
    def some(lanes, value, other):
        if lanes == LANES:
            return value
        lane = lax.broadcasted_iota(jnp.int32, value.shape, 1)
        return jnp.where(lane < lanes, value, other)


class AttendForward(Layer):
    work_steps = 1
    length = 42.0

    def __init__(self, split, heads, own, w_in, w_out, cosine, sine, gain, begins):
        rows = 2 * len(split.links) * own.shape[0]
        self.heads = heads
        super().__init__(
            split,
            own,
            (w_in, w_out, cosine, sine, gain, begins),
            (
                jax.ShapeDtypeStruct((2, len(split.links)) + own.shape, jnp.bfloat16),
                jax.ShapeDtypeStruct((rows, heads.width), jnp.float32),
                jax.ShapeDtypeStruct((rows, heads.width), jnp.bfloat16),
                jax.ShapeDtypeStruct((rows, heads.heads * HEAD), jnp.bfloat16),
                jax.ShapeDtypeStruct((rows, heads.heads), jnp.float32),
            ),
        )

    def open(self):
        _, self.w_in, self.w_out, self.cosine, self.sine, self.gain, self.begins = self.ins
        _, self.kept, self.projected, self.turned, self.out, self.lse = self.outs

    def take(self, core, chip):
        value = self.slots[core, chip]
        self.kept[core, chip] = value
        rows = self.at(core, chip)
        projected = matmul(value, self.w_in[...])
        self.projected[rows] = projected
        for lanes, count in self.heads.tiles():
            raw = projected[:, lanes]
            if count:
                unit = raw * lax.rsqrt(head_means(raw * raw) + EPSILON)
                normed = unit * self.gain[:, lanes]
                spun = normed * self.cosine[rows] + half_turned(normed) * self.sine[rows]
                raw = self.heads.some(count, spun, raw)
            self.turned[rows, lanes] = to_low(raw)

    def work(self):
        for place in range(2 * self.chips):
            rows = slice(place * self.rows, (place + 1) * self.rows)
            bias, seen = hidden_scores(self.begins[rows], place, self.rows)
            for head in range(self.heads.heads):
                scores = (
                    contract_last(
                        self.turned[rows, self.heads.q(head)], self.turned[:seen, self.heads.k(head)]
                    )
                    * HEAD ** (-0.5)
                    + bias
                )
                peak = jnp.max(scores, axis=-1, keepdims=True)
                expo = jnp.exp(scores - peak)
                count = jnp.sum(expo, axis=-1, keepdims=True)
                probs = to_low(expo * (1.0 / count))
                self.out[rows, self.heads.q(head)] = to_low(
                    matmul(probs, self.turned[:seen, self.heads.v(head)])
                )
                self.lse[rows, head : head + 1] = peak + jnp.log(count)
            yield True

    def give(self, core, chip):
        return matmul(self.out[self.at(core, chip)], self.w_out[...])


def hidden_scores(begins, place, rows):
    seen = (place + 1) * rows
    row = place * rows + lax.broadcasted_iota(jnp.int32, (rows, seen), 0)
    column = lax.broadcasted_iota(jnp.int32, (rows, seen), 1)
    allowed = (column >= begins) & (column <= row)
    return jnp.where(allowed, 0.0, MASKED_SCORE), seen


class AttendBack(Layer):
    work_steps = 2
    after_steps = 1
    length = 52.0

    def __init__(
        self, split, heads, own, w_in, w_out, cosine, sine, gain, begins, kept, projected, turned, out, lse
    ):
        rows = 2 * len(split.links) * own.shape[0]
        self.heads = heads
        super().__init__(
            split,
            own,
            (w_in, w_out, cosine, sine, gain, begins, kept, projected, turned, out, lse),
            (
                jax.ShapeDtypeStruct(w_in.shape, jnp.float32),
                jax.ShapeDtypeStruct(w_out.shape, jnp.float32),
                jax.ShapeDtypeStruct((8, heads.width), jnp.float32),
            ),
            (
                pltpu.VMEM((rows, heads.heads * HEAD), jnp.bfloat16),
                pltpu.VMEM((rows, heads.width), jnp.float32),
                pltpu.VMEM((rows, heads.width), jnp.bfloat16),
            ),
        )

    def open(self):
        _, self.w_in, self.w_out, self.cosine, self.sine, self.gain, self.begins = self.ins[:7]
        self.kept, self.projected, self.turned, self.out, self.lse = self.ins[7:]
        _, self.grad_in, self.grad_out, self.grad_gain = self.outs
        self.grad_heads, self.grad_turned, self.grad_projected = self.more

    def take(self, core, chip):
        grad = self.slots[core, chip]
        rows = self.at(core, chip)
        self.grad_heads[rows] = to_low(contract_last(grad, self.w_out[...]))
        term = contract_first(self.out[rows], grad)
        if (core, chip) == (0, 0):
            self.grad_out[...] = term
        else:
            self.grad_out[...] += term

    def work(self):
        factor = HEAD ** (-0.5)
        self.grad_turned[...] = jnp.zeros(self.grad_turned.shape, jnp.float32)
        self.grad_gain[...] = jnp.zeros(self.grad_gain.shape, jnp.float32)
        for place in range(2 * self.chips):
            rows = slice(place * self.rows, (place + 1) * self.rows)
            bias, seen = hidden_scores(self.begins[rows], place, self.rows)
            for head in range(self.heads.heads):
                own, key, value = self.heads.q(head), self.heads.k(head), self.heads.v(head)
                query, grad = self.turned[rows, own], self.grad_heads[rows, own]
                scores = contract_last(query, self.turned[:seen, key]) * factor + bias
                probs = jnp.exp(scores - self.lse[rows, head : head + 1])
                grad_probs = contract_last(grad, self.turned[:seen, value])
                row_dot = jnp.sum(probs * grad_probs, axis=-1, keepdims=True)
                grad_scores = to_low(probs * (grad_probs - row_dot))
                self.grad_turned[rows, own] = matmul(grad_scores, self.turned[:seen, key]) * factor
                self.grad_turned[:seen, key] += contract_first(grad_scores, query) * factor
                self.grad_turned[:seen, value] += contract_first(to_low(probs), grad)
            yield True
        for place in range(2 * self.chips):
            rows = slice(place * self.rows, (place + 1) * self.rows)
            for lanes, count in self.heads.tiles():
                low = to_low(self.grad_turned[rows, lanes])
                if count:
                    grad = low.astype(jnp.float32)
                    normed = grad * self.cosine[rows] + half_turned(grad * self.sine[rows])
                    raw = self.projected[rows, lanes]
                    scale = lax.rsqrt(head_means(raw * raw) + EPSILON)
                    unit = raw * scale
                    gain_term = self.heads.some(count, normed * unit, jnp.zeros_like(unit))
                    self.grad_gain[0:1, lanes] += jnp.sum(gain_term, axis=0, keepdims=True)
                    weighted = normed * self.gain[:, lanes]
                    back = scale * (weighted - unit * head_means(weighted * unit))
                    low = to_low(self.heads.some(count, back, grad))
                self.grad_projected[rows, lanes] = low
            yield True

    def give(self, core, chip):
        return contract_last(self.grad_projected[self.at(core, chip)], self.w_in[...])

    def after(self):
        for core, chip in self.places:
            term = contract_first(
                self.kept[core, chip], self.grad_projected[self.at(core, chip)]
            )
            if (core, chip) == (0, 0):
                self.grad_in[...] = term
            else:
                self.grad_in[...] += term
            yield True


class FeedForward(Job):
    works = True

    def span(self):
        return 60.0 if self.back and self.forward else 52.0

    def steps(self):
        return 3 * self.chips

    def __init__(self, split, normed, grad, w_in, w_down, forward):
        self.split, self.forward, self.back = split, forward, grad is not None
        self.chips = len(split.links)
        width = w_in.shape[0]
        gathered = normed if normed.ndim == 2 else grad
        given = (grad if normed.ndim == 2 else normed) if self.back else None
        self.gather_normed = normed.ndim == 2
        self.rows = gathered.shape[0]
        self.half = w_in.shape[1] // 2
        self.operands = (gathered, w_in, w_down) + (() if given is None else (given,))
        row_sum = jax.ShapeDtypeStruct((self.rows, width), jnp.float32)
        self.results, self.in_vmem = (), ()
        all_terms = (2, self.chips, self.rows, width)
        if self.back:
            if forward:
                self.results += (jax.ShapeDtypeStruct(all_terms, jnp.float32),)
                self.in_vmem += (False,)
            self.results += (
                row_sum,
                jax.ShapeDtypeStruct(w_in.shape, jnp.float32),
                jax.ShapeDtypeStruct(w_down.shape, jnp.float32),
            )
            self.in_vmem += (True, True, True)
        else:
            self.results += (row_sum, jax.ShapeDtypeStruct(all_terms, jnp.bfloat16))
            self.in_vmem += (True, False)
        self.masks = [mask for mask in split.links[1:]] + [(0, 1)]
        self.copies = Spread.copies(split) + 2 * self.chips - 1
        self.locals = 5 + 2 * self.chips
        all_rows = pltpu.VMEM((2, self.chips, self.rows, width), jnp.bfloat16)
        self.scratch = (
            (all_rows,)
            + ((all_rows,) if given is not None else ())
            + (pltpu.VMEM(w_in.shape, jnp.bfloat16), pltpu.VMEM(w_down.shape, jnp.bfloat16))
        )
        self.scratch += Return.scratch(self.chips, self.rows, width)
        if self.back and forward:
            self.scratch += (pltpu.VMEM((2, self.rows, width), jnp.float32),)

    def start(self):
        held = list(self.held)
        self.slots = held.pop(0)
        self.given = held.pop(0) if self.back else None
        self.w_in, self.w_down = held.pop(0), held.pop(0)
        outs = list(self.outs)
        self.terms = outs.pop(0) if self.back and self.forward else None
        self.sums = Return(self, Spread.copies(self.split), held[:5], outs.pop(0))
        self.staged = held[5] if self.terms is not None else None
        if self.back:
            self.grad_in, self.grad_down = outs
        else:
            self.kept = outs.pop(0)
        self.arrive = Spread(self, self.ins[0], self.slots, 0)
        self.loads = [
            self.near(1, self.ins[1], self.w_in),
            self.near(2, self.ins[2], self.w_down),
        ]
        self.rest = []
        if self.back:
            self.rest = [
                self.near(3 + 2 * chip + core, self.ins[3].at[core, chip], self.given.at[core, chip])
                for chip in range(self.chips)
                for core in (0, 1)
            ]
        for copy in self.loads + self.rest:
            copy.start()

    def middle(self):
        self.stores = []
        for chip in range(self.chips):
            for core in (0, 1):
                if chip == 1:
                    for other in self.arrive.direct:
                        self.arrive.ready(0, other)
                self.arrive.ready(core, chip)
                if (core, chip) == (0, 0):
                    self.loads[0].wait()
                    self.loads[1].wait()
                if self.back:
                    self.rest[2 * chip + core].wait()
                else:
                    self.store(
                        3 + 2 * chip + core, self.slots.at[core, chip], self.kept.at[core, chip]
                    )
                self.compute(core, chip)
                yield True
            self.sums.pass_on(chip)
            yield True

    def store(self, number, source, target):
        copy = self.near(number, source, target)
        copy.start()
        self.stores.append(copy)

    def compute(self, core, chip):
        arrived = self.slots[core, chip]
        normed = arrived if self.gather_normed else self.given[core, chip]
        both = matmul(normed, self.w_in[...])
        gate, upper = both[:, : self.half], both[:, self.half :]
        sigma = jax.nn.sigmoid(gate)
        active = gate * sigma
        hidden = to_low(active * upper)
        if self.terms is not None:
            count = len(self.stores)
            if count >= 2:
                self.stores[count - 2].wait()
            self.staged[count % 2] = matmul(hidden, self.w_down[...])
            self.store(
                3 + 2 * self.chips + count % 2,
                self.staged.at[count % 2],
                self.terms.at[core, chip],
            )
        elif self.forward:
            self.sums.put(core, chip, matmul(hidden, self.w_down[...]))
        if self.back:
            grad = self.given[core, chip] if self.gather_normed else arrived
            grad_hidden = contract_last(grad, self.w_down[...])
            grad_gate = to_low(grad_hidden * upper * (sigma * (1.0 + gate * (1.0 - sigma))))
            grad_upper = to_low(grad_hidden * active)
            grad_both = jnp.concatenate([grad_gate, grad_upper], axis=1)
            self.sums.put(core, chip, contract_last(grad_both, self.w_in[...]))
            if core == 0 and chip == 0:
                self.grad_in[...] = contract_first(normed, grad_both)
                self.grad_down[...] = contract_first(hidden, grad)
            else:
                self.grad_in[...] += contract_first(normed, grad_both)
                self.grad_down[...] += contract_first(hidden, grad)

    def finish(self):
        self.sums.finish()
        self.arrive.finish()
        for store in self.stores if self.terms is None else self.stores[-2:]:
            store.wait()


def all_masks():
    seq, dp = lax.axis_size("seq"), lax.axis_size("dp")
    return [(dp_mask, seq_mask) for dp_mask in range(dp) for seq_mask in range(seq)][1:]


class Hops(Job):
    def plan(self):
        seq, dp = lax.axis_size("seq"), lax.axis_size("dp")
        self.straight = seq * dp <= FEW
        if self.straight:
            self.masks = all_masks()
        else:
            self.masks = [(0, mask) for mask in range(1, seq)] + [
                (mask, 0) for mask in range(1, dp)
            ]


FEW = 1


class Everyone(Hops):
    def steps(self):
        return 1

    def __init__(self, value):
        self.operands = (value,)
        seq, dp = lax.axis_size("seq"), lax.axis_size("dp")
        self.results = (jax.ShapeDtypeStruct((dp, seq) + value.shape, value.dtype),)
        self.plan()
        self.copies = len(self.masks)
        self.locals = 1

    def post(self, number, source, index, mask):
        out = self.outs[0]
        away = (flipped(self.dp, mask[0]), flipped(self.seq, mask[1]))
        copy = self.away(number, source, out.at[index((self.dp, self.seq))], mask)
        copy.start()
        self.sent.append(copy)
        self.arrivals.append(self.away(number, source, out.at[index(away)], mask))

    def start(self):
        out = self.outs[0]
        self.mine = self.near(0, self.ins[0], out.at[self.dp, self.seq])
        self.mine.start()
        self.sent, self.arrivals = [], []
        for number, mask in enumerate(self.masks):
            if self.straight or not mask[0]:
                self.post(number, self.ins[0], lambda place: place, mask)

    def middle(self):
        if self.straight:
            return
        self.mine.wait()
        for arrival in self.arrivals:
            arrival.wait_recv()
        self.arrivals = []
        for number, mask in enumerate(self.masks):
            if mask[0]:
                self.post(number, self.outs[0].at[self.dp], lambda place: place[0], mask)
        yield True

    def finish(self):
        if self.straight:
            self.mine.wait()
        for arrival in self.arrivals:
            arrival.wait_recv()
        for copy in self.sent:
            copy.wait_send()


class SumAll(Hops):
    out_in_vmem = True

    def steps(self):
        return 1 if self.straight else 3

    def __init__(self, value):
        self.operands = (value,)
        self.results = (jax.ShapeDtypeStruct(value.shape, value.dtype),)
        seq, dp = value.shape[:2]
        self.plan()
        self.copies = 2 * len(self.masks)
        self.locals = 1
        self.scratch = (pltpu.VMEM(value.shape, jnp.float32),)
        if self.straight:
            self.scratch += (pltpu.VMEM((len(self.masks),) + value.shape[2:], jnp.float32),)
        else:
            self.scratch += (
                pltpu.VMEM((seq - 1,) + value.shape[1:], jnp.float32),
                pltpu.VMEM((dp - 1,) + value.shape[2:], jnp.float32),
            )

    def block(self, ref, mask, whole=False):
        seq, dp = flipped(self.seq, mask[1]), flipped(self.dp, mask[0])
        return ref.at[seq] if whole else ref.at[seq, dp]

    def round(self, masks, source, target):
        copies = []
        for number, mask in enumerate(masks):
            copy = self.away(self.number + number, source(mask), target(number, mask), mask)
            copy.start()
            copies.append(copy)
        self.number += len(masks)
        self.sent += copies
        return copies

    def start(self):
        self.load = self.near(0, self.ins[0], self.held[0])
        self.load.start()
        self.load.wait()
        self.number, self.sent = 0, []
        masks = [mask for mask in self.masks if self.straight or not mask[0]]
        self.first = self.round(
            masks,
            lambda mask: self.block(self.held[0], mask, not self.straight),
            lambda number, mask: self.held[1].at[number],
        )

    def arrived(self, masks, whole):
        out = self.outs[0]
        return [
            self.away(self.number + number, self.block(out, mask, whole), self.block(out, mask, whole), mask)
            for number, mask in enumerate(masks)
        ]

    def give_back(self, masks, whole):
        out = self.outs[0]
        arrivals = self.arrived(masks, whole)
        mine = self.block(out, (0, 0), whole)
        self.round(masks, lambda mask: mine, lambda number, mask: mine)
        return arrivals

    def middle(self):
        given, out = self.held[0], self.outs[0]
        for copy in self.first:
            copy.wait_recv()
        if self.straight:
            value = given[self.seq, self.dp]
            for number in range(len(self.masks)):
                value = value + self.held[1][number]
            out[self.seq, self.dp] = value
            self.last = self.give_back(self.masks, False)
            yield True
            return
        by_seq, by_dp = self.held[1:]
        part = given[self.seq]
        for number in range(len(self.first)):
            part = part + by_seq[number]
        given[self.seq] = part
        yield True
        masks = [mask for mask in self.masks if mask[0]]
        copies = self.round(
            masks,
            lambda mask: self.block(given, mask),
            lambda number, mask: by_dp.at[number],
        )
        for copy in copies:
            copy.wait_recv()
        value = given[self.seq, self.dp]
        for number in range(len(masks)):
            value = value + by_dp[number]
        out[self.seq, self.dp] = value
        yield True
        for arrival in self.give_back(masks, False):
            arrival.wait_recv()
        yield True
        self.last = self.give_back([mask for mask in self.masks if not mask[0]], True)

    def finish(self):
        for arrival in self.last:
            arrival.wait_recv()
        for copy in self.sent:
            copy.wait_send()


def drained(turn):
    for _ in turn:
        pass
    yield True


def in_order(jobs):
    bulk = STRETCH * sum(job.span() for job in jobs if job.bulk and not job.begin)
    steps = []
    for number, job in enumerate(jobs):
        turn, count = job.middle(), job.steps()
        span = bulk if job.bulk and not job.begin else job.span()
        if job.begin:
            steps.append((job.begin, number, -1, iter([job.start])))
        early = 0 if job.works else 1
        for step in range(count):
            steps.append((job.begin + (step + early) * span / count, number, step, turn))
        steps.append((1000.0, number, count, drained(turn)))
    return [turn for _, _, _, turn in sorted(steps, key=lambda step: step[:3])]


class Courier:
    def __init__(self):
        self.calls = 0

    def __call__(self, *jobs):
        number = self.calls
        self.calls += 1
        masks = []
        for job in jobs:
            for mask in job.masks:
                if mask not in masks:
                    masks.append(mask)
        operands = [value for job in jobs for value in job.operands]
        results = [value for job in jobs for value in job.results]
        in_vmem, given = [], []
        for job in jobs:
            given += list(job.given_in_vmem or [False] * len(job.operands))
            in_vmem += list(job.in_vmem or [job.out_in_vmem] * len(job.results))
        scratch = []
        for job in jobs:
            scratch += list(job.scratch)
            scratch += [
                pltpu.SemaphoreType.DMA((max(1, job.copies),)),
                pltpu.SemaphoreType.DMA((max(1, job.copies),)),
                pltpu.SemaphoreType.DMA((max(1, job.locals),)),
            ]

        def kernel(*refs):
            ins = list(refs[: len(operands)])
            outs = list(refs[len(operands) : len(operands) + len(results)])
            held = list(refs[len(operands) + len(results) :])
            dp, seq = lax.axis_index("dp"), lax.axis_index("seq")
            barrier = pltpu.get_barrier_semaphore()
            for mask in masks:
                pl.semaphore_signal(
                    barrier,
                    inc=1,
                    device_id=(flipped(dp, mask[0]), flipped(seq, mask[1])),
                    device_id_type=MESH,
                )
            pl.semaphore_wait(barrier, len(masks))
            for job in jobs:
                count_in, count_out = len(job.operands), len(job.results)
                own = len(job.scratch)
                job.bind(
                    ins[:count_in], outs[:count_out], held[:own], *held[own : own + 3]
                )
                ins, outs, held = ins[count_in:], outs[count_out:], held[own + 3 :]
            for job in jobs:
                if not job.begin:
                    job.start()
            for turn in in_order(jobs):
                action = next(turn, None)
                if callable(action):
                    action()
            for job in jobs:
                job.finish()

        sent = sum(value.size * value.dtype.itemsize for value in operands)
        outs = pl.pallas_call(
            kernel,
            out_shape=results,
            in_specs=[
                pl.BlockSpec(memory_space=pltpu.VMEM if vmem else pl.ANY) for vmem in given
            ],
            out_specs=[
                pl.BlockSpec(memory_space=pltpu.VMEM if vmem else pl.ANY) for vmem in in_vmem
            ],
            scratch_shapes=scratch,
            compiler_params=pltpu.CompilerParams(
                collective_id=number, has_side_effects=True, vmem_limit_bytes=60 << 20
            ),
            cost_estimate=pl.CostEstimate(flops=0, bytes_accessed=8 * sent, transcendentals=0),
            name="courier_%d" % number,
        )(*operands)
        return outs


def packed(values, blocks):
    flat = jnp.concatenate([value.reshape(-1).astype(jnp.float32) for value in values])
    each = -(-flat.shape[0] // (blocks * 1024)) * 1024
    return jnp.pad(flat, (0, blocks * each - flat.shape[0])).reshape(blocks, each // 128, 128)


def unpacked(flat, values):
    flat = flat.reshape(-1)
    out, begin = [], 0
    for value in values:
        out.append(flat[begin : begin + value.size].reshape(value.shape))
        begin += value.size
    return out


def large_sum(values):
    seq, dp = lax.axis_size("seq"), lax.axis_size("dp")
    blocks = packed(values, seq * dp)
    return SumAll(blocks.reshape((seq, dp) + blocks.shape[1:]))


def small_sum(values):
    return Everyone(packed(values, 1)[0])


def local_call(kernel, name, results, operands, flops=0):
    moved = sum(value.size * value.dtype.itemsize for value in list(operands) + list(results))
    return pl.pallas_call(
        kernel,
        out_shape=results,
        in_specs=[pl.BlockSpec(memory_space=pltpu.VMEM)] * len(operands),
        out_specs=[pl.BlockSpec(memory_space=pltpu.VMEM)] * len(results),
        compiler_params=pltpu.CompilerParams(vmem_limit_bytes=56 << 20),
        cost_estimate=pl.CostEstimate(flops=flops, bytes_accessed=moved, transcendentals=0),
        name=name,
    )(*operands)


def pieces_by_rank(split, columns):
    dp_count, seq_count = lax.axis_size("dp"), lax.axis_size("seq")
    each = columns // (dp_count * seq_count)
    out = []
    for dp in range(dp_count):
        for seq in range(seq_count):
            out.append(
                (split.rank(dp, seq), split.copy(dp) * each, (dp * seq_count + seq) * each)
            )
    return each, out


def lowered_chunks(near, wide, attn_widths, mix_in, mix_out, attn_in, attn_out, ffn_in, ffn_out, vectors):
    seq_count = lax.axis_size("seq")
    rows, width = mix_out.shape
    hidden = ffn_in.shape[-1]
    channels, mine = width // seq_count, hidden // wide.ranks

    def kernel(mix_in, mix_out, attn_in, attn_out, ffn_in, ffn_out, vectors, *outs):
        mix_chunk, attn_chunk, one, two, low_mix_out, low_attn_out, down_one, down_two, block = outs
        each, pieces = pieces_by_rank(near, width)
        for part in range(3):
            for rank, inner, outer in pieces:
                mix_chunk[rank, :, pl.ds(part * channels + inner, each)] = to_low(
                    mix_in[:, pl.ds(part * width + outer, each)]
                )
        begin, target = 0, 0
        for columns in attn_widths:
            each = columns // seq_count
            for rank in range(seq_count):
                attn_chunk[rank, :, pl.ds(target, each)] = to_low(
                    attn_in[:, pl.ds(begin + rank * each, each)]
                )
            begin, target = begin + columns, target + each
        each, pieces = pieces_by_rank(wide, hidden)
        for layer, chunk in enumerate((one, two)):
            for part in range(2):
                for rank, inner, outer in pieces:
                    chunk[rank, :, pl.ds(part * mine + inner, each)] = to_low(
                        ffn_in[layer, part, :, pl.ds(outer, each)]
                    )
        low_mix_out[...] = to_low(mix_out[...])
        low_attn_out[...] = to_low(attn_out[...])
        down_one[...] = to_low(ffn_out[0])
        down_two[...] = to_low(ffn_out[1])
        block[...] = jnp.zeros(block.shape, jnp.bfloat16)
        block[pl.ds(0, vectors.shape[0]), pl.ds(0, vectors.shape[1])] = to_low(vectors[...])

    def low(*shape):
        return jax.ShapeDtypeStruct(shape, jnp.bfloat16)

    results = (
        low(seq_count, rows, 3 * channels),
        low(seq_count, rows, sum(attn_widths) // seq_count),
        low(wide.ranks, rows, 2 * mine),
        low(wide.ranks, rows, 2 * mine),
        low(*mix_out.shape),
        low(*attn_out.shape),
        low(*ffn_out.shape[1:]),
        low(*ffn_out.shape[1:]),
        low(16, 128),
    )
    return local_call(
        kernel,
        "lower",
        results,
        (mix_in, mix_out, attn_in, attn_out, ffn_in, ffn_out, vectors),
    )


LINE = 512


class Step:
    def __init__(self, weights):
        self.weights = weights
        self.matrices = []
        begin, line = 0, 0
        for number, weight in enumerate(weights):
            lead = weight.shape[:-2]
            rows, columns = weight.shape[-2:]
            indices = [()]
            for size in lead:
                indices = [index + (place,) for index in indices for place in range(size)]
            for index in indices:
                self.matrices.append((number, index, rows, columns, begin, line))
                begin += rows
                line += columns // LINE
        self.rows, self.scalars = begin, line
        devices = lax.axis_size("dp") * lax.axis_size("seq")
        self.devices = devices
        self.lines = -(-(line + 1) // devices)
        self.sums = (lax.axis_size("seq"), lax.axis_size("dp"), self.lines, 1, LINE)

    def line(self, ref, number):
        per = self.lines
        dp = lax.axis_size("dp")
        return ref.at[number // (per * dp), (number // per) % dp, number % per]

    def natural(self):
        return [jax.ShapeDtypeStruct(weight.shape, jnp.float32) for weight in self.weights]

    def columns(self):
        return [
            jax.ShapeDtypeStruct(weight.shape[:-2] + (1, weight.shape[-1]), jnp.float32)
            for weight in self.weights
        ]

    def first(self, near, wide, attn_widths, traded, row_states, extra):
        seq_count = lax.axis_size("seq")

        def kernel(mix, attn, one, two, mix_out, attn_out, down_one, down_two, *refs):
            weights, (states, extra), refs = refs[:6], refs[6:8], refs[8:]
            grads, (rows_new, sums) = refs[:6], refs[6:]
            width = mix_out.shape[-1]
            channels = mix.shape[-1] // 3
            each, pieces = pieces_by_rank(near, width)
            for part in range(3):
                for rank, inner, outer in pieces:
                    grads[0][:, pl.ds(part * width + outer, each)] = mix[
                        rank, :, pl.ds(part * channels + inner, each)
                    ]
            grads[1][...] = mix_out[...]
            begin, source = 0, 0
            for columns in attn_widths:
                each = columns // seq_count
                for rank in range(seq_count):
                    grads[2][:, pl.ds(begin + rank * each, each)] = attn[
                        rank, :, pl.ds(source, each)
                    ]
                begin, source = begin + columns, source + each
            grads[3][...] = attn_out[...]
            hidden = grads[4].shape[-1]
            mine = one.shape[-1] // 2
            each, pieces = pieces_by_rank(wide, hidden)
            for layer, chunk in enumerate((one, two)):
                for part in range(2):
                    for rank, inner, outer in pieces:
                        grads[4][layer, part, :, pl.ds(outer, each)] = chunk[
                            rank, :, pl.ds(part * mine + inner, each)
                        ]
            grads[5][0] = down_one[...]
            grads[5][1] = down_two[...]
            lanes = lax.broadcasted_iota(jnp.int32, (1, LINE), 1)
            scalars = extra[...]
            for place in range(self.scalars + 1, self.lines * self.devices):
                self.line(sums, place)[...] = jnp.zeros((1, LINE), jnp.float32)
            for number, (which, index, rows, columns, begin, line) in enumerate(self.matrices):
                by_row = jnp.zeros((rows, LINE), jnp.float32)
                norm = jnp.zeros((1, LINE), jnp.float32)
                for strip in range(columns // LINE):
                    place = pl.ds(strip * LINE, LINE)
                    grad = grads[which][index + (slice(None), place)]
                    squares = grad * grad + SQUARE_FLOOR
                    by_row = by_row + squares
                    self.line(sums, line + strip)[...] = jnp.sum(squares, axis=0, keepdims=True)
                    weight = weights[which][index + (slice(None), place)]
                    norm = norm + jnp.sum(weight * weight, axis=0, keepdims=True)
                by_row = jnp.sum(by_row, axis=1, keepdims=True)
                norm = jnp.sum(norm, axis=1, keepdims=True)
                fresh = DECAY_RATE * states[pl.ds(begin, rows)] + (1.0 - DECAY_RATE) * (
                    by_row / columns
                )
                rows_new[pl.ds(begin, rows)] = fresh
                scalars = jnp.where(
                    lanes == number, jnp.sum(fresh, axis=0, keepdims=True), scalars
                )
                scalars = jnp.where(lanes == 16 + number, norm, scalars)
            self.line(sums, self.scalars)[...] = scalars

        results = self.natural() + [
            jax.ShapeDtypeStruct((self.rows, 1), jnp.float32),
            jax.ShapeDtypeStruct(self.sums, jnp.float32),
        ]
        return local_call(
            kernel, "step_first", results, tuple(traded) + tuple(self.weights) + (row_states, extra)
        )

    def second(self, grads, rows_new, sums, col_states):
        def kernel(*refs):
            grads, (rows_new, sums), refs = refs[:6], refs[6:8], refs[8:]
            states, cols_out, squares_out = refs[:6], refs[6:12], refs[12]
            scalars = self.line(sums, self.scalars)[...]
            lanes = lax.broadcasted_iota(jnp.int32, squares_out.shape, 1)
            out = jnp.zeros(squares_out.shape, jnp.float32)
            for number, (which, index, rows, columns, begin, line) in enumerate(self.matrices):
                norm = jnp.zeros((1, LINE), jnp.float32)
                mean_rows = scalars[:, number : number + 1] / (rows * self.devices)
                by_row = jnp.broadcast_to(mean_rows / rows_new[pl.ds(begin, rows)], (rows, LINE))
                for strip in range(columns // LINE):
                    place = pl.ds(strip * LINE, LINE)
                    spot = index + (slice(None), place)
                    cols_new = DECAY_RATE * states[which][spot] + (1.0 - DECAY_RATE) * (
                        self.line(sums, line + strip)[...] / (rows * self.devices)
                    )
                    cols_out[which][spot] = cols_new
                    grad = grads[which][spot]
                    norm = norm + jnp.sum(grad * grad * by_row, axis=0, keepdims=True) / cols_new
                out = jnp.where(lanes == number, jnp.sum(norm, axis=1, keepdims=True), out)
            squares_out[...] = out

        results = self.columns() + [jax.ShapeDtypeStruct((8, 128), jnp.float32)]
        return local_call(
            kernel, "step_second", results, tuple(grads) + (rows_new, sums) + tuple(col_states)
        )

    def third(self, grads, rows_new, sums, cols_new, squares):
        def kernel(*refs):
            grads, (rows_new, sums, squares), refs = refs[:6], refs[6:9], refs[9:]
            cols_new, weights, outs = refs[:6], refs[6:12], refs[12:]
            scalars = self.line(sums, self.scalars)[...]
            totals = jnp.sum(squares[...], axis=(0, 1))[0:1]
            for number, (which, index, rows, columns, begin, line) in enumerate(self.matrices):
                count = rows * self.devices * columns
                divisor = jnp.maximum(
                    1.0, jnp.sqrt(totals[:, number : number + 1] / count) / CLIP_LEVEL
                )
                rate = STEP_SCALE * jnp.maximum(
                    RATE_FLOOR, jnp.sqrt(scalars[:, 16 + number : 17 + number] / count)
                )
                mean_rows = scalars[:, number : number + 1] / (rows * self.devices)
                scale = (rate / divisor) * jnp.sqrt(mean_rows)
                by_row = jnp.broadcast_to(
                    scale * lax.rsqrt(rows_new[pl.ds(begin, rows)]), (rows, LINE)
                )
                for strip in range(columns // LINE):
                    spot = index + (slice(None), pl.ds(strip * LINE, LINE))
                    outs[which][spot] = weights[which][spot] - grads[which][spot] * (
                        by_row * lax.rsqrt(cols_new[which][spot])
                    )

        return local_call(
            kernel,
            "step_third",
            self.natural(),
            tuple(grads) + (rows_new, sums, squares) + tuple(cols_new) + tuple(self.weights),
        )


def moved_to_rank(shard):
    seq, dp = lax.axis_size("seq"), lax.axis_size("dp")
    pairs = [(block, (block % dp) * seq + block // dp) for block in range(seq * dp)]
    return lax.ppermute(shard, ("dp", "seq"), pairs)


def moved_to_owner(shard):
    seq, dp = lax.axis_size("seq"), lax.axis_size("dp")
    pairs = [((block % dp) * seq + block // dp, block) for block in range(seq * dp)]
    return lax.ppermute(shard, ("dp", "seq"), pairs)


def rows_of(value, like):
    return value.reshape((-1,) + like.shape)


def flat(value):
    return value.reshape(-1, value.shape[-1])


def to_trade(block, split):
    return block.reshape(split.ranks, -1, block.shape[-1])


def body(
    tokens,
    cotangent,
    lengths,
    mix_in,
    mix_in_rows,
    mix_in_cols,
    mix_out,
    mix_out_rows,
    mix_out_cols,
    attn_in,
    attn_in_rows,
    attn_in_cols,
    attn_out,
    attn_out_rows,
    attn_out_cols,
    ffn_in,
    ffn_in_rows,
    ffn_in_cols,
    ffn_out,
    ffn_out_rows,
    ffn_out_cols,
    vectors,
    vectors_moment,
    head_gain,
    head_moment,
):
    rows_here, width = tokens.shape
    seq_count = lax.axis_size("seq")
    devices = lax.axis_size("dp") * seq_count
    here = lax.axis_index("seq")
    courier = Courier()
    near, wide = Split(False), Split(True)
    total_rows = rows_here * seq_count
    positions = doc_layout(lengths[0], jnp.arange(total_rows, dtype=jnp.int32))[1]
    begins = (jnp.arange(total_rows, dtype=jnp.int32) - positions)[:, None]
    once = (positions >= 1).astype(jnp.float32)[:, None]
    twice = (positions >= 2).astype(jnp.float32)[:, None]
    cosine, sine = angles_for(positions, HEAD)
    cosine = jnp.concatenate([cosine, cosine] * (LANES // HEAD), axis=1)
    sine = jnp.concatenate([-sine, sine] * (LANES // HEAD), axis=1)
    channels = width // seq_count
    heads = HQ // seq_count
    kv_heads = KVH // seq_count
    kv_width = KVH * HEAD

    form = Heads(heads, kv_heads)
    head_gains = to_low(head_gain).astype(jnp.float32)
    gain_row = jnp.concatenate(
        [head_gains[0]] * heads + [head_gains[1]] * kv_heads + [jnp.ones(kv_heads * HEAD)]
    )[None]
    attn_widths = (width, kv_width, kv_width)
    (
        mix_chunk,
        attn_chunk,
        one_chunk,
        two_chunk,
        low_mix_out,
        attn_out_chunk,
        low_down_one,
        low_down_two,
        vector_block,
    ) = lowered_chunks(
        near, wide, attn_widths, mix_in, mix_out, attn_in, attn_out, ffn_in, ffn_out, vectors
    )
    attn_out_chunk = moved_to_rank(attn_out_chunk)
    mix_traded, gathered, attn_traded, one_traded, two_traded = courier(
        Trade(near, mix_chunk),
        Everyone(vector_block),
        Trade(near, attn_chunk),
        Trade(wide, one_chunk),
        Trade(wide, two_chunk),
    )
    gains = gathered.reshape(devices, 16, 128)[:, : vectors.shape[0], : vectors.shape[1]]
    gains = jnp.moveaxis(gains, 0, 1).reshape(-1, width).astype(jnp.float32)
    inputs = tokens.astype(jnp.float32)
    low_one, scale_one = normalize(inputs, gains[0])
    *near_weights, cotangent_all = courier(
        GatherWeights(near, flat(mix_traded), 4),
        GatherWeights(near, low_mix_out),
        GatherTokens(wide, cotangent),
    )
    w_mix_in, w_mix_out = (flat(value) for value in near_weights)
    taps = lax.dynamic_index_in_dim(
        gains[4:7].reshape(3, -1, seq_count, width // devices), here, 2, keepdims=False
    ).reshape(3, channels)

    taps = jnp.pad(taps, ((0, 5), (0, 0)))
    added, *mix_kept, w_in_one, w_down_one = courier(
        MixForward(near, to_low(low_one), w_mix_in, w_mix_out, taps, once, twice),
        GatherWeights(wide, flat(one_traded), 8, True),
        GatherWeights(wide, low_down_one, 3),
    )
    w_down_one = flat(w_down_one)
    first = inputs + added
    w_in_one = flat(w_in_one)
    normed_one, scale_two = normalize(first, gains[1])
    added, rows_one, w_attn_in, w_attn_out = courier(
        FeedForward(wide, to_low(normed_one), None, w_in_one, w_down_one, True),
        GatherWeights(near, flat(attn_traded), 4),
        GatherWeights(near, attn_out_chunk),
    )
    w_attn_in, w_attn_out = flat(w_attn_in), flat(w_attn_out)
    second = first + added

    normed_three, scale_three = normalize(second, gains[2])
    added, *attn_kept, w_in_two, w_down_two = courier(
        AttendForward(
            near, form, to_low(normed_three), w_attn_in, w_attn_out, cosine, sine, gain_row, begins
        ),
        GatherWeights(wide, flat(two_traded), 8, True),
        GatherWeights(wide, low_down_two, 3),
    )
    third = second + added
    w_in_two, w_down_two = flat(w_in_two), flat(w_down_two)
    normed_four, scale_four = normalize(third, gains[3])
    terms_two, grad_normed, grad_in_two, grad_down_two = courier(
        FeedForward(
            wide, to_low(normed_four), cotangent_all, w_in_two, w_down_two, True
        )
    )
    grad_branch, grad_gain_three = normalize_back(
        grad_normed, third, scale_four, gains[3]
    )
    grad_third = cotangent.astype(jnp.float32) + grad_branch
    (
        grad_normed_three,
        grad_attn_in,
        grad_attn_out,
        grad_heads,
        reduced_in_two,
        added,
    ) = courier(
        AttendBack(
            near,
            form,
            to_low(grad_third),
            w_attn_in,
            w_attn_out,
            cosine,
            sine,
            gain_row,
            begins,
            *attn_kept,
        ),
        ReduceWeights(wide, grad_in_two, 8, True),
        ScatterTokens(wide, terms_two),
    )
    fourth = third + added
    grad_heads = grad_heads[0].reshape(-1, HEAD)
    grad_head_q = jnp.sum(grad_heads[:heads], axis=0)
    grad_head_k = jnp.sum(grad_heads[heads : heads + kv_heads], axis=0)
    grad_branch_three, grad_gain_two = normalize_back(
        grad_normed_three, second, scale_three, gains[2]
    )
    grad_second = grad_third + grad_branch_three
    (
        grad_normed,
        grad_in_one,
        grad_down_one,
        reduced_down_two,
        reduced_attn_in,
        reduced_attn_out,
    ) = courier(
        FeedForward(wide, rows_one, to_low(grad_second), w_in_one, w_down_one, False),
        ReduceWeights(wide, grad_down_two, 6),
        ReduceWeights(near, grad_attn_in, 4),
        ReduceWeights(near, grad_attn_out),
    )
    grad_branch, grad_gain_one = normalize_back(
        grad_normed, first, scale_two, gains[1]
    )
    grad_first = grad_second + grad_branch
    mix_job = MixBack(near, to_low(grad_first), w_mix_in, w_mix_out, taps, once, twice, *mix_kept)
    one_job = ReduceWeights(wide, grad_in_one, 8, True)
    (
        grad_normed_one,
        grad_mix_in,
        grad_mix_out,
        tap_grads,
        reduced_down_one,
        _,
        two_back,
        attn_back,
        reduced_mix_in,
        one_back,
    ) = courier(
        mix_job,
        ReduceWeights(wide, grad_down_one, 6),
        one_job,
        Trade(wide, to_trade(reduced_in_two, wide)).later(20.0),
        Trade(near, to_trade(reduced_attn_in, near)).later(60.0),
        ReduceWeights(near, jax.ShapeDtypeStruct(w_mix_in.shape, jnp.float32), 4, of=(mix_job, 1)).later(70.0),
        TradeOf(wide, one_job).later(90.0),
    )
    tap_grads = tap_grads[:3]
    grad_branch_zero, grad_gain_zero = normalize_back(
        grad_normed_one, inputs, scale_one, gains[0]
    )
    token_grad = grad_first + grad_branch_zero

    gain_grads = jnp.stack([grad_gain_zero, grad_gain_one, grad_gain_two, grad_gain_three])
    tap_full = lax.dynamic_update_slice_in_dim(
        jnp.zeros((3, lax.axis_size("dp"), seq_count, width // devices), jnp.float32),
        tap_grads.reshape(3, lax.axis_size("dp"), 1, width // devices),
        here,
        2,
    ).reshape(3, width)
    early_parts = [
        jnp.concatenate([gain_grads, tap_full], axis=0),
        jnp.stack([grad_head_q, grad_head_k]),
        jnp.sum(vectors * vectors, axis=-1),
    ]
    reduced_mix_out, mix_back, early = courier(
        ReduceWeights(near, grad_mix_out),
        Trade(near, to_trade(reduced_mix_in, near)),
        large_sum(early_parts),
    )
    early = unpacked(early, early_parts)
    vector_norm = early[2]
    index = lax.axis_index("dp") * seq_count + here
    vector_grad = lax.dynamic_slice_in_dim(early[0], index * vectors.shape[1], vectors.shape[1], 1)
    head_grad = early[1]
    vector_moment_new = DECAY_RATE * vectors_moment + (1.0 - DECAY_RATE) * (
        vector_grad * vector_grad + SQUARE_FLOOR
    )
    vector_update = vector_grad * lax.rsqrt(vector_moment_new)
    vector_squares = jnp.sum(vector_update * vector_update, axis=-1)
    extra = jnp.pad(vector_squares[None], ((0, 0), (32, LINE - 32 - vector_squares.shape[0])))

    step = Step((mix_in, mix_out, attn_in, attn_out, ffn_in, ffn_out))
    row_states = (mix_in_rows, mix_out_rows, attn_in_rows, attn_out_rows, ffn_in_rows, ffn_out_rows)
    col_states = (mix_in_cols, mix_out_cols, attn_in_cols, attn_out_cols, ffn_in_cols, ffn_out_cols)
    *grads, rows_new, sums = step.first(
        near,
        wide,
        attn_widths,
        (
            mix_back,
            attn_back,
            one_back,
            two_back,
            reduced_mix_out,
            moved_to_owner(reduced_attn_out),
            reduced_down_one,
            reduced_down_two,
        ),
        jnp.concatenate([state.reshape(-1) for state in row_states])[:, None],
        extra,
    )
    (sums,) = courier(SumAll(sums))
    *cols_new, squares = step.second(
        grads, rows_new, sums, [state[..., None, :] for state in col_states]
    )
    (squares,) = courier(Everyone(squares))
    new_weights = step.third(grads, rows_new, sums, cols_new, squares)
    new_rows, begin = [], 0
    for state in row_states:
        new_rows.append(rows_new[begin : begin + state.size, 0].reshape(state.shape))
        begin += state.size
    vector_sums = sums.reshape(-1, LINE)[step.scalars, 32 : 32 + vector_squares.shape[0]]
    full_width = vectors.shape[-1] * devices
    vector_divisor = jnp.maximum(1.0, jnp.sqrt(vector_sums / full_width) / CLIP_LEVEL)
    vector_rate = STEP_SCALE * jnp.maximum(RATE_FLOOR, jnp.sqrt(vector_norm / full_width))
    vectors_new = vectors - (vector_rate / vector_divisor)[:, None] * vector_update
    head_moment_new = DECAY_RATE * head_moment + (1.0 - DECAY_RATE) * (
        head_grad * head_grad + SQUARE_FLOOR
    )
    head_update = head_grad * lax.rsqrt(head_moment_new)
    head_divisor = jnp.maximum(
        1.0, jnp.sqrt(jnp.mean(head_update * head_update, axis=-1, keepdims=True)) / CLIP_LEVEL
    )
    head_rate = STEP_SCALE * jnp.maximum(
        RATE_FLOOR, jnp.sqrt(jnp.mean(head_gain * head_gain, axis=-1, keepdims=True))
    )
    head_new = head_gain - head_rate / head_divisor * head_update
    outputs = [to_low(fourth), token_grad]
    for index in range(6):
        outputs += [grads[index], new_rows[index], cols_new[index][..., 0, :], new_weights[index]]
    return tuple(
        outputs
        + [vector_grad, vector_moment_new, vectors_new, head_grad, head_moment_new, head_new]
    )


def solution(mesh):
    return jax.shard_map(
        body,
        mesh=mesh,
        in_specs=(
            P(("dp", "seq"), None),
            P(("dp", "seq"), None),
            P("dp", None),
            P(("dp", "seq"), None),
            P(("dp", "seq")),
            P(),
            P(("dp", "seq"), None),
            P(("dp", "seq")),
            P(),
            P(("dp", "seq"), None),
            P(("dp", "seq")),
            P(),
            P(("dp", "seq"), None),
            P(("dp", "seq")),
            P(),
            P(None, None, ("dp", "seq"), None),
            P(None, None, ("dp", "seq")),
            P(),
            P(None, ("dp", "seq"), None),
            P(None, ("dp", "seq")),
            P(),
            P(None, ("dp", "seq")),
            P(None, ("dp", "seq")),
            P(),
            P(),
        ),
        out_specs=(
            P(("dp", "seq"), None),
            P(("dp", "seq"), None),
            P(("dp", "seq"), None),
            P(("dp", "seq")),
            P(),
            P(("dp", "seq"), None),
            P(("dp", "seq"), None),
            P(("dp", "seq")),
            P(),
            P(("dp", "seq"), None),
            P(("dp", "seq"), None),
            P(("dp", "seq")),
            P(),
            P(("dp", "seq"), None),
            P(("dp", "seq"), None),
            P(("dp", "seq")),
            P(),
            P(("dp", "seq"), None),
            P(None, None, ("dp", "seq"), None),
            P(None, None, ("dp", "seq")),
            P(),
            P(None, None, ("dp", "seq"), None),
            P(None, ("dp", "seq"), None),
            P(None, ("dp", "seq")),
            P(),
            P(None, ("dp", "seq"), None),
            P(None, ("dp", "seq")),
            P(None, ("dp", "seq")),
            P(None, ("dp", "seq")),
            P(),
            P(),
            P(),
        ),
        check_vma=False,
    )
```

```python
import math

import jax
import jax.numpy as jnp
from jax import lax
from jax.experimental import pallas as pl
from jax.experimental.pallas import tpu as pltpu
from jax.sharding import PartitionSpec as P

HQ = 16
KVH = 8
HEAD = 64

EPSILON = 1e-05
SQUARE_FLOOR = 1e-30
DECAY_RATE = 0.5
CLIP_LEVEL = 0.25
STEP_SCALE = 1.0
RATE_FLOOR = 0.001
MASKED_SCORE = -1e30


def matmul(operand, weight):
    return jnp.dot(operand, weight, preferred_element_type=jnp.float32)


def contract_first(operand, other):
    return lax.dot_general(
        operand, other, (((0,), (0,)), ((), ())), preferred_element_type=jnp.float32
    )


def contract_last(operand, other):
    return lax.dot_general(
        operand,
        other,
        (((operand.ndim - 1,), (other.ndim - 1,)), ((), ())),
        preferred_element_type=jnp.float32,
    )


def to_low(values):
    return values.astype(jnp.bfloat16)


def normalize(values, gain):
    scale = lax.rsqrt(jnp.mean(values * values, axis=-1, keepdims=True) + EPSILON)
    return (values * scale * gain, scale)


def normalize_back(grad_out, values, scale, gain):
    unit = values * scale
    grad_gain = jnp.sum(grad_out * unit, axis=tuple(range(values.ndim - 1)))
    weighted = grad_out * gain
    grad_values = scale * (weighted - unit * jnp.mean(weighted * unit, axis=-1, keepdims=True))
    return (grad_values, grad_gain)


def doc_layout(lens, places):
    bounds = jnp.cumsum(lens)
    passed = bounds[None, :] <= places[:, None]
    docs = jnp.sum(passed.astype(jnp.int32), axis=1)
    starts = jnp.sum(jnp.where(passed, lens[None, :], 0), axis=1)
    return (docs, places - starts)


def turns_for(positions):
    lane = jnp.arange(LANES, dtype=jnp.int32) % HEAD
    pair = (lane % (HEAD // 2)).astype(jnp.float32)
    freqs = jnp.exp(pair * (-2.0 * math.log(1000000.0) / HEAD))
    angles = positions.astype(jnp.float32) * freqs[None, :]
    sign = jnp.where(lane < HEAD // 2, -1.0, 1.0)
    return (jnp.cos(angles), jnp.sin(angles) * sign[None, :])


def bits_of(axis):
    return lax.axis_size(axis).bit_length() - 1


def flipped(value, mask):
    for bit in range(mask.bit_length()):
        if (mask >> bit) & 1:
            value = value + (1 - 2 * ((value // (1 << bit)) % 2)) * (1 << bit)
    return value


def spread(bits):
    masks = [0]
    for bit in bits:
        masks = masks + [mask | (1 << bit) for mask in masks]
    return masks


class Split:
    def __init__(self, with_z):
        dp_bits = bits_of("dp")
        x_bits = dp_bits // 2
        self.shared = [x_bits] if with_z else []
        self.x_bits = list(range(x_bits))
        self.z_bits = [bit for bit in range(x_bits, dp_bits) if bit not in self.shared]
        self.free = self.x_bits + self.z_bits
        self.seq_bits = bits_of("seq")
        self.ranks = 1 << (self.seq_bits + len(self.shared))
        self.copies = 1 << len(self.free)
        self.links = [
            (dp_mask, seq_mask)
            for dp_mask in spread(self.shared)
            for seq_mask in spread(range(1, self.seq_bits))
        ]
        self.peers = [
            (dp_mask, seq_mask)
            for dp_mask in spread(self.shared)
            for seq_mask in range(1 << self.seq_bits)
        ]

    def pick(self, value, bits):
        out = 0
        for place, bit in enumerate(bits):
            out = out + ((value // (1 << bit)) % 2) * (1 << place)
        return out

    def rank(self, dp, seq):
        return self.pick(dp, self.shared) * (1 << self.seq_bits) + seq

    def copy(self, dp):
        return self.pick(dp, self.free)

    def row_of(self, dp, piece, pieces, depth):
        per = pieces // (1 << len(self.shared))
        place = piece // per
        for number, bit in enumerate(self.shared):
            own = (dp // (1 << bit)) % 2
            dp = dp + ((place >> number) % 2 - own) * (1 << bit)
        return dp * (per * depth) + (piece % per) * depth

    def owner_order(self):
        return sorted(
            range(lax.axis_size("dp")),
            key=lambda dp: (self.pick(dp, self.free), self.pick(dp, self.shared)),
        )


MESH = pl.DeviceIdType.MESH


class Job:
    scratch = ()
    copies = 0
    locals = 0
    out_in_vmem = False
    in_vmem = ()
    given_in_vmem = ()
    bulk = False
    works = False
    begin = 0.0

    def later(self, begin):
        self.begin = begin
        return self

    def span(self):
        return 10.0

    def steps(self):
        return 0

    def last_steps(self):
        return 0

    def bind(self, operands, outs, scratch, send, recv, local):
        self.ins, self.outs, self.held = operands, outs, scratch
        self.send, self.recv, self.local = send, recv, local
        self.dp, self.seq = lax.axis_index("dp"), lax.axis_index("seq")

    def away(self, number, source, target, mask):
        return pltpu.make_async_remote_copy(
            src_ref=source,
            dst_ref=target,
            send_sem=self.send.at[number],
            recv_sem=self.recv.at[number],
            device_id=(flipped(self.dp, mask[0]), flipped(self.seq, mask[1])),
            device_id_type=MESH,
        )

    def near(self, number, source, target):
        return pltpu.make_async_copy(source, target, self.local.at[number])

    def start(self):
        pass

    def middle(self):
        return iter(())

    def finish(self):
        pass


class Spread:
    def __init__(self, job, source, slots, local):
        self.job, self.source, self.slots = job, source, slots
        links = job.split.links
        self.half = job.rows // 2
        self.mine = job.near(local, source, slots.at[0, 0])
        self.mine.start()
        self.direct, self.hops, self.beside, self.sent = {}, {}, {}, []
        self.done = set()
        number = 0
        for chip in range(1, job.chips):
            if links[chip][0] and links[chip][1]:
                self.hops[chip] = (number, number + 1)
                number += 2
                continue
            copy = job.away(number, source, slots.at[0, chip], links[chip])
            copy.start()
            self.direct[chip] = copy
            self.sent.append(copy)
            number += 1
        self.first = number
        self.send_beside(0, source)

    @staticmethod
    def copies(split):
        both = sum(1 for dp_mask, seq_mask in split.links if dp_mask and seq_mask)
        return 2 * len(split.links) - 1 + both

    def part(self, chip, number):
        return self.slots.at[0, chip, pl.ds(number * self.half, self.half)]

    def send_beside(self, chip, source):
        copy = self.job.away(self.first + chip, source, self.slots.at[1, chip], (0, 1))
        copy.start()
        self.beside[chip] = copy

    def pass_on(self, chip):
        links = self.job.split.links
        for far, numbers in self.hops.items():
            dp_mask, seq_mask = links[far]
            for which, (via, onward) in enumerate(
                (((0, seq_mask), (dp_mask, 0)), ((dp_mask, 0), (0, seq_mask)))
            ):
                if via == links[chip]:
                    copy = self.job.away(
                        numbers[which], self.part(chip, which), self.part(far, which), onward
                    )
                    copy.start()
                    self.sent.append(copy)

    def ready(self, core, chip):
        links = self.job.split.links
        if core:
            self.beside[chip].wait_recv()
            return
        if chip in self.done:
            return
        self.done.add(chip)
        if chip == 0:
            self.mine.wait()
            return
        if chip in self.direct:
            self.direct[chip].wait_recv()
            self.pass_on(chip)
        else:
            for which, number in enumerate(self.hops[chip]):
                onward = ((links[chip][0], 0), (0, links[chip][1]))[which]
                part = self.part(chip, which)
                self.job.away(number, part, part, onward).wait_recv()
        self.send_beside(chip, self.slots.at[0, chip])

    def finish(self):
        for copy in self.sent + list(self.beside.values()):
            copy.wait_send()


class GatherTokens(Job):
    def __init__(self, split, value):
        self.split = split
        self.operands = (value,)
        self.chips = len(split.links)
        self.results = (jax.ShapeDtypeStruct((2, self.chips) + value.shape, value.dtype),)
        self.masks = [mask for mask in split.links[1:]] + [(0, 1)]
        self.rows = value.shape[0]
        self.copies = Spread.copies(split)
        self.locals = 1

    def span(self):
        return 13.0 if self.chips == 2 else 26.0

    def steps(self):
        return self.chips

    def start(self):
        self.arrive = Spread(self, self.ins[0], self.outs[0], 0)

    def middle(self):
        for chip in range(self.chips):
            self.arrive.ready(0, chip)
            yield True

    def finish(self):
        for chip in range(self.chips):
            self.arrive.ready(1, chip)
        self.arrive.finish()


STRIP = 32
AHEAD = 2
STRETCH = 1.0


class ScatterTokens(Job):
    out_in_vmem = True

    def span(self):
        return 3.0 * self.chips

    def steps(self):
        return self.chips - 1

    def __init__(self, split, partial):
        self.split = split
        rows, width = partial.shape[-2:]
        self.chips = len(split.links)
        self.operands = (partial.reshape(2, self.chips, rows, width),)
        self.results = (jax.ShapeDtypeStruct((rows, width), jnp.float32),)
        self.masks = [mask for mask in split.links[1:]] + [(0, 1)]
        self.copies = 2 * self.chips - 1
        self.locals = self.chips
        self.scratch = (
            pltpu.VMEM((self.chips, rows, width), jnp.float32),
            pltpu.VMEM((2, rows, width), jnp.float32),
            pltpu.VMEM((2, rows, width), jnp.bfloat16),
            pltpu.VMEM((max(1, self.chips - 1), rows, width), jnp.bfloat16),
        )
        self.rows = rows

    def start(self):
        partial = self.ins[0]
        theirs = self.held[0]
        self.order = list(range(1, self.chips)) + [0]
        self.beside, self.loads = {}, {}
        for chip in self.order:
            self.beside[chip] = self.away(
                self.chips - 1 + chip, partial.at[1, chip], theirs.at[chip], (0, 1)
            )
            self.beside[chip].start()
        self.load(0)
        self.load(1)

    def load(self, index):
        if index < self.chips:
            chip = self.order[index]
            self.loads[chip] = self.near(
                chip, self.ins[0].at[0, chip], self.held[1].at[index % 2]
            )
            self.loads[chip].start()

    def strips(self, update):
        @pl.loop(0, self.rows // STRIP)
        def _(strip):
            update(pl.ds(pl.multiple_of(strip * STRIP, STRIP), STRIP))

    def middle(self):
        theirs, mine, sent, landed = self.held
        self.far = []
        for index, chip in enumerate(self.order[:-1]):
            self.beside[chip].wait_recv()
            self.loads[chip].wait()
            if index >= 2:
                self.far[index - 2].wait_send()

            def update(rows, index=index, chip=chip):
                sent[index % 2, rows] = to_low(theirs[chip, rows] + mine[index % 2, rows])

            self.strips(update)
            self.load(index + 2)
            copy = self.away(
                chip - 1, sent.at[index % 2], landed.at[chip - 1], self.split.links[chip]
            )
            copy.start()
            self.far.append(copy)
            yield True

    def finish(self):
        theirs, mine, _, landed = self.held
        out = self.outs[0]
        self.beside[0].wait_recv()
        self.loads[0].wait()
        for copy in self.far:
            copy.wait_recv()
        last = (self.chips - 1) % 2

        def update(rows):
            value = theirs[0, rows] + mine[last, rows]
            for chip in range(1, self.chips):
                value = value + landed[chip - 1, rows].astype(jnp.float32)
            out[rows] = value

        self.strips(update)
        for copy in self.far[-2:]:
            copy.wait_send()
        for copy in self.beside.values():
            copy.wait_send()


class Trade(Job):
    def __init__(self, split, value):
        self.split = split
        self.operands = (value,)
        self.results = (jax.ShapeDtypeStruct(value.shape, value.dtype),)
        self.masks = split.peers[1:]
        self.copies = len(self.masks)
        self.locals = 1

    def start(self):
        given, out = self.ins[0], self.outs[0]
        rank = self.split.rank(self.dp, self.seq)
        self.mine = self.near(0, given.at[rank], out.at[rank])
        self.mine.start()
        self.far = []
        for number, mask in enumerate(self.masks):
            other = self.split.rank(flipped(self.dp, mask[0]), flipped(self.seq, mask[1]))
            copy = self.away(number, given.at[other], out.at[rank], mask)
            copy.start()
            self.far.append(copy)

    def finish(self):
        self.mine.wait()
        for copy in self.far:
            copy.wait()


def pieces_of(rows, most, tile):
    for count in range(most, 1, -1):
        if rows % (count * tile) == 0:
            return count
    return 1


class TradeOf(Trade):
    def __init__(self, split, job):
        rows, columns = job.results[0].shape
        self.split, self.job = split, job
        self.depth = rows // split.ranks
        self.operands = ()
        self.results = (
            jax.ShapeDtypeStruct((split.ranks, self.depth, columns), jnp.float32),
        )
        self.masks = split.peers[1:]
        self.copies = len(self.masks)
        self.locals = 1

    def given(self, rank):
        row = pl.multiple_of(rank * self.depth, self.depth)
        return self.job.outs[0].at[pl.ds(row, self.depth)]

    def start(self):
        out = self.outs[0]
        rank = self.split.rank(self.dp, self.seq)
        self.mine = self.near(0, self.given(rank), out.at[rank])
        self.mine.start()
        self.far = []
        for number, mask in enumerate(self.masks):
            other = self.split.rank(flipped(self.dp, mask[0]), flipped(self.seq, mask[1]))
            copy = self.away(number, self.given(other), out.at[rank], mask)
            copy.start()
            self.far.append(copy)


class GatherWeights(Job):
    bulk = True

    def span(self):
        return self.operands[0].size * len(self.z_masks) * len(self.x_masks) * 2.4e-5

    def steps(self):
        return self.count

    def __init__(self, split, value, most=1, across=False):
        self.split = split
        self.operands = (value,)
        self.across = across and bool(split.shared)
        rows, columns = value.shape
        shape = (split.copies * rows, columns) if self.across else (split.copies, rows, columns)
        self.results = (jax.ShapeDtypeStruct(shape, value.dtype),)
        self.z_masks = spread(split.z_bits)
        self.x_masks = spread(split.x_bits)
        self.masks = [(mask, 0) for mask in self.z_masks[1:] + self.x_masks[1:]]
        self.count = pieces_of(rows, most, 16)
        self.depth = rows // self.count
        self.copies = (len(self.z_masks) * len(self.x_masks) - 1) * self.count
        self.locals = self.count

    def part(self, ref, piece):
        return ref if self.count == 1 else ref.at[pl.ds(piece * self.depth, self.depth)]

    def slot(self, mask, piece):
        dp = flipped(self.dp, mask)
        if not self.across:
            return self.part(self.outs[0].at[self.split.copy(dp)], piece)
        row = self.split.row_of(dp, piece, self.count, self.depth)
        return self.outs[0].at[pl.ds(pl.multiple_of(row, self.depth), self.depth)]

    def start(self):
        own = self.ins[0]
        self.mine = [
            self.near(piece, self.part(own, piece), self.slot(0, piece))
            for piece in range(self.count)
        ]
        for copy in self.mine:
            copy.start()
        self.number = 0
        self.sent, self.arrivals, self.rest = [], {}, []
        for piece in range(min(AHEAD, self.count)):
            self.send_z(piece)

    def source(self, mask, piece):
        return self.slot(mask, piece) if mask else self.part(self.ins[0], piece)

    def send_z(self, piece):
        for bit in self.split.z_bits:
            self.hop(0, piece, 1 << bit)

    def hop(self, mask, piece, onward):
        source = self.source(mask, piece)
        copy = self.away(self.number, source, self.slot(mask, piece), (onward, 0))
        copy.start()
        self.sent.append(copy)
        self.arrivals[mask | onward, piece] = self.away(
            self.number, source, self.slot(mask | onward, piece), (onward, 0)
        )
        self.number += 1

    def pass_on(self, from_mask, piece):
        source = self.source(from_mask, piece)
        for mask in self.x_masks[1:]:
            copy = self.away(self.number, source, self.slot(from_mask, piece), (mask, 0))
            copy.start()
            self.sent.append(copy)
            self.rest.append(
                self.away(self.number, source, self.slot(from_mask ^ mask, piece), (mask, 0))
            )
            self.number += 1

    def take(self, masks, piece):
        for mask in masks:
            self.arrivals[mask, piece].wait_recv()
            for bit in self.split.z_bits:
                if (1 << bit) < (mask & -mask):
                    self.hop(mask, piece, 1 << bit)
            self.pass_on(mask, piece)

    def middle(self):
        single = [mask for mask in self.z_masks[1:] if mask & (mask - 1) == 0]
        longer = [mask for mask in self.z_masks[1:] if mask & (mask - 1)]
        for piece in range(self.count):
            self.pass_on(0, piece)
            self.take(single, piece)
            if piece:
                self.take(longer, piece - 1)
            if piece + AHEAD < self.count:
                self.send_z(piece + AHEAD)
            yield True
        self.take(longer, self.count - 1)

    def finish(self):
        for copy in self.mine:
            copy.wait()
        for arrival in self.rest:
            arrival.wait_recv()
        for copy in self.sent:
            copy.wait_send()


class ReduceWeights(Job):
    out_in_vmem = True
    bulk = True

    def span(self):
        return self.size * 4.5e-5

    def steps(self):
        return len(self.units)

    def last_steps(self):
        return self.count

    def __init__(self, split, grad, most=1, across=False, of=None):
        self.split = split
        self.across = across and bool(split.shared)
        shape = (grad.shape[0] // split.copies, grad.shape[1])
        self.of = of
        if of is not None:
            self.operands = ()
        elif self.across:
            self.operands = (grad,)
        else:
            self.operands = (grad.reshape((split.copies,) + shape),)
        self.size = grad.shape[0] * grad.shape[1]
        self.results = (jax.ShapeDtypeStruct(shape, jnp.float32),)
        self.z_masks = spread(split.z_bits)
        self.x_masks = spread(split.x_bits)
        self.masks = [(mask, 0) for mask in self.z_masks[1:] + self.x_masks[1:]]
        self.count = pieces_of(shape[0], most, 8)
        self.depth = shape[0] // self.count
        far_z, far_x = len(self.z_masks) - 1, len(self.x_masks) - 1
        order = sorted(
            range(far_z + 1), key=lambda place: self.low_bit(place) or 1 << 30
        )
        stages = {}
        for place in order:
            stages.setdefault(self.low_bit(place), []).append(place)
        self.units = [
            (piece, place)
            for places in stages.values()
            for piece in range(self.count)
            for place in places
        ]
        self.copies = self.count * (far_z + (far_z + 1) * far_x)
        self.locals = len(self.units)
        self.scratch = (
            pltpu.VMEM((far_x, far_z + 1) + shape, jnp.float32),
            pltpu.VMEM((far_z + 1,) + shape, jnp.float32),
            pltpu.VMEM((far_z,) + shape, jnp.float32),
        )

    def low_bit(self, place):
        return self.z_masks[place] & -self.z_masks[place]

    def children(self, place):
        mask, low = self.z_masks[place], self.low_bit(place) or 1 << 30
        return [
            self.z_masks.index(mask | 1 << bit) for bit in self.split.z_bits if 1 << bit < low
        ]

    def rows(self, piece):
        return pl.ds(piece * self.depth, self.depth)

    def part(self, mask, piece):
        dp = flipped(self.dp, mask)
        if self.of is not None:
            job, number = self.of
            row = (self.split.copy(dp) * self.count + piece) * self.depth
            return job.outs[number].at[pl.ds(pl.multiple_of(row, self.depth), self.depth)]
        if not self.across:
            return self.ins[0].at[self.split.copy(dp), self.rows(piece)]
        row = self.split.row_of(dp, piece, self.count, self.depth)
        return self.ins[0].at[pl.ds(pl.multiple_of(row, self.depth), self.depth)]

    def start(self):
        self.number = 0
        self.sent, self.loads, self.far = {}, {}, {}
        for index in range(min(AHEAD, len(self.units))):
            self.send_x(index)

    def send_x(self, index):
        piece, place = self.units[index]
        mask = self.z_masks[place]
        by_x, mine, _ = self.held
        copies = []
        for number, x_mask in enumerate(self.x_masks[1:]):
            copy = self.away(
                self.number,
                self.part(mask ^ x_mask, piece),
                by_x.at[number, place, self.rows(piece)],
                (x_mask, 0),
            )
            copy.start()
            copies.append(copy)
            self.number += 1
        self.sent[index] = copies
        load = self.near(index, self.part(mask, piece), mine.at[place, self.rows(piece)])
        load.start()
        self.loads[index] = load

    def strips(self, piece, update):
        step = 8
        for size in (64, 32, 16):
            if self.depth % size == 0:
                step = size
                break

        @pl.loop(0, self.depth // step)
        def _(strip):
            update(pl.ds(pl.multiple_of(piece * self.depth + strip * step, 8), step))

    def middle(self):
        by_x, mine, by_z = self.held
        for index, (piece, place) in enumerate(self.units):
            self.loads[index].wait()
            for copy in self.sent[index]:
                copy.wait_recv()
            if index + AHEAD < len(self.units):
                self.send_x(index + AHEAD)

            if not place:
                yield True
                continue
            self.add(piece, place)
            copy = self.away(
                self.number,
                mine.at[place, self.rows(piece)],
                by_z.at[place - 1, self.rows(piece)],
                (self.low_bit(place), 0),
            )
            copy.start()
            self.far[(piece, place)] = copy
            self.number += 1
            yield True
        for piece in range(self.count):
            self.add(piece, 0)
            yield True

    def add(self, piece, place):
        by_x, mine, by_z = self.held
        children = self.children(place)
        for child in children:
            self.far[(piece, child)].wait_recv()
        target = mine.at[place] if place else self.outs[0]

        def update(rows):
            value = mine[place, rows]
            for number in range(len(self.x_masks) - 1):
                value = value + by_x[number, place, rows]
            for child in children:
                value = value + by_z[child - 1, rows]
            target[rows] = value

        self.strips(piece, update)

    def finish(self):
        for copy in self.far.values():
            copy.wait_send()
        for copies in self.sent.values():
            for copy in copies:
                copy.wait_send()


class Return:
    def __init__(self, job, first, scratch, out):
        self.job, self.first, self.out = job, first, out
        self.theirs, self.mine, self.stage, self.sent, self.landed = scratch
        self.beside, self.far = {}, {}

    @staticmethod
    def scratch(chips, rows, width):
        return (
            pltpu.VMEM((chips, rows, width), jnp.float32),
            pltpu.VMEM((2, rows, width), jnp.float32),
            pltpu.VMEM((2, rows, width), jnp.float32),
            pltpu.VMEM((2, rows, width), jnp.bfloat16),
            pltpu.VMEM((max(1, chips - 1), rows, width), jnp.bfloat16),
        )

    def put(self, core, chip, value):
        chips = self.job.chips
        if core == 0:
            self.mine[min(chip, 1)] = value
            return
        order = list(self.beside)
        if len(order) >= 2:
            self.beside[order[-2]].wait_send()
        spot = len(order) % 2
        self.stage[spot] = value
        copy = self.job.away(
            self.first + chips - 1 + chip, self.stage.at[spot], self.theirs.at[chip], (0, 1)
        )
        copy.start()
        self.beside[chip] = copy

    def strips(self, update):
        @pl.loop(0, self.job.rows // STRIP)
        def _(strip):
            update(pl.ds(pl.multiple_of(strip * STRIP, STRIP), STRIP))

    def pass_on(self, chip):
        if chip == 0:
            return
        self.beside[chip].wait_recv()
        order = list(self.far)
        if len(order) >= 2:
            self.far[order[-2]].wait_send()
        spot = len(order) % 2

        def update(rows):
            self.sent[spot, rows] = to_low(self.theirs[chip, rows] + self.mine[1, rows])

        self.strips(update)
        copy = self.job.away(
            self.first + chip - 1,
            self.sent.at[spot],
            self.landed.at[chip - 1],
            self.job.split.links[chip],
        )
        copy.start()
        self.far[chip] = copy

    def finish(self):
        chips = self.job.chips
        self.beside[0].wait_recv()
        for chip in range(1, chips):
            self.far[chip].wait_recv()

        def update(rows):
            value = self.theirs[0, rows] + self.mine[0, rows]
            for chip in range(1, chips):
                value = value + self.landed[chip - 1, rows].astype(jnp.float32)
            self.out[rows] = value

        self.strips(update)
        for chip in list(self.beside)[-2:]:
            self.beside[chip].wait_send()
        for chip in list(self.far)[-2:]:
            self.far[chip].wait_send()


class Layer(Job):
    works = True
    work_steps = 0
    after_steps = 0
    length = 35.0

    def span(self):
        return self.length

    def steps(self):
        return 3 * self.chips + 2 * self.chips * (self.work_steps + self.after_steps) + 2

    def __init__(self, split, own, others, results, scratch=()):
        self.split = split
        self.chips = len(split.links)
        self.rows, self.width = own.shape
        self.total = 2 * self.chips * self.rows
        self.operands = (own,) + tuple(others)
        self.given_in_vmem = (False,) + (True,) * len(others)
        slots = (2, self.chips, self.rows, self.width)
        self.results = (jax.ShapeDtypeStruct((self.rows, self.width), jnp.float32),) + tuple(results)
        self.in_vmem = (True,) * len(self.results)
        self.scratch = (
            (pltpu.VMEM(slots, jnp.bfloat16),)
            + Return.scratch(self.chips, self.rows, self.width)
            + tuple(scratch)
        )
        self.masks = [mask for mask in split.links[1:]] + [(0, 1)]
        self.copies = Spread.copies(split) + 2 * self.chips - 1
        self.locals = 2
        self.places = [(core, chip) for chip in range(self.chips) for core in (0, 1)]

    def start(self):
        self.slots = self.held[0]
        self.back = Return(self, Spread.copies(self.split), self.held[1:6], self.outs[0])
        self.more = self.held[6:]
        self.arrive = Spread(self, self.ins[0], self.slots, 0)

    def at(self, core, chip):
        place = flipped(self.seq, 2 * chip + core)
        return pl.ds(pl.multiple_of(place * self.rows, self.rows), self.rows)

    def middle(self):
        self.open()
        for core, chip in self.places:
            self.arrive.ready(core, chip)
            self.take(core, chip)
            yield True
        yield from self.work()
        for chip in list(range(1, self.chips)) + [0]:
            for core in (1, 0):
                self.back.put(core, chip, self.give(core, chip))
            yield True
            self.back.pass_on(chip)
        yield from self.after()

    def open(self):
        pass

    def work(self):
        return iter(())

    def after(self):
        return iter(())

    def finish(self):
        self.back.finish()
        self.arrive.finish()


def turned(value, steps):
    return pltpu.roll(value, steps % value.shape[0], 0)


def within(positions):
    places = positions[...]
    return jnp.where(places >= 1, 1.0, 0.0), jnp.where(places >= 2, 1.0, 0.0)


class MixForward(Layer):
    def __init__(self, split, own, w_in, w_out, taps, positions):
        rows = 2 * len(split.links) * own.shape[0]
        channels = w_out.shape[0]
        super().__init__(
            split,
            own,
            (w_in, w_out, taps, positions),
            (
                jax.ShapeDtypeStruct((2, len(split.links)) + own.shape, jnp.bfloat16),
                jax.ShapeDtypeStruct((rows, 3 * channels), jnp.float32),
                jax.ShapeDtypeStruct((rows, channels), jnp.float32),
                jax.ShapeDtypeStruct((rows, channels), jnp.bfloat16),
            ),
        )
        self.channels = channels

    def open(self):
        _, self.w_in, self.w_out, self.taps, self.positions = self.ins
        _, self.kept, self.projected, self.conv, self.gated = self.outs

    def take(self, core, chip):
        value = self.slots[core, chip]
        self.kept[core, chip] = value
        self.projected[self.at(core, chip)] = matmul(value, self.w_in[...])

    def work(self):
        each = self.channels
        mixed = to_low(self.projected[:, :each] * self.projected[:, 2 * each :]).astype(jnp.float32)
        once, twice = within(self.positions)
        conv = (
            self.taps[2:3] * mixed
            + self.taps[1:2] * turned(mixed, 1) * once
            + self.taps[0:1] * turned(mixed, 2) * twice
        )
        self.conv[...] = conv
        self.gated[...] = to_low(self.projected[:, each : 2 * each] * conv)
        yield True

    def give(self, core, chip):
        return matmul(self.gated[self.at(core, chip)], self.w_out[...])


class MixBack(Layer):
    after_steps = 1

    def __init__(self, split, own, w_in, w_out, taps, positions, kept, projected, conv, gated):
        rows = 2 * len(split.links) * own.shape[0]
        channels = w_out.shape[0]
        super().__init__(
            split,
            own,
            (w_in, w_out, taps, positions, kept, projected, conv, gated),
            (
                jax.ShapeDtypeStruct(w_in.shape, jnp.float32),
                jax.ShapeDtypeStruct(w_out.shape, jnp.float32),
                jax.ShapeDtypeStruct(taps.shape, jnp.float32),
            ),
            (
                pltpu.VMEM((rows, channels), jnp.float32),
                pltpu.VMEM((rows, 3 * channels), jnp.bfloat16),
            ),
        )
        self.channels = channels

    def open(self):
        _, self.w_in, self.w_out, self.taps, self.positions = self.ins[:5]
        self.kept, self.projected, self.conv, self.gated = self.ins[5:]
        _, self.grad_in, self.grad_out, self.grad_taps = self.outs
        self.grad_gated, self.grad_projected = self.more

    def take(self, core, chip):
        grad = self.slots[core, chip]
        self.grad_gated[self.at(core, chip)] = contract_last(grad, self.w_out[...])
        term = contract_first(self.gated[self.at(core, chip)], grad)
        if (core, chip) == (0, 0):
            self.grad_out[...] = term
        else:
            self.grad_out[...] += term

    def work(self):
        each = self.channels
        part_b = self.projected[:, :each]
        part_c = self.projected[:, each : 2 * each]
        part_v = self.projected[:, 2 * each :]
        once, twice = within(self.positions)
        mixed = to_low(part_b * part_v).astype(jnp.float32)
        grad_gated = self.grad_gated[...]
        grad_conv = grad_gated * part_c
        back_one, back_two = grad_conv * once, grad_conv * twice
        self.grad_taps[...] = jnp.zeros(self.grad_taps.shape, jnp.float32)
        self.grad_taps[0:1] = jnp.sum(back_two * turned(mixed, 2), axis=0, keepdims=True)
        self.grad_taps[1:2] = jnp.sum(back_one * turned(mixed, 1), axis=0, keepdims=True)
        self.grad_taps[2:3] = jnp.sum(grad_conv * mixed, axis=0, keepdims=True)
        grad_mixed = (
            self.taps[2:3] * grad_conv
            + turned(self.taps[1:2] * back_one, -1)
            + turned(self.taps[0:1] * back_two, -2)
        )
        grad_mixed = to_low(grad_mixed).astype(jnp.float32)
        self.grad_projected[:, :each] = to_low(grad_mixed * part_v)
        self.grad_projected[:, each : 2 * each] = to_low(grad_gated * self.conv[...])
        self.grad_projected[:, 2 * each :] = to_low(grad_mixed * part_b)
        yield True

    def give(self, core, chip):
        return contract_last(self.grad_projected[self.at(core, chip)], self.w_in[...])

    def after(self):
        for core, chip in self.places:
            term = contract_first(
                self.kept[core, chip], self.grad_projected[self.at(core, chip)]
            )
            if (core, chip) == (0, 0):
                self.grad_in[...] = term
            else:
                self.grad_in[...] += term
            yield True


LANES = 128


def head_means(value):
    row = lax.broadcasted_iota(jnp.int32, (LANES, LANES), 0) // HEAD
    column = lax.broadcasted_iota(jnp.int32, (LANES, LANES), 1) // HEAD
    same = jnp.where(row == column, 1.0 / HEAD, 0.0)
    return jnp.dot(
        value, same, preferred_element_type=jnp.float32, precision=lax.Precision.HIGHEST
    )


def half_turned(value):
    lane = lax.broadcasted_iota(jnp.int32, value.shape, 1) % HEAD
    ahead = pltpu.roll(value, LANES - HEAD // 2, 1)
    behind = pltpu.roll(value, HEAD // 2, 1)
    return jnp.where(lane < HEAD // 2, ahead, behind)


class Heads:
    def __init__(self, heads, kv_heads):
        self.heads, self.kv_heads = heads, kv_heads
        self.shared = heads // kv_heads
        self.turned = (heads + kv_heads) * HEAD
        self.width = (heads + 2 * kv_heads) * HEAD

    def tiles(self):
        for begin in range(0, self.width, LANES):
            yield slice(begin, begin + LANES), min(LANES, max(0, self.turned - begin))

    def q(self, head):
        return slice(head * HEAD, (head + 1) * HEAD)

    def k(self, head):
        begin = self.heads + head // self.shared
        return slice(begin * HEAD, (begin + 1) * HEAD)

    def v(self, head):
        begin = self.heads + self.kv_heads + head // self.shared
        return slice(begin * HEAD, (begin + 1) * HEAD)

    @staticmethod
    def some(lanes, value, other):
        if lanes == LANES:
            return value
        lane = lax.broadcasted_iota(jnp.int32, value.shape, 1)
        return jnp.where(lane < lanes, value, other)


class AttendForward(Layer):
    work_steps = 1
    length = 42.0

    def __init__(self, split, heads, own, w_in, w_out, cosine, sine, gain, positions):
        rows = 2 * len(split.links) * own.shape[0]
        self.heads = heads
        super().__init__(
            split,
            own,
            (w_in, w_out, cosine, sine, gain, positions),
            (
                jax.ShapeDtypeStruct((2, len(split.links)) + own.shape, jnp.bfloat16),
                jax.ShapeDtypeStruct((rows, heads.width), jnp.float32),
                jax.ShapeDtypeStruct((rows, heads.width), jnp.bfloat16),
                jax.ShapeDtypeStruct((rows, heads.heads * HEAD), jnp.bfloat16),
                jax.ShapeDtypeStruct((rows, heads.heads), jnp.float32),
            ),
        )

    def open(self):
        _, self.w_in, self.w_out, self.cosine, self.sine, self.gain, self.positions = self.ins
        _, self.kept, self.projected, self.turned, self.out, self.lse = self.outs

    def take(self, core, chip):
        value = self.slots[core, chip]
        self.kept[core, chip] = value
        rows = self.at(core, chip)
        projected = matmul(value, self.w_in[...])
        self.projected[rows] = projected
        for lanes, count in self.heads.tiles():
            raw = projected[:, lanes]
            if count:
                unit = raw * lax.rsqrt(head_means(raw * raw) + EPSILON)
                normed = unit * self.gain[:, lanes]
                spun = normed * self.cosine[rows] + half_turned(normed) * self.sine[rows]
                raw = self.heads.some(count, spun, raw)
            self.turned[rows, lanes] = to_low(raw)

    def work(self):
        for place in range(2 * self.chips):
            rows = slice(place * self.rows, (place + 1) * self.rows)
            bias, seen = hidden_scores(self.positions[rows], place, self.rows)
            for head in range(self.heads.heads):
                scores = (
                    contract_last(
                        self.turned[rows, self.heads.q(head)], self.turned[:seen, self.heads.k(head)]
                    )
                    * HEAD ** (-0.5)
                    + bias
                )
                peak = jnp.max(scores, axis=-1, keepdims=True)
                expo = jnp.exp(scores - peak)
                count = jnp.sum(expo, axis=-1, keepdims=True)
                probs = to_low(expo * (1.0 / count))
                self.out[rows, self.heads.q(head)] = to_low(
                    matmul(probs, self.turned[:seen, self.heads.v(head)])
                )
                self.lse[rows, head : head + 1] = peak + jnp.log(count)
            yield True

    def give(self, core, chip):
        return matmul(self.out[self.at(core, chip)], self.w_out[...])


def hidden_scores(positions, place, rows):
    seen = (place + 1) * rows
    row = place * rows + lax.broadcasted_iota(jnp.int32, (rows, seen), 0)
    column = lax.broadcasted_iota(jnp.int32, (rows, seen), 1)
    allowed = (column >= row - positions) & (column <= row)
    return jnp.where(allowed, 0.0, MASKED_SCORE), seen


class AttendBack(Layer):
    work_steps = 2
    after_steps = 1
    length = 52.0

    def __init__(
        self, split, heads, own, w_in, w_out, cosine, sine, gain, positions, kept, projected, turned, out, lse
    ):
        rows = 2 * len(split.links) * own.shape[0]
        self.heads = heads
        super().__init__(
            split,
            own,
            (w_in, w_out, cosine, sine, gain, positions, kept, projected, turned, out, lse),
            (
                jax.ShapeDtypeStruct(w_in.shape, jnp.float32),
                jax.ShapeDtypeStruct(w_out.shape, jnp.float32),
                jax.ShapeDtypeStruct((8, heads.width), jnp.float32),
            ),
            (
                pltpu.VMEM((rows, heads.heads * HEAD), jnp.bfloat16),
                pltpu.VMEM((rows, heads.width), jnp.float32),
                pltpu.VMEM((rows, heads.width), jnp.bfloat16),
            ),
        )

    def open(self):
        _, self.w_in, self.w_out, self.cosine, self.sine, self.gain, self.positions = self.ins[:7]
        self.kept, self.projected, self.turned, self.out, self.lse = self.ins[7:]
        _, self.grad_in, self.grad_out, self.grad_gain = self.outs
        self.grad_heads, self.grad_turned, self.grad_projected = self.more

    def take(self, core, chip):
        grad = self.slots[core, chip]
        rows = self.at(core, chip)
        self.grad_heads[rows] = to_low(contract_last(grad, self.w_out[...]))
        term = contract_first(self.out[rows], grad)
        if (core, chip) == (0, 0):
            self.grad_out[...] = term
        else:
            self.grad_out[...] += term

    def work(self):
        factor = HEAD ** (-0.5)
        self.grad_turned[...] = jnp.zeros(self.grad_turned.shape, jnp.float32)
        self.grad_gain[...] = jnp.zeros(self.grad_gain.shape, jnp.float32)
        for place in range(2 * self.chips):
            rows = slice(place * self.rows, (place + 1) * self.rows)
            bias, seen = hidden_scores(self.positions[rows], place, self.rows)
            for head in range(self.heads.heads):
                own, key, value = self.heads.q(head), self.heads.k(head), self.heads.v(head)
                query, grad = self.turned[rows, own], self.grad_heads[rows, own]
                scores = contract_last(query, self.turned[:seen, key]) * factor + bias
                probs = jnp.exp(scores - self.lse[rows, head : head + 1])
                grad_probs = contract_last(grad, self.turned[:seen, value])
                row_dot = jnp.sum(probs * grad_probs, axis=-1, keepdims=True)
                grad_scores = to_low(probs * (grad_probs - row_dot))
                self.grad_turned[rows, own] = matmul(grad_scores, self.turned[:seen, key]) * factor
                self.grad_turned[:seen, key] += contract_first(grad_scores, query) * factor
                self.grad_turned[:seen, value] += contract_first(to_low(probs), grad)
            yield True
        for place in range(2 * self.chips):
            rows = slice(place * self.rows, (place + 1) * self.rows)
            for lanes, count in self.heads.tiles():
                low = to_low(self.grad_turned[rows, lanes])
                if count:
                    grad = low.astype(jnp.float32)
                    normed = grad * self.cosine[rows] + half_turned(grad * self.sine[rows])
                    raw = self.projected[rows, lanes]
                    scale = lax.rsqrt(head_means(raw * raw) + EPSILON)
                    unit = raw * scale
                    gain_term = self.heads.some(count, normed * unit, jnp.zeros_like(unit))
                    self.grad_gain[0:1, lanes] += jnp.sum(gain_term, axis=0, keepdims=True)
                    weighted = normed * self.gain[:, lanes]
                    back = scale * (weighted - unit * head_means(weighted * unit))
                    low = to_low(self.heads.some(count, back, grad))
                self.grad_projected[rows, lanes] = low
            yield True

    def give(self, core, chip):
        return contract_last(self.grad_projected[self.at(core, chip)], self.w_in[...])

    def after(self):
        for core, chip in self.places:
            term = contract_first(
                self.kept[core, chip], self.grad_projected[self.at(core, chip)]
            )
            if (core, chip) == (0, 0):
                self.grad_in[...] = term
            else:
                self.grad_in[...] += term
            yield True


class FeedForward(Job):
    works = True

    def span(self):
        return 60.0 if self.back and self.forward else 52.0

    def steps(self):
        return 3 * self.chips

    def __init__(self, split, normed, grad, w_in, w_down, forward):
        self.split, self.forward, self.back = split, forward, grad is not None
        self.chips = len(split.links)
        width = w_in.shape[0]
        gathered = normed if normed.ndim == 2 else grad
        given = (grad if normed.ndim == 2 else normed) if self.back else None
        self.gather_normed = normed.ndim == 2
        self.rows = gathered.shape[0]
        self.half = w_in.shape[1] // 2
        self.operands = (gathered, w_in, w_down) + (() if given is None else (given,))
        row_sum = jax.ShapeDtypeStruct((self.rows, width), jnp.float32)
        self.results, self.in_vmem = (), ()
        all_terms = (2, self.chips, self.rows, width)
        if self.back:
            if forward:
                self.results += (jax.ShapeDtypeStruct(all_terms, jnp.float32),)
                self.in_vmem += (False,)
            self.results += (
                row_sum,
                jax.ShapeDtypeStruct(w_in.shape, jnp.float32),
                jax.ShapeDtypeStruct(w_down.shape, jnp.float32),
            )
            self.in_vmem += (True, True, True)
        else:
            self.results += (row_sum, jax.ShapeDtypeStruct(all_terms, jnp.bfloat16))
            self.in_vmem += (True, False)
        self.masks = [mask for mask in split.links[1:]] + [(0, 1)]
        self.copies = Spread.copies(split) + 2 * self.chips - 1
        self.locals = 5 + 2 * self.chips
        all_rows = pltpu.VMEM((2, self.chips, self.rows, width), jnp.bfloat16)
        self.scratch = (
            (all_rows,)
            + ((all_rows,) if given is not None else ())
            + (pltpu.VMEM(w_in.shape, jnp.bfloat16), pltpu.VMEM(w_down.shape, jnp.bfloat16))
        )
        self.scratch += Return.scratch(self.chips, self.rows, width)
        if self.back and forward:
            self.scratch += (pltpu.VMEM((2, self.rows, width), jnp.float32),)

    def start(self):
        held = list(self.held)
        self.slots = held.pop(0)
        self.given = held.pop(0) if self.back else None
        self.w_in, self.w_down = held.pop(0), held.pop(0)
        outs = list(self.outs)
        self.terms = outs.pop(0) if self.back and self.forward else None
        self.sums = Return(self, Spread.copies(self.split), held[:5], outs.pop(0))
        self.staged = held[5] if self.terms is not None else None
        if self.back:
            self.grad_in, self.grad_down = outs
        else:
            self.kept = outs.pop(0)
        self.arrive = Spread(self, self.ins[0], self.slots, 0)
        self.loads = [
            self.near(1, self.ins[1], self.w_in),
            self.near(2, self.ins[2], self.w_down),
        ]
        self.rest = []
        if self.back:
            self.rest = [
                self.near(3 + 2 * chip + core, self.ins[3].at[core, chip], self.given.at[core, chip])
                for chip in range(self.chips)
                for core in (0, 1)
            ]
        for copy in self.loads + self.rest:
            copy.start()

    def middle(self):
        self.stores = []
        for chip in range(self.chips):
            for core in (0, 1):
                if chip == 1:
                    for other in self.arrive.direct:
                        self.arrive.ready(0, other)
                self.arrive.ready(core, chip)
                if (core, chip) == (0, 0):
                    self.loads[0].wait()
                    self.loads[1].wait()
                if self.back:
                    self.rest[2 * chip + core].wait()
                else:
                    self.store(
                        3 + 2 * chip + core, self.slots.at[core, chip], self.kept.at[core, chip]
                    )
                self.compute(core, chip)
                yield True
            self.sums.pass_on(chip)
            yield True

    def store(self, number, source, target):
        copy = self.near(number, source, target)
        copy.start()
        self.stores.append(copy)

    def compute(self, core, chip):
        arrived = self.slots[core, chip]
        normed = arrived if self.gather_normed else self.given[core, chip]
        both = matmul(normed, self.w_in[...])
        gate, upper = both[:, : self.half], both[:, self.half :]
        sigma = jax.nn.sigmoid(gate)
        active = gate * sigma
        hidden = to_low(active * upper)
        if self.terms is not None:
            count = len(self.stores)
            if count >= 2:
                self.stores[count - 2].wait()
            self.staged[count % 2] = matmul(hidden, self.w_down[...])
            self.store(
                3 + 2 * self.chips + count % 2,
                self.staged.at[count % 2],
                self.terms.at[core, chip],
            )
        elif self.forward:
            self.sums.put(core, chip, matmul(hidden, self.w_down[...]))
        if self.back:
            grad = self.given[core, chip] if self.gather_normed else arrived
            grad_hidden = contract_last(grad, self.w_down[...])
            grad_gate = to_low(grad_hidden * upper * (sigma * (1.0 + gate * (1.0 - sigma))))
            grad_upper = to_low(grad_hidden * active)
            grad_both = jnp.concatenate([grad_gate, grad_upper], axis=1)
            self.sums.put(core, chip, contract_last(grad_both, self.w_in[...]))
            if core == 0 and chip == 0:
                self.grad_in[...] = contract_first(normed, grad_both)
                self.grad_down[...] = contract_first(hidden, grad)
            else:
                self.grad_in[...] += contract_first(normed, grad_both)
                self.grad_down[...] += contract_first(hidden, grad)

    def finish(self):
        self.sums.finish()
        self.arrive.finish()
        for store in self.stores if self.terms is None else self.stores[-2:]:
            store.wait()


def all_masks():
    seq, dp = lax.axis_size("seq"), lax.axis_size("dp")
    return [(dp_mask, seq_mask) for dp_mask in range(dp) for seq_mask in range(seq)][1:]


class Hops(Job):
    def plan(self):
        seq, dp = lax.axis_size("seq"), lax.axis_size("dp")
        self.straight = seq * dp <= FEW
        if self.straight:
            self.masks = all_masks()
        else:
            self.masks = [(0, mask) for mask in range(1, seq)] + [
                (mask, 0) for mask in range(1, dp)
            ]


FEW = 1


class Everyone(Hops):
    def steps(self):
        return 1

    def __init__(self, value):
        self.operands = (value,)
        seq, dp = lax.axis_size("seq"), lax.axis_size("dp")
        self.results = (jax.ShapeDtypeStruct((dp, seq) + value.shape, value.dtype),)
        self.plan()
        self.copies = len(self.masks)
        self.locals = 1

    def post(self, number, source, index, mask):
        out = self.outs[0]
        away = (flipped(self.dp, mask[0]), flipped(self.seq, mask[1]))
        copy = self.away(number, source, out.at[index((self.dp, self.seq))], mask)
        copy.start()
        self.sent.append(copy)
        self.arrivals.append(self.away(number, source, out.at[index(away)], mask))

    def start(self):
        out = self.outs[0]
        self.mine = self.near(0, self.ins[0], out.at[self.dp, self.seq])
        self.mine.start()
        self.sent, self.arrivals = [], []
        for number, mask in enumerate(self.masks):
            if self.straight or not mask[0]:
                self.post(number, self.ins[0], lambda place: place, mask)

    def middle(self):
        if self.straight:
            return
        self.mine.wait()
        for arrival in self.arrivals:
            arrival.wait_recv()
        self.arrivals = []
        for number, mask in enumerate(self.masks):
            if mask[0]:
                self.post(number, self.outs[0].at[self.dp], lambda place: place[0], mask)
        yield True

    def finish(self):
        if self.straight:
            self.mine.wait()
        for arrival in self.arrivals:
            arrival.wait_recv()
        for copy in self.sent:
            copy.wait_send()


class SumAll(Hops):
    out_in_vmem = True

    def steps(self):
        return 1 if self.straight else 3

    def __init__(self, value):
        self.operands = (value,)
        self.results = (jax.ShapeDtypeStruct(value.shape, value.dtype),)
        seq, dp = value.shape[:2]
        self.plan()
        self.copies = 2 * len(self.masks)
        self.locals = 1
        self.scratch = (pltpu.VMEM(value.shape, jnp.float32),)
        if self.straight:
            self.scratch += (pltpu.VMEM((len(self.masks),) + value.shape[2:], jnp.float32),)
        else:
            self.scratch += (
                pltpu.VMEM((seq - 1,) + value.shape[1:], jnp.float32),
                pltpu.VMEM((dp - 1,) + value.shape[2:], jnp.float32),
            )

    def block(self, ref, mask, whole=False):
        seq, dp = flipped(self.seq, mask[1]), flipped(self.dp, mask[0])
        return ref.at[seq] if whole else ref.at[seq, dp]

    def round(self, masks, source, target):
        copies = []
        for number, mask in enumerate(masks):
            copy = self.away(self.number + number, source(mask), target(number, mask), mask)
            copy.start()
            copies.append(copy)
        self.number += len(masks)
        self.sent += copies
        return copies

    def start(self):
        self.load = self.near(0, self.ins[0], self.held[0])
        self.load.start()
        self.load.wait()
        self.number, self.sent = 0, []
        masks = [mask for mask in self.masks if self.straight or not mask[0]]
        self.first = self.round(
            masks,
            lambda mask: self.block(self.held[0], mask, not self.straight),
            lambda number, mask: self.held[1].at[number],
        )

    def arrived(self, masks, whole):
        out = self.outs[0]
        return [
            self.away(self.number + number, self.block(out, mask, whole), self.block(out, mask, whole), mask)
            for number, mask in enumerate(masks)
        ]

    def give_back(self, masks, whole):
        out = self.outs[0]
        arrivals = self.arrived(masks, whole)
        mine = self.block(out, (0, 0), whole)
        self.round(masks, lambda mask: mine, lambda number, mask: mine)
        return arrivals

    def middle(self):
        given, out = self.held[0], self.outs[0]
        for copy in self.first:
            copy.wait_recv()
        if self.straight:
            value = given[self.seq, self.dp]
            for number in range(len(self.masks)):
                value = value + self.held[1][number]
            out[self.seq, self.dp] = value
            self.last = self.give_back(self.masks, False)
            yield True
            return
        by_seq, by_dp = self.held[1:]
        part = given[self.seq]
        for number in range(len(self.first)):
            part = part + by_seq[number]
        given[self.seq] = part
        yield True
        masks = [mask for mask in self.masks if mask[0]]
        copies = self.round(
            masks,
            lambda mask: self.block(given, mask),
            lambda number, mask: by_dp.at[number],
        )
        for copy in copies:
            copy.wait_recv()
        value = given[self.seq, self.dp]
        for number in range(len(masks)):
            value = value + by_dp[number]
        out[self.seq, self.dp] = value
        yield True
        for arrival in self.give_back(masks, False):
            arrival.wait_recv()
        yield True
        self.last = self.give_back([mask for mask in self.masks if not mask[0]], True)

    def finish(self):
        for arrival in self.last:
            arrival.wait_recv()
        for copy in self.sent:
            copy.wait_send()


def drained(turn):
    for _ in turn:
        pass
    yield True


def in_order(jobs):
    bulk = STRETCH * sum(job.span() for job in jobs if job.bulk and not job.begin)
    steps = []
    for number, job in enumerate(jobs):
        turn, count = job.middle(), job.steps()
        span = bulk if job.bulk and not job.begin else job.span()
        if job.begin:
            steps.append((job.begin, number, -1, iter([job.start])))
        early = 0 if job.works else 1
        for step in range(count):
            steps.append((job.begin + (step + early) * span / count, number, step, turn))
        for step in range(job.last_steps()):
            steps.append((job.begin + span + 1.0, number, count + step, turn))
        steps.append((1000.0, number, count, drained(turn)))
    return [turn for _, _, _, turn in sorted(steps, key=lambda step: step[:3])]


class Courier:
    def __init__(self):
        self.calls = 0

    def __call__(self, *jobs):
        number = self.calls
        self.calls += 1
        masks = []
        for job in jobs:
            for mask in job.masks:
                if mask not in masks:
                    masks.append(mask)
        operands = [value for job in jobs for value in job.operands]
        results = [value for job in jobs for value in job.results]
        in_vmem, given = [], []
        for job in jobs:
            given += list(job.given_in_vmem or [False] * len(job.operands))
            in_vmem += list(job.in_vmem or [job.out_in_vmem] * len(job.results))
        scratch = []
        for job in jobs:
            scratch += list(job.scratch)
            scratch += [
                pltpu.SemaphoreType.DMA((max(1, job.copies),)),
                pltpu.SemaphoreType.DMA((max(1, job.copies),)),
                pltpu.SemaphoreType.DMA((max(1, job.locals),)),
            ]

        def kernel(*refs):
            ins = list(refs[: len(operands)])
            outs = list(refs[len(operands) : len(operands) + len(results)])
            held = list(refs[len(operands) + len(results) :])
            dp, seq = lax.axis_index("dp"), lax.axis_index("seq")
            barrier = pltpu.get_barrier_semaphore()
            for mask in masks:
                pl.semaphore_signal(
                    barrier,
                    inc=1,
                    device_id=(flipped(dp, mask[0]), flipped(seq, mask[1])),
                    device_id_type=MESH,
                )
            pl.semaphore_wait(barrier, len(masks))
            for job in jobs:
                count_in, count_out = len(job.operands), len(job.results)
                own = len(job.scratch)
                job.bind(
                    ins[:count_in], outs[:count_out], held[:own], *held[own : own + 3]
                )
                ins, outs, held = ins[count_in:], outs[count_out:], held[own + 3 :]
            for job in jobs:
                if not job.begin:
                    job.start()
            for turn in in_order(jobs):
                action = next(turn, None)
                if callable(action):
                    action()
            for job in jobs:
                job.finish()

        sent = sum(value.size * value.dtype.itemsize for value in operands)
        outs = pl.pallas_call(
            kernel,
            out_shape=results,
            in_specs=[
                pl.BlockSpec(memory_space=pltpu.VMEM if vmem else pl.ANY) for vmem in given
            ],
            out_specs=[
                pl.BlockSpec(memory_space=pltpu.VMEM if vmem else pl.ANY) for vmem in in_vmem
            ],
            scratch_shapes=scratch,
            compiler_params=pltpu.CompilerParams(
                collective_id=number, has_side_effects=True, vmem_limit_bytes=60 << 20
            ),
            cost_estimate=pl.CostEstimate(flops=0, bytes_accessed=8 * sent, transcendentals=0),
            name="courier_%d" % number,
        )(*operands)
        return outs


def packed(values, blocks):
    flat = jnp.concatenate([value.reshape(-1).astype(jnp.float32) for value in values])
    each = -(-flat.shape[0] // (blocks * 1024)) * 1024
    return jnp.pad(flat, (0, blocks * each - flat.shape[0])).reshape(blocks, each // 128, 128)


def unpacked(flat, values):
    flat = flat.reshape(-1)
    out, begin = [], 0
    for value in values:
        out.append(flat[begin : begin + value.size].reshape(value.shape))
        begin += value.size
    return out


def large_sum(values):
    seq, dp = lax.axis_size("seq"), lax.axis_size("dp")
    blocks = packed(values, seq * dp)
    return SumAll(blocks.reshape((seq, dp) + blocks.shape[1:]))


def small_sum(values):
    return Everyone(packed(values, 1)[0])


def local_call(kernel, name, results, operands, flops=0):
    moved = sum(value.size * value.dtype.itemsize for value in list(operands) + list(results))
    return pl.pallas_call(
        kernel,
        out_shape=results,
        in_specs=[pl.BlockSpec(memory_space=pltpu.VMEM)] * len(operands),
        out_specs=[pl.BlockSpec(memory_space=pltpu.VMEM)] * len(results),
        compiler_params=pltpu.CompilerParams(vmem_limit_bytes=56 << 20),
        cost_estimate=pl.CostEstimate(flops=flops, bytes_accessed=moved, transcendentals=0),
        name=name,
    )(*operands)


def pieces_by_rank(split, columns):
    dp_count, seq_count = lax.axis_size("dp"), lax.axis_size("seq")
    each = columns // (dp_count * seq_count)
    out = []
    for dp in range(dp_count):
        for seq in range(seq_count):
            out.append(
                (split.rank(dp, seq), split.copy(dp) * each, (dp * seq_count + seq) * each)
            )
    return each, out


def lowered_chunks(near, wide, attn_widths, mix_in, mix_out, attn_in, attn_out, ffn_in, ffn_out, vectors):
    seq_count = lax.axis_size("seq")
    rows, width = mix_out.shape
    hidden = ffn_in.shape[-1]
    channels, mine = width // seq_count, hidden // wide.ranks

    def kernel(mix_in, mix_out, attn_in, attn_out, ffn_in, ffn_out, vectors, *outs):
        mix_chunk, attn_chunk, one, two, low_mix_out, low_attn_out, down_one, down_two, block = outs
        each, pieces = pieces_by_rank(near, width)
        for part in range(3):
            for rank, inner, outer in pieces:
                mix_chunk[rank, :, pl.ds(part * channels + inner, each)] = to_low(
                    mix_in[:, pl.ds(part * width + outer, each)]
                )
        begin, target = 0, 0
        for columns in attn_widths:
            each = columns // seq_count
            for rank in range(seq_count):
                attn_chunk[rank, :, pl.ds(target, each)] = to_low(
                    attn_in[:, pl.ds(begin + rank * each, each)]
                )
            begin, target = begin + columns, target + each
        each, pieces = pieces_by_rank(wide, hidden)
        for layer, chunk in enumerate((one, two)):
            for part in range(2):
                for rank, inner, outer in pieces:
                    chunk[rank, :, pl.ds(part * mine + inner, each)] = to_low(
                        ffn_in[layer, part, :, pl.ds(outer, each)]
                    )
        low_mix_out[...] = to_low(mix_out[...])
        low_attn_out[...] = to_low(attn_out[...])
        down_one[...] = to_low(ffn_out[0])
        down_two[...] = to_low(ffn_out[1])
        block[...] = jnp.zeros(block.shape, jnp.bfloat16)
        block[pl.ds(0, vectors.shape[0]), pl.ds(0, vectors.shape[1])] = to_low(vectors[...])

    def low(*shape):
        return jax.ShapeDtypeStruct(shape, jnp.bfloat16)

    results = (
        low(seq_count, rows, 3 * channels),
        low(seq_count, rows, sum(attn_widths) // seq_count),
        low(wide.ranks, rows, 2 * mine),
        low(wide.ranks, rows, 2 * mine),
        low(*mix_out.shape),
        low(*attn_out.shape),
        low(*ffn_out.shape[1:]),
        low(*ffn_out.shape[1:]),
        low(16, 128),
    )
    return local_call(
        kernel,
        "lower",
        results,
        (mix_in, mix_out, attn_in, attn_out, ffn_in, ffn_out, vectors),
    )


LINE = 512


class Step:
    def __init__(self, weights):
        self.weights = weights
        self.matrices = []
        begin, line = 0, 0
        for number, weight in enumerate(weights):
            lead = weight.shape[:-2]
            rows, columns = weight.shape[-2:]
            indices = [()]
            for size in lead:
                indices = [index + (place,) for index in indices for place in range(size)]
            for index in indices:
                self.matrices.append((number, index, rows, columns, begin, line))
                begin += rows
                line += columns // LINE
        self.rows, self.scalars, self.weighted = begin, 2 * line, line
        devices = lax.axis_size("dp") * lax.axis_size("seq")
        self.devices = devices
        self.lines = -(-(2 * line + 1) // devices)
        self.sums = (lax.axis_size("seq"), lax.axis_size("dp"), self.lines, 1, LINE)

    def line(self, ref, number):
        per = self.lines
        dp = lax.axis_size("dp")
        return ref.at[number // (per * dp), (number // per) % dp, number % per]

    def natural(self):
        return [jax.ShapeDtypeStruct(weight.shape, jnp.float32) for weight in self.weights]

    def columns(self):
        return [
            jax.ShapeDtypeStruct(weight.shape[:-2] + (1, weight.shape[-1]), jnp.float32)
            for weight in self.weights
        ]

    def first(self, near, wide, attn_widths, traded, row_states, extra):
        seq_count = lax.axis_size("seq")

        def kernel(mix, attn, one, two, mix_out, attn_out, down_one, down_two, *refs):
            weights, (states, extra), refs = refs[:6], refs[6:8], refs[8:]
            grads, (rows_new, sums) = refs[:6], refs[6:]
            width = mix_out.shape[-1]
            channels = mix.shape[-1] // 3
            each, pieces = pieces_by_rank(near, width)
            for part in range(3):
                for rank, inner, outer in pieces:
                    grads[0][:, pl.ds(part * width + outer, each)] = mix[
                        rank, :, pl.ds(part * channels + inner, each)
                    ]
            grads[1][...] = mix_out[...]
            begin, source = 0, 0
            for columns in attn_widths:
                each = columns // seq_count
                for rank in range(seq_count):
                    grads[2][:, pl.ds(begin + rank * each, each)] = attn[
                        rank, :, pl.ds(source, each)
                    ]
                begin, source = begin + columns, source + each
            grads[3][...] = attn_out[...]
            hidden = grads[4].shape[-1]
            mine = one.shape[-1] // 2
            each, pieces = pieces_by_rank(wide, hidden)
            for layer, chunk in enumerate((one, two)):
                for part in range(2):
                    for rank, inner, outer in pieces:
                        grads[4][layer, part, :, pl.ds(outer, each)] = chunk[
                            rank, :, pl.ds(part * mine + inner, each)
                        ]
            grads[5][0] = down_one[...]
            grads[5][1] = down_two[...]
            lanes = lax.broadcasted_iota(jnp.int32, (1, LINE), 1)
            scalars = extra[...]
            for place in range(self.scalars + 1, self.lines * self.devices):
                self.line(sums, place)[...] = jnp.zeros((1, LINE), jnp.float32)
            for number, (which, index, rows, columns, begin, line) in enumerate(self.matrices):
                by_row = jnp.zeros((rows, LINE), jnp.float32)
                norm = jnp.zeros((1, LINE), jnp.float32)
                for strip in range(columns // LINE):
                    place = pl.ds(strip * LINE, LINE)
                    grad = grads[which][index + (slice(None), place)]
                    squares = grad * grad + SQUARE_FLOOR
                    by_row = by_row + squares
                    self.line(sums, line + strip)[...] = jnp.sum(squares, axis=0, keepdims=True)
                    weight = weights[which][index + (slice(None), place)]
                    norm = norm + jnp.sum(weight * weight, axis=0, keepdims=True)
                by_row = jnp.sum(by_row, axis=1, keepdims=True)
                norm = jnp.sum(norm, axis=1, keepdims=True)
                fresh = DECAY_RATE * states[pl.ds(begin, rows)] + (1.0 - DECAY_RATE) * (
                    by_row / columns
                )
                rows_new[pl.ds(begin, rows)] = fresh
                inverse = jnp.broadcast_to(1.0 / fresh, (rows, LINE))
                for strip in range(columns // LINE):
                    grad = grads[which][index + (slice(None), pl.ds(strip * LINE, LINE))]
                    self.line(sums, self.weighted + line + strip)[...] = jnp.sum(
                        grad * grad * inverse, axis=0, keepdims=True
                    )
                scalars = jnp.where(
                    lanes == number, jnp.sum(fresh, axis=0, keepdims=True), scalars
                )
                scalars = jnp.where(lanes == 16 + number, norm, scalars)
            self.line(sums, self.scalars)[...] = scalars

        results = self.natural() + [
            jax.ShapeDtypeStruct((self.rows, 1), jnp.float32),
            jax.ShapeDtypeStruct(self.sums, jnp.float32),
        ]
        return local_call(
            kernel, "step_first", results, tuple(traded) + tuple(self.weights) + (row_states, extra)
        )

    def second(self, grads, rows_new, sums, col_states):
        def kernel(*refs):
            grads, (rows_new, sums), refs = refs[:6], refs[6:8], refs[8:]
            states, weights, cols_out, outs = refs[:6], refs[6:12], refs[12:18], refs[18:]
            scalars = self.line(sums, self.scalars)[...]
            for number, (which, index, rows, columns, begin, line) in enumerate(self.matrices):
                strips = [
                    index + (slice(None), pl.ds(strip * LINE, LINE))
                    for strip in range(columns // LINE)
                ]
                norm = jnp.zeros((1, LINE), jnp.float32)
                for strip, spot in enumerate(strips):
                    cols_new = DECAY_RATE * states[which][spot] + (1.0 - DECAY_RATE) * (
                        self.line(sums, line + strip)[...] / (rows * self.devices)
                    )
                    cols_out[which][spot] = cols_new
                    norm = norm + self.line(sums, self.weighted + line + strip)[...] / cols_new
                count = rows * self.devices * columns
                mean_rows = scalars[:, number : number + 1] / (rows * self.devices)
                squares = mean_rows * jnp.sum(norm, axis=1, keepdims=True)
                divisor = jnp.maximum(1.0, jnp.sqrt(squares / count) / CLIP_LEVEL)
                rate = STEP_SCALE * jnp.maximum(
                    RATE_FLOOR, jnp.sqrt(scalars[:, 16 + number : 17 + number] / count)
                )
                scale = (rate / divisor) * jnp.sqrt(mean_rows)
                by_row = jnp.broadcast_to(
                    scale * lax.rsqrt(rows_new[pl.ds(begin, rows)]), (rows, LINE)
                )
                for spot in strips:
                    outs[which][spot] = weights[which][spot] - grads[which][spot] * (
                        by_row * lax.rsqrt(cols_out[which][spot])
                    )

        results = self.columns() + self.natural()
        outs = local_call(
            kernel,
            "step_second",
            results,
            tuple(grads) + (rows_new, sums) + tuple(col_states) + tuple(self.weights),
        )
        return outs[:6], outs[6:]


def moved_to_rank(shard):
    seq, dp = lax.axis_size("seq"), lax.axis_size("dp")
    pairs = [(block, (block % dp) * seq + block // dp) for block in range(seq * dp)]
    return lax.ppermute(shard, ("dp", "seq"), pairs)


def moved_to_owner(shard):
    seq, dp = lax.axis_size("seq"), lax.axis_size("dp")
    pairs = [((block % dp) * seq + block // dp, block) for block in range(seq * dp)]
    return lax.ppermute(shard, ("dp", "seq"), pairs)


def rows_of(value, like):
    return value.reshape((-1,) + like.shape)


def flat(value):
    return value.reshape(-1, value.shape[-1])


def to_trade(block, split):
    return block.reshape(split.ranks, -1, block.shape[-1])


def body(
    tokens,
    cotangent,
    lengths,
    mix_in,
    mix_in_rows,
    mix_in_cols,
    mix_out,
    mix_out_rows,
    mix_out_cols,
    attn_in,
    attn_in_rows,
    attn_in_cols,
    attn_out,
    attn_out_rows,
    attn_out_cols,
    ffn_in,
    ffn_in_rows,
    ffn_in_cols,
    ffn_out,
    ffn_out_rows,
    ffn_out_cols,
    vectors,
    vectors_moment,
    head_gain,
    head_moment,
):
    rows_here, width = tokens.shape
    seq_count = lax.axis_size("seq")
    devices = lax.axis_size("dp") * seq_count
    here = lax.axis_index("seq")
    courier = Courier()
    near, wide = Split(False), Split(True)
    total_rows = rows_here * seq_count
    positions = doc_layout(lengths[0], jnp.arange(total_rows, dtype=jnp.int32))[1]
    positions = positions[:, None]
    cosine, sine = turns_for(positions)
    channels = width // seq_count
    heads = HQ // seq_count
    kv_heads = KVH // seq_count
    kv_width = KVH * HEAD

    form = Heads(heads, kv_heads)
    head_gains = to_low(head_gain).astype(jnp.float32)
    gain_row = jnp.concatenate(
        [head_gains[0]] * heads + [head_gains[1]] * kv_heads + [jnp.ones(kv_heads * HEAD)]
    )[None]
    attn_widths = (width, kv_width, kv_width)
    (
        mix_chunk,
        attn_chunk,
        one_chunk,
        two_chunk,
        low_mix_out,
        attn_out_chunk,
        low_down_one,
        low_down_two,
        vector_block,
    ) = lowered_chunks(
        near, wide, attn_widths, mix_in, mix_out, attn_in, attn_out, ffn_in, ffn_out, vectors
    )
    attn_out_chunk = moved_to_rank(attn_out_chunk)
    mix_traded, gathered, attn_traded, one_traded, two_traded = courier(
        Trade(near, mix_chunk),
        Everyone(vector_block),
        Trade(near, attn_chunk),
        Trade(wide, one_chunk),
        Trade(wide, two_chunk),
    )
    gains = gathered.reshape(devices, 16, 128)[:, : vectors.shape[0], : vectors.shape[1]]
    gains = jnp.moveaxis(gains, 0, 1).reshape(-1, width).astype(jnp.float32)
    inputs = tokens.astype(jnp.float32)
    low_one, scale_one = normalize(inputs, gains[0])
    cotangent_all, *near_weights = courier(
        GatherTokens(wide, cotangent),
        GatherWeights(near, flat(mix_traded), 4),
        GatherWeights(near, low_mix_out),
    )
    w_mix_in, w_mix_out = (flat(value) for value in near_weights)
    taps = lax.dynamic_index_in_dim(
        gains[4:7].reshape(3, -1, seq_count, width // devices), here, 2, keepdims=False
    ).reshape(3, channels)

    taps = jnp.pad(taps, ((0, 5), (0, 0)))
    added, *mix_kept, w_in_one, w_down_one = courier(
        MixForward(near, to_low(low_one), w_mix_in, w_mix_out, taps, positions),
        GatherWeights(wide, flat(one_traded), 8, True),
        GatherWeights(wide, low_down_one, 3),
    )
    w_down_one = flat(w_down_one)
    first = inputs + added
    w_in_one = flat(w_in_one)
    normed_one, scale_two = normalize(first, gains[1])
    added, rows_one, w_attn_in, w_attn_out = courier(
        FeedForward(wide, to_low(normed_one), None, w_in_one, w_down_one, True),
        GatherWeights(near, flat(attn_traded), 4),
        GatherWeights(near, attn_out_chunk),
    )
    w_attn_in, w_attn_out = flat(w_attn_in), flat(w_attn_out)
    second = first + added

    normed_three, scale_three = normalize(second, gains[2])
    added, *attn_kept, w_in_two, w_down_two = courier(
        AttendForward(
            near, form, to_low(normed_three), w_attn_in, w_attn_out, cosine, sine, gain_row, positions
        ),
        GatherWeights(wide, flat(two_traded), 8, True),
        GatherWeights(wide, low_down_two, 3),
    )
    third = second + added
    w_in_two, w_down_two = flat(w_in_two), flat(w_down_two)
    normed_four, scale_four = normalize(third, gains[3])
    terms_two, grad_normed, grad_in_two, grad_down_two = courier(
        FeedForward(
            wide, to_low(normed_four), cotangent_all, w_in_two, w_down_two, True
        )
    )
    grad_branch, grad_gain_three = normalize_back(
        grad_normed, third, scale_four, gains[3]
    )
    grad_third = cotangent.astype(jnp.float32) + grad_branch
    (
        grad_normed_three,
        grad_attn_in,
        grad_attn_out,
        grad_heads,
        reduced_in_two,
        added,
    ) = courier(
        AttendBack(
            near,
            form,
            to_low(grad_third),
            w_attn_in,
            w_attn_out,
            cosine,
            sine,
            gain_row,
            positions,
            *attn_kept,
        ),
        ReduceWeights(wide, grad_in_two, 8, True),
        ScatterTokens(wide, terms_two),
    )
    fourth = third + added
    grad_heads = grad_heads[0].reshape(-1, HEAD)
    grad_head_q = jnp.sum(grad_heads[:heads], axis=0)
    grad_head_k = jnp.sum(grad_heads[heads : heads + kv_heads], axis=0)
    grad_branch_three, grad_gain_two = normalize_back(
        grad_normed_three, second, scale_three, gains[2]
    )
    grad_second = grad_third + grad_branch_three
    (
        grad_normed,
        grad_in_one,
        grad_down_one,
        reduced_down_two,
        reduced_attn_in,
        reduced_attn_out,
    ) = courier(
        FeedForward(wide, rows_one, to_low(grad_second), w_in_one, w_down_one, False),
        ReduceWeights(wide, grad_down_two, 6),
        ReduceWeights(near, grad_attn_in, 2),
        ReduceWeights(near, grad_attn_out),
    )
    grad_branch, grad_gain_one = normalize_back(
        grad_normed, first, scale_two, gains[1]
    )
    grad_first = grad_second + grad_branch
    mix_job = MixBack(near, to_low(grad_first), w_mix_in, w_mix_out, taps, positions, *mix_kept)
    one_job = ReduceWeights(wide, grad_in_one, 8, True)
    (
        grad_normed_one,
        grad_mix_in,
        grad_mix_out,
        tap_grads,
        reduced_down_one,
        _,
        two_back,
        attn_back,
        reduced_mix_in,
        one_back,
    ) = courier(
        mix_job,
        ReduceWeights(wide, grad_down_one, 6),
        one_job,
        Trade(wide, to_trade(reduced_in_two, wide)).later(20.0),
        Trade(near, to_trade(reduced_attn_in, near)).later(60.0),
        ReduceWeights(near, jax.ShapeDtypeStruct(w_mix_in.shape, jnp.float32), 4, of=(mix_job, 1)).later(70.0),
        TradeOf(wide, one_job).later(90.0),
    )
    tap_grads = tap_grads[:3]
    grad_branch_zero, grad_gain_zero = normalize_back(
        grad_normed_one, inputs, scale_one, gains[0]
    )
    token_grad = grad_first + grad_branch_zero

    gain_grads = jnp.stack([grad_gain_zero, grad_gain_one, grad_gain_two, grad_gain_three])
    tap_full = lax.dynamic_update_slice_in_dim(
        jnp.zeros((3, lax.axis_size("dp"), seq_count, width // devices), jnp.float32),
        tap_grads.reshape(3, lax.axis_size("dp"), 1, width // devices),
        here,
        2,
    ).reshape(3, width)
    early_parts = [
        jnp.concatenate([gain_grads, tap_full], axis=0),
        jnp.stack([grad_head_q, grad_head_k]),
        jnp.sum(vectors * vectors, axis=-1),
    ]
    reduced_mix_out, mix_back, early = courier(
        ReduceWeights(near, grad_mix_out),
        Trade(near, to_trade(reduced_mix_in, near)),
        large_sum(early_parts),
    )
    early = unpacked(early, early_parts)
    vector_norm = early[2]
    index = lax.axis_index("dp") * seq_count + here
    vector_grad = lax.dynamic_slice_in_dim(early[0], index * vectors.shape[1], vectors.shape[1], 1)
    head_grad = early[1]
    vector_moment_new = DECAY_RATE * vectors_moment + (1.0 - DECAY_RATE) * (
        vector_grad * vector_grad + SQUARE_FLOOR
    )
    vector_update = vector_grad * lax.rsqrt(vector_moment_new)
    vector_squares = jnp.sum(vector_update * vector_update, axis=-1)
    extra = jnp.pad(vector_squares[None], ((0, 0), (32, LINE - 32 - vector_squares.shape[0])))

    step = Step((mix_in, mix_out, attn_in, attn_out, ffn_in, ffn_out))
    row_states = (mix_in_rows, mix_out_rows, attn_in_rows, attn_out_rows, ffn_in_rows, ffn_out_rows)
    col_states = (mix_in_cols, mix_out_cols, attn_in_cols, attn_out_cols, ffn_in_cols, ffn_out_cols)
    *grads, rows_new, sums = step.first(
        near,
        wide,
        attn_widths,
        (
            mix_back,
            attn_back,
            one_back,
            two_back,
            reduced_mix_out,
            moved_to_owner(reduced_attn_out),
            reduced_down_one,
            reduced_down_two,
        ),
        jnp.concatenate([state.reshape(-1) for state in row_states])[:, None],
        extra,
    )
    (sums,) = courier(SumAll(sums))
    cols_new, new_weights = step.second(
        grads, rows_new, sums, [state[..., None, :] for state in col_states]
    )
    new_rows, begin = [], 0
    for state in row_states:
        new_rows.append(rows_new[begin : begin + state.size, 0].reshape(state.shape))
        begin += state.size
    vector_sums = sums.reshape(-1, LINE)[step.scalars, 32 : 32 + vector_squares.shape[0]]
    full_width = vectors.shape[-1] * devices
    vector_divisor = jnp.maximum(1.0, jnp.sqrt(vector_sums / full_width) / CLIP_LEVEL)
    vector_rate = STEP_SCALE * jnp.maximum(RATE_FLOOR, jnp.sqrt(vector_norm / full_width))
    vectors_new = vectors - (vector_rate / vector_divisor)[:, None] * vector_update
    head_moment_new = DECAY_RATE * head_moment + (1.0 - DECAY_RATE) * (
        head_grad * head_grad + SQUARE_FLOOR
    )
    head_update = head_grad * lax.rsqrt(head_moment_new)
    head_divisor = jnp.maximum(
        1.0, jnp.sqrt(jnp.mean(head_update * head_update, axis=-1, keepdims=True)) / CLIP_LEVEL
    )
    head_rate = STEP_SCALE * jnp.maximum(
        RATE_FLOOR, jnp.sqrt(jnp.mean(head_gain * head_gain, axis=-1, keepdims=True))
    )
    head_new = head_gain - head_rate / head_divisor * head_update
    outputs = [to_low(fourth), token_grad]
    for index in range(6):
        outputs += [grads[index], new_rows[index], cols_new[index][..., 0, :], new_weights[index]]
    return tuple(
        outputs
        + [vector_grad, vector_moment_new, vectors_new, head_grad, head_moment_new, head_new]
    )


def solution(mesh):
    return jax.shard_map(
        body,
        mesh=mesh,
        in_specs=(
            P(("dp", "seq"), None),
            P(("dp", "seq"), None),
            P("dp", None),
            P(("dp", "seq"), None),
            P(("dp", "seq")),
            P(),
            P(("dp", "seq"), None),
            P(("dp", "seq")),
            P(),
            P(("dp", "seq"), None),
            P(("dp", "seq")),
            P(),
            P(("dp", "seq"), None),
            P(("dp", "seq")),
            P(),
            P(None, None, ("dp", "seq"), None),
            P(None, None, ("dp", "seq")),
            P(),
            P(None, ("dp", "seq"), None),
            P(None, ("dp", "seq")),
            P(),
            P(None, ("dp", "seq")),
            P(None, ("dp", "seq")),
            P(),
            P(),
        ),
        out_specs=(
            P(("dp", "seq"), None),
            P(("dp", "seq"), None),
            P(("dp", "seq"), None),
            P(("dp", "seq")),
            P(),
            P(("dp", "seq"), None),
            P(("dp", "seq"), None),
            P(("dp", "seq")),
            P(),
            P(("dp", "seq"), None),
            P(("dp", "seq"), None),
            P(("dp", "seq")),
            P(),
            P(("dp", "seq"), None),
            P(("dp", "seq"), None),
            P(("dp", "seq")),
            P(),
            P(("dp", "seq"), None),
            P(None, None, ("dp", "seq"), None),
            P(None, None, ("dp", "seq")),
            P(),
            P(None, None, ("dp", "seq"), None),
            P(None, ("dp", "seq"), None),
            P(None, ("dp", "seq")),
            P(),
            P(None, ("dp", "seq"), None),
            P(None, ("dp", "seq")),
            P(None, ("dp", "seq")),
            P(None, ("dp", "seq")),
            P(),
            P(),
            P(),
        ),
        check_vma=False,
    )
```

```python
import math

import jax
import jax.numpy as jnp
from jax import lax
from jax.experimental import pallas as pl
from jax.experimental.pallas import tpu as pltpu
from jax.sharding import PartitionSpec as P

HQ = 16
KVH = 8
HEAD = 64

EPSILON = 1e-05
SQUARE_FLOOR = 1e-30
DECAY_RATE = 0.5
CLIP_LEVEL = 0.25
STEP_SCALE = 1.0
RATE_FLOOR = 0.001
MASKED_SCORE = -1e30


def matmul(operand, weight):
    return jnp.dot(operand, weight, preferred_element_type=jnp.float32)


def contract_first(operand, other):
    return lax.dot_general(
        operand, other, (((0,), (0,)), ((), ())), preferred_element_type=jnp.float32
    )


def contract_last(operand, other):
    return lax.dot_general(
        operand,
        other,
        (((operand.ndim - 1,), (other.ndim - 1,)), ((), ())),
        preferred_element_type=jnp.float32,
    )


def to_low(values):
    return values.astype(jnp.bfloat16)


def normalize(values, gain):
    scale = lax.rsqrt(jnp.mean(values * values, axis=-1, keepdims=True) + EPSILON)
    return (values * scale * gain, scale)


def normalize_back(grad_out, values, scale, gain):
    unit = values * scale
    grad_gain = jnp.sum(grad_out * unit, axis=tuple(range(values.ndim - 1)))
    weighted = grad_out * gain
    grad_values = scale * (weighted - unit * jnp.mean(weighted * unit, axis=-1, keepdims=True))
    return (grad_values, grad_gain)


def doc_layout(lens, places):
    bounds = jnp.cumsum(lens)
    passed = bounds[None, :] <= places[:, None]
    docs = jnp.sum(passed.astype(jnp.int32), axis=1)
    starts = jnp.sum(jnp.where(passed, lens[None, :], 0), axis=1)
    return (docs, places - starts)


def turns_for(positions):
    lane = jnp.arange(LANES, dtype=jnp.int32) % HEAD
    pair = (lane % (HEAD // 2)).astype(jnp.float32)
    freqs = jnp.exp(pair * (-2.0 * math.log(1000000.0) / HEAD))
    angles = positions.astype(jnp.float32) * freqs[None, :]
    sign = jnp.where(lane < HEAD // 2, -1.0, 1.0)
    return (jnp.cos(angles), jnp.sin(angles) * sign[None, :])


def bits_of(axis):
    return lax.axis_size(axis).bit_length() - 1


def flipped(value, mask):
    for bit in range(mask.bit_length()):
        if (mask >> bit) & 1:
            value = value + (1 - 2 * ((value // (1 << bit)) % 2)) * (1 << bit)
    return value


def spread(bits):
    masks = [0]
    for bit in bits:
        masks = masks + [mask | (1 << bit) for mask in masks]
    return masks


class Split:
    def __init__(self, with_z):
        dp_bits = bits_of("dp")
        x_bits = dp_bits // 2
        self.shared = [x_bits] if with_z else []
        self.x_bits = list(range(x_bits))
        self.z_bits = [bit for bit in range(x_bits, dp_bits) if bit not in self.shared]
        self.free = self.x_bits + self.z_bits
        self.seq_bits = bits_of("seq")
        self.ranks = 1 << (self.seq_bits + len(self.shared))
        self.copies = 1 << len(self.free)
        self.links = [
            (dp_mask, seq_mask)
            for dp_mask in spread(self.shared)
            for seq_mask in spread(range(1, self.seq_bits))
        ]
        self.peers = [
            (dp_mask, seq_mask)
            for dp_mask in spread(self.shared)
            for seq_mask in range(1 << self.seq_bits)
        ]

    def pick(self, value, bits):
        out = 0
        for place, bit in enumerate(bits):
            out = out + ((value // (1 << bit)) % 2) * (1 << place)
        return out

    def rank(self, dp, seq):
        return self.pick(dp, self.shared) * (1 << self.seq_bits) + seq

    def copy(self, dp):
        return self.pick(dp, self.free)

    def row_of(self, dp, piece, pieces, depth):
        per = pieces // (1 << len(self.shared))
        place = piece // per
        for number, bit in enumerate(self.shared):
            own = (dp // (1 << bit)) % 2
            dp = dp + ((place >> number) % 2 - own) * (1 << bit)
        return dp * (per * depth) + (piece % per) * depth

    def owner_order(self):
        return sorted(
            range(lax.axis_size("dp")),
            key=lambda dp: (self.pick(dp, self.free), self.pick(dp, self.shared)),
        )


MESH = pl.DeviceIdType.MESH


class Job:
    scratch = ()
    copies = 0
    locals = 0
    out_in_vmem = False
    in_vmem = ()
    given_in_vmem = ()
    bulk = False
    works = False
    begin = 0.0

    def later(self, begin):
        self.begin = begin
        return self

    def span(self):
        return 10.0

    def steps(self):
        return 0

    def last_steps(self):
        return 0

    def bind(self, operands, outs, scratch, send, recv, local):
        self.ins, self.outs, self.held = operands, outs, scratch
        self.send, self.recv, self.local = send, recv, local
        self.dp, self.seq = lax.axis_index("dp"), lax.axis_index("seq")

    def away(self, number, source, target, mask):
        return pltpu.make_async_remote_copy(
            src_ref=source,
            dst_ref=target,
            send_sem=self.send.at[number],
            recv_sem=self.recv.at[number],
            device_id=(flipped(self.dp, mask[0]), flipped(self.seq, mask[1])),
            device_id_type=MESH,
        )

    def near(self, number, source, target):
        return pltpu.make_async_copy(source, target, self.local.at[number])

    def start(self):
        pass

    def middle(self):
        return iter(())

    def finish(self):
        pass


class Spread:
    def __init__(self, job, source, slots, local):
        self.job, self.source, self.slots = job, source, slots
        links = job.split.links
        self.half = job.rows // 2
        self.mine = job.near(local, source, slots.at[0, 0])
        self.mine.start()
        self.direct, self.hops, self.beside, self.sent = {}, {}, {}, []
        self.done = set()
        number = 0
        for chip in range(1, job.chips):
            if links[chip][0] and links[chip][1]:
                self.hops[chip] = (number, number + 1)
                number += 2
                continue
            copy = job.away(number, source, slots.at[0, chip], links[chip])
            copy.start()
            self.direct[chip] = copy
            self.sent.append(copy)
            number += 1
        self.first = number
        self.send_beside(0, source)

    @staticmethod
    def copies(split):
        both = sum(1 for dp_mask, seq_mask in split.links if dp_mask and seq_mask)
        return 2 * len(split.links) - 1 + both

    def part(self, chip, number):
        return self.slots.at[0, chip, pl.ds(number * self.half, self.half)]

    def send_beside(self, chip, source):
        copy = self.job.away(self.first + chip, source, self.slots.at[1, chip], (0, 1))
        copy.start()
        self.beside[chip] = copy

    def pass_on(self, chip):
        links = self.job.split.links
        for far, numbers in self.hops.items():
            dp_mask, seq_mask = links[far]
            for which, (via, onward) in enumerate(
                (((0, seq_mask), (dp_mask, 0)), ((dp_mask, 0), (0, seq_mask)))
            ):
                if via == links[chip]:
                    copy = self.job.away(
                        numbers[which], self.part(chip, which), self.part(far, which), onward
                    )
                    copy.start()
                    self.sent.append(copy)

    def ready(self, core, chip):
        links = self.job.split.links
        if core:
            self.beside[chip].wait_recv()
            return
        if chip in self.done:
            return
        self.done.add(chip)
        if chip == 0:
            self.mine.wait()
            return
        if chip in self.direct:
            self.direct[chip].wait_recv()
            self.pass_on(chip)
        else:
            for which, number in enumerate(self.hops[chip]):
                onward = ((links[chip][0], 0), (0, links[chip][1]))[which]
                part = self.part(chip, which)
                self.job.away(number, part, part, onward).wait_recv()
        self.send_beside(chip, self.slots.at[0, chip])

    def finish(self):
        for copy in self.sent + list(self.beside.values()):
            copy.wait_send()


class GatherTokens(Job):
    def __init__(self, split, value):
        self.split = split
        self.operands = (value,)
        self.chips = len(split.links)
        self.results = (jax.ShapeDtypeStruct((2, self.chips) + value.shape, value.dtype),)
        self.masks = [mask for mask in split.links[1:]] + [(0, 1)]
        self.rows = value.shape[0]
        self.copies = Spread.copies(split)
        self.locals = 1

    def span(self):
        return 13.0 if self.chips == 2 else 26.0

    def steps(self):
        return self.chips

    def start(self):
        self.arrive = Spread(self, self.ins[0], self.outs[0], 0)

    def middle(self):
        for chip in range(self.chips):
            self.arrive.ready(0, chip)
            yield True

    def finish(self):
        for chip in range(self.chips):
            self.arrive.ready(1, chip)
        self.arrive.finish()


STRIP = 32
AHEAD = 2
STRETCH = 1.0


class ScatterTokens(Job):
    out_in_vmem = True

    def span(self):
        return 3.0 * self.chips

    def steps(self):
        return self.chips - 1

    def __init__(self, split, partial):
        self.split = split
        rows, width = partial.shape[-2:]
        self.chips = len(split.links)
        self.operands = (partial.reshape(2, self.chips, rows, width),)
        self.results = (jax.ShapeDtypeStruct((rows, width), jnp.float32),)
        self.masks = [mask for mask in split.links[1:]] + [(0, 1)]
        self.copies = 2 * self.chips - 1
        self.locals = self.chips
        self.scratch = (
            pltpu.VMEM((self.chips, rows, width), jnp.float32),
            pltpu.VMEM((2, rows, width), jnp.float32),
            pltpu.VMEM((2, rows, width), jnp.bfloat16),
            pltpu.VMEM((max(1, self.chips - 1), rows, width), jnp.bfloat16),
        )
        self.rows = rows

    def start(self):
        partial = self.ins[0]
        theirs = self.held[0]
        self.order = list(range(1, self.chips)) + [0]
        self.beside, self.loads = {}, {}
        for chip in self.order:
            self.beside[chip] = self.away(
                self.chips - 1 + chip, partial.at[1, chip], theirs.at[chip], (0, 1)
            )
            self.beside[chip].start()
        self.load(0)
        self.load(1)

    def load(self, index):
        if index < self.chips:
            chip = self.order[index]
            self.loads[chip] = self.near(
                chip, self.ins[0].at[0, chip], self.held[1].at[index % 2]
            )
            self.loads[chip].start()

    def strips(self, update):
        @pl.loop(0, self.rows // STRIP)
        def _(strip):
            update(pl.ds(pl.multiple_of(strip * STRIP, STRIP), STRIP))

    def middle(self):
        theirs, mine, sent, landed = self.held
        self.far = []
        for index, chip in enumerate(self.order[:-1]):
            self.beside[chip].wait_recv()
            self.loads[chip].wait()
            if index >= 2:
                self.far[index - 2].wait_send()

            def update(rows, index=index, chip=chip):
                sent[index % 2, rows] = to_low(theirs[chip, rows] + mine[index % 2, rows])

            self.strips(update)
            self.load(index + 2)
            copy = self.away(
                chip - 1, sent.at[index % 2], landed.at[chip - 1], self.split.links[chip]
            )
            copy.start()
            self.far.append(copy)
            yield True

    def finish(self):
        theirs, mine, _, landed = self.held
        out = self.outs[0]
        self.beside[0].wait_recv()
        self.loads[0].wait()
        for copy in self.far:
            copy.wait_recv()
        last = (self.chips - 1) % 2

        def update(rows):
            value = theirs[0, rows] + mine[last, rows]
            for chip in range(1, self.chips):
                value = value + landed[chip - 1, rows].astype(jnp.float32)
            out[rows] = value

        self.strips(update)
        for copy in self.far[-2:]:
            copy.wait_send()
        for copy in self.beside.values():
            copy.wait_send()


class Trade(Job):
    def __init__(self, split, value):
        self.split = split
        self.operands = (value,)
        self.results = (jax.ShapeDtypeStruct(value.shape, value.dtype),)
        self.masks = split.peers[1:]
        self.copies = len(self.masks)
        self.locals = 1

    def start(self):
        given, out = self.ins[0], self.outs[0]
        rank = self.split.rank(self.dp, self.seq)
        self.mine = self.near(0, given.at[rank], out.at[rank])
        self.mine.start()
        self.far = []
        for number, mask in enumerate(self.masks):
            other = self.split.rank(flipped(self.dp, mask[0]), flipped(self.seq, mask[1]))
            copy = self.away(number, given.at[other], out.at[rank], mask)
            copy.start()
            self.far.append(copy)

    def finish(self):
        self.mine.wait()
        for copy in self.far:
            copy.wait()


def pieces_of(rows, most, tile):
    for count in range(most, 1, -1):
        if rows % (count * tile) == 0:
            return count
    return 1


class TradeOf(Trade):
    def __init__(self, split, job):
        rows, columns = job.results[0].shape
        self.split, self.job = split, job
        self.depth = rows // split.ranks
        self.operands = ()
        self.results = (
            jax.ShapeDtypeStruct((split.ranks, self.depth, columns), jnp.float32),
        )
        self.masks = split.peers[1:]
        self.copies = len(self.masks)
        self.locals = 1

    def given(self, rank):
        row = pl.multiple_of(rank * self.depth, self.depth)
        return self.job.outs[0].at[pl.ds(row, self.depth)]

    def start(self):
        out = self.outs[0]
        rank = self.split.rank(self.dp, self.seq)
        self.mine = self.near(0, self.given(rank), out.at[rank])
        self.mine.start()
        self.far = []
        for number, mask in enumerate(self.masks):
            other = self.split.rank(flipped(self.dp, mask[0]), flipped(self.seq, mask[1]))
            copy = self.away(number, self.given(other), out.at[rank], mask)
            copy.start()
            self.far.append(copy)


class GatherWeights(Job):
    bulk = True

    def span(self):
        return self.operands[0].size * len(self.z_masks) * len(self.x_masks) * 2.4e-5

    def steps(self):
        return self.count

    def __init__(self, split, value, most=1, across=False):
        self.split = split
        self.operands = (value,)
        self.across = across and bool(split.shared)
        rows, columns = value.shape
        shape = (split.copies * rows, columns) if self.across else (split.copies, rows, columns)
        self.results = (jax.ShapeDtypeStruct(shape, value.dtype),)
        self.z_masks = spread(split.z_bits)
        self.x_masks = spread(split.x_bits)
        self.masks = [(mask, 0) for mask in self.z_masks[1:] + self.x_masks[1:]]
        self.count = pieces_of(rows, most, 16)
        self.depth = rows // self.count
        self.copies = (len(self.z_masks) * len(self.x_masks) - 1) * self.count
        self.locals = self.count

    def part(self, ref, piece):
        return ref if self.count == 1 else ref.at[pl.ds(piece * self.depth, self.depth)]

    def slot(self, mask, piece):
        dp = flipped(self.dp, mask)
        if not self.across:
            return self.part(self.outs[0].at[self.split.copy(dp)], piece)
        row = self.split.row_of(dp, piece, self.count, self.depth)
        return self.outs[0].at[pl.ds(pl.multiple_of(row, self.depth), self.depth)]

    def start(self):
        own = self.ins[0]
        self.mine = [
            self.near(piece, self.part(own, piece), self.slot(0, piece))
            for piece in range(self.count)
        ]
        for copy in self.mine:
            copy.start()
        self.number = 0
        self.sent, self.arrivals, self.rest = [], {}, []
        for piece in range(min(AHEAD, self.count)):
            self.send_z(piece)

    def source(self, mask, piece):
        return self.slot(mask, piece) if mask else self.part(self.ins[0], piece)

    def send_z(self, piece):
        for bit in self.split.z_bits:
            self.hop(0, piece, 1 << bit)

    def hop(self, mask, piece, onward):
        source = self.source(mask, piece)
        copy = self.away(self.number, source, self.slot(mask, piece), (onward, 0))
        copy.start()
        self.sent.append(copy)
        self.arrivals[mask | onward, piece] = self.away(
            self.number, source, self.slot(mask | onward, piece), (onward, 0)
        )
        self.number += 1

    def pass_on(self, from_mask, piece):
        source = self.source(from_mask, piece)
        for mask in self.x_masks[1:]:
            copy = self.away(self.number, source, self.slot(from_mask, piece), (mask, 0))
            copy.start()
            self.sent.append(copy)
            self.rest.append(
                self.away(self.number, source, self.slot(from_mask ^ mask, piece), (mask, 0))
            )
            self.number += 1

    def take(self, masks, piece):
        for mask in masks:
            self.arrivals[mask, piece].wait_recv()
            for bit in self.split.z_bits:
                if (1 << bit) < (mask & -mask):
                    self.hop(mask, piece, 1 << bit)
            self.pass_on(mask, piece)

    def middle(self):
        single = [mask for mask in self.z_masks[1:] if mask & (mask - 1) == 0]
        longer = [mask for mask in self.z_masks[1:] if mask & (mask - 1)]
        for piece in range(self.count):
            self.pass_on(0, piece)
            self.take(single, piece)
            if piece:
                self.take(longer, piece - 1)
            if piece + AHEAD < self.count:
                self.send_z(piece + AHEAD)
            yield True
        self.take(longer, self.count - 1)

    def finish(self):
        for copy in self.mine:
            copy.wait()
        for arrival in self.rest:
            arrival.wait_recv()
        for copy in self.sent:
            copy.wait_send()


class ReduceWeights(Job):
    out_in_vmem = True
    bulk = True

    def span(self):
        return self.size * 4.5e-5

    def steps(self):
        return len(self.units)

    def last_steps(self):
        return self.count

    def __init__(self, split, grad, most=1, across=False, of=None):
        self.split = split
        self.across = across and bool(split.shared)
        shape = (grad.shape[0] // split.copies, grad.shape[1])
        self.of = of
        if of is not None:
            self.operands = ()
        elif self.across:
            self.operands = (grad,)
        else:
            self.operands = (grad.reshape((split.copies,) + shape),)
        self.size = grad.shape[0] * grad.shape[1]
        self.results = (jax.ShapeDtypeStruct(shape, jnp.float32),)
        self.z_masks = spread(split.z_bits)
        self.x_masks = spread(split.x_bits)
        self.masks = [(mask, 0) for mask in self.z_masks[1:] + self.x_masks[1:]]
        self.count = pieces_of(shape[0], most, 8)
        self.depth = shape[0] // self.count
        far_z, far_x = len(self.z_masks) - 1, len(self.x_masks) - 1
        order = sorted(
            range(far_z + 1), key=lambda place: self.low_bit(place) or 1 << 30
        )
        stages = {}
        for place in order:
            stages.setdefault(self.low_bit(place), []).append(place)
        self.units = [
            (piece, place)
            for places in stages.values()
            for piece in range(self.count)
            for place in places
        ]
        self.copies = self.count * (far_z + (far_z + 1) * far_x)
        self.locals = len(self.units)
        self.scratch = (
            pltpu.VMEM((far_x, far_z + 1) + shape, jnp.float32),
            pltpu.VMEM((far_z + 1,) + shape, jnp.float32),
            pltpu.VMEM((far_z,) + shape, jnp.float32),
        )

    def low_bit(self, place):
        return self.z_masks[place] & -self.z_masks[place]

    def children(self, place):
        mask, low = self.z_masks[place], self.low_bit(place) or 1 << 30
        return [
            self.z_masks.index(mask | 1 << bit) for bit in self.split.z_bits if 1 << bit < low
        ]

    def rows(self, piece):
        return pl.ds(piece * self.depth, self.depth)

    def part(self, mask, piece):
        dp = flipped(self.dp, mask)
        if self.of is not None:
            job, number = self.of
            row = (self.split.copy(dp) * self.count + piece) * self.depth
            return job.outs[number].at[pl.ds(pl.multiple_of(row, self.depth), self.depth)]
        if not self.across:
            return self.ins[0].at[self.split.copy(dp), self.rows(piece)]
        row = self.split.row_of(dp, piece, self.count, self.depth)
        return self.ins[0].at[pl.ds(pl.multiple_of(row, self.depth), self.depth)]

    def start(self):
        self.number = 0
        self.sent, self.loads, self.far = {}, {}, {}
        for index in range(min(AHEAD, len(self.units))):
            self.send_x(index)

    def send_x(self, index):
        piece, place = self.units[index]
        mask = self.z_masks[place]
        by_x, mine, _ = self.held
        copies = []
        for number, x_mask in enumerate(self.x_masks[1:]):
            copy = self.away(
                self.number,
                self.part(mask ^ x_mask, piece),
                by_x.at[number, place, self.rows(piece)],
                (x_mask, 0),
            )
            copy.start()
            copies.append(copy)
            self.number += 1
        self.sent[index] = copies
        load = self.near(index, self.part(mask, piece), mine.at[place, self.rows(piece)])
        load.start()
        self.loads[index] = load

    def strips(self, piece, update):
        step = 8
        for size in (64, 32, 16):
            if self.depth % size == 0:
                step = size
                break

        @pl.loop(0, self.depth // step)
        def _(strip):
            update(pl.ds(pl.multiple_of(piece * self.depth + strip * step, 8), step))

    def middle(self):
        by_x, mine, by_z = self.held
        for index, (piece, place) in enumerate(self.units):
            self.loads[index].wait()
            for copy in self.sent[index]:
                copy.wait_recv()
            if index + AHEAD < len(self.units):
                self.send_x(index + AHEAD)

            if not place:
                yield True
                continue
            self.add(piece, place)
            copy = self.away(
                self.number,
                mine.at[place, self.rows(piece)],
                by_z.at[place - 1, self.rows(piece)],
                (self.low_bit(place), 0),
            )
            copy.start()
            self.far[(piece, place)] = copy
            self.number += 1
            yield True
        for piece in range(self.count):
            self.add(piece, 0)
            yield True

    def add(self, piece, place):
        by_x, mine, by_z = self.held
        children = self.children(place)
        for child in children:
            self.far[(piece, child)].wait_recv()
        target = mine.at[place] if place else self.outs[0]

        def update(rows):
            value = mine[place, rows]
            for number in range(len(self.x_masks) - 1):
                value = value + by_x[number, place, rows]
            for child in children:
                value = value + by_z[child - 1, rows]
            target[rows] = value

        self.strips(piece, update)

    def finish(self):
        for copy in self.far.values():
            copy.wait_send()
        for copies in self.sent.values():
            for copy in copies:
                copy.wait_send()


class Return:
    def __init__(self, job, first, scratch, out):
        self.job, self.first, self.out = job, first, out
        self.theirs, self.mine, self.stage, self.sent, self.landed = scratch
        self.beside, self.far = {}, {}

    @staticmethod
    def scratch(chips, rows, width):
        return (
            pltpu.VMEM((chips, rows, width), jnp.float32),
            pltpu.VMEM((2, rows, width), jnp.float32),
            pltpu.VMEM((2, rows, width), jnp.float32),
            pltpu.VMEM((2, rows, width), jnp.bfloat16),
            pltpu.VMEM((max(1, chips - 1), rows, width), jnp.bfloat16),
        )

    def put(self, core, chip, value):
        chips = self.job.chips
        if core == 0:
            self.mine[min(chip, 1)] = value
            return
        order = list(self.beside)
        if len(order) >= 2:
            self.beside[order[-2]].wait_send()
        spot = len(order) % 2
        self.stage[spot] = value
        copy = self.job.away(
            self.first + chips - 1 + chip, self.stage.at[spot], self.theirs.at[chip], (0, 1)
        )
        copy.start()
        self.beside[chip] = copy

    def strips(self, update):
        @pl.loop(0, self.job.rows // STRIP)
        def _(strip):
            update(pl.ds(pl.multiple_of(strip * STRIP, STRIP), STRIP))

    def pass_on(self, chip):
        if chip == 0:
            return
        self.beside[chip].wait_recv()
        order = list(self.far)
        if len(order) >= 2:
            self.far[order[-2]].wait_send()
        spot = len(order) % 2

        def update(rows):
            self.sent[spot, rows] = to_low(self.theirs[chip, rows] + self.mine[1, rows])

        self.strips(update)
        copy = self.job.away(
            self.first + chip - 1,
            self.sent.at[spot],
            self.landed.at[chip - 1],
            self.job.split.links[chip],
        )
        copy.start()
        self.far[chip] = copy

    def finish(self):
        chips = self.job.chips
        self.beside[0].wait_recv()
        for chip in range(1, chips):
            self.far[chip].wait_recv()

        def update(rows):
            value = self.theirs[0, rows] + self.mine[0, rows]
            for chip in range(1, chips):
                value = value + self.landed[chip - 1, rows].astype(jnp.float32)
            self.out[rows] = value

        self.strips(update)
        for chip in list(self.beside)[-2:]:
            self.beside[chip].wait_send()
        for chip in list(self.far)[-2:]:
            self.far[chip].wait_send()


class Layer(Job):
    works = True
    work_steps = 0
    after_steps = 0
    length = 35.0

    def span(self):
        return self.length

    def steps(self):
        return 3 * self.chips + 2 * self.chips * (self.work_steps + self.after_steps) + 2

    def __init__(self, split, own, others, results, scratch=()):
        self.split = split
        self.chips = len(split.links)
        self.rows, self.width = own.shape
        self.total = 2 * self.chips * self.rows
        self.operands = (own,) + tuple(others)
        self.given_in_vmem = (False,) + (True,) * len(others)
        slots = (2, self.chips, self.rows, self.width)
        self.results = (jax.ShapeDtypeStruct((self.rows, self.width), jnp.float32),) + tuple(results)
        self.in_vmem = (True,) * len(self.results)
        self.scratch = (
            (pltpu.VMEM(slots, jnp.bfloat16),)
            + Return.scratch(self.chips, self.rows, self.width)
            + tuple(scratch)
        )
        self.masks = [mask for mask in split.links[1:]] + [(0, 1)]
        self.copies = Spread.copies(split) + 2 * self.chips - 1
        self.locals = 2
        self.places = [(core, chip) for chip in range(self.chips) for core in (0, 1)]

    def start(self):
        self.slots = self.held[0]
        self.back = Return(self, Spread.copies(self.split), self.held[1:6], self.outs[0])
        self.more = self.held[6:]
        self.arrive = Spread(self, self.ins[0], self.slots, 0)

    def at(self, core, chip):
        place = flipped(self.seq, 2 * chip + core)
        return pl.ds(pl.multiple_of(place * self.rows, self.rows), self.rows)

    def middle(self):
        self.open()
        for core, chip in self.places:
            self.arrive.ready(core, chip)
            self.take(core, chip)
            yield True
        yield from self.work()
        for chip in list(range(1, self.chips)) + [0]:
            for core in (1, 0):
                self.back.put(core, chip, self.give(core, chip))
            yield True
            self.back.pass_on(chip)
        yield from self.after()

    def open(self):
        pass

    def work(self):
        return iter(())

    def after(self):
        return iter(())

    def finish(self):
        self.back.finish()
        self.arrive.finish()


def turned(value, steps):
    return pltpu.roll(value, steps % value.shape[0], 0)


def within(positions):
    places = positions[...]
    return jnp.where(places >= 1, 1.0, 0.0), jnp.where(places >= 2, 1.0, 0.0)


class MixForward(Layer):
    def __init__(self, split, own, w_in, w_out, taps, positions):
        rows = 2 * len(split.links) * own.shape[0]
        channels = w_out.shape[0]
        super().__init__(
            split,
            own,
            (w_in, w_out, taps, positions),
            (
                jax.ShapeDtypeStruct((2, len(split.links)) + own.shape, jnp.bfloat16),
                jax.ShapeDtypeStruct((rows, 3 * channels), jnp.float32),
                jax.ShapeDtypeStruct((rows, channels), jnp.float32),
                jax.ShapeDtypeStruct((rows, channels), jnp.bfloat16),
            ),
        )
        self.channels = channels

    def open(self):
        _, self.w_in, self.w_out, self.taps, self.positions = self.ins
        _, self.kept, self.projected, self.conv, self.gated = self.outs

    def take(self, core, chip):
        value = self.slots[core, chip]
        self.kept[core, chip] = value
        self.projected[self.at(core, chip)] = matmul(value, self.w_in[...])

    def work(self):
        each = self.channels
        mixed = to_low(self.projected[:, :each] * self.projected[:, 2 * each :]).astype(jnp.float32)
        once, twice = within(self.positions)
        conv = (
            self.taps[2:3] * mixed
            + self.taps[1:2] * turned(mixed, 1) * once
            + self.taps[0:1] * turned(mixed, 2) * twice
        )
        self.conv[...] = conv
        self.gated[...] = to_low(self.projected[:, each : 2 * each] * conv)
        yield True

    def give(self, core, chip):
        return matmul(self.gated[self.at(core, chip)], self.w_out[...])


class MixBack(Layer):
    after_steps = 1

    def __init__(self, split, own, w_in, w_out, taps, positions, kept, projected, conv, gated):
        rows = 2 * len(split.links) * own.shape[0]
        channels = w_out.shape[0]
        super().__init__(
            split,
            own,
            (w_in, w_out, taps, positions, kept, projected, conv, gated),
            (
                jax.ShapeDtypeStruct(w_in.shape, jnp.float32),
                jax.ShapeDtypeStruct(w_out.shape, jnp.float32),
                jax.ShapeDtypeStruct(taps.shape, jnp.float32),
            ),
            (
                pltpu.VMEM((rows, channels), jnp.float32),
                pltpu.VMEM((rows, 3 * channels), jnp.bfloat16),
            ),
        )
        self.channels = channels

    def open(self):
        _, self.w_in, self.w_out, self.taps, self.positions = self.ins[:5]
        self.kept, self.projected, self.conv, self.gated = self.ins[5:]
        _, self.grad_in, self.grad_out, self.grad_taps = self.outs
        self.grad_gated, self.grad_projected = self.more

    def take(self, core, chip):
        grad = self.slots[core, chip]
        self.grad_gated[self.at(core, chip)] = contract_last(grad, self.w_out[...])
        term = contract_first(self.gated[self.at(core, chip)], grad)
        if (core, chip) == (0, 0):
            self.grad_out[...] = term
        else:
            self.grad_out[...] += term

    def work(self):
        each = self.channels
        part_b = self.projected[:, :each]
        part_c = self.projected[:, each : 2 * each]
        part_v = self.projected[:, 2 * each :]
        once, twice = within(self.positions)
        mixed = to_low(part_b * part_v).astype(jnp.float32)
        grad_gated = self.grad_gated[...]
        grad_conv = grad_gated * part_c
        back_one, back_two = grad_conv * once, grad_conv * twice
        self.grad_taps[...] = jnp.zeros(self.grad_taps.shape, jnp.float32)
        self.grad_taps[0:1] = jnp.sum(back_two * turned(mixed, 2), axis=0, keepdims=True)
        self.grad_taps[1:2] = jnp.sum(back_one * turned(mixed, 1), axis=0, keepdims=True)
        self.grad_taps[2:3] = jnp.sum(grad_conv * mixed, axis=0, keepdims=True)
        grad_mixed = (
            self.taps[2:3] * grad_conv
            + turned(self.taps[1:2] * back_one, -1)
            + turned(self.taps[0:1] * back_two, -2)
        )
        grad_mixed = to_low(grad_mixed).astype(jnp.float32)
        self.grad_projected[:, :each] = to_low(grad_mixed * part_v)
        self.grad_projected[:, each : 2 * each] = to_low(grad_gated * self.conv[...])
        self.grad_projected[:, 2 * each :] = to_low(grad_mixed * part_b)
        yield True

    def give(self, core, chip):
        return contract_last(self.grad_projected[self.at(core, chip)], self.w_in[...])

    def after(self):
        for core, chip in self.places:
            term = contract_first(
                self.kept[core, chip], self.grad_projected[self.at(core, chip)]
            )
            if (core, chip) == (0, 0):
                self.grad_in[...] = term
            else:
                self.grad_in[...] += term
            yield True


LANES = 128


def head_means(value):
    row = lax.broadcasted_iota(jnp.int32, (LANES, LANES), 0) // HEAD
    column = lax.broadcasted_iota(jnp.int32, (LANES, LANES), 1) // HEAD
    same = jnp.where(row == column, 1.0 / HEAD, 0.0)
    return jnp.dot(
        value, same, preferred_element_type=jnp.float32, precision=lax.Precision.HIGHEST
    )


def half_turned(value):
    lane = lax.broadcasted_iota(jnp.int32, value.shape, 1) % HEAD
    ahead = pltpu.roll(value, LANES - HEAD // 2, 1)
    behind = pltpu.roll(value, HEAD // 2, 1)
    return jnp.where(lane < HEAD // 2, ahead, behind)


class Heads:
    def __init__(self, heads, kv_heads):
        self.heads, self.kv_heads = heads, kv_heads
        self.shared = heads // kv_heads
        self.turned = (heads + kv_heads) * HEAD
        self.width = (heads + 2 * kv_heads) * HEAD

    def tiles(self):
        for begin in range(0, self.width, LANES):
            yield slice(begin, begin + LANES), min(LANES, max(0, self.turned - begin))

    def q(self, head):
        return slice(head * HEAD, (head + 1) * HEAD)

    def k(self, head):
        begin = self.heads + head // self.shared
        return slice(begin * HEAD, (begin + 1) * HEAD)

    def v(self, head):
        begin = self.heads + self.kv_heads + head // self.shared
        return slice(begin * HEAD, (begin + 1) * HEAD)

    @staticmethod
    def some(lanes, value, other):
        if lanes == LANES:
            return value
        lane = lax.broadcasted_iota(jnp.int32, value.shape, 1)
        return jnp.where(lane < lanes, value, other)


class AttendForward(Layer):
    work_steps = 1
    length = 42.0

    def __init__(self, split, heads, own, w_in, w_out, cosine, sine, gain, positions):
        rows = 2 * len(split.links) * own.shape[0]
        self.heads = heads
        super().__init__(
            split,
            own,
            (w_in, w_out, cosine, sine, gain, positions),
            (
                jax.ShapeDtypeStruct((2, len(split.links)) + own.shape, jnp.bfloat16),
                jax.ShapeDtypeStruct((rows, heads.width), jnp.float32),
                jax.ShapeDtypeStruct((rows, heads.width), jnp.bfloat16),
                jax.ShapeDtypeStruct((rows, heads.heads * HEAD), jnp.bfloat16),
                jax.ShapeDtypeStruct((rows, heads.heads), jnp.float32),
            ),
        )

    def open(self):
        _, self.w_in, self.w_out, self.cosine, self.sine, self.gain, self.positions = self.ins
        _, self.kept, self.projected, self.turned, self.out, self.lse = self.outs

    def take(self, core, chip):
        value = self.slots[core, chip]
        self.kept[core, chip] = value
        rows = self.at(core, chip)
        projected = matmul(value, self.w_in[...])
        self.projected[rows] = projected
        for lanes, count in self.heads.tiles():
            raw = projected[:, lanes]
            if count:
                unit = raw * lax.rsqrt(head_means(raw * raw) + EPSILON)
                normed = unit * self.gain[:, lanes]
                spun = normed * self.cosine[rows] + half_turned(normed) * self.sine[rows]
                raw = self.heads.some(count, spun, raw)
            self.turned[rows, lanes] = to_low(raw)

    def work(self):
        for place in range(2 * self.chips):
            rows = slice(place * self.rows, (place + 1) * self.rows)
            bias, seen = hidden_scores(self.positions[rows], place, self.rows)
            for head in range(self.heads.heads):
                scores = (
                    contract_last(
                        self.turned[rows, self.heads.q(head)], self.turned[:seen, self.heads.k(head)]
                    )
                    * HEAD ** (-0.5)
                    + bias
                )
                peak = jnp.max(scores, axis=-1, keepdims=True)
                expo = jnp.exp(scores - peak)
                count = jnp.sum(expo, axis=-1, keepdims=True)
                probs = to_low(expo * (1.0 / count))
                self.out[rows, self.heads.q(head)] = to_low(
                    matmul(probs, self.turned[:seen, self.heads.v(head)])
                )
                self.lse[rows, head : head + 1] = peak + jnp.log(count)
            yield True

    def give(self, core, chip):
        return matmul(self.out[self.at(core, chip)], self.w_out[...])


def hidden_scores(positions, place, rows):
    seen = (place + 1) * rows
    row = place * rows + lax.broadcasted_iota(jnp.int32, (rows, seen), 0)
    column = lax.broadcasted_iota(jnp.int32, (rows, seen), 1)
    allowed = (column >= row - positions) & (column <= row)
    return jnp.where(allowed, 0.0, MASKED_SCORE), seen


class AttendBack(Layer):
    work_steps = 2
    after_steps = 1
    length = 52.0

    def __init__(
        self, split, heads, own, w_in, w_out, cosine, sine, gain, positions, kept, projected, turned, out, lse
    ):
        rows = 2 * len(split.links) * own.shape[0]
        self.heads = heads
        super().__init__(
            split,
            own,
            (w_in, w_out, cosine, sine, gain, positions, kept, projected, turned, out, lse),
            (
                jax.ShapeDtypeStruct(w_in.shape, jnp.float32),
                jax.ShapeDtypeStruct(w_out.shape, jnp.float32),
                jax.ShapeDtypeStruct((8, heads.width), jnp.float32),
            ),
            (
                pltpu.VMEM((rows, heads.heads * HEAD), jnp.bfloat16),
                pltpu.VMEM((rows, heads.width), jnp.float32),
                pltpu.VMEM((rows, heads.width), jnp.bfloat16),
            ),
        )

    def open(self):
        _, self.w_in, self.w_out, self.cosine, self.sine, self.gain, self.positions = self.ins[:7]
        self.kept, self.projected, self.turned, self.out, self.lse = self.ins[7:]
        _, self.grad_in, self.grad_out, self.grad_gain = self.outs
        self.grad_heads, self.grad_turned, self.grad_projected = self.more

    def take(self, core, chip):
        grad = self.slots[core, chip]
        rows = self.at(core, chip)
        self.grad_heads[rows] = to_low(contract_last(grad, self.w_out[...]))
        term = contract_first(self.out[rows], grad)
        if (core, chip) == (0, 0):
            self.grad_out[...] = term
        else:
            self.grad_out[...] += term

    def work(self):
        factor = HEAD ** (-0.5)
        self.grad_turned[...] = jnp.zeros(self.grad_turned.shape, jnp.float32)
        self.grad_gain[...] = jnp.zeros(self.grad_gain.shape, jnp.float32)
        for place in range(2 * self.chips):
            rows = slice(place * self.rows, (place + 1) * self.rows)
            bias, seen = hidden_scores(self.positions[rows], place, self.rows)
            for head in range(self.heads.heads):
                own, key, value = self.heads.q(head), self.heads.k(head), self.heads.v(head)
                query, grad = self.turned[rows, own], self.grad_heads[rows, own]
                scores = contract_last(query, self.turned[:seen, key]) * factor + bias
                probs = jnp.exp(scores - self.lse[rows, head : head + 1])
                grad_probs = contract_last(grad, self.turned[:seen, value])
                row_dot = jnp.sum(probs * grad_probs, axis=-1, keepdims=True)
                grad_scores = to_low(probs * (grad_probs - row_dot))
                self.grad_turned[rows, own] = matmul(grad_scores, self.turned[:seen, key]) * factor
                self.grad_turned[:seen, key] += contract_first(grad_scores, query) * factor
                self.grad_turned[:seen, value] += contract_first(to_low(probs), grad)
            yield True
        for place in range(2 * self.chips):
            rows = slice(place * self.rows, (place + 1) * self.rows)
            for lanes, count in self.heads.tiles():
                low = to_low(self.grad_turned[rows, lanes])
                if count:
                    grad = low.astype(jnp.float32)
                    normed = grad * self.cosine[rows] + half_turned(grad * self.sine[rows])
                    raw = self.projected[rows, lanes]
                    scale = lax.rsqrt(head_means(raw * raw) + EPSILON)
                    unit = raw * scale
                    gain_term = self.heads.some(count, normed * unit, jnp.zeros_like(unit))
                    self.grad_gain[0:1, lanes] += jnp.sum(gain_term, axis=0, keepdims=True)
                    weighted = normed * self.gain[:, lanes]
                    back = scale * (weighted - unit * head_means(weighted * unit))
                    low = to_low(self.heads.some(count, back, grad))
                self.grad_projected[rows, lanes] = low
            yield True

    def give(self, core, chip):
        return contract_last(self.grad_projected[self.at(core, chip)], self.w_in[...])

    def after(self):
        for core, chip in self.places:
            term = contract_first(
                self.kept[core, chip], self.grad_projected[self.at(core, chip)]
            )
            if (core, chip) == (0, 0):
                self.grad_in[...] = term
            else:
                self.grad_in[...] += term
            yield True


class FeedForward(Job):
    works = True

    def span(self):
        return 60.0 if self.back and self.forward else 52.0

    def steps(self):
        return 3 * self.chips

    def __init__(self, split, normed, grad, w_in, w_down, forward):
        self.split, self.forward, self.back = split, forward, grad is not None
        self.chips = len(split.links)
        width = w_in.shape[0]
        gathered = normed if normed.ndim == 2 else grad
        given = (grad if normed.ndim == 2 else normed) if self.back else None
        self.gather_normed = normed.ndim == 2
        self.rows = gathered.shape[0]
        self.half = w_in.shape[1] // 2
        self.operands = (gathered, w_in, w_down) + (() if given is None else (given,))
        row_sum = jax.ShapeDtypeStruct((self.rows, width), jnp.float32)
        self.results, self.in_vmem = (), ()
        all_terms = (2, self.chips, self.rows, width)
        if self.back:
            if forward:
                self.results += (jax.ShapeDtypeStruct(all_terms, jnp.float32),)
                self.in_vmem += (False,)
            self.results += (
                row_sum,
                jax.ShapeDtypeStruct(w_in.shape, jnp.float32),
                jax.ShapeDtypeStruct(w_down.shape, jnp.float32),
            )
            self.in_vmem += (True, True, True)
        else:
            self.results += (row_sum, jax.ShapeDtypeStruct(all_terms, jnp.bfloat16))
            self.in_vmem += (True, False)
        self.masks = [mask for mask in split.links[1:]] + [(0, 1)]
        self.copies = Spread.copies(split) + 2 * self.chips - 1
        self.locals = 5 + 2 * self.chips
        all_rows = pltpu.VMEM((2, self.chips, self.rows, width), jnp.bfloat16)
        self.scratch = (
            (all_rows,)
            + ((all_rows,) if given is not None else ())
            + (pltpu.VMEM(w_in.shape, jnp.bfloat16), pltpu.VMEM(w_down.shape, jnp.bfloat16))
        )
        self.scratch += Return.scratch(self.chips, self.rows, width)
        if self.back and forward:
            self.scratch += (pltpu.VMEM((2, self.rows, width), jnp.float32),)

    def start(self):
        held = list(self.held)
        self.slots = held.pop(0)
        self.given = held.pop(0) if self.back else None
        self.w_in, self.w_down = held.pop(0), held.pop(0)
        outs = list(self.outs)
        self.terms = outs.pop(0) if self.back and self.forward else None
        self.sums = Return(self, Spread.copies(self.split), held[:5], outs.pop(0))
        self.staged = held[5] if self.terms is not None else None
        if self.back:
            self.grad_in, self.grad_down = outs
        else:
            self.kept = outs.pop(0)
        self.arrive = Spread(self, self.ins[0], self.slots, 0)
        self.loads = [
            self.near(1, self.ins[1], self.w_in),
            self.near(2, self.ins[2], self.w_down),
        ]
        self.rest = []
        if self.back:
            self.rest = [
                self.near(3 + 2 * chip + core, self.ins[3].at[core, chip], self.given.at[core, chip])
                for chip in range(self.chips)
                for core in (0, 1)
            ]
        for copy in self.loads + self.rest:
            copy.start()

    def middle(self):
        self.stores = []
        for chip in range(self.chips):
            for core in (0, 1):
                if chip == 1:
                    for other in self.arrive.direct:
                        self.arrive.ready(0, other)
                self.arrive.ready(core, chip)
                if (core, chip) == (0, 0):
                    self.loads[0].wait()
                    self.loads[1].wait()
                if self.back:
                    self.rest[2 * chip + core].wait()
                else:
                    self.store(
                        3 + 2 * chip + core, self.slots.at[core, chip], self.kept.at[core, chip]
                    )
                self.compute(core, chip)
                yield True
            self.sums.pass_on(chip)
            yield True

    def store(self, number, source, target):
        copy = self.near(number, source, target)
        copy.start()
        self.stores.append(copy)

    def compute(self, core, chip):
        arrived = self.slots[core, chip]
        normed = arrived if self.gather_normed else self.given[core, chip]
        both = matmul(normed, self.w_in[...])
        gate, upper = both[:, : self.half], both[:, self.half :]
        sigma = jax.nn.sigmoid(gate)
        active = gate * sigma
        hidden = to_low(active * upper)
        if self.terms is not None:
            count = len(self.stores)
            if count >= 2:
                self.stores[count - 2].wait()
            self.staged[count % 2] = matmul(hidden, self.w_down[...])
            self.store(
                3 + 2 * self.chips + count % 2,
                self.staged.at[count % 2],
                self.terms.at[core, chip],
            )
        elif self.forward:
            self.sums.put(core, chip, matmul(hidden, self.w_down[...]))
        if self.back:
            grad = self.given[core, chip] if self.gather_normed else arrived
            grad_hidden = contract_last(grad, self.w_down[...])
            grad_gate = to_low(grad_hidden * upper * (sigma * (1.0 + gate * (1.0 - sigma))))
            grad_upper = to_low(grad_hidden * active)
            grad_both = jnp.concatenate([grad_gate, grad_upper], axis=1)
            self.sums.put(core, chip, contract_last(grad_both, self.w_in[...]))
            if core == 0 and chip == 0:
                self.grad_in[...] = contract_first(normed, grad_both)
                self.grad_down[...] = contract_first(hidden, grad)
            else:
                self.grad_in[...] += contract_first(normed, grad_both)
                self.grad_down[...] += contract_first(hidden, grad)

    def finish(self):
        self.sums.finish()
        self.arrive.finish()
        for store in self.stores if self.terms is None else self.stores[-2:]:
            store.wait()


def all_masks():
    seq, dp = lax.axis_size("seq"), lax.axis_size("dp")
    return [(dp_mask, seq_mask) for dp_mask in range(dp) for seq_mask in range(seq)][1:]


class Hops(Job):
    def plan(self):
        seq, dp = lax.axis_size("seq"), lax.axis_size("dp")
        self.straight = seq * dp <= FEW
        if self.straight:
            self.masks = all_masks()
        else:
            self.masks = [(0, mask) for mask in range(1, seq)] + [
                (mask, 0) for mask in range(1, dp)
            ]


FEW = 1


class Everyone(Hops):
    def steps(self):
        return 1

    def __init__(self, value):
        self.operands = (value,)
        seq, dp = lax.axis_size("seq"), lax.axis_size("dp")
        self.results = (jax.ShapeDtypeStruct((dp, seq) + value.shape, value.dtype),)
        self.plan()
        self.copies = len(self.masks)
        self.locals = 1

    def post(self, number, source, index, mask):
        out = self.outs[0]
        away = (flipped(self.dp, mask[0]), flipped(self.seq, mask[1]))
        copy = self.away(number, source, out.at[index((self.dp, self.seq))], mask)
        copy.start()
        self.sent.append(copy)
        self.arrivals.append(self.away(number, source, out.at[index(away)], mask))

    def start(self):
        out = self.outs[0]
        self.mine = self.near(0, self.ins[0], out.at[self.dp, self.seq])
        self.mine.start()
        self.sent, self.arrivals = [], []
        for number, mask in enumerate(self.masks):
            if self.straight or not mask[0]:
                self.post(number, self.ins[0], lambda place: place, mask)

    def middle(self):
        if self.straight:
            return
        self.mine.wait()
        for arrival in self.arrivals:
            arrival.wait_recv()
        self.arrivals = []
        for number, mask in enumerate(self.masks):
            if mask[0]:
                self.post(number, self.outs[0].at[self.dp], lambda place: place[0], mask)
        yield True

    def finish(self):
        if self.straight:
            self.mine.wait()
        for arrival in self.arrivals:
            arrival.wait_recv()
        for copy in self.sent:
            copy.wait_send()


class SumAll(Hops):
    out_in_vmem = True

    def steps(self):
        return 1 if self.straight else 3

    def __init__(self, value):
        self.operands = (value,)
        self.results = (jax.ShapeDtypeStruct(value.shape, value.dtype),)
        seq, dp = value.shape[:2]
        self.plan()
        self.copies = 2 * len(self.masks)
        self.locals = 1
        self.scratch = (pltpu.VMEM(value.shape, jnp.float32),)
        if self.straight:
            self.scratch += (pltpu.VMEM((len(self.masks),) + value.shape[2:], jnp.float32),)
        else:
            self.scratch += (
                pltpu.VMEM((seq - 1,) + value.shape[1:], jnp.float32),
                pltpu.VMEM((dp - 1,) + value.shape[2:], jnp.float32),
            )

    def block(self, ref, mask, whole=False):
        seq, dp = flipped(self.seq, mask[1]), flipped(self.dp, mask[0])
        return ref.at[seq] if whole else ref.at[seq, dp]

    def round(self, masks, source, target):
        copies = []
        for number, mask in enumerate(masks):
            copy = self.away(self.number + number, source(mask), target(number, mask), mask)
            copy.start()
            copies.append(copy)
        self.number += len(masks)
        self.sent += copies
        return copies

    def start(self):
        self.load = self.near(0, self.ins[0], self.held[0])
        self.load.start()
        self.load.wait()
        self.number, self.sent = 0, []
        masks = [mask for mask in self.masks if self.straight or not mask[0]]
        self.first = self.round(
            masks,
            lambda mask: self.block(self.held[0], mask, not self.straight),
            lambda number, mask: self.held[1].at[number],
        )

    def arrived(self, masks, whole):
        out = self.outs[0]
        return [
            self.away(self.number + number, self.block(out, mask, whole), self.block(out, mask, whole), mask)
            for number, mask in enumerate(masks)
        ]

    def give_back(self, masks, whole):
        out = self.outs[0]
        arrivals = self.arrived(masks, whole)
        mine = self.block(out, (0, 0), whole)
        self.round(masks, lambda mask: mine, lambda number, mask: mine)
        return arrivals

    def middle(self):
        given, out = self.held[0], self.outs[0]
        for copy in self.first:
            copy.wait_recv()
        if self.straight:
            value = given[self.seq, self.dp]
            for number in range(len(self.masks)):
                value = value + self.held[1][number]
            out[self.seq, self.dp] = value
            self.last = self.give_back(self.masks, False)
            yield True
            return
        by_seq, by_dp = self.held[1:]
        part = given[self.seq]
        for number in range(len(self.first)):
            part = part + by_seq[number]
        given[self.seq] = part
        yield True
        masks = [mask for mask in self.masks if mask[0]]
        copies = self.round(
            masks,
            lambda mask: self.block(given, mask),
            lambda number, mask: by_dp.at[number],
        )
        for copy in copies:
            copy.wait_recv()
        value = given[self.seq, self.dp]
        for number in range(len(masks)):
            value = value + by_dp[number]
        out[self.seq, self.dp] = value
        yield True
        for arrival in self.give_back(masks, False):
            arrival.wait_recv()
        yield True
        self.last = self.give_back([mask for mask in self.masks if not mask[0]], True)

    def finish(self):
        for arrival in self.last:
            arrival.wait_recv()
        for copy in self.sent:
            copy.wait_send()


def drained(turn):
    for _ in turn:
        pass
    yield True


def in_order(jobs):
    bulk = STRETCH * sum(job.span() for job in jobs if job.bulk and not job.begin)
    steps = []
    for number, job in enumerate(jobs):
        turn, count = job.middle(), job.steps()
        span = bulk if job.bulk and not job.begin else job.span()
        if job.begin:
            steps.append((job.begin, number, -1, iter([job.start])))
        early = 0 if job.works else 1
        for step in range(count):
            steps.append((job.begin + (step + early) * span / count, number, step, turn))
        for step in range(job.last_steps()):
            steps.append((job.begin + span + 1.0, number, count + step, turn))
        steps.append((1000.0, number, count, drained(turn)))
    return [turn for _, _, _, turn in sorted(steps, key=lambda step: step[:3])]


class Courier:
    def __init__(self):
        self.calls = 0

    def __call__(self, *jobs):
        number = self.calls
        self.calls += 1
        masks = []
        for job in jobs:
            for mask in job.masks:
                if mask not in masks:
                    masks.append(mask)
        operands = [value for job in jobs for value in job.operands]
        results = [value for job in jobs for value in job.results]
        in_vmem, given = [], []
        for job in jobs:
            given += list(job.given_in_vmem or [False] * len(job.operands))
            in_vmem += list(job.in_vmem or [job.out_in_vmem] * len(job.results))
        scratch = []
        for job in jobs:
            scratch += list(job.scratch)
            scratch += [
                pltpu.SemaphoreType.DMA((max(1, job.copies),)),
                pltpu.SemaphoreType.DMA((max(1, job.copies),)),
                pltpu.SemaphoreType.DMA((max(1, job.locals),)),
            ]

        def kernel(*refs):
            ins = list(refs[: len(operands)])
            outs = list(refs[len(operands) : len(operands) + len(results)])
            held = list(refs[len(operands) + len(results) :])
            dp, seq = lax.axis_index("dp"), lax.axis_index("seq")
            barrier = pltpu.get_barrier_semaphore()
            for mask in masks:
                pl.semaphore_signal(
                    barrier,
                    inc=1,
                    device_id=(flipped(dp, mask[0]), flipped(seq, mask[1])),
                    device_id_type=MESH,
                )
            pl.semaphore_wait(barrier, len(masks))
            for job in jobs:
                count_in, count_out = len(job.operands), len(job.results)
                own = len(job.scratch)
                job.bind(
                    ins[:count_in], outs[:count_out], held[:own], *held[own : own + 3]
                )
                ins, outs, held = ins[count_in:], outs[count_out:], held[own + 3 :]
            for job in jobs:
                if not job.begin:
                    job.start()
            for turn in in_order(jobs):
                action = next(turn, None)
                if callable(action):
                    action()
            for job in jobs:
                job.finish()

        sent = sum(value.size * value.dtype.itemsize for value in operands)
        outs = pl.pallas_call(
            kernel,
            out_shape=results,
            in_specs=[
                pl.BlockSpec(memory_space=pltpu.VMEM if vmem else pl.ANY) for vmem in given
            ],
            out_specs=[
                pl.BlockSpec(memory_space=pltpu.VMEM if vmem else pl.ANY) for vmem in in_vmem
            ],
            scratch_shapes=scratch,
            compiler_params=pltpu.CompilerParams(
                collective_id=number, has_side_effects=True, vmem_limit_bytes=60 << 20
            ),
            cost_estimate=pl.CostEstimate(flops=0, bytes_accessed=8 * sent, transcendentals=0),
            name="courier_%d" % number,
        )(*operands)
        return outs


def packed(values, blocks):
    flat = jnp.concatenate([value.reshape(-1).astype(jnp.float32) for value in values])
    each = -(-flat.shape[0] // (blocks * 1024)) * 1024
    return jnp.pad(flat, (0, blocks * each - flat.shape[0])).reshape(blocks, each // 128, 128)


def unpacked(flat, values):
    flat = flat.reshape(-1)
    out, begin = [], 0
    for value in values:
        out.append(flat[begin : begin + value.size].reshape(value.shape))
        begin += value.size
    return out


def large_sum(values):
    seq, dp = lax.axis_size("seq"), lax.axis_size("dp")
    blocks = packed(values, seq * dp)
    return SumAll(blocks.reshape((seq, dp) + blocks.shape[1:]))


def small_sum(values):
    return Everyone(packed(values, 1)[0])


def local_call(kernel, name, results, operands, flops=0):
    moved = sum(value.size * value.dtype.itemsize for value in list(operands) + list(results))
    return pl.pallas_call(
        kernel,
        out_shape=results,
        in_specs=[pl.BlockSpec(memory_space=pltpu.VMEM)] * len(operands),
        out_specs=[pl.BlockSpec(memory_space=pltpu.VMEM)] * len(results),
        compiler_params=pltpu.CompilerParams(vmem_limit_bytes=56 << 20),
        cost_estimate=pl.CostEstimate(flops=flops, bytes_accessed=moved, transcendentals=0),
        name=name,
    )(*operands)


def pieces_by_rank(split, columns):
    dp_count, seq_count = lax.axis_size("dp"), lax.axis_size("seq")
    each = columns // (dp_count * seq_count)
    out = []
    for dp in range(dp_count):
        for seq in range(seq_count):
            out.append(
                (split.rank(dp, seq), split.copy(dp) * each, (dp * seq_count + seq) * each)
            )
    return each, out


def lowered_chunks(near, wide, attn_widths, mix_in, mix_out, attn_in, attn_out, ffn_in, ffn_out, vectors):
    seq_count = lax.axis_size("seq")
    rows, width = mix_out.shape
    hidden = ffn_in.shape[-1]
    channels, mine = width // seq_count, hidden // wide.ranks

    def kernel(mix_in, mix_out, attn_in, attn_out, ffn_in, ffn_out, vectors, *outs):
        mix_chunk, attn_chunk, one, two, low_mix_out, low_attn_out, down_one, down_two, block = outs
        each, pieces = pieces_by_rank(near, width)
        for part in range(3):
            for rank, inner, outer in pieces:
                mix_chunk[rank, :, pl.ds(part * channels + inner, each)] = to_low(
                    mix_in[:, pl.ds(part * width + outer, each)]
                )
        begin, target = 0, 0
        for columns in attn_widths:
            each = columns // seq_count
            for rank in range(seq_count):
                attn_chunk[rank, :, pl.ds(target, each)] = to_low(
                    attn_in[:, pl.ds(begin + rank * each, each)]
                )
            begin, target = begin + columns, target + each
        each, pieces = pieces_by_rank(wide, hidden)
        for layer, chunk in enumerate((one, two)):
            for part in range(2):
                for rank, inner, outer in pieces:
                    chunk[rank, :, pl.ds(part * mine + inner, each)] = to_low(
                        ffn_in[layer, part, :, pl.ds(outer, each)]
                    )
        low_mix_out[...] = to_low(mix_out[...])
        low_attn_out[...] = to_low(attn_out[...])
        down_one[...] = to_low(ffn_out[0])
        down_two[...] = to_low(ffn_out[1])
        block[...] = jnp.zeros(block.shape, jnp.bfloat16)
        block[pl.ds(0, vectors.shape[0]), pl.ds(0, vectors.shape[1])] = to_low(vectors[...])

    def low(*shape):
        return jax.ShapeDtypeStruct(shape, jnp.bfloat16)

    results = (
        low(seq_count, rows, 3 * channels),
        low(seq_count, rows, sum(attn_widths) // seq_count),
        low(wide.ranks, rows, 2 * mine),
        low(wide.ranks, rows, 2 * mine),
        low(*mix_out.shape),
        low(*attn_out.shape),
        low(*ffn_out.shape[1:]),
        low(*ffn_out.shape[1:]),
        low(16, 128),
    )
    return local_call(
        kernel,
        "lower",
        results,
        (mix_in, mix_out, attn_in, attn_out, ffn_in, ffn_out, vectors),
    )


LINE = 512


class Step:
    def __init__(self, weights):
        self.weights = weights
        self.matrices = []
        begin, line = 0, 0
        for number, weight in enumerate(weights):
            lead = weight.shape[:-2]
            rows, columns = weight.shape[-2:]
            indices = [()]
            for size in lead:
                indices = [index + (place,) for index in indices for place in range(size)]
            for index in indices:
                self.matrices.append((number, index, rows, columns, begin, line))
                begin += rows
                line += columns // LINE
        self.rows, self.scalars, self.weighted = begin, 2 * line, line
        devices = lax.axis_size("dp") * lax.axis_size("seq")
        self.devices = devices
        self.lines = -(-(2 * line + 1) // devices)
        self.sums = (lax.axis_size("seq"), lax.axis_size("dp"), self.lines, 1, LINE)

    def line(self, ref, number):
        per = self.lines
        dp = lax.axis_size("dp")
        return ref.at[number // (per * dp), (number // per) % dp, number % per]

    def natural(self):
        return [jax.ShapeDtypeStruct(weight.shape, jnp.float32) for weight in self.weights]

    def columns(self):
        return [
            jax.ShapeDtypeStruct(weight.shape[:-2] + (1, weight.shape[-1]), jnp.float32)
            for weight in self.weights
        ]

    def first(self, near, wide, attn_widths, traded, row_states, extra):
        seq_count = lax.axis_size("seq")

        def kernel(mix, attn, one, two, mix_out, attn_out, down_one, down_two, *refs):
            weights, (states, extra), refs = refs[:6], refs[6:8], refs[8:]
            grads, (rows_new, sums) = refs[:6], refs[6:]
            width = mix_out.shape[-1]
            channels = mix.shape[-1] // 3
            each, pieces = pieces_by_rank(near, width)
            for part in range(3):
                for rank, inner, outer in pieces:
                    grads[0][:, pl.ds(part * width + outer, each)] = mix[
                        rank, :, pl.ds(part * channels + inner, each)
                    ]
            grads[1][...] = mix_out[...]
            begin, source = 0, 0
            for columns in attn_widths:
                each = columns // seq_count
                for rank in range(seq_count):
                    grads[2][:, pl.ds(begin + rank * each, each)] = attn[
                        rank, :, pl.ds(source, each)
                    ]
                begin, source = begin + columns, source + each
            grads[3][...] = attn_out[...]
            hidden = grads[4].shape[-1]
            mine = one.shape[-1] // 2
            each, pieces = pieces_by_rank(wide, hidden)
            for layer, chunk in enumerate((one, two)):
                for part in range(2):
                    for rank, inner, outer in pieces:
                        grads[4][layer, part, :, pl.ds(outer, each)] = chunk[
                            rank, :, pl.ds(part * mine + inner, each)
                        ]
            grads[5][0] = down_one[...]
            grads[5][1] = down_two[...]
            lanes = lax.broadcasted_iota(jnp.int32, (1, LINE), 1)
            scalars = extra[...]
            for place in range(self.scalars + 1, self.lines * self.devices):
                self.line(sums, place)[...] = jnp.zeros((1, LINE), jnp.float32)
            for number, (which, index, rows, columns, begin, line) in enumerate(self.matrices):
                by_row = jnp.zeros((rows, LINE), jnp.float32)
                norm = jnp.zeros((1, LINE), jnp.float32)
                for strip in range(columns // LINE):
                    place = pl.ds(strip * LINE, LINE)
                    grad = grads[which][index + (slice(None), place)]
                    squares = grad * grad + SQUARE_FLOOR
                    by_row = by_row + squares
                    self.line(sums, line + strip)[...] = jnp.sum(squares, axis=0, keepdims=True)
                    weight = weights[which][index + (slice(None), place)]
                    norm = norm + jnp.sum(weight * weight, axis=0, keepdims=True)
                by_row = jnp.sum(by_row, axis=1, keepdims=True)
                norm = jnp.sum(norm, axis=1, keepdims=True)
                fresh = DECAY_RATE * states[pl.ds(begin, rows)] + (1.0 - DECAY_RATE) * (
                    by_row / columns
                )
                rows_new[pl.ds(begin, rows)] = fresh
                inverse = jnp.broadcast_to(1.0 / fresh, (rows, LINE))
                for strip in range(columns // LINE):
                    grad = grads[which][index + (slice(None), pl.ds(strip * LINE, LINE))]
                    self.line(sums, self.weighted + line + strip)[...] = jnp.sum(
                        grad * grad * inverse, axis=0, keepdims=True
                    )
                scalars = jnp.where(
                    lanes == number, jnp.sum(fresh, axis=0, keepdims=True), scalars
                )
                scalars = jnp.where(lanes == 16 + number, norm, scalars)
            self.line(sums, self.scalars)[...] = scalars

        results = self.natural() + [
            jax.ShapeDtypeStruct((self.rows, 1), jnp.float32),
            jax.ShapeDtypeStruct(self.sums, jnp.float32),
        ]
        return local_call(
            kernel, "step_first", results, tuple(traded) + tuple(self.weights) + (row_states, extra)
        )

    def second(self, grads, rows_new, sums, col_states):
        def kernel(*refs):
            grads, (rows_new, sums), refs = refs[:6], refs[6:8], refs[8:]
            states, weights, cols_out, outs = refs[:6], refs[6:12], refs[12:18], refs[18:]
            scalars = self.line(sums, self.scalars)[...]
            for number, (which, index, rows, columns, begin, line) in enumerate(self.matrices):
                strips = [
                    index + (slice(None), pl.ds(strip * LINE, LINE))
                    for strip in range(columns // LINE)
                ]
                norm = jnp.zeros((1, LINE), jnp.float32)
                for strip, spot in enumerate(strips):
                    cols_new = DECAY_RATE * states[which][spot] + (1.0 - DECAY_RATE) * (
                        self.line(sums, line + strip)[...] / (rows * self.devices)
                    )
                    cols_out[which][spot] = cols_new
                    norm = norm + self.line(sums, self.weighted + line + strip)[...] / cols_new
                count = rows * self.devices * columns
                mean_rows = scalars[:, number : number + 1] / (rows * self.devices)
                squares = mean_rows * jnp.sum(norm, axis=1, keepdims=True)
                divisor = jnp.maximum(1.0, jnp.sqrt(squares / count) / CLIP_LEVEL)
                rate = STEP_SCALE * jnp.maximum(
                    RATE_FLOOR, jnp.sqrt(scalars[:, 16 + number : 17 + number] / count)
                )
                scale = (rate / divisor) * jnp.sqrt(mean_rows)
                by_row = jnp.broadcast_to(
                    scale * lax.rsqrt(rows_new[pl.ds(begin, rows)]), (rows, LINE)
                )
                for spot in strips:
                    outs[which][spot] = weights[which][spot] - grads[which][spot] * (
                        by_row * lax.rsqrt(cols_out[which][spot])
                    )

        results = self.columns() + self.natural()
        outs = local_call(
            kernel,
            "step_second",
            results,
            tuple(grads) + (rows_new, sums) + tuple(col_states) + tuple(self.weights),
        )
        return outs[:6], outs[6:]


def moved_to_rank(shard):
    seq, dp = lax.axis_size("seq"), lax.axis_size("dp")
    pairs = [(block, (block % dp) * seq + block // dp) for block in range(seq * dp)]
    return lax.ppermute(shard, ("dp", "seq"), pairs)


def moved_to_owner(shard):
    seq, dp = lax.axis_size("seq"), lax.axis_size("dp")
    pairs = [((block % dp) * seq + block // dp, block) for block in range(seq * dp)]
    return lax.ppermute(shard, ("dp", "seq"), pairs)


def rows_of(value, like):
    return value.reshape((-1,) + like.shape)


def flat(value):
    return value.reshape(-1, value.shape[-1])


def to_trade(block, split):
    return block.reshape(split.ranks, -1, block.shape[-1])


def body(
    tokens,
    cotangent,
    lengths,
    mix_in,
    mix_in_rows,
    mix_in_cols,
    mix_out,
    mix_out_rows,
    mix_out_cols,
    attn_in,
    attn_in_rows,
    attn_in_cols,
    attn_out,
    attn_out_rows,
    attn_out_cols,
    ffn_in,
    ffn_in_rows,
    ffn_in_cols,
    ffn_out,
    ffn_out_rows,
    ffn_out_cols,
    vectors,
    vectors_moment,
    head_gain,
    head_moment,
):
    rows_here, width = tokens.shape
    seq_count = lax.axis_size("seq")
    devices = lax.axis_size("dp") * seq_count
    here = lax.axis_index("seq")
    courier = Courier()
    near, wide = Split(False), Split(True)
    total_rows = rows_here * seq_count
    positions = doc_layout(lengths[0], jnp.arange(total_rows, dtype=jnp.int32))[1]
    positions = positions[:, None]
    cosine, sine = turns_for(positions)
    channels = width // seq_count
    heads = HQ // seq_count
    kv_heads = KVH // seq_count
    kv_width = KVH * HEAD

    form = Heads(heads, kv_heads)
    head_gains = to_low(head_gain).astype(jnp.float32)
    gain_row = jnp.concatenate(
        [head_gains[0]] * heads + [head_gains[1]] * kv_heads + [jnp.ones(kv_heads * HEAD)]
    )[None]
    attn_widths = (width, kv_width, kv_width)
    (
        mix_chunk,
        attn_chunk,
        one_chunk,
        two_chunk,
        low_mix_out,
        attn_out_chunk,
        low_down_one,
        low_down_two,
        vector_block,
    ) = lowered_chunks(
        near, wide, attn_widths, mix_in, mix_out, attn_in, attn_out, ffn_in, ffn_out, vectors
    )
    attn_out_chunk = moved_to_rank(attn_out_chunk)
    mix_traded, gathered, moments, attn_traded, one_traded, two_traded = courier(
        Trade(near, mix_chunk),
        Everyone(vector_block),
        Everyone(
            jnp.pad(
                vectors_moment,
                ((0, 8 - vectors_moment.shape[0]), (0, 128 - vectors_moment.shape[1])),
            )
        ),
        Trade(near, attn_chunk),
        Trade(wide, one_chunk),
        Trade(wide, two_chunk),
    )
    gains = gathered.reshape(devices, 16, 128)[:, : vectors.shape[0], : vectors.shape[1]]
    gains = jnp.moveaxis(gains, 0, 1).reshape(-1, width).astype(jnp.float32)
    inputs = tokens.astype(jnp.float32)
    low_one, scale_one = normalize(inputs, gains[0])
    cotangent_all, *near_weights = courier(
        GatherTokens(wide, cotangent),
        GatherWeights(near, flat(mix_traded), 4),
        GatherWeights(near, low_mix_out),
    )
    w_mix_in, w_mix_out = (flat(value) for value in near_weights)
    taps = lax.dynamic_index_in_dim(
        gains[4:7].reshape(3, -1, seq_count, width // devices), here, 2, keepdims=False
    ).reshape(3, channels)

    taps = jnp.pad(taps, ((0, 5), (0, 0)))
    added, *mix_kept, w_in_one, w_down_one = courier(
        MixForward(near, to_low(low_one), w_mix_in, w_mix_out, taps, positions),
        GatherWeights(wide, flat(one_traded), 8, True),
        GatherWeights(wide, low_down_one, 3),
    )
    w_down_one = flat(w_down_one)
    first = inputs + added
    w_in_one = flat(w_in_one)
    normed_one, scale_two = normalize(first, gains[1])
    added, rows_one, w_attn_in, w_attn_out = courier(
        FeedForward(wide, to_low(normed_one), None, w_in_one, w_down_one, True),
        GatherWeights(near, flat(attn_traded), 4),
        GatherWeights(near, attn_out_chunk),
    )
    w_attn_in, w_attn_out = flat(w_attn_in), flat(w_attn_out)
    second = first + added

    normed_three, scale_three = normalize(second, gains[2])
    added, *attn_kept, w_in_two, w_down_two = courier(
        AttendForward(
            near, form, to_low(normed_three), w_attn_in, w_attn_out, cosine, sine, gain_row, positions
        ),
        GatherWeights(wide, flat(two_traded), 8, True),
        GatherWeights(wide, low_down_two, 3),
    )
    third = second + added
    w_in_two, w_down_two = flat(w_in_two), flat(w_down_two)
    normed_four, scale_four = normalize(third, gains[3])
    terms_two, grad_normed, grad_in_two, grad_down_two = courier(
        FeedForward(
            wide, to_low(normed_four), cotangent_all, w_in_two, w_down_two, True
        )
    )
    grad_branch, grad_gain_three = normalize_back(
        grad_normed, third, scale_four, gains[3]
    )
    grad_third = cotangent.astype(jnp.float32) + grad_branch
    (
        grad_normed_three,
        grad_attn_in,
        grad_attn_out,
        grad_heads,
        reduced_in_two,
        added,
    ) = courier(
        AttendBack(
            near,
            form,
            to_low(grad_third),
            w_attn_in,
            w_attn_out,
            cosine,
            sine,
            gain_row,
            positions,
            *attn_kept,
        ),
        ReduceWeights(wide, grad_in_two, 8, True),
        ScatterTokens(wide, terms_two),
    )
    fourth = third + added
    grad_heads = grad_heads[0].reshape(-1, HEAD)
    grad_head_q = jnp.sum(grad_heads[:heads], axis=0)
    grad_head_k = jnp.sum(grad_heads[heads : heads + kv_heads], axis=0)
    grad_branch_three, grad_gain_two = normalize_back(
        grad_normed_three, second, scale_three, gains[2]
    )
    grad_second = grad_third + grad_branch_three
    (
        grad_normed,
        grad_in_one,
        grad_down_one,
        reduced_down_two,
        reduced_attn_in,
        reduced_attn_out,
    ) = courier(
        FeedForward(wide, rows_one, to_low(grad_second), w_in_one, w_down_one, False),
        ReduceWeights(wide, grad_down_two, 6),
        ReduceWeights(near, grad_attn_in, 2),
        ReduceWeights(near, grad_attn_out),
    )
    grad_branch, grad_gain_one = normalize_back(
        grad_normed, first, scale_two, gains[1]
    )
    grad_first = grad_second + grad_branch
    mix_job = MixBack(near, to_low(grad_first), w_mix_in, w_mix_out, taps, positions, *mix_kept)
    one_job = ReduceWeights(wide, grad_in_one, 8, True)
    (
        grad_normed_one,
        grad_mix_in,
        grad_mix_out,
        tap_grads,
        reduced_down_one,
        _,
        two_back,
        attn_back,
        reduced_mix_in,
        one_back,
    ) = courier(
        mix_job,
        ReduceWeights(wide, grad_down_one, 6),
        one_job,
        Trade(wide, to_trade(reduced_in_two, wide)).later(20.0),
        Trade(near, to_trade(reduced_attn_in, near)).later(60.0),
        ReduceWeights(near, jax.ShapeDtypeStruct(w_mix_in.shape, jnp.float32), 4, of=(mix_job, 1)).later(70.0),
        TradeOf(wide, one_job).later(90.0),
    )
    tap_grads = tap_grads[:3]
    grad_branch_zero, grad_gain_zero = normalize_back(
        grad_normed_one, inputs, scale_one, gains[0]
    )
    token_grad = grad_first + grad_branch_zero

    gain_grads = jnp.stack([grad_gain_zero, grad_gain_one, grad_gain_two, grad_gain_three])
    tap_full = lax.dynamic_update_slice_in_dim(
        jnp.zeros((3, lax.axis_size("dp"), seq_count, width // devices), jnp.float32),
        tap_grads.reshape(3, lax.axis_size("dp"), 1, width // devices),
        here,
        2,
    ).reshape(3, width)
    early_parts = [
        jnp.concatenate([gain_grads, tap_full], axis=0),
        jnp.stack([grad_head_q, grad_head_k]),
        jnp.sum(vectors * vectors, axis=-1),
    ]
    reduced_mix_out, mix_back = courier(
        ReduceWeights(near, grad_mix_out),
        Trade(near, to_trade(reduced_mix_in, near)),
    )
    extra = jnp.zeros((1, LINE), jnp.float32)

    step = Step((mix_in, mix_out, attn_in, attn_out, ffn_in, ffn_out))
    row_states = (mix_in_rows, mix_out_rows, attn_in_rows, attn_out_rows, ffn_in_rows, ffn_out_rows)
    col_states = (mix_in_cols, mix_out_cols, attn_in_cols, attn_out_cols, ffn_in_cols, ffn_out_cols)
    *grads, rows_new, sums = step.first(
        near,
        wide,
        attn_widths,
        (
            mix_back,
            attn_back,
            one_back,
            two_back,
            reduced_mix_out,
            moved_to_owner(reduced_attn_out),
            reduced_down_one,
            reduced_down_two,
        ),
        jnp.concatenate([state.reshape(-1) for state in row_states])[:, None],
        extra,
    )
    sums, early = courier(SumAll(sums), large_sum(early_parts))
    full_grad, head_grad, vector_norm = unpacked(early, early_parts)
    full_moment = moments.reshape(devices, 8, 128)[:, : vectors.shape[0], : vectors.shape[1]]
    full_moment = jnp.moveaxis(full_moment, 0, 1).reshape(-1, width)
    full_update = full_grad * lax.rsqrt(
        DECAY_RATE * full_moment + (1.0 - DECAY_RATE) * (full_grad * full_grad + SQUARE_FLOOR)
    )
    vector_sums = jnp.sum(full_update * full_update, axis=-1)
    index = lax.axis_index("dp") * seq_count + here
    vector_grad = lax.dynamic_slice_in_dim(full_grad, index * vectors.shape[1], vectors.shape[1], 1)
    vector_moment_new = DECAY_RATE * vectors_moment + (1.0 - DECAY_RATE) * (
        vector_grad * vector_grad + SQUARE_FLOOR
    )
    vector_update = vector_grad * lax.rsqrt(vector_moment_new)
    cols_new, new_weights = step.second(
        grads, rows_new, sums, [state[..., None, :] for state in col_states]
    )
    new_rows, begin = [], 0
    for state in row_states:
        new_rows.append(rows_new[begin : begin + state.size, 0].reshape(state.shape))
        begin += state.size
    full_width = vectors.shape[-1] * devices
    vector_divisor = jnp.maximum(1.0, jnp.sqrt(vector_sums / full_width) / CLIP_LEVEL)
    vector_rate = STEP_SCALE * jnp.maximum(RATE_FLOOR, jnp.sqrt(vector_norm / full_width))
    vectors_new = vectors - (vector_rate / vector_divisor)[:, None] * vector_update
    head_moment_new = DECAY_RATE * head_moment + (1.0 - DECAY_RATE) * (
        head_grad * head_grad + SQUARE_FLOOR
    )
    head_update = head_grad * lax.rsqrt(head_moment_new)
    head_divisor = jnp.maximum(
        1.0, jnp.sqrt(jnp.mean(head_update * head_update, axis=-1, keepdims=True)) / CLIP_LEVEL
    )
    head_rate = STEP_SCALE * jnp.maximum(
        RATE_FLOOR, jnp.sqrt(jnp.mean(head_gain * head_gain, axis=-1, keepdims=True))
    )
    head_new = head_gain - head_rate / head_divisor * head_update
    outputs = [to_low(fourth), token_grad]
    for index in range(6):
        outputs += [grads[index], new_rows[index], cols_new[index][..., 0, :], new_weights[index]]
    return tuple(
        outputs
        + [vector_grad, vector_moment_new, vectors_new, head_grad, head_moment_new, head_new]
    )


def solution(mesh):
    return jax.shard_map(
        body,
        mesh=mesh,
        in_specs=(
            P(("dp", "seq"), None),
            P(("dp", "seq"), None),
            P("dp", None),
            P(("dp", "seq"), None),
            P(("dp", "seq")),
            P(),
            P(("dp", "seq"), None),
            P(("dp", "seq")),
            P(),
            P(("dp", "seq"), None),
            P(("dp", "seq")),
            P(),
            P(("dp", "seq"), None),
            P(("dp", "seq")),
            P(),
            P(None, None, ("dp", "seq"), None),
            P(None, None, ("dp", "seq")),
            P(),
            P(None, ("dp", "seq"), None),
            P(None, ("dp", "seq")),
            P(),
            P(None, ("dp", "seq")),
            P(None, ("dp", "seq")),
            P(),
            P(),
        ),
        out_specs=(
            P(("dp", "seq"), None),
            P(("dp", "seq"), None),
            P(("dp", "seq"), None),
            P(("dp", "seq")),
            P(),
            P(("dp", "seq"), None),
            P(("dp", "seq"), None),
            P(("dp", "seq")),
            P(),
            P(("dp", "seq"), None),
            P(("dp", "seq"), None),
            P(("dp", "seq")),
            P(),
            P(("dp", "seq"), None),
            P(("dp", "seq"), None),
            P(("dp", "seq")),
            P(),
            P(("dp", "seq"), None),
            P(None, None, ("dp", "seq"), None),
            P(None, None, ("dp", "seq")),
            P(),
            P(None, None, ("dp", "seq"), None),
            P(None, ("dp", "seq"), None),
            P(None, ("dp", "seq")),
            P(),
            P(None, ("dp", "seq"), None),
            P(None, ("dp", "seq")),
            P(None, ("dp", "seq")),
            P(None, ("dp", "seq")),
            P(),
            P(),
            P(),
        ),
        check_vma=False,
    )
```
